32 devices in a mesh: seq: 2 (over core), batch: 16 (over z, y, x).
Axes of the slice: x: 2, y: 2, z: 4, core: 2. Of those that a mesh axis runs over, the one named last changes fastest.
Arguments:
- activations: bfloat16 [32, 1024, 768], P('batch', 'seq'), may hold values from -6 to 6
- cotangent: bfloat16 [32, 1024, 768], P('batch', 'seq'), may hold values from -6 to 6
- lengths: int32 [32], P('batch'), may hold values from 512 to 1024, as said below
- weights_qkv: bfloat16 [2, 768, 2304], replicated, may hold values from -0.21875 to 0.21875
- conv_taps: float32 [2, 2304, 3], replicated, may hold values from -3 to 3
- weights_out: bfloat16 [2, 768, 768], replicated, may hold values from -0.875 to 0.875
- weights_up: bfloat16 [2, 768, 3072], replicated, may hold values from -0.21875 to 0.21875
- weights_down: bfloat16 [2, 3072, 768], replicated, may hold values from -0.109375 to 0.109375
- norm_gains: float32 [2, 768, 2], replicated, may hold values from 0.5 to 1.5
- norm_biases: float32 [2, 768, 2], replicated, may hold values from -1.8 to 1.8
Outputs:
- block_out: bfloat16 [32, 1024, 768], P('batch', 'seq')
- grad_input: bfloat16 [32, 1024, 768], P('batch', 'seq')
- grad_qkv: float32 [2, 768, 2304], P(None, ('seq', 'batch'))
- grad_taps: float32 [2, 2304, 3], P(None, ('seq', 'batch'))
- grad_out: float32 [2, 768, 768], P(None, ('seq', 'batch'))
- grad_up: float32 [2, 768, 3072], P(None, ('seq', 'batch'))
- grad_down: float32 [2, 3072, 768], P(None, ('seq', 'batch'))
- grad_gains: float32 [2, 768, 2], P(None, ('seq', 'batch'))
- grad_biases: float32 [2, 768, 2], P(None, ('seq', 'batch'))
The draws below stay inside these ranges and needn't reach their ends.
Inputs may be any that keep to these rules, and one draw needn't show every extreme that they name: `lengths`: each value is 1024 or 512; among the 2 sequences of one index of batch (an aligned block of 2 entries) one, chosen by the seed, has 1024.
All inputs are finite; a program needn't handle non-finite values.
Results may differ from the reference program's by a relative error of at most 0.02.
Values may be sent and summed in bfloat16 or wider, within the bound.
A program may use at most 384 MiB of HBM per device.

```python
import jax
import jax.numpy as jnp
from jax import lax

D = 768
HEADS = 12
HEAD_DIM = 64
FF = 3072
LAYERS = 2
SEQS = 2
CAP = 1024
SEQS_ALL = 32


def draw_lengths(key, part):
    key = jax.random.fold_in(key, 7)
    pick_key, coin_key = jax.random.split(key)
    groups = SEQS_ALL // SEQS
    chosen = jax.random.randint(pick_key, (groups,), 0, SEQS)
    flips = jax.random.randint(coin_key, (groups, SEQS), 0, 2)
    longer = (jnp.arange(SEQS)[None, :] == chosen[:, None]) | (flips == 1)
    return jnp.where(longer, CAP, CAP // 2).astype(jnp.int32).reshape(SEQS_ALL)


def shard_levels(key, shape, shards, low, high):
    loudness = 1.0
    for axis_at, shards_of in shards:
        steps = jax.random.uniform(jax.random.fold_in(jax.random.fold_in(key, 6), axis_at), (shards_of,), jnp.float32, low / len(shards), high / len(shards))
        loudness = loudness * jnp.repeat(jnp.exp(steps), shape[axis_at] // shards_of).reshape((-1,) + (1,) * (len(shape) - 1 - axis_at))
    return loudness


def centred(rng, shape, scale, most, cuts=(), held_as=jnp.bfloat16):
    level = shard_levels(rng, shape, cuts, -0.22, 0.18) if cuts else 1.0
    entries = jax.random.normal(rng, shape, jnp.float32) * scale * level
    return jnp.minimum(jnp.maximum(entries, -most), most).astype(held_as)


def setup_inputs(seed: int = 0) -> dict:
    splits = jax.random.split(jax.random.key(seed), 11)
    return {
        "activations": centred(splits[0], (SEQS_ALL, CAP, D), 1.0, 6.0, ((0, 16), (1, 2))),
        "cotangent": centred(splits[1], (SEQS_ALL, CAP, D), 1.0, 6.0, ((0, 16), (1, 2))),
        "lengths": draw_lengths(jax.random.fold_in(splits[10], 71), 0),
        "weights_qkv": centred(splits[3], (LAYERS, D, 3 * D), D ** -0.5, 0.21875),
        "conv_taps": centred(splits[4], (LAYERS, 3 * D, 3), 0.6, 3.0, (), jnp.float32),
        "weights_out": centred(splits[5], (LAYERS, D, D), (D // 16) ** -0.5, 0.875),
        "weights_up": centred(splits[6], (LAYERS, D, FF), D ** -0.5, 0.21875),
        "weights_down": centred(splits[7], (LAYERS, FF, D), FF ** -0.5, 0.109375),
        "norm_gains": jnp.clip(1.0 + 0.1 * jax.random.normal(splits[8], (LAYERS, D, 2), jnp.float32), 0.5, 1.5),
        "norm_biases": centred(splits[9], (LAYERS, D, 2), 0.3, 1.8, (), jnp.float32),
    }


@jax.custom_vjp
def low(v):
    return lax.optimization_barrier(v.astype(jnp.bfloat16)).astype(jnp.float32)

@jax.custom_vjp
def low_back(v):
    return v

def low_keep(v):
    return (low(v), None)

def low_pass(kept, grad):
    return (grad,)

def back_keep(v):
    return (v, None)

def back_low(kept, grad):
    return (low(grad),)
low.defvjp(low_keep, low_pass)
low_back.defvjp(back_keep, back_low)

def norm_of(stream, gain, offset):
    average = lax.optimization_barrier(jnp.mean(stream, -1, keepdims=True))
    centered = stream - average
    variance = lax.optimization_barrier(jnp.mean(centered * centered, -1, keepdims=True))
    return centered * lax.rsqrt(variance + 1e-05) * gain + offset

def matmul(left, right):
    return jnp.einsum('std,df->stf', left, right, precision=lax.Precision.HIGHEST)

def attend_one(items):
    query_seq, key_seq, value_seq, length = items
    heads_q = query_seq.reshape(CAP, HEADS, HEAD_DIM)
    heads_k = key_seq.reshape(CAP, HEADS, HEAD_DIM)
    heads_v = value_seq.reshape(CAP, HEADS, HEAD_DIM)
    scores = jnp.einsum('qhd,khd->hqk', heads_q, heads_k, precision=lax.Precision.HIGHEST) * HEAD_DIM ** (-0.5)
    scores = low_back(scores)
    places = jnp.arange(CAP)
    allowed = (places[None, :] < length) & ((places[None, :] <= places[:, None]) | (places[:, None] >= length))
    masked = jnp.where(allowed[None], scores, -1e+30)
    highest = lax.optimization_barrier(jnp.max(masked, -1, keepdims=True))
    expo = jnp.exp(masked - highest)
    probs = expo / lax.optimization_barrier(jnp.sum(expo, -1, keepdims=True))
    mixed = jnp.einsum('hqk,khd->qhd', low(probs), heads_v, precision=lax.Precision.HIGHEST)
    return low_back(low(mixed.reshape(CAP, HEADS * HEAD_DIM)))

def block(stream, lengths, w_qkv, taps, w_out, w_up, w_down, gains, offsets):
    width = stream.shape[-1]
    attn_in = low(norm_of(stream, gains[:, 0], offsets[:, 0]))
    projected = low_back(matmul(attn_in, w_qkv))
    padded = jnp.pad(projected, ((0, 0), (2, 0), (0, 0)))
    conv_out = taps[:, 0] * projected + taps[:, 1] * padded[:, 1:-1] + taps[:, 2] * padded[:, :-2]
    mixed_qkv = low(conv_out)
    queries = mixed_qkv[..., :width]
    keys_all = mixed_qkv[..., width:2 * width]
    values_all = mixed_qkv[..., 2 * width:]
    attended = lax.map(jax.checkpoint(attend_one), (queries, keys_all, values_all, lengths))
    middle = stream + low_back(matmul(attended, w_out))
    ff_in = low(norm_of(middle, gains[:, 1], offsets[:, 1]))
    hidden_pre = low_back(matmul(ff_in, w_up))
    hidden = low(jax.nn.relu(hidden_pre) ** 2)
    return middle + low_back(matmul(hidden, w_down))

def reference(activations, cotangent, lengths, weights_qkv, conv_taps, weights_out, weights_up, weights_down, norm_gains, norm_biases):

    def forward(inputs, w_qkv, taps, w_out, w_up, w_down, gains, offsets):
        stream = inputs
        for layer_num in range(LAYERS):
            stream = block(stream, lengths, w_qkv[layer_num], taps[layer_num], w_out[layer_num], w_up[layer_num], w_down[layer_num], gains[layer_num], offsets[layer_num])
        return stream
    result, pull = jax.vjp(forward, activations.astype(jnp.float32), weights_qkv.astype(jnp.float32), conv_taps.astype(jnp.float32), weights_out.astype(jnp.float32), weights_up.astype(jnp.float32), weights_down.astype(jnp.float32), norm_gains.astype(jnp.float32), norm_biases.astype(jnp.float32))
    grads = pull(cotangent.astype(jnp.float32))
    return (result.astype(jnp.bfloat16), grads[0].astype(jnp.bfloat16), grads[1], grads[2], grads[3], grads[4], grads[5], grads[6], grads[7])
```

```python
import functools

import jax
import jax.numpy as jnp
from jax import lax
from jax.experimental import pallas as pl
from jax.experimental.pallas import tpu as pltpu
from jax.sharding import PartitionSpec as P

HEAD_DIM = 64
LAYERS = 2


def shifted(x, axis, by):
    size = lax.axis_size(axis)
    pairs = [(i, i + by) for i in range(size) if 0 <= i + by < size]
    return lax.ppermute(x, axis, pairs)


def normalize(stream):
    average = jnp.mean(stream, -1, keepdims=True)
    centered = stream - average
    scaling = lax.rsqrt(jnp.mean(centered * centered, -1, keepdims=True) + 1e-05)
    return (centered * scaling, scaling)


def norm_back(grad_norm, normed, scaling, gain):
    scaled = grad_norm * gain
    return scaling * (
        scaled
        - jnp.mean(scaled, -1, keepdims=True)
        - normed * jnp.mean(scaled * normed, -1, keepdims=True)
    )


def split_heads(block):
    return block.reshape(block.shape[0], -1, HEAD_DIM)


def masked_scores(query_seq, key_seq, length, positions):
    scores = jnp.einsum(
        "qhd,khd->hqk",
        split_heads(query_seq),
        split_heads(key_seq),
        preferred_element_type=jnp.float32,
    ) * HEAD_DIM ** (-0.5)
    key_place = jnp.arange(key_seq.shape[0], dtype=jnp.int32)
    allowed = (key_place[None, :] < length) & (
        (key_place[None, :] <= positions[:, None]) | (positions[:, None] >= length)
    )
    return jnp.where(allowed[None], scores, -1e30)


def attention_forward(queries, keys_all, values_all, lengths, positions):

    def one_sequence(items):
        query_seq, key_seq, value_seq, length = items
        scores = masked_scores(query_seq, key_seq, length, positions)
        highest = jnp.max(scores, -1, keepdims=True)
        expo = jnp.exp(scores - highest)
        totals = jnp.sum(expo, -1, keepdims=True)
        probs = (expo / totals).astype(jnp.bfloat16)
        mixed = jnp.einsum(
            "hqk,khd->qhd", probs, split_heads(value_seq), preferred_element_type=jnp.float32
        )
        log_total = (highest + jnp.log(totals))[..., 0]
        return (mixed.reshape(query_seq.shape).astype(jnp.bfloat16), log_total)

    return lax.map(one_sequence, (queries, keys_all, values_all, lengths))


def attention_backward(
    queries, keys_all, values_all, lengths, positions, log_totals, grad_attended
):

    def one_sequence(items):
        query_seq, key_seq, value_seq, length, log_total, grad_seq = items
        scores = masked_scores(query_seq, key_seq, length, positions)
        probs = jnp.exp(scores - log_total[..., None])
        grad_heads = split_heads(grad_seq)
        grad_probs = jnp.einsum(
            "qhd,khd->hqk", grad_heads, split_heads(value_seq), preferred_element_type=jnp.float32
        )
        inner = jnp.sum(probs * grad_probs, -1, keepdims=True)
        grad_scores = (probs * (grad_probs - inner)).astype(jnp.bfloat16)
        grad_query = jnp.einsum(
            "hqk,khd->qhd", grad_scores, split_heads(key_seq), preferred_element_type=jnp.float32
        ) * HEAD_DIM ** (-0.5)
        grad_key = jnp.einsum(
            "hqk,qhd->khd", grad_scores, split_heads(query_seq), preferred_element_type=jnp.float32
        ) * HEAD_DIM ** (-0.5)
        grad_value = jnp.einsum(
            "hqk,qhd->khd",
            probs.astype(jnp.bfloat16),
            grad_heads,
            preferred_element_type=jnp.float32,
        )
        return (
            grad_query.reshape(query_seq.shape),
            grad_key.reshape(key_seq.shape),
            grad_value.reshape(key_seq.shape),
        )

    return lax.map(
        one_sequence, (queries, keys_all, values_all, lengths, log_totals, grad_attended)
    )


def layer_forward(stream, lengths, positions, w_qkv, taps, w_out, w_up, w_down, gains, offsets):
    seqs_here, rows, width = stream.shape
    tokens = seqs_here * rows
    normed_one, scale_one = normalize(stream)
    attn_in = (normed_one * gains[:, 0] + offsets[:, 0]).astype(jnp.bfloat16)
    projected = jnp.dot(
        attn_in.reshape(tokens, width), w_qkv, preferred_element_type=jnp.float32
    ).reshape(seqs_here, rows, 3 * width)
    before = shifted(projected[:, rows - 2 :, :].astype(jnp.bfloat16), "seq", 1).astype(jnp.float32)
    extended = jnp.concatenate([before, projected], 1)
    conv_out = (
        taps[:, 0] * extended[:, 2:]
        + taps[:, 1] * extended[:, 1 : rows + 1]
        + taps[:, 2] * extended[:, :rows]
    )
    mixed_qkv = conv_out.astype(jnp.bfloat16)
    queries = mixed_qkv[..., :width]
    keys_here = mixed_qkv[..., width : 2 * width]
    values_here = mixed_qkv[..., 2 * width :]
    keys_all, values_all = (
        lax.all_gather(keys_here, "seq", axis=1, tiled=True),
        lax.all_gather(values_here, "seq", axis=1, tiled=True),
    )
    attended, log_totals = attention_forward(queries, keys_all, values_all, lengths, positions)
    branch = jnp.dot(attended.reshape(tokens, width), w_out, preferred_element_type=jnp.float32)
    middle = stream + branch.reshape(stream.shape)
    normed_two, scale_two = normalize(middle)
    ff_in = (normed_two * gains[:, 1] + offsets[:, 1]).astype(jnp.bfloat16).reshape(tokens, width)
    hidden_pre = jnp.dot(ff_in, w_up, preferred_element_type=jnp.float32)
    hidden = (jax.nn.relu(hidden_pre) ** 2).astype(jnp.bfloat16)
    result = middle + jnp.dot(hidden, w_down, preferred_element_type=jnp.float32).reshape(
        stream.shape
    )
    kept_keys = (keys_all, values_all)
    saved = (
        normed_one,
        scale_one,
        attn_in,
        extended,
        queries,
        kept_keys,
        attended,
        log_totals,
        normed_two,
        scale_two,
        ff_in,
        hidden_pre,
        hidden,
    )
    return (result, saved)


def layer_backward(grad_stream, lengths, positions, saved, w_qkv, taps, w_out, w_up, w_down, gains):
    (
        normed_one,
        scale_one,
        attn_in,
        extended,
        queries,
        kept_keys,
        attended,
        log_totals,
        normed_two,
        scale_two,
        ff_in,
        hidden_pre,
        hidden,
    ) = saved
    seqs_here, rows, width = grad_stream.shape
    tokens = seqs_here * rows
    grad_down_in = grad_stream.reshape(tokens, width).astype(jnp.bfloat16)
    grad_down = jnp.einsum("tf,td->fd", hidden, grad_down_in, preferred_element_type=jnp.float32)
    grad_hidden = jnp.dot(grad_down_in, w_down.T, preferred_element_type=jnp.float32)
    grad_pre = (grad_hidden * 2.0 * jax.nn.relu(hidden_pre)).astype(jnp.bfloat16)
    grad_up = jnp.einsum("td,tf->df", ff_in, grad_pre, preferred_element_type=jnp.float32)
    grad_ffin = jnp.dot(grad_pre, w_up.T, preferred_element_type=jnp.float32).reshape(
        grad_stream.shape
    )
    gain_two = jnp.sum(grad_ffin * normed_two, (0, 1))
    offset_two = jnp.sum(grad_ffin, (0, 1))
    grad_middle = grad_stream + norm_back(grad_ffin, normed_two, scale_two, gains[:, 1])
    grad_branch = grad_middle.reshape(tokens, width).astype(jnp.bfloat16)
    grad_out = jnp.einsum(
        "td,te->de",
        attended.reshape(tokens, width),
        grad_branch,
        preferred_element_type=jnp.float32,
    )
    grad_attended = jnp.dot(grad_branch, w_out.T, preferred_element_type=jnp.float32)
    grad_attended = grad_attended.astype(jnp.bfloat16).reshape(grad_stream.shape)
    keys_all, values_all = kept_keys
    grad_query, grad_key_all, grad_value_all = attention_backward(
        queries, keys_all, values_all, lengths, positions, log_totals, grad_attended
    )
    grad_key, grad_value = (
        lax.psum_scatter(
            grad_key_all.astype(jnp.bfloat16), "seq", scatter_dimension=1, tiled=True
        ).astype(jnp.float32),
        lax.psum_scatter(
            grad_value_all.astype(jnp.bfloat16), "seq", scatter_dimension=1, tiled=True
        ).astype(jnp.float32),
    )
    grad_conv = jnp.concatenate([grad_query, grad_key, grad_value], -1)
    after = shifted(grad_conv[:, :2, :].astype(jnp.bfloat16), "seq", -1).astype(jnp.float32)
    grad_ext = jnp.concatenate([grad_conv, after], 1)
    grad_proj = (
        taps[:, 0] * grad_ext[:, :rows]
        + taps[:, 1] * grad_ext[:, 1 : rows + 1]
        + taps[:, 2] * grad_ext[:, 2:]
    )
    grad_taps = jnp.stack(
        [
            jnp.sum(grad_conv * extended[:, 2:], (0, 1)),
            jnp.sum(grad_conv * extended[:, 1 : rows + 1], (0, 1)),
            jnp.sum(grad_conv * extended[:, :rows], (0, 1)),
        ],
        -1,
    )
    grad_proj_low = grad_proj.reshape(tokens, 3 * width).astype(jnp.bfloat16)
    grad_qkv = jnp.einsum(
        "td,tf->df",
        attn_in.reshape(tokens, width),
        grad_proj_low,
        preferred_element_type=jnp.float32,
    )
    grad_attn_in = jnp.dot(grad_proj_low, w_qkv.T, preferred_element_type=jnp.float32).reshape(
        grad_stream.shape
    )
    gain_one = jnp.sum(grad_attn_in * normed_one, (0, 1))
    offset_one = jnp.sum(grad_attn_in, (0, 1))
    grad_input = grad_middle + norm_back(grad_attn_in, normed_one, scale_one, gains[:, 0])
    grad_gains = jnp.stack([gain_one, gain_two], -1)
    grad_biases = jnp.stack([offset_one, offset_two], -1)
    return (
        grad_input,
        (grad_qkv, grad_taps, grad_out, grad_up, grad_down, grad_gains, grad_biases),
    )


def reduce_grads(grad_qkv, grad_taps, grad_out, grad_up, grad_down, grad_gains, grad_biases):
    part_qkv, part_taps, part_out, part_up, part_down, part_gains, part_biases = (
        lax.psum_scatter(
            grad_qkv.astype(jnp.bfloat16), "seq", scatter_dimension=0, tiled=True
        ).astype(jnp.float32),
        lax.psum_scatter(
            grad_taps.astype(jnp.bfloat16), "seq", scatter_dimension=0, tiled=True
        ).astype(jnp.float32),
        lax.psum_scatter(
            grad_out.astype(jnp.bfloat16), "seq", scatter_dimension=0, tiled=True
        ).astype(jnp.float32),
        lax.psum_scatter(
            grad_up.astype(jnp.bfloat16), "seq", scatter_dimension=0, tiled=True
        ).astype(jnp.float32),
        lax.psum_scatter(
            grad_down.astype(jnp.bfloat16), "seq", scatter_dimension=0, tiled=True
        ).astype(jnp.float32),
        lax.psum_scatter(
            grad_gains.astype(jnp.bfloat16), "seq", scatter_dimension=0, tiled=True
        ).astype(jnp.float32),
        lax.psum_scatter(
            grad_biases.astype(jnp.bfloat16), "seq", scatter_dimension=0, tiled=True
        ).astype(jnp.float32),
    )
    return (
        lax.psum_scatter(
            part_qkv.astype(jnp.bfloat16), "batch", scatter_dimension=0, tiled=True
        ).astype(jnp.float32),
        lax.psum_scatter(
            part_taps.astype(jnp.bfloat16), "batch", scatter_dimension=0, tiled=True
        ).astype(jnp.float32),
        lax.psum_scatter(
            part_out.astype(jnp.bfloat16), "batch", scatter_dimension=0, tiled=True
        ).astype(jnp.float32),
        lax.psum_scatter(
            part_up.astype(jnp.bfloat16), "batch", scatter_dimension=0, tiled=True
        ).astype(jnp.float32),
        lax.psum_scatter(
            part_down.astype(jnp.bfloat16), "batch", scatter_dimension=0, tiled=True
        ).astype(jnp.float32),
        lax.psum_scatter(
            part_gains.astype(jnp.bfloat16), "batch", scatter_dimension=0, tiled=True
        ).astype(jnp.float32),
        lax.psum_scatter(
            part_biases.astype(jnp.bfloat16), "batch", scatter_dimension=0, tiled=True
        ).astype(jnp.float32),
    )


def local(
    activations,
    cotangent,
    lengths,
    weights_qkv,
    conv_taps,
    weights_out,
    weights_up,
    weights_down,
    norm_gains,
    norm_biases,
):
    seqs_here, rows, width = activations.shape
    positions = lax.axis_index("seq") * rows + jnp.arange(rows, dtype=jnp.int32)
    stream = activations.astype(jnp.float32)
    saved_all = []
    for layer_num in range(LAYERS):
        stream, saved = layer_forward(
            stream,
            lengths,
            positions,
            weights_qkv[layer_num],
            conv_taps[layer_num],
            weights_out[layer_num],
            weights_up[layer_num],
            weights_down[layer_num],
            norm_gains[layer_num],
            norm_biases[layer_num],
        )
        saved_all.append(saved)
    block_out = stream.astype(jnp.bfloat16)
    grad_stream = cotangent.astype(jnp.float32)
    collected = []
    for layer_num in reversed(range(LAYERS)):
        grad_stream, layer_grads = layer_backward(
            grad_stream,
            lengths,
            positions,
            saved_all[layer_num],
            weights_qkv[layer_num],
            conv_taps[layer_num],
            weights_out[layer_num],
            weights_up[layer_num],
            weights_down[layer_num],
            norm_gains[layer_num],
        )
        grad_qkv, grad_taps, grad_out, grad_up, grad_down, grad_gains, grad_biases = layer_grads
        collected.append(
            reduce_grads(grad_qkv, grad_taps, grad_out, grad_up, grad_down, grad_gains, grad_biases)
        )
    collected = collected[::-1]
    stacked = [jnp.stack([member[index] for member in collected], 0) for index in range(7)]
    return (
        block_out,
        grad_stream.astype(jnp.bfloat16),
        stacked[0],
        stacked[1],
        stacked[2],
        stacked[3],
        stacked[4],
        stacked[5],
        stacked[6],
    )


TILE = 256
LANES = 128
MIB = 2**20


def dot_nt(left, right):
    return lax.dot_general(
        left, right, (((1,), (1,)), ((), ())), preferred_element_type=jnp.float32
    )


def dot_nn(left, right):
    return lax.dot_general(
        left, right, (((1,), (0,)), ((), ())), preferred_element_type=jnp.float32
    )


def dot_tn(left, right):
    return lax.dot_general(
        left, right, (((0,), (0,)), ((), ())), preferred_element_type=jnp.float32
    )


def head_lanes(head):
    lane = lax.broadcasted_iota(jnp.int32, (1, LANES), 1)
    return (lane >= head * HEAD_DIM) & (lane < (head + 1) * HEAD_DIM)


def causal_tile():
    keys = lax.broadcasted_iota(jnp.int32, (TILE, TILE), 0)
    queries = lax.broadcasted_iota(jnp.int32, (TILE, TILE), 1)
    return keys <= queries


def attend_kernel(length_ref, conv_ref, out_ref, log_ref):
    cap = conv_ref.shape[2]
    whole = length_ref[pl.program_id(0)] == cap
    queries = conv_ref[0, 0]
    keys = conv_ref[0, 1] * jnp.bfloat16(HEAD_DIM**-0.5)
    keys = [jnp.where(head_lanes(head), keys, jnp.bfloat16(0)) for head in range(2)]
    values_t = conv_ref[0, 2].T

    def query_block(block, key_count, diagonal):
        rows = slice(block * TILE, (block + 1) * TILE)
        mixed = []
        for head in range(2):
            below = key_count - TILE if diagonal else key_count
            parts = []
            if below:
                parts.append(dot_nt(keys[head][:below], queries[rows]))
            if diagonal:
                tile = dot_nt(keys[head][below:key_count], queries[rows])
                parts.append(jnp.where(causal_tile(), tile, -1e30))
            highest = functools.reduce(
                jnp.maximum, [jnp.max(part, 0, keepdims=True) for part in parts]
            )
            expo = [jnp.exp(part - highest) for part in parts]
            total = sum(jnp.sum(part, 0, keepdims=True) for part in expo)
            value_head = values_t[head * HEAD_DIM : (head + 1) * HEAD_DIM]
            got, at = None, 0
            for part in expo:
                size = part.shape[0]
                term = dot_nn(value_head[:, at : at + size], part.astype(jnp.bfloat16))
                got = term if got is None else got + term
                at += size
            mixed.append(got / total)
            log_ref[0, 0, head : head + 1, rows] = highest + jnp.log(total)
        out_ref[0, rows, :] = jnp.concatenate(mixed, 0).T.astype(jnp.bfloat16)

    blocks = cap // TILE
    for block in range(blocks // 2):
        query_block(block, (block + 1) * TILE, True)

    @pl.when(whole)
    def _():
        for block in range(blocks // 2, blocks):
            query_block(block, (block + 1) * TILE, True)

    @pl.when(jnp.logical_not(whole))
    def _():
        for block in range(blocks // 2, blocks):
            query_block(block, cap // 2, False)


def attend(mixed, lengths):
    seqs, _, cap, width = mixed.shape
    pairs = width // LANES
    return pl.pallas_call(
        attend_kernel,
        grid_spec=pltpu.PrefetchScalarGridSpec(
            num_scalar_prefetch=1,
            grid=(seqs, pairs),
            in_specs=[pl.BlockSpec((1, 3, cap, LANES), lambda s, p, n: (s, 0, 0, p))],
            out_specs=[
                pl.BlockSpec((1, cap, LANES), lambda s, p, n: (s, 0, p)),
                pl.BlockSpec((1, 1, 2, cap), lambda s, p, n: (s, p, 0, 0)),
            ],
        ),
        out_shape=[
            jax.ShapeDtypeStruct((seqs, cap, width), jnp.bfloat16),
            jax.ShapeDtypeStruct((seqs, pairs, 2, cap), jnp.float32),
        ],
        compiler_params=pltpu.CompilerParams(vmem_limit_bytes=48 * MIB),
        cost_estimate=pl.CostEstimate(
            flops=30_000_000_000, bytes_accessed=8_000_000, transcendentals=8_000_000
        ),
        name="attend",
    )(lengths, mixed)


def attend_back_kernel(
    length_ref,
    conv_ref,
    proj_ref,
    grad_ref,
    out_ref,
    log_ref,
    taps_ref,
    back_ref,
    grad_taps_ref,
    query_t_acc,
    shift_acc,
):
    cap = conv_ref.shape[2]
    whole = length_ref[pl.program_id(0)] == cap
    factor = jnp.bfloat16(HEAD_DIM**-0.5)
    queries = conv_ref[0, 0] * factor
    grads = grad_ref[0]
    keys_t = (conv_ref[0, 1] * factor).T
    product_t = (grads.astype(jnp.float32) * out_ref[0].astype(jnp.float32)).T
    inner = [
        jnp.sum(product_t[head * HEAD_DIM : (head + 1) * HEAD_DIM], 0, keepdims=True)
        for head in range(2)
    ]
    query_t_acc[...] = jnp.zeros_like(query_t_acc)
    shift_acc[:, pl.ds(cap, 8), :] = jnp.zeros((3, 8, LANES), jnp.float32)

    def key_block(block):
        start = block * TILE
        rows = slice(start, start + TILE)
        first = head_lanes(0)
        grad_key, grad_value = [], []
        for head in range(2):
            key_head = jnp.where(head_lanes(head), conv_ref[0, 1, rows, :], jnp.bfloat16(0))
            value_head = jnp.where(head_lanes(head), conv_ref[0, 2, rows, :], jnp.bfloat16(0))
            lanes = slice(head * HEAD_DIM, (head + 1) * HEAD_DIM)
            logs = log_ref[0, 0, head : head + 1, :]
            key_sum = value_sum = None
            for size, at in ((TILE, start), (cap - start - TILE, start + TILE)):
                if size == 0:
                    continue
                cols = slice(at, at + size)
                probs = jnp.exp(dot_nt(key_head, queries[cols]) - logs[:, cols])
                if at == start:
                    probs = jnp.where(causal_tile(), probs, 0.0)
                grad_probs = dot_nt(value_head, grads[cols])
                scores = (probs * (grad_probs - inner[head][:, cols])).astype(jnp.bfloat16)
                value_term = dot_nn(probs.astype(jnp.bfloat16), grads[cols])
                key_term = dot_nn(scores, queries[cols])
                key_sum = key_term if key_sum is None else key_sum + key_term
                value_sum = value_term if value_sum is None else value_sum + value_term
                query_t_acc[lanes, cols] += dot_nn(keys_t[lanes, rows], scores)
            grad_key.append(key_sum)
            grad_value.append(value_sum)
        shift_acc[1, rows, :] = jnp.where(first, grad_key[0], grad_key[1])
        shift_acc[2, rows, :] = jnp.where(first, grad_value[0], grad_value[1])

    blocks = cap // TILE
    for block in range(blocks // 2):
        key_block(block)

    @pl.when(whole)
    def _():
        for block in range(blocks // 2, blocks):
            key_block(block)

    @pl.when(jnp.logical_not(whole))
    def _():
        shift_acc[1:, cap // 2 : cap, :] = jnp.zeros((2, cap // 2, LANES), jnp.float32)

    shift_acc[0, :cap, :] = query_t_acc[...].T
    for kind in range(3):
        proj = proj_ref[0, kind].astype(jnp.float32)
        total = 0.0
        for lag in range(3):
            moved = shift_acc[kind, lag : lag + cap, :]
            total = total + taps_ref[kind, lag : lag + 1, :] * moved
            grad_taps_ref[0, kind, lag : lag + 1, :] = jnp.sum(moved * proj, 0, keepdims=True)
        back_ref[0, kind] = total.astype(jnp.bfloat16)


def attend_back(mixed, proj, grad, out, logs, taps, lengths):
    seqs, _, cap, width = mixed.shape
    pairs = width // LANES
    triple = pl.BlockSpec((1, 3, cap, LANES), lambda s, p, n: (s, 0, 0, p))
    single = pl.BlockSpec((1, cap, LANES), lambda s, p, n: (s, 0, p))
    return pl.pallas_call(
        attend_back_kernel,
        grid_spec=pltpu.PrefetchScalarGridSpec(
            num_scalar_prefetch=1,
            grid=(seqs, pairs),
            in_specs=[
                triple,
                triple,
                single,
                single,
                pl.BlockSpec((1, 1, 2, cap), lambda s, p, n: (s, p, 0, 0)),
                pl.BlockSpec((3, 3, LANES), lambda s, p, n: (0, 0, p)),
            ],
            out_specs=[
                triple,
                pl.BlockSpec((1, 3, 3, LANES), lambda s, p, n: (s, 0, 0, p)),
            ],
            scratch_shapes=[
                pltpu.VMEM((LANES, cap), jnp.float32),
                pltpu.VMEM((3, cap + 8, LANES), jnp.float32),
            ],
        ),
        out_shape=[
            jax.ShapeDtypeStruct(mixed.shape, jnp.bfloat16),
            jax.ShapeDtypeStruct((seqs, 3, 3, width), jnp.float32),
        ],
        compiler_params=pltpu.CompilerParams(vmem_limit_bytes=48 * MIB),
        cost_estimate=pl.CostEstimate(
            flops=70_000_000_000, bytes_accessed=16_000_000, transcendentals=8_000_000
        ),
        name="attend_back",
    )(lengths, mixed, proj, grad, out, logs, taps)


def weight_grad_kernel(place_ref, left_ref, right_ref, out_ref):
    parts, rows, _ = out_ref.shape
    step = max(1, 512 // rows)
    while parts % step:
        step -= 1
    for at in range(0, parts, step):
        product = dot_tn(left_ref[:, at * rows : (at + step) * rows], right_ref[...])
        for part in range(step):
            out_ref[place_ref[at + part]] = product[part * rows : (part + 1) * rows].astype(
                jnp.bfloat16
            )


def weight_grad(left, right, place, columns):
    tokens, rows = left.shape
    width = right.shape[1]
    parts = place.shape[0]
    return pl.pallas_call(
        weight_grad_kernel,
        grid_spec=pltpu.PrefetchScalarGridSpec(
            num_scalar_prefetch=1,
            grid=(width // columns,),
            in_specs=[
                pl.BlockSpec((tokens, rows), lambda i, n: (0, 0)),
                pl.BlockSpec((tokens, columns), lambda i, n: (0, i)),
            ],
            out_specs=pl.BlockSpec((parts, rows // parts, columns), lambda i, n: (0, 0, i)),
        ),
        out_shape=jax.ShapeDtypeStruct((parts, rows // parts, width), jnp.bfloat16),
        compiler_params=pltpu.CompilerParams(vmem_limit_bytes=48 * MIB),
        cost_estimate=pl.CostEstimate(
            flops=2 * tokens * rows * width,
            bytes_accessed=2 * (tokens * (rows + width) + rows * width),
            transcendentals=0,
        ),
        name="weight_grad",
    )(place, left, right)


def swap_core(x):
    return lax.ppermute(x, "seq", [(0, 1), (1, 0)])


def stage_pairs(stage, groups):
    low = groups.bit_length() - 1
    order = list(range(low))
    other = [1, 0] + order[2:] if low > 1 else order
    pairs = []
    for core, bits in enumerate((order, other)):
        for group in range(groups):
            pairs.append((core * groups + group, core * groups + (group ^ (1 << bits[stage]))))
    return pairs


def shard_places(core, group, groups):
    low = groups.bit_length() - 1
    shard = jnp.arange(groups, dtype=jnp.int32)
    place = jnp.zeros((groups,), jnp.int32)
    for stage in range(low):
        bit = stage
        if low > 1 and stage < 2:
            bit = jnp.where(core == 0, stage, 1 - stage)
        same = ((shard >> bit) & 1) == ((group >> bit) & 1)
        place = place * 2 + same.astype(jnp.int32)
    return place


def sum_over_groups(halves, groups):
    stages = groups.bit_length() - 1
    for stage in range(stages):
        count = halves.shape[0] // 2
        got = lax.ppermute(halves[:count], ("seq", "batch"), stage_pairs(stage, groups))
        halves = (halves[count:].astype(jnp.float32) + got.astype(jnp.float32)).astype(
            jnp.bfloat16 if stage < stages - 1 else jnp.float32
        )
    return halves[0]


def local_pair(
    activations,
    cotangent,
    lengths,
    weights_qkv,
    conv_taps,
    weights_out,
    weights_up,
    weights_down,
    norm_gains,
    norm_biases,
):
    seqs, rows, width = activations.shape
    tokens = seqs * rows
    cap = 2 * rows
    half = width // 2
    core = lax.axis_index("seq")
    group = lax.axis_index("batch")
    groups = lax.axis_size("batch")
    place_by_core = [shard_places(c, group, groups) for c in range(2)]
    place_own = jnp.where(core == 0, place_by_core[0], place_by_core[1])
    place_other = jnp.where(core == 0, place_by_core[1], place_by_core[0])
    place_all = jnp.where(
        core == 0,
        jnp.concatenate([place_own + groups, place_other]),
        jnp.concatenate([place_other, place_own + groups]),
    )

    def whole_tokens(own):
        other = swap_core(own)
        return jnp.concatenate(
            [jnp.where(core == 0, own, other), jnp.where(core == 0, other, own)], 1
        )

    def own_tokens(x):
        return lax.dynamic_slice_in_dim(x, core * rows, rows, 1)

    def other_tokens(x):
        return lax.dynamic_slice_in_dim(x, (1 - core) * rows, rows, 1)

    def layer_weights(layer):
        w_qkv = lax.dynamic_slice_in_dim(
            weights_qkv[layer].reshape(width, 3, width), core * half, half, 2
        )
        taps = lax.dynamic_slice_in_dim(
            conv_taps[layer].reshape(3, width, 3), core * half, half, 1
        ).transpose(0, 2, 1)
        w_out_rows = lax.dynamic_slice_in_dim(weights_out[layer], core * half, half, 0)
        return w_qkv, taps, w_out_rows

    def forward(stream, layer):
        w_qkv, taps, _ = layer_weights(layer)
        gains, offsets = norm_gains[layer], norm_biases[layer]
        normed_one, scale_one = normalize(stream)
        attn_in = whole_tokens((normed_one * gains[:, 0] + offsets[:, 0]).astype(jnp.bfloat16))
        proj = jnp.einsum("std,dgc->sgtc", attn_in, w_qkv, preferred_element_type=jnp.float32)
        padded = jnp.pad(proj, ((0, 0), (0, 0), (2, 0), (0, 0)))
        mixed = (
            taps[:, 0][:, None] * proj
            + taps[:, 1][:, None] * padded[:, :, 1:-1]
            + taps[:, 2][:, None] * padded[:, :, :-2]
        ).astype(jnp.bfloat16)
        out_heads, logs = attend(mixed, lengths)
        got = swap_core(other_tokens(out_heads))
        kept = own_tokens(out_heads)
        out_own = jnp.concatenate(
            [jnp.where(core == 0, kept, got), jnp.where(core == 0, got, kept)], 2
        )
        middle = stream + jnp.einsum(
            "std,de->ste", out_own, weights_out[layer], preferred_element_type=jnp.float32
        )
        normed_two, scale_two = normalize(middle)
        ff_in = (normed_two * gains[:, 1] + offsets[:, 1]).astype(jnp.bfloat16)
        pre = jnp.einsum("std,df->stf", ff_in, weights_up[layer], preferred_element_type=jnp.float32)
        positive = jnp.maximum(pre, 0.0)
        hidden = (positive * positive).astype(jnp.bfloat16)
        result = middle + jnp.einsum(
            "stf,fd->std", hidden, weights_down[layer], preferred_element_type=jnp.float32
        )
        saved = (
            normed_one,
            scale_one,
            attn_in,
            proj.astype(jnp.bfloat16),
            mixed,
            out_heads,
            logs,
            normed_two,
            scale_two,
            ff_in,
            positive.astype(jnp.bfloat16),
            hidden,
        )
        return result, saved

    def backward(grad, layer, saved):
        (
            normed_one,
            scale_one,
            attn_in,
            proj,
            mixed,
            out_heads,
            logs,
            normed_two,
            scale_two,
            ff_in,
            positive,
            hidden,
        ) = saved
        w_qkv, taps, w_out_rows = layer_weights(layer)
        gains = norm_gains[layer]
        grad_low = grad.astype(jnp.bfloat16)
        down = weight_grad(
            hidden.reshape(tokens, -1), grad_low.reshape(tokens, width), place_all, 384
        )
        grad_hidden = jnp.einsum(
            "std,fd->stf", grad_low, weights_down[layer], preferred_element_type=jnp.float32
        )
        grad_pre = (grad_hidden * 2.0 * positive.astype(jnp.float32)).astype(jnp.bfloat16)
        up = weight_grad(ff_in.reshape(tokens, width), grad_pre.reshape(tokens, -1), place_all, 768)
        grad_ffin = jnp.einsum(
            "stf,df->std", grad_pre, weights_up[layer], preferred_element_type=jnp.float32
        )
        gain_two = jnp.sum(grad_ffin * normed_two, (0, 1))
        offset_two = jnp.sum(grad_ffin, (0, 1))
        grad_middle = grad + norm_back(grad_ffin, normed_two, scale_two, gains[:, 1])
        grad_branch = whole_tokens(grad_middle.astype(jnp.bfloat16))
        grad_heads = jnp.einsum(
            "ste,de->std", grad_branch, w_out_rows, preferred_element_type=jnp.float32
        ).astype(jnp.bfloat16)
        out = weight_grad(
            out_heads.reshape(2 * tokens, half),
            grad_branch.reshape(2 * tokens, width),
            place_own,
            384,
        )
        grad_proj, grad_taps = attend_back(mixed, proj, grad_heads, out_heads, logs, taps, lengths)
        grad_taps = jnp.sum(grad_taps, 0)
        qkv = weight_grad_three(
            attn_in.reshape(2 * tokens, width), grad_proj, place_all
        )
        partial = jnp.einsum(
            "sgtc,dgc->std", grad_proj, w_qkv, preferred_element_type=jnp.float32
        )
        grad_attn_in = own_tokens(partial) + swap_core(
            other_tokens(partial).astype(jnp.bfloat16)
        ).astype(jnp.float32)
        gain_one = jnp.sum(grad_attn_in * normed_one, (0, 1))
        offset_one = jnp.sum(grad_attn_in, (0, 1))
        grad_input = grad_middle + norm_back(grad_attn_in, normed_one, scale_one, gains[:, 0])
        norms = jnp.stack(
            [jnp.stack([gain_one, gain_two], -1), jnp.stack([offset_one, offset_two], -1)]
        )
        return grad_input, (down, up, out, qkv, grad_taps, norms)

    def weight_grad_three(left, grad_proj, place):
        parts = [
            weight_grad(left, grad_proj[:, kind].reshape(2 * tokens, half), place, half)
            for kind in range(3)
        ]
        return jnp.stack(parts, 2)

    def add_core(both):
        return (
            both[groups:].astype(jnp.float32) + swap_core(both[:groups]).astype(jnp.float32)
        ).astype(jnp.bfloat16)

    def reduce_layer(parts):
        down, up, out, qkv, grad_taps, norms = parts
        down = sum_over_groups(add_core(down), groups)
        up = sum_over_groups(add_core(up), groups)
        out = sum_over_groups(out, groups)
        got, kept = swap_core(qkv[:groups]), qkv[groups:]
        qkv = jnp.concatenate(
            [jnp.where(core == 0, kept, got), jnp.where(core == 0, got, kept)], 3
        )
        qkv = sum_over_groups(qkv.reshape(groups, qkv.shape[1], -1), groups)
        return down, up, out, qkv, grad_taps, norms

    stream = activations.astype(jnp.float32)
    kept = []
    for layer in range(LAYERS):
        stream, saved = forward(stream, layer)
        kept.append(saved)
    grad = cotangent.astype(jnp.float32)
    reduced = [None] * LAYERS
    for layer in reversed(range(LAYERS)):
        grad, parts = backward(grad, layer, kept[layer])
        reduced[layer] = reduce_layer(parts)
    down, up, out, qkv = (jnp.stack([layer[i] for layer in reduced]) for i in range(4))
    taps_all = []
    for layer in range(LAYERS):
        mine = reduced[layer][4]
        zero = jnp.zeros_like(mine)
        wide = jnp.concatenate(
            [jnp.where(core == 0, mine, zero), jnp.where(core == 0, zero, mine)], 2
        )
        taps_all.append(wide.transpose(0, 2, 1).reshape(3 * width, 3))
    small = jnp.concatenate(
        [
            jnp.stack(taps_all).reshape(LAYERS, 2 * groups, -1),
            jnp.stack([layer[5][0] for layer in reduced]).reshape(LAYERS, 2 * groups, -1),
            jnp.stack([layer[5][1] for layer in reduced]).reshape(LAYERS, 2 * groups, -1),
        ],
        2,
    ).transpose(1, 0, 2)
    mine = lax.dynamic_slice_in_dim(small, core * groups, groups, 0)
    theirs = lax.dynamic_slice_in_dim(small, (1 - core) * groups, groups, 0)
    mine = mine + swap_core(theirs)
    size, step = groups, groups // 2
    while step:
        low = (group // step) % 2
        send = lax.dynamic_slice_in_dim(mine, (1 - low) * step, step, 0)
        got = lax.ppermute(send, "batch", [(i, i ^ step) for i in range(groups)])
        mine = lax.dynamic_slice_in_dim(mine, low * step, step, 0) + got
        step //= 2
    mine = mine[0]
    n_taps = 3 * width * 3 // (2 * groups)
    n_norm = width * 2 // (2 * groups)
    grad_taps = mine[:, :n_taps].reshape(LAYERS, -1, 3)
    grad_gains = mine[:, n_taps : n_taps + n_norm].reshape(LAYERS, -1, 2)
    grad_biases = mine[:, n_taps + n_norm :].reshape(LAYERS, -1, 2)
    return (
        stream.astype(jnp.bfloat16),
        grad.astype(jnp.bfloat16),
        qkv,
        grad_taps,
        out,
        up,
        down,
        grad_gains,
        grad_biases,
    )


def solution(mesh):
    chosen = local_pair if mesh.shape["seq"] == 2 else local
    placed = (
        P("batch", "seq", None),
        P("batch", "seq", None),
        P("batch"),
        P(),
        P(),
        P(),
        P(),
        P(),
        P(),
        P(),
    )
    return jax.shard_map(
        chosen,
        mesh=mesh,
        in_specs=placed,
        out_specs=(
            P("batch", "seq", None),
            P("batch", "seq", None),
            P(None, ("seq", "batch"), None),
            P(None, ("seq", "batch"), None),
            P(None, ("seq", "batch"), None),
            P(None, ("seq", "batch"), None),
            P(None, ("seq", "batch"), None),
            P(None, ("seq", "batch"), None),
            P(None, ("seq", "batch"), None),
        ),
        check_vma=False,
    )
```

```python
import functools

import jax
import jax.numpy as jnp
from jax import lax
from jax.experimental import pallas as pl
from jax.experimental.pallas import tpu as pltpu
from jax.sharding import PartitionSpec as P

HEAD_DIM = 64
LAYERS = 2


def shifted(x, axis, by):
    size = lax.axis_size(axis)
    pairs = [(i, i + by) for i in range(size) if 0 <= i + by < size]
    return lax.ppermute(x, axis, pairs)


def normalize(stream):
    average = jnp.mean(stream, -1, keepdims=True)
    centered = stream - average
    scaling = lax.rsqrt(jnp.mean(centered * centered, -1, keepdims=True) + 1e-05)
    return (centered * scaling, scaling)


def norm_back(grad_norm, normed, scaling, gain):
    scaled = grad_norm * gain
    return scaling * (
        scaled
        - jnp.mean(scaled, -1, keepdims=True)
        - normed * jnp.mean(scaled * normed, -1, keepdims=True)
    )


def split_heads(block):
    return block.reshape(block.shape[0], -1, HEAD_DIM)


def masked_scores(query_seq, key_seq, length, positions):
    scores = jnp.einsum(
        "qhd,khd->hqk",
        split_heads(query_seq),
        split_heads(key_seq),
        preferred_element_type=jnp.float32,
    ) * HEAD_DIM ** (-0.5)
    key_place = jnp.arange(key_seq.shape[0], dtype=jnp.int32)
    allowed = (key_place[None, :] < length) & (
        (key_place[None, :] <= positions[:, None]) | (positions[:, None] >= length)
    )
    return jnp.where(allowed[None], scores, -1e30)


def attention_forward(queries, keys_all, values_all, lengths, positions):

    def one_sequence(items):
        query_seq, key_seq, value_seq, length = items
        scores = masked_scores(query_seq, key_seq, length, positions)
        highest = jnp.max(scores, -1, keepdims=True)
        expo = jnp.exp(scores - highest)
        totals = jnp.sum(expo, -1, keepdims=True)
        probs = (expo / totals).astype(jnp.bfloat16)
        mixed = jnp.einsum(
            "hqk,khd->qhd", probs, split_heads(value_seq), preferred_element_type=jnp.float32
        )
        log_total = (highest + jnp.log(totals))[..., 0]
        return (mixed.reshape(query_seq.shape).astype(jnp.bfloat16), log_total)

    return lax.map(one_sequence, (queries, keys_all, values_all, lengths))


def attention_backward(
    queries, keys_all, values_all, lengths, positions, log_totals, grad_attended
):

    def one_sequence(items):
        query_seq, key_seq, value_seq, length, log_total, grad_seq = items
        scores = masked_scores(query_seq, key_seq, length, positions)
        probs = jnp.exp(scores - log_total[..., None])
        grad_heads = split_heads(grad_seq)
        grad_probs = jnp.einsum(
            "qhd,khd->hqk", grad_heads, split_heads(value_seq), preferred_element_type=jnp.float32
        )
        inner = jnp.sum(probs * grad_probs, -1, keepdims=True)
        grad_scores = (probs * (grad_probs - inner)).astype(jnp.bfloat16)
        grad_query = jnp.einsum(
            "hqk,khd->qhd", grad_scores, split_heads(key_seq), preferred_element_type=jnp.float32
        ) * HEAD_DIM ** (-0.5)
        grad_key = jnp.einsum(
            "hqk,qhd->khd", grad_scores, split_heads(query_seq), preferred_element_type=jnp.float32
        ) * HEAD_DIM ** (-0.5)
        grad_value = jnp.einsum(
            "hqk,qhd->khd",
            probs.astype(jnp.bfloat16),
            grad_heads,
            preferred_element_type=jnp.float32,
        )
        return (
            grad_query.reshape(query_seq.shape),
            grad_key.reshape(key_seq.shape),
            grad_value.reshape(key_seq.shape),
        )

    return lax.map(
        one_sequence, (queries, keys_all, values_all, lengths, log_totals, grad_attended)
    )


def layer_forward(stream, lengths, positions, w_qkv, taps, w_out, w_up, w_down, gains, offsets):
    seqs_here, rows, width = stream.shape
    tokens = seqs_here * rows
    normed_one, scale_one = normalize(stream)
    attn_in = (normed_one * gains[:, 0] + offsets[:, 0]).astype(jnp.bfloat16)
    projected = jnp.dot(
        attn_in.reshape(tokens, width), w_qkv, preferred_element_type=jnp.float32
    ).reshape(seqs_here, rows, 3 * width)
    before = shifted(projected[:, rows - 2 :, :].astype(jnp.bfloat16), "seq", 1).astype(jnp.float32)
    extended = jnp.concatenate([before, projected], 1)
    conv_out = (
        taps[:, 0] * extended[:, 2:]
        + taps[:, 1] * extended[:, 1 : rows + 1]
        + taps[:, 2] * extended[:, :rows]
    )
    mixed_qkv = conv_out.astype(jnp.bfloat16)
    queries = mixed_qkv[..., :width]
    keys_here = mixed_qkv[..., width : 2 * width]
    values_here = mixed_qkv[..., 2 * width :]
    keys_all, values_all = (
        lax.all_gather(keys_here, "seq", axis=1, tiled=True),
        lax.all_gather(values_here, "seq", axis=1, tiled=True),
    )
    attended, log_totals = attention_forward(queries, keys_all, values_all, lengths, positions)
    branch = jnp.dot(attended.reshape(tokens, width), w_out, preferred_element_type=jnp.float32)
    middle = stream + branch.reshape(stream.shape)
    normed_two, scale_two = normalize(middle)
    ff_in = (normed_two * gains[:, 1] + offsets[:, 1]).astype(jnp.bfloat16).reshape(tokens, width)
    hidden_pre = jnp.dot(ff_in, w_up, preferred_element_type=jnp.float32)
    hidden = (jax.nn.relu(hidden_pre) ** 2).astype(jnp.bfloat16)
    result = middle + jnp.dot(hidden, w_down, preferred_element_type=jnp.float32).reshape(
        stream.shape
    )
    kept_keys = (keys_all, values_all)
    saved = (
        normed_one,
        scale_one,
        attn_in,
        extended,
        queries,
        kept_keys,
        attended,
        log_totals,
        normed_two,
        scale_two,
        ff_in,
        hidden_pre,
        hidden,
    )
    return (result, saved)


def layer_backward(grad_stream, lengths, positions, saved, w_qkv, taps, w_out, w_up, w_down, gains):
    (
        normed_one,
        scale_one,
        attn_in,
        extended,
        queries,
        kept_keys,
        attended,
        log_totals,
        normed_two,
        scale_two,
        ff_in,
        hidden_pre,
        hidden,
    ) = saved
    seqs_here, rows, width = grad_stream.shape
    tokens = seqs_here * rows
    grad_down_in = grad_stream.reshape(tokens, width).astype(jnp.bfloat16)
    grad_down = jnp.einsum("tf,td->fd", hidden, grad_down_in, preferred_element_type=jnp.float32)
    grad_hidden = jnp.dot(grad_down_in, w_down.T, preferred_element_type=jnp.float32)
    grad_pre = (grad_hidden * 2.0 * jax.nn.relu(hidden_pre)).astype(jnp.bfloat16)
    grad_up = jnp.einsum("td,tf->df", ff_in, grad_pre, preferred_element_type=jnp.float32)
    grad_ffin = jnp.dot(grad_pre, w_up.T, preferred_element_type=jnp.float32).reshape(
        grad_stream.shape
    )
    gain_two = jnp.sum(grad_ffin * normed_two, (0, 1))
    offset_two = jnp.sum(grad_ffin, (0, 1))
    grad_middle = grad_stream + norm_back(grad_ffin, normed_two, scale_two, gains[:, 1])
    grad_branch = grad_middle.reshape(tokens, width).astype(jnp.bfloat16)
    grad_out = jnp.einsum(
        "td,te->de",
        attended.reshape(tokens, width),
        grad_branch,
        preferred_element_type=jnp.float32,
    )
    grad_attended = jnp.dot(grad_branch, w_out.T, preferred_element_type=jnp.float32)
    grad_attended = grad_attended.astype(jnp.bfloat16).reshape(grad_stream.shape)
    keys_all, values_all = kept_keys
    grad_query, grad_key_all, grad_value_all = attention_backward(
        queries, keys_all, values_all, lengths, positions, log_totals, grad_attended
    )
    grad_key, grad_value = (
        lax.psum_scatter(
            grad_key_all.astype(jnp.bfloat16), "seq", scatter_dimension=1, tiled=True
        ).astype(jnp.float32),
        lax.psum_scatter(
            grad_value_all.astype(jnp.bfloat16), "seq", scatter_dimension=1, tiled=True
        ).astype(jnp.float32),
    )
    grad_conv = jnp.concatenate([grad_query, grad_key, grad_value], -1)
    after = shifted(grad_conv[:, :2, :].astype(jnp.bfloat16), "seq", -1).astype(jnp.float32)
    grad_ext = jnp.concatenate([grad_conv, after], 1)
    grad_proj = (
        taps[:, 0] * grad_ext[:, :rows]
        + taps[:, 1] * grad_ext[:, 1 : rows + 1]
        + taps[:, 2] * grad_ext[:, 2:]
    )
    grad_taps = jnp.stack(
        [
            jnp.sum(grad_conv * extended[:, 2:], (0, 1)),
            jnp.sum(grad_conv * extended[:, 1 : rows + 1], (0, 1)),
            jnp.sum(grad_conv * extended[:, :rows], (0, 1)),
        ],
        -1,
    )
    grad_proj_low = grad_proj.reshape(tokens, 3 * width).astype(jnp.bfloat16)
    grad_qkv = jnp.einsum(
        "td,tf->df",
        attn_in.reshape(tokens, width),
        grad_proj_low,
        preferred_element_type=jnp.float32,
    )
    grad_attn_in = jnp.dot(grad_proj_low, w_qkv.T, preferred_element_type=jnp.float32).reshape(
        grad_stream.shape
    )
    gain_one = jnp.sum(grad_attn_in * normed_one, (0, 1))
    offset_one = jnp.sum(grad_attn_in, (0, 1))
    grad_input = grad_middle + norm_back(grad_attn_in, normed_one, scale_one, gains[:, 0])
    grad_gains = jnp.stack([gain_one, gain_two], -1)
    grad_biases = jnp.stack([offset_one, offset_two], -1)
    return (
        grad_input,
        (grad_qkv, grad_taps, grad_out, grad_up, grad_down, grad_gains, grad_biases),
    )


def reduce_grads(grad_qkv, grad_taps, grad_out, grad_up, grad_down, grad_gains, grad_biases):
    part_qkv, part_taps, part_out, part_up, part_down, part_gains, part_biases = (
        lax.psum_scatter(
            grad_qkv.astype(jnp.bfloat16), "seq", scatter_dimension=0, tiled=True
        ).astype(jnp.float32),
        lax.psum_scatter(
            grad_taps.astype(jnp.bfloat16), "seq", scatter_dimension=0, tiled=True
        ).astype(jnp.float32),
        lax.psum_scatter(
            grad_out.astype(jnp.bfloat16), "seq", scatter_dimension=0, tiled=True
        ).astype(jnp.float32),
        lax.psum_scatter(
            grad_up.astype(jnp.bfloat16), "seq", scatter_dimension=0, tiled=True
        ).astype(jnp.float32),
        lax.psum_scatter(
            grad_down.astype(jnp.bfloat16), "seq", scatter_dimension=0, tiled=True
        ).astype(jnp.float32),
        lax.psum_scatter(
            grad_gains.astype(jnp.bfloat16), "seq", scatter_dimension=0, tiled=True
        ).astype(jnp.float32),
        lax.psum_scatter(
            grad_biases.astype(jnp.bfloat16), "seq", scatter_dimension=0, tiled=True
        ).astype(jnp.float32),
    )
    return (
        lax.psum_scatter(
            part_qkv.astype(jnp.bfloat16), "batch", scatter_dimension=0, tiled=True
        ).astype(jnp.float32),
        lax.psum_scatter(
            part_taps.astype(jnp.bfloat16), "batch", scatter_dimension=0, tiled=True
        ).astype(jnp.float32),
        lax.psum_scatter(
            part_out.astype(jnp.bfloat16), "batch", scatter_dimension=0, tiled=True
        ).astype(jnp.float32),
        lax.psum_scatter(
            part_up.astype(jnp.bfloat16), "batch", scatter_dimension=0, tiled=True
        ).astype(jnp.float32),
        lax.psum_scatter(
            part_down.astype(jnp.bfloat16), "batch", scatter_dimension=0, tiled=True
        ).astype(jnp.float32),
        lax.psum_scatter(
            part_gains.astype(jnp.bfloat16), "batch", scatter_dimension=0, tiled=True
        ).astype(jnp.float32),
        lax.psum_scatter(
            part_biases.astype(jnp.bfloat16), "batch", scatter_dimension=0, tiled=True
        ).astype(jnp.float32),
    )


def local(
    activations,
    cotangent,
    lengths,
    weights_qkv,
    conv_taps,
    weights_out,
    weights_up,
    weights_down,
    norm_gains,
    norm_biases,
):
    seqs_here, rows, width = activations.shape
    positions = lax.axis_index("seq") * rows + jnp.arange(rows, dtype=jnp.int32)
    stream = activations.astype(jnp.float32)
    saved_all = []
    for layer_num in range(LAYERS):
        stream, saved = layer_forward(
            stream,
            lengths,
            positions,
            weights_qkv[layer_num],
            conv_taps[layer_num],
            weights_out[layer_num],
            weights_up[layer_num],
            weights_down[layer_num],
            norm_gains[layer_num],
            norm_biases[layer_num],
        )
        saved_all.append(saved)
    block_out = stream.astype(jnp.bfloat16)
    grad_stream = cotangent.astype(jnp.float32)
    collected = []
    for layer_num in reversed(range(LAYERS)):
        grad_stream, layer_grads = layer_backward(
            grad_stream,
            lengths,
            positions,
            saved_all[layer_num],
            weights_qkv[layer_num],
            conv_taps[layer_num],
            weights_out[layer_num],
            weights_up[layer_num],
            weights_down[layer_num],
            norm_gains[layer_num],
        )
        grad_qkv, grad_taps, grad_out, grad_up, grad_down, grad_gains, grad_biases = layer_grads
        collected.append(
            reduce_grads(grad_qkv, grad_taps, grad_out, grad_up, grad_down, grad_gains, grad_biases)
        )
    collected = collected[::-1]
    stacked = [jnp.stack([member[index] for member in collected], 0) for index in range(7)]
    return (
        block_out,
        grad_stream.astype(jnp.bfloat16),
        stacked[0],
        stacked[1],
        stacked[2],
        stacked[3],
        stacked[4],
        stacked[5],
        stacked[6],
    )


TILE = 256
LANES = 128
VMEM_LIMIT = 60 * 2**20


def dot_nt(left, right):
    return lax.dot_general(
        left, right, (((1,), (1,)), ((), ())), preferred_element_type=jnp.float32
    )


def dot_nn(left, right):
    return lax.dot_general(
        left, right, (((1,), (0,)), ((), ())), preferred_element_type=jnp.float32
    )


def dot_tn(left, right):
    return lax.dot_general(
        left, right, (((0,), (0,)), ((), ())), preferred_element_type=jnp.float32
    )


def head_lanes(head):
    lane = lax.broadcasted_iota(jnp.int32, (1, LANES), 1)
    return (lane >= head * HEAD_DIM) & (lane < (head + 1) * HEAD_DIM)


def causal_tile():
    keys = lax.broadcasted_iota(jnp.int32, (TILE, TILE), 0)
    queries = lax.broadcasted_iota(jnp.int32, (TILE, TILE), 1)
    return keys <= queries


def attend_kernel(length_ref, conv_ref, out_ref, log_ref):
    cap = conv_ref.shape[1]
    whole = length_ref[pl.program_id(0)] == cap
    queries = conv_ref[0, :, :LANES]
    keys = conv_ref[0, :, LANES : 2 * LANES] * jnp.bfloat16(HEAD_DIM**-0.5)
    keys = [jnp.where(head_lanes(head), keys, jnp.bfloat16(0)) for head in range(2)]
    values_t = conv_ref[0, :, 2 * LANES :].T

    hidden = jnp.where(whole, 0.0, -1e30)

    def query_block(block):
        rows = slice(block * TILE, (block + 1) * TILE)
        mixed = []
        for head in range(2):
            bounds = sorted({0, min(block * TILE, cap // 2), block * TILE, (block + 1) * TILE})
            spans = list(zip(bounds[:-1], bounds[1:]))
            parts = []
            for start, stop in spans:
                part = dot_nt(keys[head][start:stop], queries[rows])
                if start == block * TILE:
                    part = jnp.where(causal_tile(), part, -1e30)
                if start >= cap // 2:
                    part = part + hidden
                parts.append(part)
            highest = functools.reduce(
                jnp.maximum, [jnp.max(part, 0, keepdims=True) for part in parts]
            )
            expo = [jnp.exp(part - highest) for part in parts]
            total = sum(jnp.sum(part, 0, keepdims=True) for part in expo)
            value_head = values_t[head * HEAD_DIM : (head + 1) * HEAD_DIM]
            got = sum(
                dot_nn(value_head[:, start:stop], part.astype(jnp.bfloat16))
                for (start, stop), part in zip(spans, expo)
            )
            mixed.append(got / total)
            log_ref[0, 0, head : head + 1, rows] = highest + jnp.log(total)
        out_ref[0, rows, :] = jnp.concatenate(mixed, 0).T.astype(jnp.bfloat16)

    for block in range(cap // TILE):
        query_block(block)


def attend(mixed, lengths, after=()):
    seqs, cap, wide = mixed.shape
    pairs = wide // (3 * LANES)
    return call(
        attend_kernel, "attend", 1, (seqs, pairs),
        [pl.BlockSpec((1, cap, 3 * LANES), lambda s, p, n: (s, 0, p))],
        [
            pl.BlockSpec((1, cap, LANES), lambda s, p, n: (s, 0, p)),
            pl.BlockSpec((1, 1, 2, cap), lambda s, p, n: (s, p, 0, 0)),
        ],
        [
            jax.ShapeDtypeStruct((seqs, cap, wide // 3), jnp.bfloat16),
            jax.ShapeDtypeStruct((seqs, pairs, 2, cap), jnp.float32),
        ],
        [], 0, 8_000_000, after,
    )(lengths, mixed)


def attend_back_kernel(
    length_ref,
    conv_ref,
    proj_ref,
    grad_ref,
    out_ref,
    log_ref,
    taps_ref,
    back_ref,
    grad_taps_ref,
    query_t_acc,
    shift_acc,
):
    cap = conv_ref.shape[1]
    whole = length_ref[pl.program_id(0)] == cap
    factor = jnp.bfloat16(HEAD_DIM**-0.5)
    queries = conv_ref[0, :, :LANES] * factor
    grads = grad_ref[0]
    keys_t = (conv_ref[0, :, LANES : 2 * LANES] * factor).T
    product_t = (grads.astype(jnp.float32) * out_ref[0].astype(jnp.float32)).T
    inner = [
        jnp.sum(product_t[head * HEAD_DIM : (head + 1) * HEAD_DIM], 0, keepdims=True)
        for head in range(2)
    ]
    query_t_acc[...] = jnp.zeros_like(query_t_acc)
    shift_acc[:, pl.ds(cap, 8), :] = jnp.zeros((3, 8, LANES), jnp.float32)

    def key_block(block):
        start = block * TILE
        rows = slice(start, start + TILE)
        first = head_lanes(0)
        grad_key, grad_value = [], []
        for head in range(2):
            key_head = jnp.where(head_lanes(head), conv_ref[0, rows, LANES : 2 * LANES], jnp.bfloat16(0))
            value_head = jnp.where(head_lanes(head), conv_ref[0, rows, 2 * LANES :], jnp.bfloat16(0))
            lanes = slice(head * HEAD_DIM, (head + 1) * HEAD_DIM)
            logs = log_ref[0, 0, head : head + 1, :]
            if start >= cap // 2:
                logs = jnp.where(whole, logs, 1e30)
            key_sum = value_sum = None
            for size, at in ((TILE, start), (cap - start - TILE, start + TILE)):
                if size == 0:
                    continue
                cols = slice(at, at + size)
                probs = jnp.exp(dot_nt(key_head, queries[cols]) - logs[:, cols])
                if at == start:
                    probs = jnp.where(causal_tile(), probs, 0.0)
                grad_probs = dot_nt(value_head, grads[cols])
                scores = (probs * (grad_probs - inner[head][:, cols])).astype(jnp.bfloat16)
                value_term = dot_nn(probs.astype(jnp.bfloat16), grads[cols])
                key_term = dot_nn(scores, queries[cols])
                key_sum = key_term if key_sum is None else key_sum + key_term
                value_sum = value_term if value_sum is None else value_sum + value_term
                query_t_acc[lanes, cols] += dot_nn(keys_t[lanes, rows], scores)
            grad_key.append(key_sum)
            grad_value.append(value_sum)
        shift_acc[1, rows, :] = jnp.where(first, grad_key[0], grad_key[1])
        shift_acc[2, rows, :] = jnp.where(first, grad_value[0], grad_value[1])

    for block in range(cap // TILE):
        key_block(block)

    shift_acc[0, :cap, :] = query_t_acc[...].T
    for kind in range(3):
        lanes = slice(kind * LANES, (kind + 1) * LANES)
        proj = proj_ref[0, :, lanes].astype(jnp.float32)
        total = 0.0
        for lag in range(3):
            moved = shift_acc[kind, lag : lag + cap, :]
            total = total + taps_ref[lag : lag + 1, lanes] * moved
            grad_taps_ref[0, lag : lag + 1, lanes] = jnp.sum(moved * proj, 0, keepdims=True)
        back_ref[0, :, lanes] = total.astype(jnp.bfloat16)


def attend_back(mixed, proj, grad, out, logs, taps, lengths, rides, collective_id, groups):
    seqs, cap, wide = mixed.shape
    pairs = wide // (3 * LANES)
    triple = pl.BlockSpec((1, cap, 3 * LANES), lambda s, p, n: (s, 0, p))
    single = pl.BlockSpec((1, cap, LANES), lambda s, p, n: (s, 0, p))
    return call(
        attend_back_kernel, "attend_back", 1, (seqs, pairs),
        [
            triple,
            triple,
            single,
            single,
            pl.BlockSpec((1, 1, 2, cap), lambda s, p, n: (s, p, 0, 0)),
            pl.BlockSpec((3, 3 * LANES), lambda s, p, n: (0, p)),
        ],
        [triple, pl.BlockSpec((1, 3, 3 * LANES), lambda s, p, n: (s, 0, p))],
        [
            jax.ShapeDtypeStruct(mixed.shape, jnp.bfloat16),
            jax.ShapeDtypeStruct((seqs, 3, wide), jnp.float32),
        ],
        [pltpu.VMEM((LANES, cap), jnp.float32), pltpu.VMEM((3, cap + 8, LANES), jnp.float32)],
        0, 16_000_000, rides=rides, collective_id=collective_id, groups=groups,
    )(lengths, mixed, proj, grad, out, logs, taps)


def swap_core(x):
    return lax.ppermute(x, "seq", [(0, 1), (1, 0)])


def group_bits(groups):
    order = list(range(groups.bit_length() - 1))
    return order, [1, 0] + order[2:]


def exchange(x, flips, groups):
    pairs = []
    for core, bits in enumerate(group_bits(groups)):
        mask = sum(1 << bits[flip] for flip in flips)
        for group in range(groups):
            pairs.append((core * groups + group, core * groups + (group ^ mask)))
    return lax.ppermute(x, ("seq", "batch"), pairs)


def shard_places(core, group, groups):
    shard = jnp.arange(groups, dtype=jnp.int32)
    place = jnp.zeros((groups,), jnp.int32)
    first, second = group_bits(groups)
    for one, other in zip(first, second):
        bit = jnp.where(core == 0, one, other)
        same = ((shard >> bit) & 1) == ((group >> bit) & 1)
        place = place * 2 + same.astype(jnp.int32)
    return place


def normal(x):
    average = jnp.mean(x, -1, keepdims=True)
    centered = x - average
    scaling = lax.rsqrt(jnp.mean(centered * centered, -1, keepdims=True) + 1e-05)
    return centered * scaling, scaling


def blocks_of(rows, size=512):
    return [slice(at, at + size) for at in range(0, rows, size)]


def flip(value, bit):
    return value + (1 - 2 * (value // 2**bit % 2)) * 2**bit


def partner(flips, groups):
    core, group = lax.axis_index("seq"), lax.axis_index("batch")
    if not flips:
        return {"seq": 1 - core, "batch": group}
    to = []
    for bits in group_bits(groups):
        other = group
        for place in flips:
            other = flip(other, bits[place])
        to.append(other)
    return {"seq": core, "batch": (1 - core) * to[0] + core * to[1]}


def meet(partners):
    barrier = pltpu.get_barrier_semaphore()
    for device in partners:
        pl.semaphore_signal(barrier, inc=1, device_id=device, device_id_type=pl.DeviceIdType.MESH)
    pl.semaphore_wait(barrier, len(partners))


def remote(source, target, sends, receives, device):
    return pltpu.make_async_remote_copy(
        src_ref=source,
        dst_ref=target,
        send_sem=sends,
        recv_sem=receives,
        device_id=device,
        device_id_type=pl.DeviceIdType.MESH,
    )


def call(
    kernel, name, scalars, grid, in_specs, out_specs, out_shape, scratch, flops, moved, after=(),
    rides=(), collective_id=None, others=(), groups=None,
):
    sources = {id(ride[0]): ride[0] for ride in rides}
    extra = list(after) + list(sources.values())
    where_of = {key: len(after) + at for at, key in enumerate(sources)}
    many = isinstance(out_specs, list)
    outs = out_specs if many else [out_specs]
    shapes = out_shape if many else [out_shape]
    landing = [
        jax.ShapeDtypeStruct((ride[2],) + ride[0].shape[1:], ride[0].dtype) for ride in rides
    ]

    def body(*refs):
        refs = list(refs)
        prefetch, refs = refs[:scalars], refs[scalars:]
        extras, refs = refs[: len(extra)], refs[len(extra) :]
        given, refs = refs[: len(in_specs) + len(outs)], refs[len(in_specs) + len(outs) :]
        landed, refs = refs[: len(rides)], refs[len(rides) :]
        if not rides and not others:
            kernel(*prefetch, *given, *refs)
            return
        send_sems, receive_sems = refs[-2:] if rides else (None, None)
        copies = [
            remote(
                extras[where_of[id(array)]].at[pl.ds(start, count)],
                landed[at],
                send_sems.at[at],
                receive_sems.at[at],
                partner(flips, groups),
            )
            for at, (array, start, count, flips) in enumerate(rides)
        ]
        first = functools.reduce(
            jnp.logical_and, [pl.program_id(axis) == 0 for axis in range(len(grid))]
        )
        last = functools.reduce(
            jnp.logical_and,
            [pl.program_id(axis) == pl.num_programs(axis) - 1 for axis in range(len(grid))],
        )

        @pl.when(first)
        def _():
            meet([partner(flips, groups) for flips in sorted({ride[3] for ride in rides} | set(others))])
            for copy in copies:
                copy.start()

        kernel(*prefetch, *given, *(refs[:-2] if rides else refs))

        @pl.when(last)
        def _():
            for copy in copies:
                copy.wait()

    anywhere = pl.BlockSpec(memory_space=pl.ANY)
    params = {"vmem_limit_bytes": VMEM_LIMIT}
    if collective_id is not None:
        params.update(collective_id=collective_id, has_side_effects=True)
    made = pl.pallas_call(
        body,
        grid_spec=pltpu.PrefetchScalarGridSpec(
            num_scalar_prefetch=scalars,
            grid=grid,
            in_specs=[anywhere] * len(extra) + in_specs,
            out_specs=outs + [anywhere] * len(rides),
            scratch_shapes=scratch + [pltpu.SemaphoreType.DMA((len(rides),))] * (2 if rides else 0),
        ),
        out_shape=shapes + landing,
        compiler_params=pltpu.CompilerParams(**params),
        cost_estimate=pl.CostEstimate(
            flops=int(flops), bytes_accessed=int(moved), transcendentals=0
        ),
        name=name,
    )

    def run(*args):
        got = made(*args[:scalars], *extra, *args[scalars:])
        return got if many or rides else got[0]

    return run


def full_spec(shape):
    return pl.BlockSpec(shape, lambda *_: (0,) * len(shape))


def norm_kernel(stream_ref, norms_ref, out_ref):
    normed, _ = normal(stream_ref[0].astype(jnp.float32))
    out_ref[0] = (normed * norms_ref[0:1] + norms_ref[1:2]).astype(jnp.bfloat16)


def norm(stream, norms):
    seqs, rows, width = stream.shape
    spec = pl.BlockSpec((1, rows, width), lambda s: (s, 0, 0))
    return call(
        norm_kernel, "norm", 0, (seqs,), [spec, full_spec(norms.shape)], spec,
        jax.ShapeDtypeStruct(stream.shape, jnp.bfloat16), [], 0, 6 * stream.size,
    )(stream, norms)


def head_weight_copies(weight_hbm, layer, weight, sems, core):
    width = weight.shape[0]
    pairs = weight.shape[1] // (3 * LANES)
    copies = []
    for pair in range(pairs):
        for kind in range(3):
            at = pl.multiple_of(kind * width + core * (width // 2) + pair * LANES, LANES)
            copies.append(
                pltpu.make_async_copy(
                    weight_hbm.at[layer, :, pl.ds(at, LANES)],
                    weight.at[:, pl.ds((3 * pair + kind) * LANES, LANES)],
                    sems.at[3 * pair + kind],
                )
            )
    return copies


def project_kernel(
    layer, core_ref, own_ref, got_ref, weight_hbm, taps_ref, mixed_ref, proj_ref, inputs, longer, weight, sems
):
    core = core_ref[0]
    rows = own_ref.shape[0]

    @pl.when(pl.program_id(0) == 0)
    def _():
        copies = head_weight_copies(weight_hbm, layer, weight, sems, core)
        for copy in copies:
            copy.start()
        for copy in copies:
            copy.wait()

    inputs[pl.ds(pl.multiple_of(core * rows, rows), rows), :] = own_ref[...]
    inputs[pl.ds(pl.multiple_of((1 - core) * rows, rows), rows), :] = got_ref[...]
    longer[0:8] = jnp.zeros((8, longer.shape[1]), jnp.float32)
    for block in blocks_of(2 * rows, TILE):
        at = 8 + block.start
        here = dot_nn(inputs[block], weight[...])
        longer[at : at + TILE, :] = here
        proj_ref[block] = here.astype(jnp.bfloat16)
        mixed_ref[block] = (
            taps_ref[0:1] * here
            + taps_ref[1:2] * longer[at - 1 : at - 1 + TILE, :]
            + taps_ref[2:3] * longer[at - 2 : at - 2 + TILE, :]
        ).astype(jnp.bfloat16)


def project(core, own, got, weight, taps, layer):
    seqs, rows, width = own.shape
    wide = taps.shape[2]
    part = pl.BlockSpec((None, rows, width), lambda s, c: (s, 0, 0))
    out = pl.BlockSpec((None, 2 * rows, wide), lambda s, c: (s, 0, 0))
    shape = jax.ShapeDtypeStruct((seqs, 2 * rows, wide), jnp.bfloat16)
    return call(
        functools.partial(project_kernel, layer), "project", 1, (seqs,),
        [
            part,
            part,
            pl.BlockSpec(memory_space=pl.ANY),
            pl.BlockSpec((None, 3, wide), lambda s, c: (layer, 0, 0)),
        ],
        [out, out], [shape, shape],
        [
            pltpu.VMEM((2 * rows, width), jnp.bfloat16),
            pltpu.VMEM((2 * rows + 8, wide), jnp.float32),
            pltpu.VMEM((width, wide), jnp.bfloat16),
            pltpu.SemaphoreType.DMA((wide // LANES,)),
        ],
        4 * seqs * rows * width * wide, 20_000_000,
    )(core, own, got, weight, taps)


def feed_kernel(
    last_layer, core_ref, stream_ref, heads_ref, got_ref, w_out_ref, w_up_ref, w_down_ref, norms_ref,
    next_norms_ref, *refs
):
    if last_layer:
        middle_hbm, ff_in_hbm, positive_ref, result_ref, total, middle, ff_in, sems = refs
    else:
        middle_hbm, ff_in_hbm, positive_ref, result_ref, next_ref, total, middle, ff_in, sems = refs
    core = core_ref[0]
    step = pl.program_id(0)
    seqs, rows, _ = stream_ref.shape
    copies = [
        pltpu.make_async_copy(middle, middle_hbm, sems.at[0]),
        pltpu.make_async_copy(ff_in, ff_in_hbm, sems.at[1]),
    ]

    @pl.when(step == 0)
    def _():
        for seq in range(seqs):
            for block in blocks_of(rows):
                value = stream_ref[seq, block].astype(jnp.float32) + (
                    dot_nn(heads_ref[seq, block], w_out_ref[core])
                    + dot_nn(got_ref[seq, block], w_out_ref[1 - core])
                )
                middle[seq, block] = value
                total[seq, block] = value
                normed, _ = normal(value)
                ff_in[seq, block] = (normed * norms_ref[0:1] + norms_ref[1:2]).astype(jnp.bfloat16)
        for copy in copies:
            copy.start()

    for seq in range(seqs):
        for block in blocks_of(rows):
            positive = jnp.maximum(dot_nn(ff_in[seq, block], w_up_ref[...]), 0.0)
            positive_ref[seq, block] = positive.astype(jnp.bfloat16)
            hidden = (positive * positive).astype(jnp.bfloat16)
            total[seq, block] += dot_nn(hidden, w_down_ref[...])

    @pl.when(step == pl.num_programs(0) - 1)
    def _():
        for seq in range(seqs):
            for block in blocks_of(rows):
                value = total[seq, block]
                result_ref[seq, block] = value.astype(result_ref.dtype)
                if not last_layer:
                    normed, _ = normal(value)
                    next_ref[seq, block] = (
                        normed * next_norms_ref[0:1] + next_norms_ref[1:2]
                    ).astype(jnp.bfloat16)
        for copy in copies:
            copy.wait()


def feed(core, stream, heads, got, w_out, w_up, w_down, norms, next_norms, layer, last_layer):
    seqs, rows, width = stream.shape
    half = width // 2
    ff = w_up.shape[2]
    chunk = 768
    tokens = (seqs, rows, width)
    f32, bf16 = jnp.float32, jnp.bfloat16
    out_specs = [
        pl.BlockSpec(memory_space=pl.ANY),
        pl.BlockSpec(memory_space=pl.ANY),
        pl.BlockSpec((seqs, rows, chunk), lambda i, c: (0, 0, i)),
        full_spec(tokens),
    ]
    out_shape = [
        jax.ShapeDtypeStruct(tokens, f32),
        jax.ShapeDtypeStruct(tokens, bf16),
        jax.ShapeDtypeStruct((seqs, rows, ff), bf16),
        jax.ShapeDtypeStruct(tokens, bf16 if last_layer else f32),
    ]
    if not last_layer:
        out_specs.append(full_spec(tokens))
        out_shape.append(jax.ShapeDtypeStruct(tokens, bf16))
    return call(
        functools.partial(feed_kernel, last_layer), "feed", 1, (ff // chunk,),
        [
            full_spec(tokens),
            pl.BlockSpec((seqs, rows, half), lambda i, c: (0, c[0], 0)),
            full_spec((seqs, rows, half)),
            pl.BlockSpec((None, 2, half, width), lambda i, c: (layer, 0, 0, 0)),
            pl.BlockSpec((None, width, chunk), lambda i, c: (layer, 0, i)),
            pl.BlockSpec((None, chunk, width), lambda i, c: (layer, i, 0)),
            full_spec(norms.shape),
            full_spec(next_norms.shape),
        ],
        out_specs, out_shape,
        [
            pltpu.VMEM(tokens, f32),
            pltpu.VMEM(tokens, f32),
            pltpu.VMEM(tokens, bf16),
            pltpu.SemaphoreType.DMA((2,)),
        ],
        2 * seqs * rows * width * (width + 2 * ff), 40_000_000,
    )(core, stream, heads, got, w_out.reshape(-1, 2, half, width), w_up, w_down, norms, next_norms)


def place_of(shard, owner, groups):
    group = lax.axis_index("batch")
    place = 0
    for one, other in zip(*group_bits(groups)):
        differs = [(shard // 2**bit % 2 + group // 2**bit % 2) % 2 for bit in (one, other)]
        place = 2 * place + 1 - ((1 - owner) * differs[0] + owner * differs[1])
    return place


def feed_back_kernel(
    groups, grad_ref, positive_ref, middle_ref, ff_in_ref, w_down_ref, w_up_ref, norms_ref,
    sum_hbm, grad_middle_ref, branch_ref, norm_grad_ref,
    low, ff_in_t, grad_pre, hidden, grad_ffin, up_mine, down_mine, up_send, down_send, up_got, down_got,
    up_sends, up_gets, down_sends, down_gets, up_outs, down_outs,
):
    core = lax.axis_index("seq")
    other = partner((), groups)
    step = pl.program_id(0)
    steps = pl.num_programs(0)
    seqs, rows, width = grad_ref.shape
    chunk = w_down_ref.shape[0]
    _, shard_rows, ff = down_mine.shape[1:]
    shards = down_mine.shape[1]
    half = width // 2

    def up_remote(at):
        return remote(up_send.at[at], up_got.at[at], up_sends.at[at], up_gets.at[at], other)

    def down_remote(at):
        return remote(down_send.at[at], down_got.at[at], down_sends.at[at], down_gets.at[at], other)

    def up_out(slot, at):
        return pltpu.make_async_copy(
            up_mine.at[slot],
            sum_hbm.at[:, :, pl.ds(pl.multiple_of(at * chunk, chunk), chunk)],
            up_outs.at[slot],
        )

    def down_out(slot, shard, place):
        return pltpu.make_async_copy(
            down_mine.at[slot, shard], sum_hbm.at[place, :, pl.ds(ff, ff)], down_outs.at[slot, shard]
        )

    def write_out(at):
        slot = lax.rem(at, 2)
        up_remote(at).wait_recv()
        up_mine[slot] = (
            up_mine[slot].astype(jnp.float32) + up_got[at].astype(jnp.float32)
        ).astype(jnp.bfloat16)
        up_out(slot, at).start()

        @pl.when(at // (steps // 2) == core)
        def _():
            mine = lax.rem(at, steps // 2)
            down_remote(mine).wait_recv()
            for shard in range(shards):
                down_mine[slot, shard] = (
                    down_mine[slot, shard].astype(jnp.float32)
                    + down_got[mine, shard].astype(jnp.float32)
                ).astype(jnp.bfloat16)
                down_out(slot, shard, place_of(mine * shards + shard, core, groups)).start()

    def wait_out(at):
        slot = lax.rem(at, 2)
        up_out(slot, at).wait()

        @pl.when(at // (steps // 2) == core)
        def _():
            for shard in range(shards):
                down_out(slot, shard, 0).wait()

    @pl.when(step == 0)
    def _():
        for seq in range(seqs):
            here = slice(seq * rows, (seq + 1) * rows)
            low[here] = grad_ref[seq].astype(jnp.bfloat16)
            ff_in_t[:, here] = ff_in_ref[seq].T
        grad_ffin[...] = jnp.zeros_like(grad_ffin)

    for seq in range(seqs):
        here = slice(seq * rows, (seq + 1) * rows)
        positive = positive_ref[seq].astype(jnp.float32)
        grad_hidden = dot_nt(low[here], w_down_ref[...])
        pre = (grad_hidden * (2.0 * positive)).astype(jnp.bfloat16)
        grad_pre[here] = pre
        hidden[here] = (positive * positive).astype(jnp.bfloat16)
        grad_ffin[here] += dot_nt(pre, w_up_ref[...])

    slot = lax.rem(step, 2)

    @pl.when(step >= 2)
    def _():
        wait_out(step - 2)

    left = ff_in_t[pl.ds(pl.multiple_of((1 - core) * half, half), half), :]
    product = dot_nn(left, grad_pre[...])
    for shard in range(groups):
        up_send[step, place_of(shard, 1 - core, groups)] = product[
            shard * shard_rows : (shard + 1) * shard_rows
        ].astype(jnp.bfloat16)
    up_remote(step).start()

    product = dot_tn(hidden[...], low[...])
    parts = chunk // shards // shard_rows

    def store_down(ref, at):
        for shard in range(shards):
            for part in range(parts):
                row = (shard * parts + part) * shard_rows
                ref[at, shard, :, part * width : (part + 1) * width] = product[
                    row : row + shard_rows
                ].astype(jnp.bfloat16)

    quarter = lax.rem(step, steps // 2)

    @pl.when(step // (steps // 2) == core)
    def _():
        store_down(down_mine, slot)

    @pl.when(step // (steps // 2) != core)
    def _():
        store_down(down_send, quarter)
        down_remote(quarter).start()

    left = ff_in_t[pl.ds(pl.multiple_of(core * half, half), half), :]
    product = dot_nn(left, grad_pre[...])
    for shard in range(groups):
        up_mine[slot, place_of(shard, core, groups)] = product[
            shard * shard_rows : (shard + 1) * shard_rows
        ].astype(jnp.bfloat16)

    @pl.when(step >= 1)
    def _():
        write_out(step - 1)

    @pl.when(step == steps - 1)
    def _():
        gain_sum = offset_sum = 0.0
        for seq in range(seqs):
            for block in blocks_of(rows):
                here = slice(seq * rows + block.start, seq * rows + block.stop)
                grad_in = grad_ffin[here]
                normed, scaling = normal(middle_ref[seq, block])
                gain_sum += jnp.sum(grad_in * normed, 0, keepdims=True)
                offset_sum += jnp.sum(grad_in, 0, keepdims=True)
                value = grad_ref[seq, block].astype(jnp.float32) + norm_back(
                    grad_in, normed, scaling, norms_ref[0:1]
                )
                grad_middle_ref[seq, block] = value
                branch_ref[seq, block] = value.astype(jnp.bfloat16)
        norm_grad_ref[0:1] = gain_sum
        norm_grad_ref[1:2] = offset_sum
        write_out(step)
        wait_out(step - 1)
        wait_out(step)
        for at in range(4):
            up_remote(at).wait_send()
        for at in range(2):
            down_remote(at).wait_send()


def feed_back(grad, positive, middle, ff_in, w_down, w_up, norms, layer, groups, rides, collective_id):
    seqs, rows, width = grad.shape
    ff = w_up.shape[2]
    steps = 4
    chunk = ff // steps
    tokens = (seqs, rows, width)
    flat = (seqs * rows, width)
    f32, bf16 = jnp.float32, jnp.bfloat16
    shard_rows = width // 2 // groups
    shards = groups // 2
    dma = pltpu.SemaphoreType.DMA

    def once(shape):
        return pl.BlockSpec(shape, lambda i: (0,) * len(shape), pipeline_mode=pl.Buffered(1))

    return call(
        functools.partial(feed_back_kernel, groups), "feed_back", 0, (steps,),
        [
            once(tokens),
            pl.BlockSpec((seqs, rows, chunk), lambda i: (0, 0, i)),
            once(tokens),
            once(tokens),
            pl.BlockSpec((None, chunk, width), lambda i: (layer, i, 0)),
            pl.BlockSpec((None, width, chunk), lambda i: (layer, 0, i)),
            full_spec(norms.shape),
        ],
        [pl.BlockSpec(memory_space=pl.ANY), once(tokens), once(tokens), full_spec((2, width))],
        [
            jax.ShapeDtypeStruct((groups, shard_rows, 2 * ff), bf16),
            jax.ShapeDtypeStruct(tokens, f32),
            jax.ShapeDtypeStruct(tokens, bf16),
            jax.ShapeDtypeStruct((2, width), f32),
        ],
        [
            pltpu.VMEM(flat, bf16),
            pltpu.VMEM((width, seqs * rows), bf16),
            pltpu.VMEM((seqs * rows, chunk), bf16),
            pltpu.VMEM((seqs * rows, chunk), bf16),
            pltpu.VMEM(flat, f32),
            pltpu.VMEM((2, groups, shard_rows, chunk), bf16),
            pltpu.VMEM((2, shards, shard_rows, ff), bf16),
            pltpu.VMEM((steps, groups, shard_rows, chunk), bf16),
            pltpu.VMEM((steps // 2, shards, shard_rows, ff), bf16),
            pltpu.VMEM((steps, groups, shard_rows, chunk), bf16),
            pltpu.VMEM((steps // 2, shards, shard_rows, ff), bf16),
            dma((steps,)),
            dma((steps,)),
            dma((steps // 2,)),
            dma((steps // 2,)),
            dma((2,)),
            dma((2, shards)),
        ],
        8 * seqs * rows * width * ff, 50_000_000,
        rides=rides, collective_id=collective_id, others=((),), groups=groups,
    )(grad, positive, middle, ff_in, w_down, w_up, norms)


def heads_back_kernel(core_ref, place_ref, own_ref, got_ref, heads_ref, w_out_ref, grad_ref, out_ref, total):
    core = core_ref[0]
    rows = own_ref.shape[0]
    step = pl.program_id(0)
    sums = 0.0
    for part_ref, at in ((own_ref, core), (got_ref, 1 - core)):
        here = pl.ds(pl.multiple_of(at * rows, rows), rows)
        grad_ref[here, :] = dot_nt(part_ref[...], w_out_ref[...]).astype(jnp.bfloat16)
        sums += dot_tn(heads_ref[here, :], part_ref[...])

    @pl.when(step == 0)
    def _():
        total[...] = sums

    @pl.when(step > 0)
    def _():
        total[...] += sums

    @pl.when(step == pl.num_programs(0) - 1)
    def _():
        groups, shard, _ = out_ref.shape
        for part in range(groups):
            out_ref[place_ref[1, part]] = total[part * shard : (part + 1) * shard].astype(jnp.bfloat16)


def heads_back(core, place, own, got, heads, w_out, layer, after=()):
    seqs, rows, width = own.shape
    half = width // 2
    groups = place.shape[1]
    part = pl.BlockSpec((None, rows, width), lambda s, c, p: (s, 0, 0))
    head = pl.BlockSpec((None, 2 * rows, half), lambda s, c, p: (s, 0, 0))
    out_shape = (groups, half // groups, width)
    return call(
        heads_back_kernel, "heads_back", 2, (seqs,),
        [part, part, head, pl.BlockSpec((None, half, width), lambda s, c, p: (layer, c[0], 0))],
        [head, full_spec(out_shape)],
        [
            jax.ShapeDtypeStruct((seqs, 2 * rows, half), jnp.bfloat16),
            jax.ShapeDtypeStruct(out_shape, jnp.bfloat16),
        ],
        [pltpu.VMEM((half, width), jnp.float32)],
        8 * seqs * rows * width * half, 20_000_000, after,
    )(core, place, own, got, heads, w_out)


def project_back_kernel(
    layer, groups, grad_hbm, weight_hbm, own_hbm, got_hbm, stream_hbm, middle_hbm, out_grad_hbm, norms_ref,
    sum_hbm, out_hbm, norm_grad_ref,
    grad, weight, own, got, stream, middle, result, partial, partial_got, total, keep, send,
    weight_sems, load_sems, partial_sends, partial_gets, send_sem, get_sem, keep_sem, other_sem, out_sems,
):
    core = lax.axis_index("seq")
    other = partner((), groups)
    seqs, rows, width = own.shape
    half = width // 2
    shard_rows, wide = keep.shape[1:]

    def grad_rows(seq, owner):
        return grad.at[seq, pl.ds(pl.multiple_of(owner * rows, rows), rows)]

    def grad_load(seq, which):
        owner = (1 - core, core)[which]
        return pltpu.make_async_copy(
            grad_hbm.at[seq, pl.ds(pl.multiple_of(owner * rows, rows), rows)],
            grad_rows(seq, owner),
            load_sems.at[which, seq],
        )

    loads = head_weight_copies(weight_hbm, layer, weight, weight_sems, core)
    for copy in loads:
        copy.start()
    for which in range(2):
        for seq in range(seqs):
            grad_load(seq, which).start()
    inputs = [
        pltpu.make_async_copy(source, target, load_sems.at[2 + at, 0])
        for at, (source, target) in enumerate(
            ((own_hbm, own), (got_hbm, got), (stream_hbm, stream), (middle_hbm, middle))
        )
    ]
    for copy in inputs:
        copy.start()
    others = pltpu.make_async_copy(out_grad_hbm, sum_hbm.at[:, :, pl.ds(2 * wide, width)], other_sem)
    others.start()
    for copy in loads:
        copy.wait()

    swaps = [
        remote(partial.at[seq], partial_got.at[seq], partial_sends.at[seq], partial_gets.at[seq], other)
        for seq in range(seqs)
    ]
    for seq in range(seqs):
        grad_load(seq, 0).wait()
        partial[seq] = dot_nt(grad_rows(seq, 1 - core)[...], weight[...]).astype(jnp.bfloat16)
        swaps[seq].start()

    for seq in range(seqs):
        grad_load(seq, 1).wait()
    for copy in inputs[:2]:
        copy.wait()
    left = (own, got)
    for owner, target in ((1 - core, send), (core, keep)):
        lanes = pl.ds(pl.multiple_of(owner * half, half), half)
        sums = 0.0
        for seq in range(seqs):
            for part, at in ((own, core), (got, 1 - core)):
                sums += dot_tn(part[seq, :, lanes], grad_rows(seq, at)[...])
        total[...] = sums
        for shard in range(groups):
            target[place_of(shard, owner, groups)] = total[
                shard * shard_rows : (shard + 1) * shard_rows
            ].astype(jnp.bfloat16)
        if target is send:
            swap = remote(send, sum_hbm.at[:, :, pl.ds(wide, wide)], send_sem, get_sem, other)
            swap.start()
        else:
            kept = pltpu.make_async_copy(keep, sum_hbm.at[:, :, pl.ds(0, wide)], keep_sem)
            kept.start()

    for copy in inputs[2:]:
        copy.wait()
    gain_sum = offset_sum = 0.0
    outs = []
    for seq in range(seqs):
        here = dot_nt(grad_rows(seq, core)[...], weight[...])
        swaps[seq].wait_recv()
        here = here + partial_got[seq].astype(jnp.float32)
        normed, scaling = normal(stream[seq].astype(jnp.float32))
        gain_sum += jnp.sum(here * normed, 0, keepdims=True)
        offset_sum += jnp.sum(here, 0, keepdims=True)
        value = middle[seq] + norm_back(here, normed, scaling, norms_ref[0:1])
        result[seq] = value.astype(result.dtype)
        outs.append(pltpu.make_async_copy(result.at[seq], out_hbm.at[seq], out_sems.at[seq]))
        outs[-1].start()
    norm_grad_ref[0:1] = gain_sum
    norm_grad_ref[1:2] = offset_sum
    for copy in outs + [kept, others]:
        copy.wait()
    for copy in swaps:
        copy.wait_send()
    swap.wait()


def project_back(
    grad_proj, weight, own, got, stream, middle, out_grad, norms, layer, dtype, groups, rides, collective_id
):
    seqs, cap, wide = grad_proj.shape
    rows, width = cap // 2, own.shape[2]
    tokens = (seqs, rows, width)
    shard_rows = width // 2 // groups
    f32, bf16 = jnp.float32, jnp.bfloat16
    dma = pltpu.SemaphoreType.DMA
    anywhere = pl.BlockSpec(memory_space=pl.ANY)
    return call(
        functools.partial(project_back_kernel, layer, groups), "project_back", 0, (1,),
        [anywhere] * 7 + [full_spec(norms.shape)],
        [anywhere, anywhere, full_spec((2, width))],
        [
            jax.ShapeDtypeStruct((groups, shard_rows, 2 * wide + width), bf16),
            jax.ShapeDtypeStruct(tokens, dtype),
            jax.ShapeDtypeStruct((2, width), f32),
        ],
        [
            pltpu.VMEM(grad_proj.shape, bf16),
            pltpu.VMEM((width, wide), bf16),
            pltpu.VMEM(tokens, bf16),
            pltpu.VMEM(tokens, bf16),
            pltpu.VMEM(tokens, stream.dtype),
            pltpu.VMEM(tokens, f32),
            pltpu.VMEM(tokens, dtype),
            pltpu.VMEM(tokens, bf16),
            pltpu.VMEM(tokens, bf16),
            pltpu.VMEM((width // 2, wide), f32),
            pltpu.VMEM((groups, shard_rows, wide), bf16),
            pltpu.VMEM((groups, shard_rows, wide), bf16),
            dma((wide // LANES,)),
            dma((6, seqs)),
            dma((seqs,)),
            dma((seqs,)),
            dma,
            dma,
            dma,
            dma,
            dma((seqs,)),
        ],
        8 * seqs * rows * width * wide, 30_000_000,
        rides=rides, collective_id=collective_id, others=((),), groups=groups,
    )(grad_proj, weight, own, got, stream, middle, out_grad, norms)


def merge_kernel(keep_ref, got_ref, out_ref):
    out_ref[...] = (keep_ref[...].astype(jnp.float32) + got_ref[...].astype(jnp.float32)).astype(
        out_ref.dtype
    )


def merge(keep, got, after=()):
    count, rows, width = got.shape
    some = min(count, 2)
    spec = pl.BlockSpec((some, rows, width), lambda i: (i, 0, 0))
    return call(
        merge_kernel, "merge", 0, (count // some,),
        [pl.BlockSpec((some, rows, width), lambda i: (i + count // some, 0, 0)), spec],
        spec, jax.ShapeDtypeStruct(got.shape, got.dtype), [], 0, 6 * got.size, after,
    )(keep, got)


def finish(parts, got):
    return sum(part[0].astype(jnp.float32) for part in [parts[3:4], *got])


def local_pair(
    activations,
    cotangent,
    lengths,
    weights_qkv,
    conv_taps,
    weights_out,
    weights_up,
    weights_down,
    norm_gains,
    norm_biases,
):
    seqs, rows, width = activations.shape
    half = width // 2
    ff = weights_up.shape[2]
    pairs = half // LANES
    core = lax.axis_index("seq")
    group = lax.axis_index("batch")
    groups = lax.axis_size("batch")
    core_arg = core.astype(jnp.int32).reshape(1)
    place = jnp.stack([shard_places(1 - core, group, groups), shard_places(core, group, groups)])

    def head_columns(x):
        lead = x.shape[:-1]
        x = x.reshape(*lead, 3, 2, pairs, LANES)
        x = lax.dynamic_index_in_dim(x, core, len(lead) + 1, keepdims=False)
        return jnp.swapaxes(x, -3, -2).reshape(*lead, 3 * half)

    taps = head_columns(conv_taps.transpose(0, 2, 1))
    norms = jnp.stack([norm_gains, norm_biases], 1).transpose(0, 3, 1, 2)
    last = groups.bit_length() - 1
    line = ((last - 2, last - 1), (last - 2,), (last - 1,))
    sizes = [groups >> (stage + 1) for stage in range(last)]

    stream = activations
    attn_in = norm(stream, norms[0, 0])
    kept = []
    for layer in range(LAYERS):
        last = layer == LAYERS - 1
        attn_got = swap_core(attn_in)
        mixed, proj = project(core_arg, attn_in, attn_got, weights_qkv, taps, layer)
        heads, logs = attend(mixed, lengths)
        heads_got = swap_core(lax.dynamic_slice_in_dim(heads, (1 - core) * rows, rows, 1))
        middle, ff_in, positive, result, *rest = feed(
            core_arg, stream, heads, heads_got, weights_out, weights_up, weights_down,
            norms[layer, 1], norms[min(layer + 1, LAYERS - 1), 0], layer, last,
        )
        kept.append((stream, attn_in, attn_got, mixed, proj, heads, logs, middle, ff_in, positive))
        stream = result
        attn_in = None if last else rest[0]

    def line_rides(parts):
        return [(parts, at, 1, flips) for at, flips in enumerate(line)]

    grad = cotangent
    ff_done, attn_done, small = [], [], []
    ff_parts = attn_sum = None
    for layer in reversed(range(LAYERS)):
        below, attn_in, attn_got, mixed, proj, heads, logs, middle, ff_in, positive = kept[layer]
        above = attn_sum is not None
        ids = 3 * layer
        rides = line_rides(ff_parts) + [(attn_sum, 0, sizes[0], (0,))] if above else []
        ff_sum, grad_middle, branch, norm_two, *got = feed_back(
            grad, positive, middle, ff_in, weights_down, weights_up, norms[layer, 1], layer, groups,
            rides, ids,
        )
        branch_got = swap_core(branch)
        rides = [(ff_sum, 0, sizes[0], (0,))]
        if above:
            ff_done.append(finish(ff_parts, got[:3]))
            attn_parts = merge(attn_sum, got[3])
            rides.append((attn_parts, 0, sizes[1], (1,)))
        grad_heads, out = heads_back(core_arg, place, branch, branch_got, heads, weights_out, layer)
        grad_proj, grad_taps, *got = attend_back(
            mixed, proj, grad_heads, heads, logs, taps[layer], lengths, rides, ids + 1, groups
        )
        ff_parts = merge(ff_sum, got[0])
        rides = [(ff_parts, 0, sizes[1], (1,))]
        if above:
            attn_parts = merge(attn_parts, got[1])
            rides += line_rides(attn_parts)
        attn_sum, grad, norm_one, *got = project_back(
            grad_proj, weights_qkv, attn_in, attn_got, below, grad_middle, out, norms[layer, 0], layer,
            jnp.bfloat16 if layer == 0 else jnp.float32, groups, rides, ids + 2,
        )
        ff_parts = merge(ff_parts, got[0])
        if above:
            attn_done.append(finish(attn_parts, got[1:]))
        taps_mine = jnp.sum(grad_taps, 0).reshape(3, pairs, 3, LANES).transpose(0, 2, 1, 3)
        zero = jnp.zeros((3, 3, half), jnp.float32)
        taps_mine = taps_mine.reshape(3, 3, half)
        taps_wide = jnp.concatenate(
            [jnp.where(core == 0, taps_mine, zero), jnp.where(core == 0, zero, taps_mine)], 2
        ).transpose(1, 2, 0)
        small.append(
            jnp.concatenate(
                [
                    taps_wide.reshape(2 * groups, -1),
                    jnp.stack([norm_one[0], norm_two[0]], -1).reshape(2 * groups, -1),
                    jnp.stack([norm_one[1], norm_two[1]], -1).reshape(2 * groups, -1),
                ],
                1,
            )
        )
    ff_done.append(
        finish(ff_parts, [exchange(x[at : at + 1], flips, groups) for x, at, _, flips in line_rides(ff_parts)])
    )
    attn_parts = merge(attn_sum, exchange(attn_sum[: sizes[0]], (0,), groups))
    attn_parts = merge(attn_parts, exchange(attn_parts[: sizes[1]], (1,), groups))
    attn_done.append(
        finish(attn_parts, [exchange(x[at : at + 1], flips, groups) for x, at, _, flips in line_rides(attn_parts)])
    )

    ff_done = jnp.stack(ff_done[::-1])
    attn_done = jnp.stack(attn_done[::-1])
    shard = ff_done.shape[1]
    up = ff_done[:, :, :ff]
    down = ff_done[:, :, ff:].reshape(LAYERS, shard, -1, width).transpose(0, 2, 1, 3)
    down = down.reshape(LAYERS, -1, width)
    out = attn_done[:, :, 6 * half :]
    qkv = attn_done[:, :, : 6 * half].reshape(LAYERS, shard, 2, pairs, 3, LANES)
    qkv = jnp.where(core == 0, qkv, qkv[:, :, ::-1])
    qkv = qkv.transpose(0, 1, 4, 2, 3, 5).reshape(LAYERS, shard, 3 * width)

    small = jnp.stack(small[::-1], 1)
    mine = lax.dynamic_slice_in_dim(small, core * groups, groups, 0)
    theirs = lax.dynamic_slice_in_dim(small, (1 - core) * groups, groups, 0)
    mine = mine + swap_core(theirs)
    step = groups // 2
    while step:
        low = (group // step) % 2
        send = lax.dynamic_slice_in_dim(mine, (1 - low) * step, step, 0)
        got = lax.ppermute(send, "batch", [(i, i ^ step) for i in range(groups)])
        mine = lax.dynamic_slice_in_dim(mine, low * step, step, 0) + got
        step //= 2
    mine = mine[0]
    n_taps = 9 * width // (2 * groups)
    n_norm = 2 * width // (2 * groups)
    return (
        stream,
        grad,
        qkv,
        mine[:, :n_taps].reshape(LAYERS, -1, 3),
        out,
        up,
        down,
        mine[:, n_taps : n_taps + n_norm].reshape(LAYERS, -1, 2),
        mine[:, n_taps + n_norm :].reshape(LAYERS, -1, 2),
    )


def solution(mesh):
    chosen = local_pair if mesh.shape["seq"] == 2 else local
    placed = (
        P("batch", "seq", None),
        P("batch", "seq", None),
        P("batch"),
        P(),
        P(),
        P(),
        P(),
        P(),
        P(),
        P(),
    )
    return jax.shard_map(
        chosen,
        mesh=mesh,
        in_specs=placed,
        out_specs=(
            P("batch", "seq", None),
            P("batch", "seq", None),
            P(None, ("seq", "batch"), None),
            P(None, ("seq", "batch"), None),
            P(None, ("seq", "batch"), None),
            P(None, ("seq", "batch"), None),
            P(None, ("seq", "batch"), None),
            P(None, ("seq", "batch"), None),
            P(None, ("seq", "batch"), None),
        ),
        check_vma=False,
    )
```

```python
import functools
import types

import jax
import jax.numpy as jnp
from jax import lax
from jax.experimental import pallas as pl
from jax.experimental.pallas import tpu as pltpu
from jax.sharding import PartitionSpec as P

HEAD_DIM = 64
LAYERS = 2


def shifted(x, axis, by):
    size = lax.axis_size(axis)
    pairs = [(i, i + by) for i in range(size) if 0 <= i + by < size]
    return lax.ppermute(x, axis, pairs)


def normalize(stream):
    average = jnp.mean(stream, -1, keepdims=True)
    centered = stream - average
    scaling = lax.rsqrt(jnp.mean(centered * centered, -1, keepdims=True) + 1e-05)
    return (centered * scaling, scaling)


def norm_back(grad_norm, normed, scaling, gain):
    scaled = grad_norm * gain
    return scaling * (
        scaled
        - jnp.mean(scaled, -1, keepdims=True)
        - normed * jnp.mean(scaled * normed, -1, keepdims=True)
    )


def split_heads(block):
    return block.reshape(block.shape[0], -1, HEAD_DIM)


def masked_scores(query_seq, key_seq, length, positions):
    scores = jnp.einsum(
        "qhd,khd->hqk",
        split_heads(query_seq),
        split_heads(key_seq),
        preferred_element_type=jnp.float32,
    ) * HEAD_DIM ** (-0.5)
    key_place = jnp.arange(key_seq.shape[0], dtype=jnp.int32)
    allowed = (key_place[None, :] < length) & (
        (key_place[None, :] <= positions[:, None]) | (positions[:, None] >= length)
    )
    return jnp.where(allowed[None], scores, -1e30)


def attention_forward(queries, keys_all, values_all, lengths, positions):

    def one_sequence(items):
        query_seq, key_seq, value_seq, length = items
        scores = masked_scores(query_seq, key_seq, length, positions)
        highest = jnp.max(scores, -1, keepdims=True)
        expo = jnp.exp(scores - highest)
        totals = jnp.sum(expo, -1, keepdims=True)
        probs = (expo / totals).astype(jnp.bfloat16)
        mixed = jnp.einsum(
            "hqk,khd->qhd", probs, split_heads(value_seq), preferred_element_type=jnp.float32
        )
        log_total = (highest + jnp.log(totals))[..., 0]
        return (mixed.reshape(query_seq.shape).astype(jnp.bfloat16), log_total)

    return lax.map(one_sequence, (queries, keys_all, values_all, lengths))


def attention_backward(
    queries, keys_all, values_all, lengths, positions, log_totals, grad_attended
):

    def one_sequence(items):
        query_seq, key_seq, value_seq, length, log_total, grad_seq = items
        scores = masked_scores(query_seq, key_seq, length, positions)
        probs = jnp.exp(scores - log_total[..., None])
        grad_heads = split_heads(grad_seq)
        grad_probs = jnp.einsum(
            "qhd,khd->hqk", grad_heads, split_heads(value_seq), preferred_element_type=jnp.float32
        )
        inner = jnp.sum(probs * grad_probs, -1, keepdims=True)
        grad_scores = (probs * (grad_probs - inner)).astype(jnp.bfloat16)
        grad_query = jnp.einsum(
            "hqk,khd->qhd", grad_scores, split_heads(key_seq), preferred_element_type=jnp.float32
        ) * HEAD_DIM ** (-0.5)
        grad_key = jnp.einsum(
            "hqk,qhd->khd", grad_scores, split_heads(query_seq), preferred_element_type=jnp.float32
        ) * HEAD_DIM ** (-0.5)
        grad_value = jnp.einsum(
            "hqk,qhd->khd",
            probs.astype(jnp.bfloat16),
            grad_heads,
            preferred_element_type=jnp.float32,
        )
        return (
            grad_query.reshape(query_seq.shape),
            grad_key.reshape(key_seq.shape),
            grad_value.reshape(key_seq.shape),
        )

    return lax.map(
        one_sequence, (queries, keys_all, values_all, lengths, log_totals, grad_attended)
    )


def layer_forward(stream, lengths, positions, w_qkv, taps, w_out, w_up, w_down, gains, offsets):
    seqs_here, rows, width = stream.shape
    tokens = seqs_here * rows
    normed_one, scale_one = normalize(stream)
    attn_in = (normed_one * gains[:, 0] + offsets[:, 0]).astype(jnp.bfloat16)
    projected = jnp.dot(
        attn_in.reshape(tokens, width), w_qkv, preferred_element_type=jnp.float32
    ).reshape(seqs_here, rows, 3 * width)
    before = shifted(projected[:, rows - 2 :, :].astype(jnp.bfloat16), "seq", 1).astype(jnp.float32)
    extended = jnp.concatenate([before, projected], 1)
    conv_out = (
        taps[:, 0] * extended[:, 2:]
        + taps[:, 1] * extended[:, 1 : rows + 1]
        + taps[:, 2] * extended[:, :rows]
    )
    mixed_qkv = conv_out.astype(jnp.bfloat16)
    queries = mixed_qkv[..., :width]
    keys_here = mixed_qkv[..., width : 2 * width]
    values_here = mixed_qkv[..., 2 * width :]
    keys_all, values_all = (
        lax.all_gather(keys_here, "seq", axis=1, tiled=True),
        lax.all_gather(values_here, "seq", axis=1, tiled=True),
    )
    attended, log_totals = attention_forward(queries, keys_all, values_all, lengths, positions)
    branch = jnp.dot(attended.reshape(tokens, width), w_out, preferred_element_type=jnp.float32)
    middle = stream + branch.reshape(stream.shape)
    normed_two, scale_two = normalize(middle)
    ff_in = (normed_two * gains[:, 1] + offsets[:, 1]).astype(jnp.bfloat16).reshape(tokens, width)
    hidden_pre = jnp.dot(ff_in, w_up, preferred_element_type=jnp.float32)
    hidden = (jax.nn.relu(hidden_pre) ** 2).astype(jnp.bfloat16)
    result = middle + jnp.dot(hidden, w_down, preferred_element_type=jnp.float32).reshape(
        stream.shape
    )
    kept_keys = (keys_all, values_all)
    saved = (
        normed_one,
        scale_one,
        attn_in,
        extended,
        queries,
        kept_keys,
        attended,
        log_totals,
        normed_two,
        scale_two,
        ff_in,
        hidden_pre,
        hidden,
    )
    return (result, saved)


def layer_backward(grad_stream, lengths, positions, saved, w_qkv, taps, w_out, w_up, w_down, gains):
    (
        normed_one,
        scale_one,
        attn_in,
        extended,
        queries,
        kept_keys,
        attended,
        log_totals,
        normed_two,
        scale_two,
        ff_in,
        hidden_pre,
        hidden,
    ) = saved
    seqs_here, rows, width = grad_stream.shape
    tokens = seqs_here * rows
    grad_down_in = grad_stream.reshape(tokens, width).astype(jnp.bfloat16)
    grad_down = jnp.einsum("tf,td->fd", hidden, grad_down_in, preferred_element_type=jnp.float32)
    grad_hidden = jnp.dot(grad_down_in, w_down.T, preferred_element_type=jnp.float32)
    grad_pre = (grad_hidden * 2.0 * jax.nn.relu(hidden_pre)).astype(jnp.bfloat16)
    grad_up = jnp.einsum("td,tf->df", ff_in, grad_pre, preferred_element_type=jnp.float32)
    grad_ffin = jnp.dot(grad_pre, w_up.T, preferred_element_type=jnp.float32).reshape(
        grad_stream.shape
    )
    gain_two = jnp.sum(grad_ffin * normed_two, (0, 1))
    offset_two = jnp.sum(grad_ffin, (0, 1))
    grad_middle = grad_stream + norm_back(grad_ffin, normed_two, scale_two, gains[:, 1])
    grad_branch = grad_middle.reshape(tokens, width).astype(jnp.bfloat16)
    grad_out = jnp.einsum(
        "td,te->de",
        attended.reshape(tokens, width),
        grad_branch,
        preferred_element_type=jnp.float32,
    )
    grad_attended = jnp.dot(grad_branch, w_out.T, preferred_element_type=jnp.float32)
    grad_attended = grad_attended.astype(jnp.bfloat16).reshape(grad_stream.shape)
    keys_all, values_all = kept_keys
    grad_query, grad_key_all, grad_value_all = attention_backward(
        queries, keys_all, values_all, lengths, positions, log_totals, grad_attended
    )
    grad_key, grad_value = (
        lax.psum_scatter(
            grad_key_all.astype(jnp.bfloat16), "seq", scatter_dimension=1, tiled=True
        ).astype(jnp.float32),
        lax.psum_scatter(
            grad_value_all.astype(jnp.bfloat16), "seq", scatter_dimension=1, tiled=True
        ).astype(jnp.float32),
    )
    grad_conv = jnp.concatenate([grad_query, grad_key, grad_value], -1)
    after = shifted(grad_conv[:, :2, :].astype(jnp.bfloat16), "seq", -1).astype(jnp.float32)
    grad_ext = jnp.concatenate([grad_conv, after], 1)
    grad_proj = (
        taps[:, 0] * grad_ext[:, :rows]
        + taps[:, 1] * grad_ext[:, 1 : rows + 1]
        + taps[:, 2] * grad_ext[:, 2:]
    )
    grad_taps = jnp.stack(
        [
            jnp.sum(grad_conv * extended[:, 2:], (0, 1)),
            jnp.sum(grad_conv * extended[:, 1 : rows + 1], (0, 1)),
            jnp.sum(grad_conv * extended[:, :rows], (0, 1)),
        ],
        -1,
    )
    grad_proj_low = grad_proj.reshape(tokens, 3 * width).astype(jnp.bfloat16)
    grad_qkv = jnp.einsum(
        "td,tf->df",
        attn_in.reshape(tokens, width),
        grad_proj_low,
        preferred_element_type=jnp.float32,
    )
    grad_attn_in = jnp.dot(grad_proj_low, w_qkv.T, preferred_element_type=jnp.float32).reshape(
        grad_stream.shape
    )
    gain_one = jnp.sum(grad_attn_in * normed_one, (0, 1))
    offset_one = jnp.sum(grad_attn_in, (0, 1))
    grad_input = grad_middle + norm_back(grad_attn_in, normed_one, scale_one, gains[:, 0])
    grad_gains = jnp.stack([gain_one, gain_two], -1)
    grad_biases = jnp.stack([offset_one, offset_two], -1)
    return (
        grad_input,
        (grad_qkv, grad_taps, grad_out, grad_up, grad_down, grad_gains, grad_biases),
    )


def reduce_grads(grad_qkv, grad_taps, grad_out, grad_up, grad_down, grad_gains, grad_biases):
    part_qkv, part_taps, part_out, part_up, part_down, part_gains, part_biases = (
        lax.psum_scatter(
            grad_qkv.astype(jnp.bfloat16), "seq", scatter_dimension=0, tiled=True
        ).astype(jnp.float32),
        lax.psum_scatter(
            grad_taps.astype(jnp.bfloat16), "seq", scatter_dimension=0, tiled=True
        ).astype(jnp.float32),
        lax.psum_scatter(
            grad_out.astype(jnp.bfloat16), "seq", scatter_dimension=0, tiled=True
        ).astype(jnp.float32),
        lax.psum_scatter(
            grad_up.astype(jnp.bfloat16), "seq", scatter_dimension=0, tiled=True
        ).astype(jnp.float32),
        lax.psum_scatter(
            grad_down.astype(jnp.bfloat16), "seq", scatter_dimension=0, tiled=True
        ).astype(jnp.float32),
        lax.psum_scatter(
            grad_gains.astype(jnp.bfloat16), "seq", scatter_dimension=0, tiled=True
        ).astype(jnp.float32),
        lax.psum_scatter(
            grad_biases.astype(jnp.bfloat16), "seq", scatter_dimension=0, tiled=True
        ).astype(jnp.float32),
    )
    return (
        lax.psum_scatter(
            part_qkv.astype(jnp.bfloat16), "batch", scatter_dimension=0, tiled=True
        ).astype(jnp.float32),
        lax.psum_scatter(
            part_taps.astype(jnp.bfloat16), "batch", scatter_dimension=0, tiled=True
        ).astype(jnp.float32),
        lax.psum_scatter(
            part_out.astype(jnp.bfloat16), "batch", scatter_dimension=0, tiled=True
        ).astype(jnp.float32),
        lax.psum_scatter(
            part_up.astype(jnp.bfloat16), "batch", scatter_dimension=0, tiled=True
        ).astype(jnp.float32),
        lax.psum_scatter(
            part_down.astype(jnp.bfloat16), "batch", scatter_dimension=0, tiled=True
        ).astype(jnp.float32),
        lax.psum_scatter(
            part_gains.astype(jnp.bfloat16), "batch", scatter_dimension=0, tiled=True
        ).astype(jnp.float32),
        lax.psum_scatter(
            part_biases.astype(jnp.bfloat16), "batch", scatter_dimension=0, tiled=True
        ).astype(jnp.float32),
    )


def local(
    activations,
    cotangent,
    lengths,
    weights_qkv,
    conv_taps,
    weights_out,
    weights_up,
    weights_down,
    norm_gains,
    norm_biases,
):
    seqs_here, rows, width = activations.shape
    positions = lax.axis_index("seq") * rows + jnp.arange(rows, dtype=jnp.int32)
    stream = activations.astype(jnp.float32)
    saved_all = []
    for layer_num in range(LAYERS):
        stream, saved = layer_forward(
            stream,
            lengths,
            positions,
            weights_qkv[layer_num],
            conv_taps[layer_num],
            weights_out[layer_num],
            weights_up[layer_num],
            weights_down[layer_num],
            norm_gains[layer_num],
            norm_biases[layer_num],
        )
        saved_all.append(saved)
    block_out = stream.astype(jnp.bfloat16)
    grad_stream = cotangent.astype(jnp.float32)
    collected = []
    for layer_num in reversed(range(LAYERS)):
        grad_stream, layer_grads = layer_backward(
            grad_stream,
            lengths,
            positions,
            saved_all[layer_num],
            weights_qkv[layer_num],
            conv_taps[layer_num],
            weights_out[layer_num],
            weights_up[layer_num],
            weights_down[layer_num],
            norm_gains[layer_num],
        )
        grad_qkv, grad_taps, grad_out, grad_up, grad_down, grad_gains, grad_biases = layer_grads
        collected.append(
            reduce_grads(grad_qkv, grad_taps, grad_out, grad_up, grad_down, grad_gains, grad_biases)
        )
    collected = collected[::-1]
    stacked = [jnp.stack([member[index] for member in collected], 0) for index in range(7)]
    return (
        block_out,
        grad_stream.astype(jnp.bfloat16),
        stacked[0],
        stacked[1],
        stacked[2],
        stacked[3],
        stacked[4],
        stacked[5],
        stacked[6],
    )


TILE = 256
LANES = 128
VMEM_LIMIT = 60 * 2**20


def dot_nt(left, right):
    return lax.dot_general(
        left, right, (((1,), (1,)), ((), ())), preferred_element_type=jnp.float32
    )


def dot_nn(left, right):
    return lax.dot_general(
        left, right, (((1,), (0,)), ((), ())), preferred_element_type=jnp.float32
    )


def dot_tn(left, right):
    return lax.dot_general(
        left, right, (((0,), (0,)), ((), ())), preferred_element_type=jnp.float32
    )


def head_lanes(head):
    lane = lax.broadcasted_iota(jnp.int32, (1, LANES), 1)
    return (lane >= head * HEAD_DIM) & (lane < (head + 1) * HEAD_DIM)


def causal_tile():
    keys = lax.broadcasted_iota(jnp.int32, (TILE, TILE), 0)
    queries = lax.broadcasted_iota(jnp.int32, (TILE, TILE), 1)
    return keys <= queries


def attend_heads(whole, conv_ref, out_ref, log_ref):
    cap = conv_ref.shape[0]
    hidden = jnp.where(whole, 0.0, -1e30)
    queries = conv_ref[:, :LANES]
    keys = conv_ref[:, LANES : 2 * LANES] * jnp.bfloat16(HEAD_DIM**-0.5)
    keys = [jnp.where(head_lanes(head), keys, jnp.bfloat16(0)) for head in range(2)]
    values_t = conv_ref[:, 2 * LANES :].T
    ones = jnp.ones((16, cap), jnp.bfloat16)
    values = [
        jnp.concatenate([values_t[head * HEAD_DIM : (head + 1) * HEAD_DIM], ones], 0) for head in range(2)
    ]

    def scores_of(block, head):
        rows = slice(block * TILE, (block + 1) * TILE)
        parts = []
        for start in range(0, (block + 1) * TILE, TILE):
            part = dot_nt(keys[head][start : start + TILE], queries[rows])
            if start == block * TILE:
                part = jnp.where(causal_tile(), part, -1e30)
            if start >= cap // 2:
                part = part + hidden
            parts.append(part)
        return parts

    def weights_of(parts):
        highest = functools.reduce(jnp.maximum, [jnp.max(part, 0, keepdims=True) for part in parts])
        return highest, [jnp.exp(part - highest).astype(jnp.bfloat16) for part in parts]

    def finish(block, head, highest, expo):
        got = sum(
            dot_nn(values[head][:, at * TILE : (at + 1) * TILE], part) for at, part in enumerate(expo)
        )
        total = got[HEAD_DIM : HEAD_DIM + 1]
        log_ref[head : head + 1, block * TILE : (block + 1) * TILE] = highest + jnp.log(total)
        return got[:HEAD_DIM] / total

    items = [(block, head) for block in range(cap // TILE) for head in range(2)]
    ahead = scores_of(*items[0])
    waiting = None
    mixed = []

    def close(item):
        mixed.append(finish(*item))
        if len(mixed) == 2:
            rows = slice(item[0] * TILE, (item[0] + 1) * TILE)
            out_ref[rows, :] = jnp.concatenate(mixed, 0).T.astype(jnp.bfloat16)
            mixed.clear()

    for at, item in enumerate(items):
        parts = ahead
        if at + 1 < len(items):
            ahead = scores_of(*items[at + 1])
        if waiting is not None:
            close(waiting)
        waiting = (*item, *weights_of(parts))
    close(waiting)


def attend_back_heads(
    whole, conv_ref, proj_ref, grad_ref, out_ref, log_ref, taps_ref, back_ref, grad_taps_ref, query_t_acc, shift_acc
):
    cap = conv_ref.shape[0]
    factor = jnp.bfloat16(HEAD_DIM**-0.5)
    queries = conv_ref[:, :LANES] * factor
    grads = grad_ref[...]
    keys = [
        jnp.where(head_lanes(head), conv_ref[:, LANES : 2 * LANES], jnp.bfloat16(0)) for head in range(2)
    ]
    values = [
        jnp.where(head_lanes(head), conv_ref[:, 2 * LANES :], jnp.bfloat16(0)) for head in range(2)
    ]
    keys_t = (conv_ref[:, LANES : 2 * LANES] * factor).T
    queries_t = queries.T
    grads_t = grads.T
    product_t = (grads.astype(jnp.float32) * out_ref[...].astype(jnp.float32)).T
    inner = [
        jnp.sum(product_t[head * HEAD_DIM : (head + 1) * HEAD_DIM], 0, keepdims=True)
        for head in range(2)
    ]
    logs = [log_ref[head : head + 1, :] for head in range(2)]
    blocks = cap // TILE

    def products(item):
        head, key, query = item
        rows, cols = slice(key * TILE, (key + 1) * TILE), slice(query * TILE, (query + 1) * TILE)
        return dot_nt(keys[head][rows], queries[cols]), dot_nt(values[head][rows], grads[cols])

    def weights_of(item, raw):
        head, key, query = item
        cols = slice(query * TILE, (query + 1) * TILE)
        log = logs[head][:, cols]
        if key * TILE >= cap // 2:
            log = jnp.where(whole, log, 1e30)
        probs = jnp.exp(raw[0] - log)
        if key == query:
            probs = jnp.where(causal_tile(), probs, 0.0)
        scores = probs * (raw[1] - inner[head][:, cols])
        return probs.astype(jnp.bfloat16), scores.astype(jnp.bfloat16)

    query_t_acc[...] = jnp.zeros_like(query_t_acc)
    grad_value = {}
    grad_key = {}
    grad_query = {}

    def add(store, at, term):
        store[at] = term if at not in store else store[at] + term

    def finish(item, probs, scores):
        head, key, query = item
        lanes = slice(head * HEAD_DIM, (head + 1) * HEAD_DIM)
        rows, cols = slice(key * TILE, (key + 1) * TILE), slice(query * TILE, (query + 1) * TILE)
        add(grad_value, (head, key), dot_nt(grads_t[lanes, cols], probs))
        add(grad_key, (head, key), dot_nt(queries_t[lanes, cols], scores))
        query_t_acc[lanes, cols] += dot_nn(keys_t[lanes, rows], scores)

    items = [(head, key, query) for key in range(blocks) for head in range(2) for query in range(key, blocks)]
    ahead = products(items[0])
    waiting = None
    for at, item in enumerate(items):
        raw = ahead
        if at + 1 < len(items):
            ahead = products(items[at + 1])
        if waiting is not None:
            finish(*waiting)
        waiting = (item, *weights_of(item, raw))
    finish(*waiting)
    for key in range(blocks):
        rows = slice(key * TILE, (key + 1) * TILE)
        shift_acc[1, rows, :] = jnp.concatenate([grad_key[0, key], grad_key[1, key]], 0).T
        shift_acc[2, rows, :] = jnp.concatenate([grad_value[0, key], grad_value[1, key]], 0).T
    shift_acc[0, :cap, :] = query_t_acc[...].T
    shift_acc[:, pl.ds(cap, 8), :] = jnp.zeros((3, 8, LANES), jnp.float32)
    for kind in range(3):
        lanes = slice(kind * LANES, (kind + 1) * LANES)
        proj = proj_ref[:, lanes].astype(jnp.float32)
        total = 0.0
        for lag in range(3):
            moved = shift_acc[kind, lag : lag + cap, :]
            total = total + taps_ref[lag : lag + 1, lanes] * moved
            grad_taps_ref[lag : lag + 1, lanes] = jnp.sum(moved * proj, 0, keepdims=True)
        back_ref[:, lanes] = total.astype(jnp.bfloat16)


def group_bits(groups):
    order = list(range(groups.bit_length() - 1))
    return order, [1, 0] + order[2:]


def normal(x):
    average = jnp.mean(x, -1, keepdims=True)
    centered = x - average
    scaling = lax.rsqrt(jnp.mean(centered * centered, -1, keepdims=True) + 1e-05)
    return centered * scaling, scaling


def blocks_of(rows, size=512):
    return [slice(at, at + size) for at in range(0, rows, size)]


def flip(value, bit):
    return value + (1 - 2 * (value // 2**bit % 2)) * 2**bit


def partner(flips, groups):
    core, group = lax.axis_index("seq"), lax.axis_index("batch")
    if not flips:
        return dict(seq=1 - core, batch=group)
    to = []
    for bits in group_bits(groups):
        other = group
        for place in flips:
            other = flip(other, bits[place])
        to.append(other)
    return dict(seq=core, batch=(1 - core) * to[0] + core * to[1])


def meet(partners):
    greet(partners)
    pl.semaphore_wait(pltpu.get_barrier_semaphore(), len(partners))


def greet(partners):
    barrier = pltpu.get_barrier_semaphore()
    for device in partners:
        pl.semaphore_signal(barrier, inc=1, device_id=device, device_id_type=pl.DeviceIdType.MESH)


def remote(source, target, sends, receives, device):
    return pltpu.make_async_remote_copy(
        src_ref=source,
        dst_ref=target,
        send_sem=sends,
        recv_sem=receives,
        device_id=device,
        device_id_type=pl.DeviceIdType.MESH,
    )


def full_spec(shape):
    return pl.BlockSpec(shape, lambda *_: (0,) * len(shape))


def stage(
    name, body, inputs, small, outputs, scratch, copies, groups, collective_id, flops, moved, lengths=None
):
    partners = scratch.pop("partners")
    scalars = {} if lengths is None else dict(lengths=lengths)
    names = [*scalars, *inputs, *small, *outputs, *scratch]

    def kernel(*refs):
        r = types.SimpleNamespace(**dict(zip(names, refs)))
        local_sems, send_sems, get_sems = refs[len(names) :]
        counts = [0, 0]

        def local(source, target):
            at = counts[0]
            counts[0] += 1
            return Move(lambda: pltpu.make_async_copy(ref(source), ref(target), local_sems.at[at]))

        def send(source, target, flips=()):
            at = counts[1]
            counts[1] += 1

            def make():
                return remote(
                    ref(source), ref(target), send_sems.at[at], get_sems.at[at], partner(flips, groups)
                )

            return Move(make)

        r.local, r.send, r.groups = local, send, groups
        r.core = lax.axis_index("seq")
        greet([partner(flips, groups) for flips in partners])
        r.meet = lambda: pl.semaphore_wait(pltpu.get_barrier_semaphore(), len(partners))
        body(r)
        assert counts[0] <= copies[0] and counts[1] <= copies[1], counts

    anywhere = pl.BlockSpec(memory_space=pl.ANY)
    return pl.pallas_call(
        kernel,
        in_specs=[pl.BlockSpec(memory_space=pltpu.SMEM)] * len(scalars)
        + [anywhere] * len(inputs)
        + [pl.BlockSpec(memory_space=pltpu.VMEM)] * len(small),
        out_specs=[anywhere] * len(outputs),
        out_shape=list(outputs.values()),
        scratch_shapes=list(scratch.values())
        + [pltpu.SemaphoreType.DMA((count,)) for count in (copies[0], copies[1], copies[1])],
        compiler_params=pltpu.CompilerParams(
            vmem_limit_bytes=VMEM_LIMIT + 3 * 2**20, collective_id=collective_id, has_side_effects=True
        ),
        cost_estimate=pl.CostEstimate(
            flops=int(flops), bytes_accessed=int(moved), transcendentals=0
        ),
        name=name,
    )(*scalars.values(), *inputs.values(), *small.values())


NORM_ROWS = 64


def rows_of(r, seq, block=None):
    rows = r.result.shape[1] if hasattr(r, "result") else r.grad_middle.shape[1]
    block = block or slice(0, rows)
    return slice(seq * rows + block.start, seq * rows + block.stop)


def ref(given):
    return given() if callable(given) else given


class Move:
    def __init__(self, make):
        self.make = make
        make().start()

    def wait(self):
        self.make().wait()

    def wait_recv(self):
        self.make().wait_recv()

    def wait_send(self):
        self.make().wait_send()


def ahead(makers):
    later = None
    for make in makers:
        now, later = later, make()
        if now is not None:
            yield now
    yield later


def span(index, size):
    return pl.ds(pl.multiple_of(index * size, size), size)


def wait_all(copies):
    for copy in copies:
        copy.wait()


def wait_sent(copies):
    for copy in copies:
        copy.wait_send()


def load_head_weight(r, layer):
    width, wide = r.w_qkv_v.shape
    copies = []
    for pair in range(wide // (3 * LANES)):
        for kind in range(3):
            at = pl.multiple_of(kind * width + r.core * (width // 2) + pair * LANES, LANES)
            copies.append(
                r.local(
                    r.w_qkv.at[layer, :, pl.ds(at, LANES)],
                    r.w_qkv_v.at[:, pl.ds((3 * pair + kind) * LANES, LANES)],
                )
            )
    return copies


def scaled(normed, norms):
    return (normed * norms[0:1] + norms[1:2]).astype(jnp.bfloat16)


def norm_rows(r, stream, seq, norms):
    rows = stream.shape[1]
    for block in blocks_of(rows, NORM_ROWS):
        normed, _ = normal(stream[seq, block].astype(jnp.float32))
        at = pl.multiple_of(r.core * rows + block.start, NORM_ROWS)
        r.attn_v[seq, pl.ds(at, NORM_ROWS)] = scaled(normed, norms)


def project(r, layer, seq, targets):
    cap = r.attn_v.shape[1]
    taps = r.taps[layer]
    r.longer[0:8] = jnp.zeros((8, r.longer.shape[1]), jnp.float32)
    blocks = blocks_of(cap, TILE)
    products = ahead(
        [functools.partial(lambda block: dot_nn(r.attn_v[seq, block], r.w_qkv_v[...]), b) for b in blocks]
    )
    for block, here in zip(blocks, products):
        at = 8 + block.start
        r.longer[at : at + TILE, :] = here
        r.proj_v[seq, block] = here.astype(jnp.bfloat16)
        r.mixed_v[seq, block] = (
            taps[0:1] * here
            + taps[1:2] * r.longer[at - 1 : at - 1 + TILE, :]
            + taps[2:3] * r.longer[at - 2 : at - 2 + TILE, :]
        ).astype(jnp.bfloat16)
    sources = (r.mixed_v, r.proj_v, r.attn_v)
    return [r.local(source.at[seq], target.at[seq]) for source, target in zip(sources, targets)]


def project_shapes(seqs, rows, width):
    bf16, f32 = jnp.bfloat16, jnp.float32
    wide = 3 * width // 2
    outputs = {}
    for layer in range(LAYERS):
        for name, columns in (("mixed", wide), ("proj", wide), ("attn", width)):
            outputs[name + str(layer)] = jax.ShapeDtypeStruct((seqs, 2 * rows, columns), bf16)
    scratch = dict(
        w_qkv_v=pltpu.VMEM((width, wide), bf16),
        attn_v=pltpu.VMEM((seqs, 2 * rows, width), bf16),
        longer=pltpu.VMEM((2 * rows + 8, wide), f32),
        proj_v=pltpu.VMEM((seqs, 2 * rows, wide), bf16),
        mixed_v=pltpu.VMEM((seqs, 2 * rows, wide), bf16),
    )
    return outputs, scratch


def load_rows(r, source, target):
    seqs, rows, _ = source.shape
    return [
        r.local(source.at[seq], target.at[pl.ds(seq * rows, rows)]) for seq in range(seqs)
    ]


def share_rows(r, buffer, seq, rows):
    here = span(r.core, rows)
    return r.send(buffer.at[seq, here], buffer.at[seq, here])


def attention(r, seqs, rows, before_send=None):
    half = r.heads_all.shape[1]
    cap = 2 * rows
    mine, theirs = span(r.core, rows), span(1 - r.core, rows)
    loads, sends, outs = [], [], []
    pairs = half // LANES
    if not before_send:
        for pair in range(pairs):
            columns = pl.ds(pair * 3 * LANES, 3 * LANES)
            loads.append(r.local(r.mixed_in.at[:, :, columns], r.mixed_v.at[:, :, columns]))
        r.meet()
    yield
    for pair in range(pairs):
        columns = slice(pair * 3 * LANES, (pair + 1) * 3 * LANES)
        lanes = slice(pair * LANES, (pair + 1) * LANES)
        if loads:
            loads[pair].wait()

        def one(seq, none):
            attend_heads(
                r.lengths[seq] == cap,
                r.mixed_v.at[seq, :, columns],
                r.heads_all.at[pl.ds(pl.multiple_of(seq * cap, cap), cap), lanes],
                r.logs_v.at[seq, pair],
            )

        lax.fori_loop(0, seqs, one, None)
        if pair == 0 and before_send:
            before_send()
        for seq in range(seqs):
            to = pl.ds(pl.multiple_of(r.core * half + pair * LANES, LANES), LANES)
            here = pl.ds(seq * rows, rows)
            own, other = (span(2 * seq + owner, rows) for owner in (r.core, 1 - r.core))
            sends.append(r.send(r.heads_all.at[other, pl.ds(pair * LANES, LANES)], r.heads_v.at[here, to]))
            r.heads_v[here, to] = r.heads_all[own, lanes]
    for seq in range(seqs):
        outs.append(r.local(r.heads_all.at[pl.ds(seq * cap, cap)], r.heads.at[seq]))
    outs.append(r.local(r.logs_v, r.logs))
    for copy in sends:
        copy.wait()
    yield outs


def attention_shapes(seqs, rows, width):
    half = width // 2
    pairs = half // LANES
    bf16, f32 = jnp.bfloat16, jnp.float32
    outputs = dict(
        heads=jax.ShapeDtypeStruct((seqs, 2 * rows, half), bf16),
        logs=jax.ShapeDtypeStruct((seqs, pairs, 2, 2 * rows), f32),
    )
    scratch = dict(
        mixed_v=pltpu.VMEM((seqs, 2 * rows, 3 * half), bf16),
        heads_all=pltpu.VMEM((seqs * 2 * rows, half), bf16),
        logs_v=pltpu.VMEM((seqs, pairs, 2, 2 * rows), f32),
        heads_v=pltpu.VMEM((seqs * rows, width), bf16),
    )
    return outputs, scratch


def out_project(r, layer, seq, norms):
    r.middle_v[seq] += dot_nn(r.heads_v[rows_of(r, seq)], r.w_out_v[...])
    for block in blocks_of(r.middle_v.shape[1], NORM_ROWS):
        normed, _ = normal(r.middle_v[seq, block])
        r.ff_in_v[rows_of(r, seq, block)] = scaled(normed, norms)


def feed(r, seq, hidden, result):
    ff = r.w_up_v.shape[1]
    here = rows_of(r, seq)
    chunks = blocks_of(ff, 768)
    products = ahead(
        [functools.partial(lambda lanes: dot_nn(r.ff_in_v[here], r.w_up_v[:, lanes]), c) for c in chunks]
    )
    for lanes, value in zip(chunks, products):
        positive = jnp.maximum(value, 0.0)
        r.positive_v[here, lanes] = positive.astype(jnp.bfloat16)
        hidden[:, lanes] = (positive * positive).astype(jnp.bfloat16)
    for lanes in blocks_of(r.middle_v.shape[2], TILE):
        value = r.middle_v[seq, :, lanes] + dot_nn(hidden[...], r.w_down_v[:, lanes])
        result[seq, :, lanes] = value.astype(result.dtype)


def load_feed_weights(r, layer):
    return [
        r.local(r.w_out.at[layer], r.w_out_v),
        r.local(r.w_up.at[layer], r.w_up_v),
        r.local(r.w_down.at[layer], r.w_down_v),
    ]


def feed_shapes(seqs, rows, width, ff):
    bf16, f32 = jnp.bfloat16, jnp.float32
    return dict(
        w_out_v=pltpu.VMEM((width, width), bf16),
        w_up_v=pltpu.VMEM((width, ff), bf16),
        w_down_v=pltpu.VMEM((ff, width), bf16),
        middle_v=pltpu.VMEM((seqs, rows, width), f32),
        ff_in_v=pltpu.VMEM((seqs * rows, width), bf16),
        positive_v=pltpu.VMEM((seqs * rows, ff), bf16),
    )


def feed_forward(lengths, stream, weights, taps, norms, groups, collective_id):
    layer = 0
    seqs, rows, width = stream.shape
    ff = weights["w_up"].shape[2]
    tokens = (seqs, rows, width)
    bf16, f32 = jnp.bfloat16, jnp.float32
    outputs, scratch = project_shapes(seqs, rows, width)

    def body(r):
        streams = [r.local(r.stream.at[seq], r.stream_v.at[seq]) for seq in range(seqs)]
        heads_weight = load_head_weight(r, 0)
        r.meet()
        shared, early = [], []
        for seq in range(seqs):
            streams[seq].wait()
            norm_rows(r, r.stream_v, seq, r.norms[0, 0])
            shared.append(share_rows(r, r.attn_v, seq, rows))
        feeds = load_feed_weights(r, layer)
        wait_all(heads_weight)
        for seq in range(seqs):
            shared[seq].wait()
            early += project(r, 0, seq, (r.mixed0, r.proj0, r.attn0))
        feeds += load_head_weight(r, 1)
        heads = attention(r, seqs, rows, lambda: wait_all(early))
        next(heads)
        outs = next(heads)
        wait_all(feeds)
        shared = []
        for seq in range(seqs):
            r.middle_v[seq] = r.stream_v[seq].astype(f32)
            out_project(r, layer, seq, r.norms[layer, 1])
            outs.append(r.local(r.middle_v.at[seq], r.middle.at[seq]))
            here = pl.ds(seq * rows, rows)
            outs.append(r.local(r.ff_in_v.at[here], r.ff_in.at[here]))
            feed(r, seq, r.hidden_v, r.result_v)
            outs.append(r.local(r.positive_v.at[here], r.positive.at[here]))
            outs.append(r.local(r.result_v.at[seq], r.result.at[seq]))
            norm_rows(r, r.result_v, seq, r.norms[layer + 1, 0])
            shared.append(share_rows(r, r.attn_v, seq, rows))
        for seq in range(seqs):
            shared[seq].wait_recv()
            outs += project(r, layer + 1, seq, (r.mixed1, r.proj1, r.attn1))
        wait_sent(shared)
        wait_all(outs)

    more, room = attention_shapes(seqs, rows, width)
    outputs.update(
        more,
        middle=jax.ShapeDtypeStruct(tokens, f32),
        ff_in=jax.ShapeDtypeStruct((seqs * rows, width), bf16),
        positive=jax.ShapeDtypeStruct((seqs * rows, ff), bf16),
        result=jax.ShapeDtypeStruct(tokens, f32),
    )
    scratch.update(room)
    scratch.update(feed_shapes(seqs, rows, width, ff))
    scratch.update(
        stream_v=pltpu.VMEM(tokens, stream.dtype),
        hidden_v=pltpu.VMEM((rows, ff), bf16),
        result_v=pltpu.VMEM(tokens, f32),
        partners=((),),
    )
    return stage(
        "feed_forward", body, dict(stream=stream, **weights), dict(norms=norms, taps=taps),
        outputs, scratch, (60, 12), groups, collective_id,
        2 * seqs * rows * width * (9 * width + 2 * ff), 60_000_000, lengths,
    )


def place_of(shard, owner, groups):
    group = lax.axis_index("batch")
    place = 0
    for one, other in list(zip(*group_bits(groups)))[:2]:
        differs = [(shard // 2**bit % 2 + group // 2**bit % 2) % 2 for bit in (one, other)]
        place = 2 * place + 1 - ((1 - owner) * differs[0] + owner * differs[1])
    line = shard // 4
    return 4 * place + 2 * (line % 2) + line // 2


def feed_back(r, layer, seqs, rows, norms, hooks=None):
    groups, core = r.groups, r.core
    width, ff = r.w_up_v.shape
    half = width // 2
    shard_rows = half // groups
    f32, bf16 = jnp.float32, jnp.bfloat16
    chunk = 768
    hooks = hooks or (lambda *_: None,) * 4
    needed, after_first, before_products, after_ups = hooks
    gain_sum = offset_sum = 0.0
    shared, outs = [], []
    for seq in range(seqs):
        if seq == 1:
            after_first()
        here = rows_of(r, seq)
        r.low[here] = r.grad_v[seq].astype(bf16)
        if seq == 0:
            needed(2)
        chunks = blocks_of(ff, chunk)
        backs = ahead(
            [functools.partial(lambda lanes: dot_nt(r.low[here], r.w_down_v[lanes]), c) for c in chunks]
        )
        for lanes, back in zip(chunks, backs):
            r.pre[here, lanes] = (back * (2.0 * r.positive_v[here, lanes].astype(f32))).astype(bf16)
        if seq == 0:
            needed(3)
        for lanes in blocks_of(width, TILE):
            r.total[:, lanes] = dot_nt(r.pre[here], r.w_up_v[lanes])
        for block in blocks_of(rows, NORM_ROWS):
            grad_in = r.total[block]
            normed, scaling = normal(r.middle_v[seq, block])
            gain_sum += jnp.sum(grad_in * normed, 0, keepdims=True)
            offset_sum += jnp.sum(grad_in, 0, keepdims=True)
            value = r.grad_v[seq, block].astype(f32) + norm_back(grad_in, normed, scaling, norms[0:1])
            r.middle_v[seq, block] = value
            at = pl.multiple_of((2 * seq + core) * rows + block.start, NORM_ROWS)
            r.branch[pl.ds(at, NORM_ROWS)] = value.astype(bf16)
        at = span(2 * seq + core, rows)
        shared.append(r.send(r.branch.at[at], r.branch.at[at]))
        outs.append(r.local(r.middle_v.at[seq], r.grad_middle.at[seq]))
    r.norm_grad_v[0:1] = gain_sum
    r.norm_grad_v[1:2] = offset_sum
    outs.append(r.local(r.norm_grad_v, r.norm_grad))
    before_products()

    up_rows, down_rows = 2 * shard_rows, ff // 2 // groups
    down_start = up_rows * (ff // chunk)

    def up_product(owner, lanes):
        return dot_tn(r.ff_in_v[:, span(owner, half)], r.pre[:, lanes])

    def down_product(owner, lanes):
        at = pl.multiple_of(owner * (ff // 2) + lanes.start, chunk)
        positive = r.positive_v[:, pl.ds(at, chunk)].astype(f32)
        return dot_tn((positive * positive).astype(bf16), r.low[...])

    def products(owner):
        ups, downs = blocks_of(ff, chunk), blocks_of(ff // 2, chunk)
        makers = [functools.partial(up_product, owner, lanes) for lanes in ups]
        makers += [functools.partial(down_product, owner, lanes) for lanes in downs]
        for at, value in enumerate(ahead(makers)):
            size = shard_rows if at < len(ups) else down_rows
            first = 0 if at < len(ups) else (at - len(ups)) * (chunk // down_rows)
            row = at * up_rows if at < len(ups) else down_start
            yield [
                (first + count, row, halves(value[count * size : (count + 1) * size]))
                for count in range(value.shape[0] // size)
            ]

    places = [[place_of(shard, owner, groups) for shard in range(groups)] for owner in (1 - core, core)]
    sends = []
    for at, pieces in enumerate(products(1 - core)):
        for shard, row, piece in pieces:
            r.ff_send[places[0][shard], row : row + piece.shape[0]] = piece.astype(bf16)
        if at == ff // chunk - 1:
            where = (slice(None), pl.ds(0, down_start))
            sends.append(r.send(r.ff_send.at[where], r.ff_got.at[where]))
    where = (slice(None), pl.ds(down_start, 2 * down_rows))
    sends.append(r.send(r.ff_send.at[where], r.ff_got.at[where]))
    for at, pieces in enumerate(products(core)):
        if at == 0:
            sends[0].wait()
        if at == ff // chunk:
            sends[1].wait()
        for shard, row, piece in pieces:
            place = places[1][shard]
            rows_of_piece = slice(row, row + piece.shape[0])
            r.ff_sum_v[place, rows_of_piece] = (
                piece + r.ff_got[place, rows_of_piece].astype(f32)
            ).astype(bf16)
        if at == ff // chunk - 1:
            where = (slice(None), pl.ds(0, down_start))
            outs.append(r.local(r.ff_sum_v.at[where], r.ff_sum.at[where]))
            after_ups()
    where = (slice(None), pl.ds(down_start, 2 * down_rows))
    outs.append(r.local(r.ff_sum_v.at[where], r.ff_sum.at[where]))
    return shared, outs


def halves(value):
    half = value.shape[1] // 2
    return jnp.concatenate([value[:, :half], value[:, half:]], 0)


def heads_back(r, shared, seqs, rows):
    groups, core = r.groups, r.core
    half = r.grad_heads.shape[2]
    shard_rows = half // groups
    out_grad = r.low.at[pl.ds(0, 2 * half), pl.ds(0, half)]
    outs = []
    for copy in shared:
        copy.wait_recv()
    places = [place_of(shard, core, groups) for shard in range(groups)]
    total = dot_tn(r.heads_all[...], r.branch[...])
    for shard, place in enumerate(places):
        piece = halves(total[shard * shard_rows : (shard + 1) * shard_rows])
        out_grad[span(place, 2 * shard_rows)] = piece.astype(jnp.bfloat16)
    for seq in range(seqs):
        here = slice(seq * 2 * rows, (seq + 1) * 2 * rows)
        grad = dot_nt(r.branch[here], r.w_out_v[span(core, half)])
        r.heads_all[here] = grad.astype(jnp.bfloat16)
        where = pl.ds(here.start, 2 * rows)
        outs.append(r.local(r.heads_all.at[where], r.grad_heads.at[seq]))
    outs.append(r.local(out_grad, r.out_grad))
    wait_sent(shared)
    return outs


def back_shapes(seqs, rows, width, ff, groups):
    bf16, f32 = jnp.bfloat16, jnp.float32
    half = width // 2
    shard_rows = half // groups
    tokens = (seqs, rows, width)
    outputs = dict(
        ff_sum=jax.ShapeDtypeStruct((groups, 4 * ff // groups // 2, half), bf16),
        grad_middle=jax.ShapeDtypeStruct(tokens, f32),
        norm_grad=jax.ShapeDtypeStruct((8, width), f32),
        grad_heads=jax.ShapeDtypeStruct((seqs, 2 * rows, half), bf16),
        out_grad=jax.ShapeDtypeStruct((groups * 2 * shard_rows, half), bf16),
    )
    scratch = dict(
        low=pltpu.VMEM((seqs * rows, width), bf16),
        pre=pltpu.VMEM((seqs * rows, ff), bf16),
        branch=pltpu.VMEM((seqs * 2 * rows, width), bf16),
        norm_grad_v=pltpu.VMEM((8, width), f32),
        ff_send=pltpu.VMEM((groups, 4 * ff // groups // 2, half), bf16),
        ff_got=pltpu.VMEM((groups, 4 * ff // groups // 2, half), bf16),
        heads_all=pltpu.VMEM((seqs * 2 * rows, half), bf16),
    )
    return outputs, scratch


def turn(layer, lengths, mixed, stream, cotangent, weights, norms, groups, collective_id):
    seqs, rows, width = stream.shape
    ff = weights["w_up"].shape[2]
    tokens = (seqs, rows, width)
    bf16, f32 = jnp.bfloat16, jnp.float32
    outputs, scratch = back_shapes(seqs, rows, width, ff, groups)

    def body(r):
        r.low, r.ff_sum_v = r.heads_v, r.ff_send
        heads = attention(r, seqs, rows)
        next(heads)
        loads = [r.local(r.stream, r.middle_v), *load_feed_weights(r, layer), r.local(r.grad, r.grad_v)]
        outs = next(heads)
        wait_all(loads)
        for seq in range(seqs):
            out_project(r, layer, seq, r.norms[layer, 1])
            feed(r, seq, r.pre.at[rows_of(r, seq)], r.result_v)
            outs.append(r.local(r.result_v.at[seq], r.result.at[seq]))
        wait_all(outs)
        shared, outs = feed_back(r, layer, seqs, rows, r.norms[layer, 1])
        wait_all(outs + heads_back(r, shared, seqs, rows))

    more, room = attention_shapes(seqs, rows, width)
    del scratch["low"]
    outputs.update(more, result=jax.ShapeDtypeStruct(tokens, bf16))
    scratch.update(room)
    scratch.update(feed_shapes(seqs, rows, width, ff))
    scratch.update(
        total=pltpu.VMEM((rows, width), f32),
        result_v=pltpu.VMEM(tokens, bf16),
        grad_v=pltpu.VMEM(tokens, cotangent.dtype),
        partners=((),),
    )
    return stage(
        "turn", body, dict(mixed_in=mixed, stream=stream, grad=cotangent, **weights), dict(norms=norms),
        outputs, scratch, (40, 16), groups, collective_id,
        2 * seqs * rows * width * (3 * width + 6 * ff + 2 * width), 60_000_000, lengths,
    )


class Chain:
    def __init__(self, r, shards, got, source=None):
        self.r, self.shards, self.first = r, shards, 8 if source is not None else 0
        self.source = shards if source is None else source
        self.got_a, self.got_b, self.got_z = got
        self.sends = {}

    def part(self, ref, start, count, rows):
        return ref.at[pl.ds(start, count), pl.ds(rows.start, rows.stop - rows.start)]

    def add(self, start, got, rows):
        f32 = jnp.float32
        for at in range(got.shape[0]):
            to = start - self.first + at
            self.shards[to, rows] = (
                self.shards[to, rows].astype(f32) + got[at, rows].astype(f32)
            ).astype(jnp.bfloat16)

    def start_a(self, rows, alone=None):
        source = self.part(self.source, 0, 8, rows) if alone is None else alone.at[pl.ds(0, 8)]
        self.sends["a", rows.start] = self.r.send(source, self.part(self.got_a, 0, 8, rows), (0,))

    def start_b(self, rows):
        if ("a", rows.start) in self.sends:
            self.sends["a", rows.start].wait_recv()
        self.add(8, self.got_a, rows)
        self.sends["b", rows.start] = self.r.send(
            self.part(self.shards, 8 - self.first, 4, rows), self.part(self.got_b, 0, 4, rows), (1,)
        )

    def end_b(self, rows):
        self.sends["b", rows.start].wait_recv()
        self.add(12, self.got_b, rows)

    def start_c(self, rows):
        self.end_b(rows)
        self.sends["c", rows.start] = self.r.send(
            lambda: self.part(self.shards, 12 - self.first + 2 * (1 - line_bits()[0]), 2, rows),
            self.part(self.got_z, 0, 2, rows),
            (2,),
        )

    def start_d(self, rows):
        self.sends["c", rows.start].wait_recv()
        low, high = line_bits()
        to = 12 - self.first + 2 * low
        for at in range(2):
            self.shards[to + at, rows] = (
                self.shards[to + at, rows].astype(jnp.float32) + self.got_z[at, rows].astype(jnp.float32)
            ).astype(jnp.bfloat16)
        self.sends["d", rows.start] = self.r.send(
            lambda: self.part(
                self.shards, 12 - self.first + 2 * line_bits()[0] + 1 - line_bits()[1], 1, rows
            ),
            self.part(self.got_z, 2, 1, rows),
            (3,),
        )

    def end_d(self, rows):
        low, high = line_bits()
        mine = 12 - self.first + 2 * low + high
        self.sends["d", rows.start].wait_recv()
        return self.shards[mine, rows].astype(jnp.float32) + self.got_z[2, rows].astype(jnp.float32)

    def close(self):
        wait_sent(self.sends.values())


def line_bits():
    line = lax.axis_index("batch") // 4
    return line % 2, line // 2


def done_shapes(width, ff, groups):
    rows = width // 2 // groups
    return {
        name: jax.ShapeDtypeStruct(shape, jnp.float32)
        for name, shape in (
            ("qkv_done", (rows, 3 * width)),
            ("out_done", (rows, width)),
            ("up_done", (rows, ff)),
            ("down_done", (ff // 2 // groups, width)),
        )
    }


def attn_rows(shard_rows, pairs):
    size = 2 * shard_rows
    starts = [size * at for at in range(pairs + 2)]
    return [slice(start, start + size) for start in starts[:-1]] + [slice(starts[-1], starts[-1] + 16)]


def set_ff(r, total, up, down):
    shard_rows, ff = up.shape
    half = total.shape[1]
    for at in range(ff // half):
        up[:, at * half : (at + 1) * half] = total[at * shard_rows : (at + 1) * shard_rows]
    start = (ff // half) * shard_rows
    down_rows = down.shape[0]
    for at in range(2):
        first = start + at * down_rows
        down[:, at * half : (at + 1) * half] = total[first : first + down_rows]


def set_qkv(r, total, pair, qkv):
    shard_rows, columns = qkv.shape
    width = columns // 3
    for at, owner in enumerate((r.core, 1 - r.core)):
        for kind in range(3):
            to = pl.multiple_of(kind * width + owner * (width // 2) + pair * LANES, LANES)
            qkv[:, pl.ds(to, LANES)] = total[
                at * shard_rows : (at + 1) * shard_rows, kind * LANES : (kind + 1) * LANES
            ]


def set_out(r, total, out):
    shard_rows, width = out.shape
    out[:, : width // 2] = total[:shard_rows]
    out[:, width // 2 :] = total[shard_rows : 2 * shard_rows]


def chain_shapes(rows, columns):
    bf16 = jnp.bfloat16
    return [pltpu.VMEM((count, rows, columns), bf16) for count in (8, 4, 3)]


def attend_back_pair(r, pair):
    columns = slice(pair * 3 * LANES, (pair + 1) * 3 * LANES)
    half = r.grad_heads_v.shape[1] // 2

    def one(seq):
        cap = r.proj_v.shape[0]
        at = pl.ds(pl.multiple_of(seq * 3 * LANES, LANES), 3 * LANES)
        to = pl.ds(pl.multiple_of(seq * half + pair * LANES, LANES), LANES)
        attend_back_heads(
            r.lengths[seq] == cap,
            r.mixed_v.at[pl.ds(pair * cap, cap), at],
            r.proj_v.at[:, pl.ds(pl.multiple_of((2 * pair + seq) * 3 * LANES, LANES), 3 * LANES)],
            r.grad_heads_v.at[:, to],
            r.heads_v.at[:, to],
            r.logs.at[seq, pair],
            r.taps_layer.at[:, columns],
            r.grad_proj.at[pl.ds(pl.multiple_of(seq * cap, cap), cap), columns],
            r.grad_taps.at[seq, :, columns],
            r.query_t_acc,
            r.shift_acc,
        )

    return one


def project_back(
    r, layer, seqs, rows, norms, attn, after_pair, loading, attention_done=lambda: None,
    before_norm=lambda: None, before_first=lambda: None,
):
    groups, core = r.groups, r.core
    width, wide = r.w_qkv_v.shape
    half = width // 2
    pairs = half // LANES
    shard_rows = half // groups
    pieces = attn_rows(shard_rows, pairs)
    f32, bf16 = jnp.float32, jnp.bfloat16

    def part(seq, owner):
        return span(2 * seq + owner, rows)

    cap = 2 * rows
    first = []
    for pair in range(pairs):
        columns = pl.ds(pair * 3 * LANES, 3 * LANES)
        lanes = pl.ds(pair * LANES, LANES)
        copies = []
        for seq in range(seqs):
            to = pl.ds(seq * half + pair * LANES, LANES)
            copies += [
                r.local(
                    r.mixed.at[seq, :, columns],
                    r.mixed_v.at[pl.ds(pair * cap, cap), pl.ds(seq * 3 * LANES, 3 * LANES)],
                ),
                r.local(r.grad_heads_in.at[seq, :, lanes], r.grad_heads_v.at[:, to]),
                r.local(r.heads_in.at[seq, :, lanes], r.heads_v.at[:, to]),
                r.local(
                    r.proj.at[seq, :, columns],
                    r.proj_v.at[:, pl.ds((2 * pair + seq) * 3 * LANES, 3 * LANES)],
                ),
            ]
        first.append(copies)
    out_loaded = r.local(r.out_grad_in, attn.shards.at[:, pl.ds(pieces[pairs].start, 2 * shard_rows)])
    r.meet()
    loading()
    inputs_in = load_rows(r, r.attn, r.inputs)
    weights = load_head_weight(r, layer)
    loads = [r.local(r.below, r.below_v), r.local(r.grad_middle_in, r.grad_v)]
    places = [[place_of(shard, owner, groups) for shard in range(groups)] for owner in (1 - core, core)]
    swaps, shared = {}, []

    def merge_pair(pair):
        swaps[pair].wait()
        for place in range(groups):
            piece = jnp.concatenate(
                [r.qkv_keep[pair % 2, place], r.qkv_got[pair, place, :shard_rows].astype(f32)], 0
            )
            attn.shards[place, pieces[pair]] = piece.astype(bf16)
        attn.start_a(pieces[pair])

    for pair in range(pairs):
        wait_all(first[pair])
        if pair == 0:
            before_first()
        one = attend_back_pair(r, pair)
        lax.fori_loop(0, seqs, lambda seq, none: one(seq), None)
        if pair == 0:
            wait_all([out_loaded, *inputs_in])
        else:
            merge_pair(pair - 1)
        columns = slice(pair * 3 * LANES, (pair + 1) * 3 * LANES)
        for at, owner in enumerate((1 - core, core)):
            value = dot_tn(r.inputs[:, span(owner, half)], r.grad_proj[:, columns])
            for shard in range(groups):
                piece = value[shard * shard_rows : (shard + 1) * shard_rows]
                if at == 0:
                    piece = jnp.concatenate([piece, jnp.zeros((32 - shard_rows, half), f32)], 0)
                    r.qkv_send[pair, places[0][shard]] = piece.astype(bf16)
                else:
                    r.qkv_keep[pair % 2, places[1][shard]] = piece
            if at == 0:
                swaps[pair] = r.send(r.qkv_send.at[pair], r.qkv_got.at[pair])
        after_pair(pair)
    attention_done()
    wait_all(weights)
    for seq in range(seqs):
        here = slice(seq * rows, (seq + 1) * rows)
        value = dot_nt(r.grad_proj[part(seq, 1 - core)], r.w_qkv_v[...])
        r.heads_v[here] = value.astype(bf16)
        shared.append(r.send(r.heads_v.at[pl.ds(seq * rows, rows)], r.partial_got.at[seq]))
    merge_pair(pairs - 1)
    before_norm()
    wait_all(loads)
    gain_sum = offset_sum = 0.0
    for seq in range(seqs):
        r.total[...] = dot_nt(r.grad_proj[part(seq, core)], r.w_qkv_v[...])
        shared[seq].wait_recv()
        for block in blocks_of(rows, NORM_ROWS):
            here = r.total[block] + r.partial_got[seq, block].astype(f32)
            normed, scaling = normal(r.below_v[seq, block].astype(f32))
            gain_sum += jnp.sum(here * normed, 0, keepdims=True)
            offset_sum += jnp.sum(here, 0, keepdims=True)
            r.grad_v[seq, block] += norm_back(here, normed, scaling, norms[0:1])
    wait_sent(shared)
    r.norm_rows[3:4], r.norm_rows[4:5] = gain_sum, offset_sum
    r.taps_wide[...] = jnp.zeros_like(r.taps_wide)
    for pair in range(pairs):
        for kind in range(3):
            at = slice((3 * pair + kind) * LANES, (3 * pair + kind + 1) * LANES)
            to = pl.multiple_of(kind * width + core * half + pair * LANES, LANES)
            r.taps_wide[0:3, pl.ds(to, LANES)] = sum(r.grad_taps[seq, 0:3, at] for seq in range(seqs))


def project_back_shapes(seqs, rows, width, below, groups):
    f32, bf16 = jnp.float32, jnp.bfloat16
    cap, wide, half = 2 * rows, 3 * width // 2, width // 2
    pairs = half // LANES
    shard_rows = half // groups
    own = dict(
        grad_proj=pltpu.VMEM((seqs * cap, wide), bf16),
        grad_taps=pltpu.VMEM((seqs, 8, wide), f32),
        query_t_acc=pltpu.VMEM((LANES, cap), f32),
        shift_acc=pltpu.VMEM((3, cap + 8, LANES), f32),
        inputs=pltpu.VMEM((seqs * cap, width), bf16),
        w_qkv_v=pltpu.VMEM((width, wide), bf16),
        below_v=pltpu.VMEM((seqs, rows, width), below.dtype),
        qkv_send=pltpu.VMEM((pairs, groups, 32, half), bf16),
        qkv_keep=pltpu.VMEM((2, groups, shard_rows, half), f32),
    )
    shared = dict(
        partial_got=pltpu.VMEM((seqs, rows, width), bf16),
        qkv_got=pltpu.VMEM((pairs, groups, 32, half), bf16),
        total=pltpu.VMEM((rows, width), f32),
        grad_v=pltpu.VMEM((seqs, rows, width), f32),
        norm_rows=pltpu.VMEM((8, width), f32),
        taps_wide=pltpu.VMEM((8, 3 * width), f32),
    )
    operands = dict(
        mixed_v=pltpu.VMEM((pairs * cap, seqs * 3 * LANES), bf16),
        proj_v=pltpu.VMEM((cap, pairs * seqs * 3 * LANES), bf16),
        grad_heads_v=pltpu.VMEM((cap, seqs * half), bf16),
        heads_v=pltpu.VMEM((cap, seqs * half), bf16),
    )
    return own, shared, operands


def back_link(
    layer, lengths, saved, grad_heads, out_grad, grad_middle, ff_sum, lower, weights_qkv, weights, norms, taps,
    groups, collective_id,
):
    below = saved["below"]
    seqs, rows, width = below.shape
    ff = weights["w_up"].shape[2]
    half = width // 2
    pairs = half // LANES
    shard_rows = half // groups
    bf16, f32 = jnp.bfloat16, jnp.float32
    outputs, scratch = back_shapes(seqs, rows, width, ff, groups)
    pieces = attn_rows(shard_rows, pairs)[: pairs + 1]
    all_ff = slice(0, ff_sum.shape[1])
    ups, downs = slice(0, all_ff.stop // 2), slice(all_ff.stop // 2, all_ff.stop)
    own, shared, _ = project_back_shapes(seqs, rows, width, below, groups)
    shapes = feed_shapes(seqs, rows, width, ff)
    later = {name: scratch.pop(name) for name in ("pre", "ff_send")}
    del scratch["heads_all"]
    later.update({name: shapes.pop(name) for name in ("w_up_v", "middle_v")})
    del shapes["w_out_v"]
    scratch.update(shapes)

    def body(r):
        chain = Chain(r, r.ff_parts, (r.ff_got_a, r.ff_got_b, r.ff_got_z), r.ff_sum_in)
        attn_chain = Chain(r, r.attn_sum_v, (r.attn_got_a, r.attn_got_b, r.attn_got_z))
        summed = []

        def loading():
            attn_chain.start_a(pieces[pairs], r.out_grad_in)
            chain.start_a(ups)
            chain.start_a(downs)
            summed.append(r.local(lambda: r.ff_sum_in.at[pl.ds(8, 8)], r.ff_parts))

        def after_pair(pair):
            if pair == 1:
                summed[0].wait()
                chain.start_b(ups)

        r.mixed_v, r.proj_v, r.grad_heads_v, r.heads_v = r.w_down_v, r.positive_v, r.ff_in_v, r.low
        loads = []

        def attention_done():
            loads.append(r.local(lambda: r.w_down.at[layer - 1], r.w_down_v))
            loads.append(r.local(r.positive, r.positive_v))
            loads.append(r.local(r.ff_in, r.ff_in_v))

        def first(*scope):
            vars(r).update(zip(own, scope))
            project_back(
                r, layer, seqs, rows, r.norms[layer, 0], attn_chain, after_pair, loading, attention_done,
                lambda: chain.start_b(downs),
            )
            outs = [r.local(r.norm_rows, r.norm_one), r.local(r.taps_wide, r.taps_done)]
            wait_all(outs)

        pl.run_scoped(first, *own.values())

        def second(*scope):
            vars(r).update(zip(later, scope))
            r.ff_sum_v = r.ff_send
            r.down_done_v = r.total.at[pl.ds(0, done["down_done"].shape[0])]
            r.out_done_v = r.total.at[pl.ds(done["down_done"].shape[0], shard_rows)]
            r.heads_all = r.w_down_v.at[pl.ds(0, seqs * 2 * rows), pl.ds(0, half)]
            loads.append(r.local(r.w_up.at[layer - 1], r.w_up_v))
            loads.append(r.local(r.middle, r.middle_v))
            alls = []
            chain.start_c(ups)
            order = (pieces[pairs], *pieces[:pairs])
            early = []

            def needed(count):
                wait_all(loads[:count])
                del loads[:count]

            def after_first():
                chain.start_d(ups)
                chain.start_c(downs)
                for piece in order:
                    attn_chain.start_b(piece)

            def before_products():
                r.w_out_v = r.w_up_v.at[:, pl.ds(0, width)]
                alls.append(r.local(r.w_out.at[layer - 1], r.w_out_v))
                alls.extend(load_rows(r, r.heads, r.heads_all))
                chain.start_d(downs)
                for piece in order:
                    attn_chain.start_c(piece)

            def after_ups():
                for piece in order:
                    attn_chain.start_d(piece)
                early.append(r.send(r.ff_sum_v.at[pl.ds(0, 8), pl.ds(0, all_ff.stop // 2)], r.ups_got, (0,)))

            sent, ends = feed_back(
                r, layer - 1, seqs, rows, r.norms[layer - 1, 1],
                (needed, after_first, before_products, after_ups),
            )
            wait_all(alls)
            ends += heads_back(r, sent, seqs, rows)
            set_out(r, attn_chain.end_d(pieces[pairs]), r.out_done_v)
            for pair in range(pairs):
                set_qkv(r, attn_chain.end_d(pieces[pair]), pair, r.qkv_done_v)
            ends += [r.local(r.out_done_v, r.out_done), r.local(r.qkv_done_v, r.qkv_done)]
            value = jnp.concatenate([chain.end_d(ups), chain.end_d(downs)], 0)
            set_ff(r, value, r.up_done_v, r.down_done_v)
            ends += [r.local(r.up_done_v, r.up_done), r.local(r.down_done_v, r.down_done)]
            wait_all(ends + early)

        pl.run_scoped(second, *later.values())
        chain.close()
        attn_chain.close()

    attn_all = pieces[-1].stop
    done = done_shapes(width, ff, groups)
    outputs.update(
        norm_one=jax.ShapeDtypeStruct((8, width), f32),
        taps_done=jax.ShapeDtypeStruct((8, 3 * width), f32),
        ups_got=jax.ShapeDtypeStruct((8, all_ff.stop // 2, half), bf16),
        **done,
    )
    ff_got_a, ff_got_b, ff_got_z = chain_shapes(all_ff.stop, half)
    attn_got_a, attn_got_b, attn_got_z = chain_shapes(attn_all, half)
    for name in ("up_done", "qkv_done"):
        scratch[name + "_v"] = pltpu.VMEM(done[name].shape, f32)
    scratch.update(
        shared,
        ff_parts=pltpu.VMEM((8, all_ff.stop, half), bf16),
        ff_got_a=ff_got_a,
        ff_got_b=ff_got_b,
        ff_got_z=ff_got_z,
        attn_sum_v=pltpu.VMEM((groups, attn_all, half), bf16),
        attn_got_a=attn_got_a,
        attn_got_b=attn_got_b,
        attn_got_z=attn_got_z,
        partners=((), (0,), (1,), (2,), (3,)),
    )
    return stage(
        "back_link", body,
        dict(
            **{name: array for name, array in saved.items() if name != "logs"}, grad_heads_in=grad_heads, grad_middle_in=grad_middle, out_grad_in=out_grad.reshape(groups, -1, half),
            ff_sum_in=ff_sum, w_qkv=weights_qkv, **lower, **weights,
        ),
        dict(norms=norms, taps_layer=taps[layer], logs=saved["logs"]),
        outputs, scratch, (90, 40), groups, collective_id,
        2 * seqs * rows * width * (6 * width + 4 * ff + 2 * width), 60_000_000, lengths,
    )


def leave(
    lengths, saved, grad_heads, out_grad, grad_middle, ff_sum, ups_got, norm_two, small_above, weights_qkv, norms,
    taps, ff, groups, collective_id,
):
    below = saved["below"]
    seqs, rows, width = below.shape
    half = width // 2
    pairs = half // LANES
    shard_rows = half // groups
    bf16, f32 = jnp.bfloat16, jnp.float32
    ff_rows = ff_sum.shape[1]
    ups, downs = slice(0, ff_rows // 2), slice(ff_rows // 2, ff_rows)
    pieces = attn_rows(shard_rows, pairs)
    out_piece, small_piece = pieces[pairs], pieces[pairs + 1]
    done = done_shapes(width, ff, groups)

    def body(r):
        chain = Chain(r, r.ff_parts, (r.ff_got_a, r.ff_got_b, r.ff_got_z), r.ff_sum_in)
        attn_chain = Chain(r, r.attn_sum_v, (r.attn_got_a, r.attn_got_b, r.attn_got_z))
        summed = []

        def loading():
            attn_chain.start_a(out_piece, r.out_grad_in)
            chain.start_a(downs)
            summed.append(r.local(lambda: r.ff_sum_in.at[pl.ds(8, 8)], r.ff_parts))
            summed.append(r.local(r.ups_got, lambda: r.ff_got_a.at[:, pl.ds(0, ups.stop)]))

        def after_pair(pair):
            if pair == 1:
                chain.start_c(ups)
                attn_chain.start_b(out_piece)
            if pair == pairs - 1:
                chain.start_d(ups)
                chain.start_b(downs)
                attn_chain.start_c(out_piece)

        def before_first():
            wait_all(summed)
            chain.start_b(ups)

        def before_norm():
            attn_chain.start_b(pieces[0])

        outs = []
        project_back(
            r, 0, seqs, rows, r.norms[0, 0], attn_chain, after_pair, loading, before_norm=before_norm,
            before_first=before_first,
        )
        r.result_v[...] = r.grad_v[...].astype(bf16)
        outs.append(r.local(r.result_v, r.result))
        attn_chain.start_b(pieces[1])
        chain.start_c(downs)
        attn_chain.start_d(out_piece)
        attn_chain.start_c(pieces[0])
        r.taps_rows[0:8] = r.taps_wide[...]
        r.taps_rows[8:16] = r.taps_above[...]
        r.norms_rows[...] = jnp.zeros_like(r.norms_rows)
        for at, (one, two) in enumerate(((r.norm_rows, r.norm_two), (r.norm_one_above, r.norm_two_above))):
            r.norms_rows[8 * at + 3 : 8 * at + 5] = one[3:5]
            r.norms_rows[8 * at + 5 : 8 * at + 7] = two[0:2]
        r.small_all[...] = jnp.zeros_like(r.small_all)
        for shard in range(2 * groups):
            taps_at, norms_at = 3 * shard_rows * shard, shard_rows * shard
            r.small_all[shard, :, 0 : 3 * shard_rows] = r.taps_rows[:, taps_at : taps_at + 3 * shard_rows]
            r.small_all[shard, :, LANES : LANES + shard_rows] = r.norms_rows[
                :, norms_at : norms_at + shard_rows
            ]
        for shard in range(groups):
            for owner, target in ((1 - r.core, r.small_send), (r.core, r.small_keep)):
                target[place_of(shard, owner, groups)] = r.small_all[owner * groups + shard].astype(bf16)
        swap = r.send(r.small_send, r.small_got)
        for pair in range(2, pairs):
            attn_chain.start_b(pieces[pair])
        swap.wait()
        r.attn_sum_v[:, small_piece] = (
            r.small_keep[...].astype(f32) + r.small_got[...].astype(f32)
        ).astype(bf16)
        attn_chain.start_a(small_piece)
        attn_chain.start_c(pieces[1])
        chain.start_d(downs)
        attn_chain.start_b(small_piece)
        attn_chain.start_d(pieces[0])
        for pair in range(2, pairs):
            attn_chain.start_c(pieces[pair])
        attn_chain.start_d(pieces[1])
        attn_chain.start_c(small_piece)
        set_out(r, attn_chain.end_d(out_piece), r.out_done_v)
        outs.append(r.local(r.out_done_v, r.out_done))
        for pair in range(2, pairs):
            attn_chain.start_d(pieces[pair])
        attn_chain.start_d(small_piece)
        set_ff(
            r, jnp.concatenate([chain.end_d(ups), chain.end_d(downs)], 0), r.up_done_v, r.down_done_v
        )
        outs += [r.local(r.up_done_v, r.up_done), r.local(r.down_done_v, r.down_done)]
        for pair in range(pairs):
            set_qkv(r, attn_chain.end_d(pieces[pair]), pair, r.qkv_done_v)
        outs.append(r.local(r.qkv_done_v, r.qkv_done))
        r.small_done_v[...] = attn_chain.end_d(small_piece)
        outs.append(r.local(r.small_done_v, r.small_done))
        wait_all(outs)
        chain.close()
        attn_chain.close()

    attn_all = small_piece.stop
    done["small_done"] = jax.ShapeDtypeStruct((16, half), f32)
    outputs = dict(result=jax.ShapeDtypeStruct(below.shape, bf16), **done)
    ff_got_a, ff_got_b, ff_got_z = chain_shapes(ff_rows, half)
    attn_got_a, attn_got_b, attn_got_z = chain_shapes(attn_all, half)
    piece = pltpu.VMEM((groups, 16, half), bf16)
    own, shared, operands = project_back_shapes(seqs, rows, width, below, groups)
    scratch = dict(
        **own,
        **shared,
        **operands,
        result_v=pltpu.VMEM((seqs, rows, width), bf16),
        taps_rows=pltpu.VMEM((16, 3 * width), f32),
        norms_rows=pltpu.VMEM((16, width), f32),
        small_all=pltpu.VMEM((2 * groups, 16, half), f32),
        small_send=piece, small_keep=piece, small_got=piece,
        ff_parts=pltpu.VMEM((8, ff_rows, half), bf16),
        ff_got_a=ff_got_a, ff_got_b=ff_got_b, ff_got_z=ff_got_z,
        **{name + "_v": pltpu.VMEM(shape.shape, f32) for name, shape in done.items()},
        attn_sum_v=pltpu.VMEM((groups, attn_all, half), bf16),
        attn_got_a=attn_got_a, attn_got_b=attn_got_b, attn_got_z=attn_got_z,
        partners=((), (0,), (1,), (2,), (3,)),
    )
    return stage(
        "leave", body,
        dict(
            **{name: array for name, array in saved.items() if name != "logs"}, grad_heads_in=grad_heads, grad_middle_in=grad_middle, out_grad_in=out_grad.reshape(groups, -1, half),
            ff_sum_in=ff_sum, ups_got=ups_got, w_qkv=weights_qkv,
        ),
        dict(
            norms=norms, taps_layer=taps[0], logs=saved["logs"], norm_two=norm_two, **small_above,
        ),
        outputs, scratch, (70, 48), groups, collective_id,
        8 * seqs * rows * width * 3 * half, 40_000_000, lengths,
    )


def gather(whole, pairs, small, shard_rows):
    f32 = jnp.float32
    flat = list(whole) + [array for pair in pairs for array in pair]

    def kernel(*refs):
        ins, small_ref, refs = refs[: len(flat)], refs[len(flat)], refs[len(flat) + 1 :]
        outs, rooms = refs[: len(whole) + len(pairs) + 3], refs[len(whole) + len(pairs) + 3 : -2]
        targets = list(outs[: len(whole)])
        for out in outs[len(whole) : -3]:
            targets += [out.at[layer] for layer in range(LAYERS)]
        copies = []
        for at, room in enumerate(rooms):
            copies.append(pltpu.make_async_copy(ins[at], room, refs[-2].at[at]))
            copies[-1].start()
        taps_ref, gains_ref, biases_ref = outs[-3:]
        for layer in range(LAYERS):
            rows = slice(8 * layer, 8 * layer + 8)
            taps_ref[layer] = small_ref[rows, :LANES].T[: 3 * shard_rows, :3]
            norms = small_ref[rows, LANES : 2 * LANES].T[:shard_rows]
            gains_ref[layer] = jnp.concatenate([norms[:, 3:4], norms[:, 5:6]], 1)
            biases_ref[layer] = jnp.concatenate([norms[:, 4:5], norms[:, 6:7]], 1)
        for at, room in enumerate(rooms):
            copies[at].wait()
            copies[at] = pltpu.make_async_copy(room, targets[at], refs[-1].at[at])
            copies[at].start()
        for copy in copies:
            copy.wait()

    anywhere = pl.BlockSpec(memory_space=pl.ANY)
    vmem = pl.BlockSpec(memory_space=pltpu.VMEM)
    shapes = [jax.ShapeDtypeStruct(array.shape, array.dtype) for array in whole]
    shapes += [jax.ShapeDtypeStruct((LAYERS, *pair[0].shape), f32) for pair in pairs]
    shapes += [
        jax.ShapeDtypeStruct(shape, f32)
        for shape in ((LAYERS, 3 * shard_rows, 3), (LAYERS, shard_rows, 2), (LAYERS, shard_rows, 2))
    ]
    return pl.pallas_call(
        kernel,
        in_specs=[anywhere] * len(flat) + [vmem],
        out_specs=[anywhere] * (len(shapes) - 3) + [vmem] * 3,
        out_shape=shapes,
        scratch_shapes=[pltpu.VMEM(array.shape, array.dtype) for array in flat]
        + [pltpu.SemaphoreType.DMA((len(flat),))] * 2,
        compiler_params=pltpu.CompilerParams(vmem_limit_bytes=VMEM_LIMIT),
        name="gather",
    )(*flat, small)


def local_pair(
    activations,
    cotangent,
    lengths,
    weights_qkv,
    conv_taps,
    weights_out,
    weights_up,
    weights_down,
    norm_gains,
    norm_biases,
):
    seqs, rows, width = activations.shape
    half = width // 2
    ff = weights_up.shape[2]
    pairs = half // LANES
    core = lax.axis_index("seq")
    groups = lax.axis_size("batch")
    taps = conv_taps.transpose(0, 2, 1).reshape(LAYERS, 3, 3, 2, pairs, LANES)
    taps = lax.dynamic_index_in_dim(taps, core, 3, keepdims=False)
    taps = jnp.swapaxes(taps, 2, 3).reshape(LAYERS, 3, 3 * half)
    norms = jnp.stack([norm_gains, norm_biases], 1).transpose(0, 3, 1, 2)
    weights = dict(w_out=weights_out, w_up=weights_up, w_down=weights_down)

    def saved(mixed, proj, attn, heads, logs, below):
        return dict(mixed=mixed, proj=proj, attn=attn, heads_in=heads, logs=logs, below=below)

    mixed0, proj0, attn0, mixed1, proj1, attn1, heads0, logs0, middle0, ff_in0, positive0, stream1 = feed_forward(
        lengths, activations, dict(**weights, w_qkv=weights_qkv), taps, norms, groups, 1
    )
    ff_sum1, grad_middle1, norm_two1, grad_heads1, out_grad1, heads1, logs1, block_out = turn(
        1, lengths, mixed1, stream1, cotangent, weights, norms, groups, 2
    )
    lower = dict(positive=positive0, middle=middle0, ff_in=ff_in0, heads=heads0)
    ff_sum0, grad_middle0, norm_two0, grad_heads0, out_grad0, norm_one1, taps1, ups_got, qkv1, out1, up1, down1 = (
        back_link(
            1, lengths, saved(mixed1, proj1, attn1, heads1, logs1, stream1), grad_heads1, out_grad1,
            grad_middle1, ff_sum1, lower, weights_qkv, weights, norms, taps, groups, 3,
        )
    )
    above = dict(norm_one_above=norm_one1, norm_two_above=norm_two1, taps_above=taps1)
    grad_input, qkv0, out0, up0, down0, small = leave(
        lengths, saved(mixed0, proj0, attn0, heads0, logs0, activations), grad_heads0, out_grad0, grad_middle0,
        ff_sum0, ups_got, norm_two0, above, weights_qkv, norms, taps, ff, groups, 4,
    )
    block_out, grad_input, qkv, out, up, down, grad_taps, grad_gains, grad_biases = gather(
        (block_out, grad_input), ((qkv0, qkv1), (out0, out1), (up0, up1), (down0, down1)), small, up0.shape[0]
    )
    return block_out, grad_input, qkv, grad_taps, out, up, down, grad_gains, grad_biases


def solution(mesh):
    chosen = local_pair if (mesh.shape["seq"], mesh.shape["batch"]) == (2, 16) else local
    placed = (
        P("batch", "seq", None),
        P("batch", "seq", None),
        P("batch"),
        P(),
        P(),
        P(),
        P(),
        P(),
        P(),
        P(),
    )
    return jax.shard_map(
        chosen,
        mesh=mesh,
        in_specs=placed,
        out_specs=(
            P("batch", "seq", None),
            P("batch", "seq", None),
            P(None, ("seq", "batch"), None),
            P(None, ("seq", "batch"), None),
            P(None, ("seq", "batch"), None),
            P(None, ("seq", "batch"), None),
            P(None, ("seq", "batch"), None),
            P(None, ("seq", "batch"), None),
            P(None, ("seq", "batch"), None),
        ),
        check_vma=False,
    )
```

```python
import functools
import types

import jax
import jax.numpy as jnp
from jax import lax
from jax.experimental import pallas as pl
from jax.experimental.pallas import tpu as pltpu
from jax.sharding import PartitionSpec as P

HEAD_DIM = 64
LAYERS = 2


def shifted(x, axis, by):
    size = lax.axis_size(axis)
    pairs = [(i, i + by) for i in range(size) if 0 <= i + by < size]
    return lax.ppermute(x, axis, pairs)


def normalize(stream):
    average = jnp.mean(stream, -1, keepdims=True)
    centered = stream - average
    scaling = lax.rsqrt(jnp.mean(centered * centered, -1, keepdims=True) + 1e-05)
    return (centered * scaling, scaling)


def norm_back(grad_norm, normed, scaling, gain):
    scaled = grad_norm * gain
    return scaling * (
        scaled
        - jnp.mean(scaled, -1, keepdims=True)
        - normed * jnp.mean(scaled * normed, -1, keepdims=True)
    )


def split_heads(block):
    return block.reshape(block.shape[0], -1, HEAD_DIM)


def masked_scores(query_seq, key_seq, length, positions):
    scores = jnp.einsum(
        "qhd,khd->hqk",
        split_heads(query_seq),
        split_heads(key_seq),
        preferred_element_type=jnp.float32,
    ) * HEAD_DIM ** (-0.5)
    key_place = jnp.arange(key_seq.shape[0], dtype=jnp.int32)
    allowed = (key_place[None, :] < length) & (
        (key_place[None, :] <= positions[:, None]) | (positions[:, None] >= length)
    )
    return jnp.where(allowed[None], scores, -1e30)


def attention_forward(queries, keys_all, values_all, lengths, positions):

    def one_sequence(items):
        query_seq, key_seq, value_seq, length = items
        scores = masked_scores(query_seq, key_seq, length, positions)
        highest = jnp.max(scores, -1, keepdims=True)
        expo = jnp.exp(scores - highest)
        totals = jnp.sum(expo, -1, keepdims=True)
        probs = (expo / totals).astype(jnp.bfloat16)
        mixed = jnp.einsum(
            "hqk,khd->qhd", probs, split_heads(value_seq), preferred_element_type=jnp.float32
        )
        log_total = (highest + jnp.log(totals))[..., 0]
        return (mixed.reshape(query_seq.shape).astype(jnp.bfloat16), log_total)

    return lax.map(one_sequence, (queries, keys_all, values_all, lengths))


def attention_backward(
    queries, keys_all, values_all, lengths, positions, log_totals, grad_attended
):

    def one_sequence(items):
        query_seq, key_seq, value_seq, length, log_total, grad_seq = items
        scores = masked_scores(query_seq, key_seq, length, positions)
        probs = jnp.exp(scores - log_total[..., None])
        grad_heads = split_heads(grad_seq)
        grad_probs = jnp.einsum(
            "qhd,khd->hqk", grad_heads, split_heads(value_seq), preferred_element_type=jnp.float32
        )
        inner = jnp.sum(probs * grad_probs, -1, keepdims=True)
        grad_scores = (probs * (grad_probs - inner)).astype(jnp.bfloat16)
        grad_query = jnp.einsum(
            "hqk,khd->qhd", grad_scores, split_heads(key_seq), preferred_element_type=jnp.float32
        ) * HEAD_DIM ** (-0.5)
        grad_key = jnp.einsum(
            "hqk,qhd->khd", grad_scores, split_heads(query_seq), preferred_element_type=jnp.float32
        ) * HEAD_DIM ** (-0.5)
        grad_value = jnp.einsum(
            "hqk,qhd->khd",
            probs.astype(jnp.bfloat16),
            grad_heads,
            preferred_element_type=jnp.float32,
        )
        return (
            grad_query.reshape(query_seq.shape),
            grad_key.reshape(key_seq.shape),
            grad_value.reshape(key_seq.shape),
        )

    return lax.map(
        one_sequence, (queries, keys_all, values_all, lengths, log_totals, grad_attended)
    )


def layer_forward(stream, lengths, positions, w_qkv, taps, w_out, w_up, w_down, gains, offsets):
    seqs_here, rows, width = stream.shape
    tokens = seqs_here * rows
    normed_one, scale_one = normalize(stream)
    attn_in = (normed_one * gains[:, 0] + offsets[:, 0]).astype(jnp.bfloat16)
    projected = jnp.dot(
        attn_in.reshape(tokens, width), w_qkv, preferred_element_type=jnp.float32
    ).reshape(seqs_here, rows, 3 * width)
    before = shifted(projected[:, rows - 2 :, :].astype(jnp.bfloat16), "seq", 1).astype(jnp.float32)
    extended = jnp.concatenate([before, projected], 1)
    conv_out = (
        taps[:, 0] * extended[:, 2:]
        + taps[:, 1] * extended[:, 1 : rows + 1]
        + taps[:, 2] * extended[:, :rows]
    )
    mixed_qkv = conv_out.astype(jnp.bfloat16)
    queries = mixed_qkv[..., :width]
    keys_here = mixed_qkv[..., width : 2 * width]
    values_here = mixed_qkv[..., 2 * width :]
    keys_all, values_all = (
        lax.all_gather(keys_here, "seq", axis=1, tiled=True),
        lax.all_gather(values_here, "seq", axis=1, tiled=True),
    )
    attended, log_totals = attention_forward(queries, keys_all, values_all, lengths, positions)
    branch = jnp.dot(attended.reshape(tokens, width), w_out, preferred_element_type=jnp.float32)
    middle = stream + branch.reshape(stream.shape)
    normed_two, scale_two = normalize(middle)
    ff_in = (normed_two * gains[:, 1] + offsets[:, 1]).astype(jnp.bfloat16).reshape(tokens, width)
    hidden_pre = jnp.dot(ff_in, w_up, preferred_element_type=jnp.float32)
    hidden = (jax.nn.relu(hidden_pre) ** 2).astype(jnp.bfloat16)
    result = middle + jnp.dot(hidden, w_down, preferred_element_type=jnp.float32).reshape(
        stream.shape
    )
    kept_keys = (keys_all, values_all)
    saved = (
        normed_one,
        scale_one,
        attn_in,
        extended,
        queries,
        kept_keys,
        attended,
        log_totals,
        normed_two,
        scale_two,
        ff_in,
        hidden_pre,
        hidden,
    )
    return (result, saved)


def layer_backward(grad_stream, lengths, positions, saved, w_qkv, taps, w_out, w_up, w_down, gains):
    (
        normed_one,
        scale_one,
        attn_in,
        extended,
        queries,
        kept_keys,
        attended,
        log_totals,
        normed_two,
        scale_two,
        ff_in,
        hidden_pre,
        hidden,
    ) = saved
    seqs_here, rows, width = grad_stream.shape
    tokens = seqs_here * rows
    grad_down_in = grad_stream.reshape(tokens, width).astype(jnp.bfloat16)
    grad_down = jnp.einsum("tf,td->fd", hidden, grad_down_in, preferred_element_type=jnp.float32)
    grad_hidden = jnp.dot(grad_down_in, w_down.T, preferred_element_type=jnp.float32)
    grad_pre = (grad_hidden * 2.0 * jax.nn.relu(hidden_pre)).astype(jnp.bfloat16)
    grad_up = jnp.einsum("td,tf->df", ff_in, grad_pre, preferred_element_type=jnp.float32)
    grad_ffin = jnp.dot(grad_pre, w_up.T, preferred_element_type=jnp.float32).reshape(
        grad_stream.shape
    )
    gain_two = jnp.sum(grad_ffin * normed_two, (0, 1))
    offset_two = jnp.sum(grad_ffin, (0, 1))
    grad_middle = grad_stream + norm_back(grad_ffin, normed_two, scale_two, gains[:, 1])
    grad_branch = grad_middle.reshape(tokens, width).astype(jnp.bfloat16)
    grad_out = jnp.einsum(
        "td,te->de",
        attended.reshape(tokens, width),
        grad_branch,
        preferred_element_type=jnp.float32,
    )
    grad_attended = jnp.dot(grad_branch, w_out.T, preferred_element_type=jnp.float32)
    grad_attended = grad_attended.astype(jnp.bfloat16).reshape(grad_stream.shape)
    keys_all, values_all = kept_keys
    grad_query, grad_key_all, grad_value_all = attention_backward(
        queries, keys_all, values_all, lengths, positions, log_totals, grad_attended
    )
    grad_key, grad_value = (
        lax.psum_scatter(
            grad_key_all.astype(jnp.bfloat16), "seq", scatter_dimension=1, tiled=True
        ).astype(jnp.float32),
        lax.psum_scatter(
            grad_value_all.astype(jnp.bfloat16), "seq", scatter_dimension=1, tiled=True
        ).astype(jnp.float32),
    )
    grad_conv = jnp.concatenate([grad_query, grad_key, grad_value], -1)
    after = shifted(grad_conv[:, :2, :].astype(jnp.bfloat16), "seq", -1).astype(jnp.float32)
    grad_ext = jnp.concatenate([grad_conv, after], 1)
    grad_proj = (
        taps[:, 0] * grad_ext[:, :rows]
        + taps[:, 1] * grad_ext[:, 1 : rows + 1]
        + taps[:, 2] * grad_ext[:, 2:]
    )
    grad_taps = jnp.stack(
        [
            jnp.sum(grad_conv * extended[:, 2:], (0, 1)),
            jnp.sum(grad_conv * extended[:, 1 : rows + 1], (0, 1)),
            jnp.sum(grad_conv * extended[:, :rows], (0, 1)),
        ],
        -1,
    )
    grad_proj_low = grad_proj.reshape(tokens, 3 * width).astype(jnp.bfloat16)
    grad_qkv = jnp.einsum(
        "td,tf->df",
        attn_in.reshape(tokens, width),
        grad_proj_low,
        preferred_element_type=jnp.float32,
    )
    grad_attn_in = jnp.dot(grad_proj_low, w_qkv.T, preferred_element_type=jnp.float32).reshape(
        grad_stream.shape
    )
    gain_one = jnp.sum(grad_attn_in * normed_one, (0, 1))
    offset_one = jnp.sum(grad_attn_in, (0, 1))
    grad_input = grad_middle + norm_back(grad_attn_in, normed_one, scale_one, gains[:, 0])
    grad_gains = jnp.stack([gain_one, gain_two], -1)
    grad_biases = jnp.stack([offset_one, offset_two], -1)
    return (
        grad_input,
        (grad_qkv, grad_taps, grad_out, grad_up, grad_down, grad_gains, grad_biases),
    )


def reduce_grads(grad_qkv, grad_taps, grad_out, grad_up, grad_down, grad_gains, grad_biases):
    part_qkv, part_taps, part_out, part_up, part_down, part_gains, part_biases = (
        lax.psum_scatter(
            grad_qkv.astype(jnp.bfloat16), "seq", scatter_dimension=0, tiled=True
        ).astype(jnp.float32),
        lax.psum_scatter(
            grad_taps.astype(jnp.bfloat16), "seq", scatter_dimension=0, tiled=True
        ).astype(jnp.float32),
        lax.psum_scatter(
            grad_out.astype(jnp.bfloat16), "seq", scatter_dimension=0, tiled=True
        ).astype(jnp.float32),
        lax.psum_scatter(
            grad_up.astype(jnp.bfloat16), "seq", scatter_dimension=0, tiled=True
        ).astype(jnp.float32),
        lax.psum_scatter(
            grad_down.astype(jnp.bfloat16), "seq", scatter_dimension=0, tiled=True
        ).astype(jnp.float32),
        lax.psum_scatter(
            grad_gains.astype(jnp.bfloat16), "seq", scatter_dimension=0, tiled=True
        ).astype(jnp.float32),
        lax.psum_scatter(
            grad_biases.astype(jnp.bfloat16), "seq", scatter_dimension=0, tiled=True
        ).astype(jnp.float32),
    )
    return (
        lax.psum_scatter(
            part_qkv.astype(jnp.bfloat16), "batch", scatter_dimension=0, tiled=True
        ).astype(jnp.float32),
        lax.psum_scatter(
            part_taps.astype(jnp.bfloat16), "batch", scatter_dimension=0, tiled=True
        ).astype(jnp.float32),
        lax.psum_scatter(
            part_out.astype(jnp.bfloat16), "batch", scatter_dimension=0, tiled=True
        ).astype(jnp.float32),
        lax.psum_scatter(
            part_up.astype(jnp.bfloat16), "batch", scatter_dimension=0, tiled=True
        ).astype(jnp.float32),
        lax.psum_scatter(
            part_down.astype(jnp.bfloat16), "batch", scatter_dimension=0, tiled=True
        ).astype(jnp.float32),
        lax.psum_scatter(
            part_gains.astype(jnp.bfloat16), "batch", scatter_dimension=0, tiled=True
        ).astype(jnp.float32),
        lax.psum_scatter(
            part_biases.astype(jnp.bfloat16), "batch", scatter_dimension=0, tiled=True
        ).astype(jnp.float32),
    )


def local(
    activations,
    cotangent,
    lengths,
    weights_qkv,
    conv_taps,
    weights_out,
    weights_up,
    weights_down,
    norm_gains,
    norm_biases,
):
    seqs_here, rows, width = activations.shape
    positions = lax.axis_index("seq") * rows + jnp.arange(rows, dtype=jnp.int32)
    stream = activations.astype(jnp.float32)
    saved_all = []
    for layer_num in range(LAYERS):
        stream, saved = layer_forward(
            stream,
            lengths,
            positions,
            weights_qkv[layer_num],
            conv_taps[layer_num],
            weights_out[layer_num],
            weights_up[layer_num],
            weights_down[layer_num],
            norm_gains[layer_num],
            norm_biases[layer_num],
        )
        saved_all.append(saved)
    block_out = stream.astype(jnp.bfloat16)
    grad_stream = cotangent.astype(jnp.float32)
    collected = []
    for layer_num in reversed(range(LAYERS)):
        grad_stream, layer_grads = layer_backward(
            grad_stream,
            lengths,
            positions,
            saved_all[layer_num],
            weights_qkv[layer_num],
            conv_taps[layer_num],
            weights_out[layer_num],
            weights_up[layer_num],
            weights_down[layer_num],
            norm_gains[layer_num],
        )
        grad_qkv, grad_taps, grad_out, grad_up, grad_down, grad_gains, grad_biases = layer_grads
        collected.append(
            reduce_grads(grad_qkv, grad_taps, grad_out, grad_up, grad_down, grad_gains, grad_biases)
        )
    collected = collected[::-1]
    stacked = [jnp.stack([member[index] for member in collected], 0) for index in range(7)]
    return (
        block_out,
        grad_stream.astype(jnp.bfloat16),
        stacked[0],
        stacked[1],
        stacked[2],
        stacked[3],
        stacked[4],
        stacked[5],
        stacked[6],
    )


TILE = 256
LANES = 128
VMEM_LIMIT = 60 * 2**20


def dot_nt(left, right):
    return lax.dot_general(
        left, right, (((1,), (1,)), ((), ())), preferred_element_type=jnp.float32
    )


def dot_nn(left, right):
    return lax.dot_general(
        left, right, (((1,), (0,)), ((), ())), preferred_element_type=jnp.float32
    )


def dot_tn(left, right):
    return lax.dot_general(
        left, right, (((0,), (0,)), ((), ())), preferred_element_type=jnp.float32
    )


def head_lanes(head):
    lane = lax.broadcasted_iota(jnp.int32, (1, LANES), 1)
    return (lane >= head * HEAD_DIM) & (lane < (head + 1) * HEAD_DIM)


def causal_tile():
    keys = lax.broadcasted_iota(jnp.int32, (TILE, TILE), 0)
    queries = lax.broadcasted_iota(jnp.int32, (TILE, TILE), 1)
    return keys <= queries


def attend_heads(whole, conv_ref, out_ref, log_ref):
    cap = conv_ref.shape[0]
    hidden = jnp.where(whole, 0.0, -1e30)
    queries = conv_ref[:, :LANES]
    keys = conv_ref[:, LANES : 2 * LANES] * jnp.bfloat16(HEAD_DIM**-0.5)
    keys = [jnp.where(head_lanes(head), keys, jnp.bfloat16(0)) for head in range(2)]
    values_t = conv_ref[:, 2 * LANES :].T
    ones = jnp.ones((16, cap), jnp.bfloat16)
    values = [
        jnp.concatenate([values_t[head * HEAD_DIM : (head + 1) * HEAD_DIM], ones], 0) for head in range(2)
    ]

    def scores_of(block, head):
        rows = slice(block * TILE, (block + 1) * TILE)
        parts = []
        for start in range(0, (block + 1) * TILE, TILE):
            part = dot_nt(keys[head][start : start + TILE], queries[rows])
            if start == block * TILE:
                part = jnp.where(causal_tile(), part, -1e30)
            if start >= cap // 2:
                part = part + hidden
            parts.append(part)
        return parts

    def weights_of(parts):
        highest = functools.reduce(jnp.maximum, [jnp.max(part, 0, keepdims=True) for part in parts])
        return highest, [jnp.exp(part - highest).astype(jnp.bfloat16) for part in parts]

    def finish(block, head, highest, expo):
        got = sum(
            dot_nn(values[head][:, at * TILE : (at + 1) * TILE], part) for at, part in enumerate(expo)
        )
        total = got[HEAD_DIM : HEAD_DIM + 1]
        log_ref[head : head + 1, block * TILE : (block + 1) * TILE] = highest + jnp.log(total)
        return got[:HEAD_DIM] / total

    items = [(block, head) for block in range(cap // TILE) for head in range(2)]
    ahead = scores_of(*items[0])
    waiting = None
    mixed = []

    def close(item):
        mixed.append(finish(*item))
        if len(mixed) == 2:
            rows = slice(item[0] * TILE, (item[0] + 1) * TILE)
            out_ref[rows, :] = jnp.concatenate(mixed, 0).T.astype(jnp.bfloat16)
            mixed.clear()

    for at, item in enumerate(items):
        parts = ahead
        if at + 1 < len(items):
            ahead = scores_of(*items[at + 1])
        if waiting is not None:
            close(waiting)
        waiting = (*item, *weights_of(parts))
    close(waiting)


def attend_back_heads(
    whole, conv_ref, proj_ref, grad_ref, out_ref, log_ref, taps_ref, back_ref, grad_taps_ref, query_t_acc, shift_acc
):
    cap = conv_ref.shape[0]
    factor = jnp.bfloat16(HEAD_DIM**-0.5)
    queries = conv_ref[:, :LANES] * factor
    grads = grad_ref[...]
    keys = [
        jnp.where(head_lanes(head), conv_ref[:, LANES : 2 * LANES], jnp.bfloat16(0)) for head in range(2)
    ]
    values = [
        jnp.where(head_lanes(head), conv_ref[:, 2 * LANES :], jnp.bfloat16(0)) for head in range(2)
    ]
    keys_t = (conv_ref[:, LANES : 2 * LANES] * factor).T
    queries_t = queries.T
    grads_t = grads.T
    product_t = (grads.astype(jnp.float32) * out_ref[...].astype(jnp.float32)).T
    inner = [
        jnp.sum(product_t[head * HEAD_DIM : (head + 1) * HEAD_DIM], 0, keepdims=True)
        for head in range(2)
    ]
    logs = [log_ref[head : head + 1, :] for head in range(2)]
    blocks = cap // TILE

    def products(item):
        head, key, query = item
        rows, cols = slice(key * TILE, (key + 1) * TILE), slice(query * TILE, (query + 1) * TILE)
        return dot_nt(keys[head][rows], queries[cols]), dot_nt(values[head][rows], grads[cols])

    def weights_of(item, raw):
        head, key, query = item
        cols = slice(query * TILE, (query + 1) * TILE)
        log = logs[head][:, cols]
        if key * TILE >= cap // 2:
            log = jnp.where(whole, log, 1e30)
        probs = jnp.exp(raw[0] - log)
        if key == query:
            probs = jnp.where(causal_tile(), probs, 0.0)
        scores = probs * (raw[1] - inner[head][:, cols])
        return probs.astype(jnp.bfloat16), scores.astype(jnp.bfloat16)

    query_t_acc[...] = jnp.zeros_like(query_t_acc)
    grad_value = {}
    grad_key = {}
    grad_query = {}

    def add(store, at, term):
        store[at] = term if at not in store else store[at] + term

    def finish(item, probs, scores):
        head, key, query = item
        lanes = slice(head * HEAD_DIM, (head + 1) * HEAD_DIM)
        rows, cols = slice(key * TILE, (key + 1) * TILE), slice(query * TILE, (query + 1) * TILE)
        add(grad_value, (head, key), dot_nt(grads_t[lanes, cols], probs))
        add(grad_key, (head, key), dot_nt(queries_t[lanes, cols], scores))
        query_t_acc[lanes, cols] += dot_nn(keys_t[lanes, rows], scores)

    items = [(head, key, query) for key in range(blocks) for head in range(2) for query in range(key, blocks)]
    ahead = products(items[0])
    waiting = None
    for at, item in enumerate(items):
        raw = ahead
        if at + 1 < len(items):
            ahead = products(items[at + 1])
        if waiting is not None:
            finish(*waiting)
        waiting = (item, *weights_of(item, raw))
    finish(*waiting)
    for key in range(blocks):
        rows = slice(key * TILE, (key + 1) * TILE)
        shift_acc[1, rows, :] = jnp.concatenate([grad_key[0, key], grad_key[1, key]], 0).T
        shift_acc[2, rows, :] = jnp.concatenate([grad_value[0, key], grad_value[1, key]], 0).T
    shift_acc[0, :cap, :] = query_t_acc[...].T
    shift_acc[:, pl.ds(cap, 8), :] = jnp.zeros((3, 8, LANES), jnp.float32)
    for kind in range(3):
        lanes = slice(kind * LANES, (kind + 1) * LANES)
        proj = proj_ref[:, lanes].astype(jnp.float32)
        total = 0.0
        for lag in range(3):
            moved = shift_acc[kind, lag : lag + cap, :]
            total = total + taps_ref[lag : lag + 1, lanes] * moved
            grad_taps_ref[lag : lag + 1, lanes] = jnp.sum(moved * proj, 0, keepdims=True)
        back_ref[:, lanes] = total.astype(jnp.bfloat16)


def group_bits(groups):
    order = list(range(groups.bit_length() - 1))
    return order, [1, 0] + order[2:]


def normal(x):
    average = jnp.mean(x, -1, keepdims=True)
    centered = x - average
    scaling = lax.rsqrt(jnp.mean(centered * centered, -1, keepdims=True) + 1e-05)
    return centered * scaling, scaling


def blocks_of(rows, size=512):
    return [slice(at, at + size) for at in range(0, rows, size)]


def flip(value, bit):
    return value + (1 - 2 * (value // 2**bit % 2)) * 2**bit


def partner(flips, groups):
    core, group = lax.axis_index("seq"), lax.axis_index("batch")
    if not flips:
        return dict(seq=1 - core, batch=group)
    to = []
    for bits in group_bits(groups):
        other = group
        for place in flips:
            other = flip(other, bits[place])
        to.append(other)
    return dict(seq=core, batch=(1 - core) * to[0] + core * to[1])


def meet(partners):
    greet(partners)
    pl.semaphore_wait(pltpu.get_barrier_semaphore(), len(partners))


def greet(partners):
    barrier = pltpu.get_barrier_semaphore()
    for device in partners:
        pl.semaphore_signal(barrier, inc=1, device_id=device, device_id_type=pl.DeviceIdType.MESH)


def remote(source, target, sends, receives, device):
    return pltpu.make_async_remote_copy(
        src_ref=source,
        dst_ref=target,
        send_sem=sends,
        recv_sem=receives,
        device_id=device,
        device_id_type=pl.DeviceIdType.MESH,
    )


def full_spec(shape):
    return pl.BlockSpec(shape, lambda *_: (0,) * len(shape))


def stage(
    name, body, inputs, small, outputs, scratch, copies, groups, collective_id, flops, moved, lengths=None
):
    partners = scratch.pop("partners")
    scalars = {} if lengths is None else dict(lengths=lengths)
    width = small["gains"].shape[2]
    scratch["norms"] = pltpu.VMEM((LAYERS, 2, 2, width), jnp.float32)
    scratch["taps"] = pltpu.VMEM((LAYERS, 3, 3 * width // 2), jnp.float32)
    names = [*scalars, *inputs, *small, *outputs, *scratch]

    def kernel(*refs):
        r = types.SimpleNamespace(**dict(zip(names, refs)))
        local_sems, send_sems, get_sems = refs[len(names) :]
        counts = [0, 0]

        def local(source, target):
            at = counts[0]
            counts[0] += 1
            return Move(lambda: pltpu.make_async_copy(ref(source), ref(target), local_sems.at[at]))

        def send(source, target, flips=()):
            at = counts[1]
            counts[1] += 1

            def make():
                return remote(
                    ref(source), ref(target), send_sems.at[at], get_sems.at[at], partner(flips, groups)
                )

            return Move(make)

        r.local, r.send, r.groups = local, send, groups
        r.core = lax.axis_index("seq")
        greet([partner(flips, groups) for flips in partners])
        r.meet = lambda: pl.semaphore_wait(pltpu.get_barrier_semaphore(), len(partners))
        for layer in range(LAYERS):
            for which in range(2):
                r.norms[layer, which, 0:1] = r.gains[layer, which : which + 1]
                r.norms[layer, which, 1:2] = r.biases[layer, which : which + 1]
            for block in range(3 * width // 2 // LANES):
                pair, kind = block // 3, block % 3
                at = pl.multiple_of(kind * width + r.core * (width // 2) + pair * LANES, LANES)
                for lag in range(3):
                    row = r.all_taps[lag, layer : layer + 1, pl.ds(at, LANES)]
                    r.taps[layer, lag : lag + 1, block * LANES : (block + 1) * LANES] = row
        body(r)
        assert counts[0] <= copies[0] and counts[1] <= copies[1], counts

    anywhere = pl.BlockSpec(memory_space=pl.ANY)
    return pl.pallas_call(
        kernel,
        in_specs=[pl.BlockSpec(memory_space=pltpu.SMEM)] * len(scalars)
        + [anywhere] * len(inputs)
        + [pl.BlockSpec(memory_space=pltpu.VMEM)] * len(small),
        out_specs=[anywhere] * len(outputs),
        out_shape=list(outputs.values()),
        scratch_shapes=list(scratch.values())
        + [pltpu.SemaphoreType.DMA((count,)) for count in (copies[0], copies[1], copies[1])],
        compiler_params=pltpu.CompilerParams(
            vmem_limit_bytes=VMEM_LIMIT + 3 * 2**20, collective_id=collective_id, has_side_effects=True
        ),
        cost_estimate=pl.CostEstimate(
            flops=int(flops), bytes_accessed=int(moved), transcendentals=0
        ),
        name=name,
    )(*scalars.values(), *inputs.values(), *small.values())


NORM_ROWS = 64


def rows_of(r, seq, block=None):
    rows = r.result.shape[1] if hasattr(r, "result") else r.grad_middle.shape[1]
    block = block or slice(0, rows)
    return slice(seq * rows + block.start, seq * rows + block.stop)


def ref(given):
    return given() if callable(given) else given


class Move:
    def __init__(self, make):
        self.make = make
        make().start()

    def wait(self):
        self.make().wait()

    def wait_recv(self):
        self.make().wait_recv()

    def wait_send(self):
        self.make().wait_send()


def ahead(makers):
    later = None
    for make in makers:
        now, later = later, make()
        if now is not None:
            yield now
    yield later


def span(index, size):
    return pl.ds(pl.multiple_of(index * size, size), size)


def wait_all(copies):
    for copy in copies:
        copy.wait()


def wait_sent(copies):
    for copy in copies:
        copy.wait_send()


def load_head_weight(r, layer):
    width, wide = r.w_qkv_v.shape
    copies = []
    for pair in range(wide // (3 * LANES)):
        for kind in range(3):
            at = pl.multiple_of(kind * width + r.core * (width // 2) + pair * LANES, LANES)
            copies.append(
                r.local(
                    r.w_qkv.at[layer, :, pl.ds(at, LANES)],
                    r.w_qkv_v.at[:, pl.ds((3 * pair + kind) * LANES, LANES)],
                )
            )
    return copies


def scaled(normed, norms):
    return (normed * norms[0:1] + norms[1:2]).astype(jnp.bfloat16)


def norm_rows(r, stream, seq, norms):
    rows = stream.shape[1]
    for block in blocks_of(rows, NORM_ROWS):
        normed, _ = normal(stream[seq, block].astype(jnp.float32))
        at = pl.multiple_of(r.core * rows + block.start, NORM_ROWS)
        r.attn_v[seq, pl.ds(at, NORM_ROWS)] = scaled(normed, norms)


def project(r, layer, seq, targets):
    cap = r.attn_v.shape[1]
    taps = r.taps[layer]
    r.longer[0:8] = jnp.zeros((8, r.longer.shape[1]), jnp.float32)
    blocks = blocks_of(cap, TILE)
    products = ahead(
        [functools.partial(lambda block: dot_nn(r.attn_v[seq, block], r.w_qkv_v[...]), b) for b in blocks]
    )
    for block, here in zip(blocks, products):
        at = 8 + block.start
        r.longer[at : at + TILE, :] = here
        r.proj_v[seq, block] = here.astype(jnp.bfloat16)
        r.mixed_v[seq, block] = (
            taps[0:1] * here
            + taps[1:2] * r.longer[at - 1 : at - 1 + TILE, :]
            + taps[2:3] * r.longer[at - 2 : at - 2 + TILE, :]
        ).astype(jnp.bfloat16)
    sources = (r.mixed_v, r.proj_v, r.attn_v)
    return [r.local(source.at[seq], target.at[seq]) for source, target in zip(sources, targets)]


def project_shapes(seqs, rows, width):
    bf16, f32 = jnp.bfloat16, jnp.float32
    wide = 3 * width // 2
    outputs = {}
    for layer in range(LAYERS):
        for name, columns in (("mixed", wide), ("proj", wide), ("attn", width)):
            outputs[name + str(layer)] = jax.ShapeDtypeStruct((seqs, 2 * rows, columns), bf16)
    scratch = dict(
        w_qkv_v=pltpu.VMEM((width, wide), bf16),
        attn_v=pltpu.VMEM((seqs, 2 * rows, width), bf16),
        longer=pltpu.VMEM((2 * rows + 8, wide), f32),
        proj_v=pltpu.VMEM((seqs, 2 * rows, wide), bf16),
        mixed_v=pltpu.VMEM((seqs, 2 * rows, wide), bf16),
    )
    return outputs, scratch


def load_rows(r, source, target):
    seqs, rows, _ = source.shape
    return [
        r.local(source.at[seq], target.at[pl.ds(seq * rows, rows)]) for seq in range(seqs)
    ]


def share_rows(r, buffer, seq, rows):
    here = span(r.core, rows)
    return r.send(buffer.at[seq, here], buffer.at[seq, here])


def attention(r, seqs, rows, before_send=None):
    half = r.heads_all.shape[1]
    cap = 2 * rows
    mine, theirs = span(r.core, rows), span(1 - r.core, rows)
    loads, sends, outs = [], [], []
    pairs = half // LANES
    if not before_send:
        for pair in range(pairs):
            columns = pl.ds(pair * 3 * LANES, 3 * LANES)
            loads.append(r.local(r.mixed_in.at[:, :, columns], r.mixed_v.at[:, :, columns]))
        r.meet()
    yield
    for pair in range(pairs):
        columns = slice(pair * 3 * LANES, (pair + 1) * 3 * LANES)
        lanes = slice(pair * LANES, (pair + 1) * LANES)
        if loads:
            loads[pair].wait()

        def one(seq, none):
            attend_heads(
                r.lengths[seq] == cap,
                r.mixed_v.at[seq, :, columns],
                r.heads_all.at[pl.ds(pl.multiple_of(seq * cap, cap), cap), lanes],
                r.logs_v.at[seq, pair],
            )

        lax.fori_loop(0, seqs, one, None)
        if pair == 0 and before_send:
            before_send()
        for seq in range(seqs):
            to = pl.ds(pl.multiple_of(r.core * half + pair * LANES, LANES), LANES)
            here = pl.ds(seq * rows, rows)
            own, other = (span(2 * seq + owner, rows) for owner in (r.core, 1 - r.core))
            sends.append(r.send(r.heads_all.at[other, pl.ds(pair * LANES, LANES)], r.heads_v.at[here, to]))
            r.heads_v[here, to] = r.heads_all[own, lanes]
    for seq in range(seqs):
        outs.append(r.local(r.heads_all.at[pl.ds(seq * cap, cap)], r.heads.at[seq]))
    outs.append(r.local(r.logs_v, r.logs))
    for copy in sends:
        copy.wait()
    yield outs


def attention_shapes(seqs, rows, width):
    half = width // 2
    pairs = half // LANES
    bf16, f32 = jnp.bfloat16, jnp.float32
    outputs = dict(
        heads=jax.ShapeDtypeStruct((seqs, 2 * rows, half), bf16),
        logs=jax.ShapeDtypeStruct((seqs, pairs, 2, 2 * rows), f32),
    )
    scratch = dict(
        mixed_v=pltpu.VMEM((seqs, 2 * rows, 3 * half), bf16),
        heads_all=pltpu.VMEM((seqs * 2 * rows, half), bf16),
        logs_v=pltpu.VMEM((seqs, pairs, 2, 2 * rows), f32),
        heads_v=pltpu.VMEM((seqs * rows, width), bf16),
    )
    return outputs, scratch


def out_project(r, layer, seq, norms):
    r.middle_v[seq] += dot_nn(r.heads_v[rows_of(r, seq)], r.w_out_v[...])
    for block in blocks_of(r.middle_v.shape[1], NORM_ROWS):
        normed, _ = normal(r.middle_v[seq, block])
        r.ff_in_v[rows_of(r, seq, block)] = scaled(normed, norms)


def feed(r, seq, hidden, result):
    ff = r.w_up_v.shape[1]
    here = rows_of(r, seq)
    chunks = blocks_of(ff, 768)
    products = ahead(
        [functools.partial(lambda lanes: dot_nn(r.ff_in_v[here], r.w_up_v[:, lanes]), c) for c in chunks]
    )
    for lanes, value in zip(chunks, products):
        positive = jnp.maximum(value, 0.0)
        r.positive_v[here, lanes] = positive.astype(jnp.bfloat16)
        hidden[:, lanes] = (positive * positive).astype(jnp.bfloat16)
    for lanes in blocks_of(r.middle_v.shape[2], TILE):
        value = r.middle_v[seq, :, lanes] + dot_nn(hidden[...], r.w_down_v[:, lanes])
        result[seq, :, lanes] = value.astype(result.dtype)


def load_feed_weights(r, layer):
    return [
        r.local(r.w_out.at[layer], r.w_out_v),
        r.local(r.w_up.at[layer], r.w_up_v),
        r.local(r.w_down.at[layer], r.w_down_v),
    ]


def feed_shapes(seqs, rows, width, ff):
    bf16, f32 = jnp.bfloat16, jnp.float32
    return dict(
        w_out_v=pltpu.VMEM((width, width), bf16),
        w_up_v=pltpu.VMEM((width, ff), bf16),
        w_down_v=pltpu.VMEM((ff, width), bf16),
        middle_v=pltpu.VMEM((seqs, rows, width), f32),
        ff_in_v=pltpu.VMEM((seqs * rows, width), bf16),
        positive_v=pltpu.VMEM((seqs * rows, ff), bf16),
    )


def feed_forward(lengths, stream, weights, norms, groups, collective_id):
    layer = 0
    seqs, rows, width = stream.shape
    ff = weights["w_up"].shape[2]
    tokens = (seqs, rows, width)
    bf16, f32 = jnp.bfloat16, jnp.float32
    outputs, scratch = project_shapes(seqs, rows, width)

    def body(r):
        streams = [r.local(r.stream.at[seq], r.stream_v.at[seq]) for seq in range(seqs)]
        heads_weight = load_head_weight(r, 0)
        r.meet()
        shared, early = [], []
        for seq in range(seqs):
            streams[seq].wait()
            norm_rows(r, r.stream_v, seq, r.norms[0, 0])
            shared.append(share_rows(r, r.attn_v, seq, rows))
        feeds = load_feed_weights(r, layer)
        wait_all(heads_weight)
        for seq in range(seqs):
            shared[seq].wait()
            early += project(r, 0, seq, (r.mixed0, r.proj0, r.attn0))
        feeds += load_head_weight(r, 1)
        heads = attention(r, seqs, rows, lambda: wait_all(early))
        next(heads)
        outs = next(heads)
        wait_all(feeds)
        shared = []
        for seq in range(seqs):
            r.middle_v[seq] = r.stream_v[seq].astype(f32)
            out_project(r, layer, seq, r.norms[layer, 1])
            outs.append(r.local(r.middle_v.at[seq], r.middle.at[seq]))
            here = pl.ds(seq * rows, rows)
            outs.append(r.local(r.ff_in_v.at[here], r.ff_in.at[here]))
            feed(r, seq, r.hidden_v, r.result_v)
            outs.append(r.local(r.positive_v.at[here], r.positive.at[here]))
            outs.append(r.local(r.result_v.at[seq], r.result.at[seq]))
            norm_rows(r, r.result_v, seq, r.norms[layer + 1, 0])
            shared.append(share_rows(r, r.attn_v, seq, rows))
        for seq in range(seqs):
            shared[seq].wait_recv()
            outs += project(r, layer + 1, seq, (r.mixed1, r.proj1, r.attn1))
        wait_sent(shared)
        wait_all(outs)

    more, room = attention_shapes(seqs, rows, width)
    outputs.update(
        more,
        middle=jax.ShapeDtypeStruct(tokens, f32),
        ff_in=jax.ShapeDtypeStruct((seqs * rows, width), bf16),
        positive=jax.ShapeDtypeStruct((seqs * rows, ff), bf16),
        result=jax.ShapeDtypeStruct(tokens, f32),
    )
    scratch.update(room)
    scratch.update(feed_shapes(seqs, rows, width, ff))
    scratch.update(
        stream_v=pltpu.VMEM(tokens, stream.dtype),
        hidden_v=pltpu.VMEM((rows, ff), bf16),
        result_v=pltpu.VMEM(tokens, f32),
        partners=((),),
    )
    return stage(
        "feed_forward", body, dict(stream=stream, **weights), norms,
        outputs, scratch, (60, 12), groups, collective_id,
        2 * seqs * rows * width * (9 * width + 2 * ff), 60_000_000, lengths,
    )


def place_of(shard, owner, groups):
    group = lax.axis_index("batch")
    place = 0
    for one, other in list(zip(*group_bits(groups)))[:2]:
        differs = [(shard // 2**bit % 2 + group // 2**bit % 2) % 2 for bit in (one, other)]
        place = 2 * place + 1 - ((1 - owner) * differs[0] + owner * differs[1])
    line = shard // 4
    return 4 * place + 2 * (line % 2) + line // 2


def feed_back(r, layer, seqs, rows, norms, hooks=None):
    groups, core = r.groups, r.core
    width, ff = r.w_up_v.shape
    half = width // 2
    shard_rows = half // groups
    f32, bf16 = jnp.float32, jnp.bfloat16
    chunk = 768
    hooks = hooks or (lambda *_: None,) * 4
    needed, after_first, before_products, after_ups = hooks
    gain_sum = offset_sum = 0.0
    shared, outs = [], []
    for seq in range(seqs):
        if seq == 1:
            after_first()
        here = rows_of(r, seq)
        r.low[here] = r.grad_v[seq].astype(bf16)
        if seq == 0:
            needed(2)
        chunks = blocks_of(ff, chunk)
        backs = ahead(
            [functools.partial(lambda lanes: dot_nt(r.low[here], r.w_down_v[lanes]), c) for c in chunks]
        )
        for lanes, back in zip(chunks, backs):
            r.pre[here, lanes] = (back * (2.0 * r.positive_v[here, lanes].astype(f32))).astype(bf16)
        if seq == 0:
            needed(3)
        for lanes in blocks_of(width, TILE):
            r.total[:, lanes] = dot_nt(r.pre[here], r.w_up_v[lanes])
        for block in blocks_of(rows, NORM_ROWS):
            grad_in = r.total[block]
            normed, scaling = normal(r.middle_v[seq, block])
            gain_sum += jnp.sum(grad_in * normed, 0, keepdims=True)
            offset_sum += jnp.sum(grad_in, 0, keepdims=True)
            value = r.grad_v[seq, block].astype(f32) + norm_back(grad_in, normed, scaling, norms[0:1])
            r.middle_v[seq, block] = value
            at = pl.multiple_of((2 * seq + core) * rows + block.start, NORM_ROWS)
            r.branch[pl.ds(at, NORM_ROWS)] = value.astype(bf16)
        at = span(2 * seq + core, rows)
        shared.append(r.send(r.branch.at[at], r.branch.at[at]))
        outs.append(r.local(r.middle_v.at[seq], r.grad_middle.at[seq]))
    r.norm_grad_v[0:1] = gain_sum
    r.norm_grad_v[1:2] = offset_sum
    outs.append(r.local(r.norm_grad_v, r.norm_grad))
    before_products()

    up_rows, down_rows = 2 * shard_rows, ff // 2 // groups
    down_start = up_rows * (ff // chunk)

    def up_product(owner, lanes):
        return dot_tn(r.ff_in_v[:, span(owner, half)], r.pre[:, lanes])

    def down_product(owner, lanes):
        at = pl.multiple_of(owner * (ff // 2) + lanes.start, chunk)
        positive = r.positive_v[:, pl.ds(at, chunk)].astype(f32)
        return dot_tn((positive * positive).astype(bf16), r.low[...])

    def products(owner):
        ups, downs = blocks_of(ff, chunk), blocks_of(ff // 2, chunk)
        makers = [functools.partial(up_product, owner, lanes) for lanes in ups]
        makers += [functools.partial(down_product, owner, lanes) for lanes in downs]
        for at, value in enumerate(ahead(makers)):
            size = shard_rows if at < len(ups) else down_rows
            first = 0 if at < len(ups) else (at - len(ups)) * (chunk // down_rows)
            row = at * up_rows if at < len(ups) else down_start
            yield [
                (first + count, row, halves(value[count * size : (count + 1) * size]))
                for count in range(value.shape[0] // size)
            ]

    places = [[place_of(shard, owner, groups) for shard in range(groups)] for owner in (1 - core, core)]
    sends = []
    for at, pieces in enumerate(products(1 - core)):
        for shard, row, piece in pieces:
            r.ff_send[places[0][shard], row : row + piece.shape[0]] = piece.astype(bf16)
        if at == ff // chunk - 1:
            where = (slice(None), pl.ds(0, down_start))
            sends.append(r.send(r.ff_send.at[where], r.ff_got.at[where]))
    where = (slice(None), pl.ds(down_start, 2 * down_rows))
    sends.append(r.send(r.ff_send.at[where], r.ff_got.at[where]))
    for at, pieces in enumerate(products(core)):
        if at == 0:
            sends[0].wait()
        if at == ff // chunk:
            sends[1].wait()
        for shard, row, piece in pieces:
            place = places[1][shard]
            rows_of_piece = slice(row, row + piece.shape[0])
            r.ff_sum_v[place, rows_of_piece] = (
                piece + r.ff_got[place, rows_of_piece].astype(f32)
            ).astype(bf16)
        if at == ff // chunk // 2 - 1:
            after_ups()
        if at == ff // chunk - 1:
            where = (slice(None), pl.ds(0, down_start))
            outs.append(r.local(r.ff_sum_v.at[where], r.ff_sum.at[where]))
    where = (slice(None), pl.ds(down_start, 2 * down_rows))
    outs.append(r.local(r.ff_sum_v.at[where], r.ff_sum.at[where]))
    return shared, outs


def halves(value):
    half = value.shape[1] // 2
    return jnp.concatenate([value[:, :half], value[:, half:]], 0)


def heads_back(r, shared, seqs, rows):
    groups, core = r.groups, r.core
    half = r.grad_heads.shape[2]
    shard_rows = half // groups
    out_grad = r.low.at[pl.ds(0, 2 * half), pl.ds(0, half)]
    outs = []
    for copy in shared:
        copy.wait_recv()
    places = [place_of(shard, core, groups) for shard in range(groups)]
    total = dot_tn(r.heads_all[...], r.branch[...])
    for shard, place in enumerate(places):
        piece = halves(total[shard * shard_rows : (shard + 1) * shard_rows])
        out_grad[span(place, 2 * shard_rows)] = piece.astype(jnp.bfloat16)
    for seq in range(seqs):
        here = slice(seq * 2 * rows, (seq + 1) * 2 * rows)
        grad = dot_nt(r.branch[here], r.w_out_v[span(core, half)])
        r.heads_all[here] = grad.astype(jnp.bfloat16)
        where = pl.ds(here.start, 2 * rows)
        outs.append(r.local(r.heads_all.at[where], r.grad_heads.at[seq]))
    outs.append(r.local(out_grad, r.out_grad))
    wait_sent(shared)
    return outs


def back_shapes(seqs, rows, width, ff, groups):
    bf16, f32 = jnp.bfloat16, jnp.float32
    half = width // 2
    shard_rows = half // groups
    tokens = (seqs, rows, width)
    outputs = dict(
        ff_sum=jax.ShapeDtypeStruct((groups, 4 * ff // groups // 2, half), bf16),
        grad_middle=jax.ShapeDtypeStruct(tokens, f32),
        norm_grad=jax.ShapeDtypeStruct((8, width), f32),
        grad_heads=jax.ShapeDtypeStruct((seqs, 2 * rows, half), bf16),
        out_grad=jax.ShapeDtypeStruct((groups * 2 * shard_rows, half), bf16),
    )
    scratch = dict(
        low=pltpu.VMEM((seqs * rows, width), bf16),
        pre=pltpu.VMEM((seqs * rows, ff), bf16),
        branch=pltpu.VMEM((seqs * 2 * rows, width), bf16),
        norm_grad_v=pltpu.VMEM((8, width), f32),
        ff_send=pltpu.VMEM((groups, 4 * ff // groups // 2, half), bf16),
        ff_got=pltpu.VMEM((groups, 4 * ff // groups // 2, half), bf16),
        heads_all=pltpu.VMEM((seqs * 2 * rows, half), bf16),
    )
    return outputs, scratch


def turn(layer, lengths, mixed, stream, cotangent, weights, norms, groups, collective_id):
    seqs, rows, width = stream.shape
    ff = weights["w_up"].shape[2]
    tokens = (seqs, rows, width)
    bf16, f32 = jnp.bfloat16, jnp.float32
    outputs, scratch = back_shapes(seqs, rows, width, ff, groups)

    def body(r):
        r.low, r.ff_sum_v = r.heads_v, r.ff_send
        heads = attention(r, seqs, rows)
        next(heads)
        loads = [r.local(r.stream, r.middle_v), *load_feed_weights(r, layer), r.local(r.grad, r.grad_v)]
        outs = next(heads)
        wait_all(loads)
        for seq in range(seqs):
            out_project(r, layer, seq, r.norms[layer, 1])
            feed(r, seq, r.pre.at[rows_of(r, seq)], r.result_v)
            outs.append(r.local(r.result_v.at[seq], r.result.at[seq]))
        wait_all(outs[:seqs])
        shared, more = feed_back(r, layer, seqs, rows, r.norms[layer, 1])
        wait_all(outs[seqs:] + more + heads_back(r, shared, seqs, rows))

    more, room = attention_shapes(seqs, rows, width)
    del scratch["low"]
    outputs.update(more, result=jax.ShapeDtypeStruct(tokens, bf16))
    scratch.update(room)
    scratch.update(feed_shapes(seqs, rows, width, ff))
    scratch.update(
        total=pltpu.VMEM((rows, width), f32),
        result_v=pltpu.VMEM(tokens, bf16),
        grad_v=pltpu.VMEM(tokens, cotangent.dtype),
        partners=((),),
    )
    return stage(
        "turn", body, dict(mixed_in=mixed, stream=stream, grad=cotangent, **weights), norms,
        outputs, scratch, (40, 16), groups, collective_id,
        2 * seqs * rows * width * (3 * width + 6 * ff + 2 * width), 60_000_000, lengths,
    )


class Chain:
    def __init__(self, r, shards, got, source=None):
        self.r, self.shards, self.first = r, shards, 8 if source is not None else 0
        self.source = shards if source is None else source
        self.got_a, self.got_b, self.got_z = got
        self.sends = {}

    def part(self, ref, start, count, rows):
        return ref.at[pl.ds(start, count), pl.ds(rows.start, rows.stop - rows.start)]

    def add(self, start, got, rows):
        f32 = jnp.float32
        for at in range(got.shape[0]):
            to = start - self.first + at
            self.shards[to, rows] = (
                self.shards[to, rows].astype(f32) + got[at, rows].astype(f32)
            ).astype(jnp.bfloat16)

    def start_a(self, rows, alone=None):
        source = self.part(self.source, 0, 8, rows) if alone is None else alone.at[pl.ds(0, 8)]
        self.sends["a", rows.start] = self.r.send(source, self.part(self.got_a, 0, 8, rows), (0,))

    def start_b(self, rows):
        if ("a", rows.start) in self.sends:
            self.sends["a", rows.start].wait_recv()
        self.add(8, self.got_a, rows)
        self.sends["b", rows.start] = self.r.send(
            self.part(self.shards, 8 - self.first, 4, rows), self.part(self.got_b, 0, 4, rows), (1,)
        )

    def end_b(self, rows):
        self.sends["b", rows.start].wait_recv()
        self.add(12, self.got_b, rows)

    def start_c(self, rows):
        self.end_b(rows)
        self.sends["c", rows.start] = self.r.send(
            lambda: self.part(self.shards, 12 - self.first + 2 * (1 - line_bits()[0]), 2, rows),
            self.part(self.got_z, 0, 2, rows),
            (2,),
        )

    def start_d(self, rows):
        self.sends["c", rows.start].wait_recv()
        low, high = line_bits()
        to = 12 - self.first + 2 * low
        for at in range(2):
            self.shards[to + at, rows] = (
                self.shards[to + at, rows].astype(jnp.float32) + self.got_z[at, rows].astype(jnp.float32)
            ).astype(jnp.bfloat16)
        self.sends["d", rows.start] = self.r.send(
            lambda: self.part(
                self.shards, 12 - self.first + 2 * line_bits()[0] + 1 - line_bits()[1], 1, rows
            ),
            self.part(self.got_z, 2, 1, rows),
            (3,),
        )

    def end_d(self, rows):
        low, high = line_bits()
        mine = 12 - self.first + 2 * low + high
        self.sends["d", rows.start].wait_recv()
        return self.shards[mine, rows].astype(jnp.float32) + self.got_z[2, rows].astype(jnp.float32)

    def close(self):
        wait_sent(self.sends.values())


def line_bits():
    line = lax.axis_index("batch") // 4
    return line % 2, line // 2


def done_shapes(width, ff, groups):
    rows = width // 2 // groups
    return {
        name: jax.ShapeDtypeStruct(shape, jnp.float32)
        for name, shape in (
            ("qkv_done", (rows, 3 * width)),
            ("out_done", (rows, width)),
            ("up_done", (rows, ff)),
            ("down_done", (ff // 2 // groups, width)),
        )
    }


def attn_rows(shard_rows, pairs):
    size = 2 * shard_rows
    starts = [size * at for at in range(pairs + 2)]
    return [slice(start, start + size) for start in starts[:-1]] + [slice(starts[-1], starts[-1] + 16)]


def set_ff(r, total, up, down):
    shard_rows, ff = up.shape
    half = total.shape[1]
    for at in range(ff // half):
        up[:, at * half : (at + 1) * half] = total[at * shard_rows : (at + 1) * shard_rows]
    start = (ff // half) * shard_rows
    down_rows = down.shape[0]
    for at in range(2):
        first = start + at * down_rows
        down[:, at * half : (at + 1) * half] = total[first : first + down_rows]


def set_qkv(r, total, pair, qkv):
    shard_rows, columns = qkv.shape
    width = columns // 3
    for at, owner in enumerate((r.core, 1 - r.core)):
        for kind in range(3):
            to = pl.multiple_of(kind * width + owner * (width // 2) + pair * LANES, LANES)
            qkv[:, pl.ds(to, LANES)] = total[
                at * shard_rows : (at + 1) * shard_rows, kind * LANES : (kind + 1) * LANES
            ]


def set_out(r, total, out):
    shard_rows, width = out.shape
    out[:, : width // 2] = total[:shard_rows]
    out[:, width // 2 :] = total[shard_rows : 2 * shard_rows]


def chain_shapes(rows, columns):
    bf16 = jnp.bfloat16
    return [pltpu.VMEM((count, rows, columns), bf16) for count in (8, 4, 3)]


def attend_back_pair(r, layer, pair):
    columns = slice(pair * 3 * LANES, (pair + 1) * 3 * LANES)
    half = r.grad_heads_v.shape[1] // 2

    def one(seq):
        cap = r.proj_v.shape[0]
        at = pl.ds(pl.multiple_of(seq * 3 * LANES, LANES), 3 * LANES)
        to = pl.ds(pl.multiple_of(seq * half + pair * LANES, LANES), LANES)
        attend_back_heads(
            r.lengths[seq] == cap,
            r.mixed_v.at[pl.ds(pair * cap, cap), at],
            r.proj_v.at[:, pl.ds(pl.multiple_of((2 * pair + seq) * 3 * LANES, LANES), 3 * LANES)],
            r.grad_heads_v.at[:, to],
            r.heads_v.at[:, to],
            r.logs.at[seq, pair],
            r.taps.at[layer, :, columns],
            r.grad_proj.at[pl.ds(pl.multiple_of(seq * cap, cap), cap), columns],
            r.grad_taps.at[seq, :, columns],
            r.query_t_acc,
            r.shift_acc,
        )

    return one


def project_back(
    r, layer, seqs, rows, norms, attn, after_pair, loading, attention_done=lambda: None,
    before_norm=lambda: None, before_first=lambda: None, partial_first=False,
):
    groups, core = r.groups, r.core
    width, wide = r.w_qkv_v.shape
    half = width // 2
    pairs = half // LANES
    shard_rows = half // groups
    pieces = attn_rows(shard_rows, pairs)
    f32, bf16 = jnp.float32, jnp.bfloat16

    def part(seq, owner):
        return span(2 * seq + owner, rows)

    cap = 2 * rows
    first = []
    for pair in range(pairs):
        columns = pl.ds(pair * 3 * LANES, 3 * LANES)
        lanes = pl.ds(pair * LANES, LANES)
        copies = []
        for seq in range(seqs):
            to = pl.ds(seq * half + pair * LANES, LANES)
            copies += [
                r.local(
                    r.mixed.at[seq, :, columns],
                    r.mixed_v.at[pl.ds(pair * cap, cap), pl.ds(seq * 3 * LANES, 3 * LANES)],
                ),
                r.local(r.grad_heads_in.at[seq, :, lanes], r.grad_heads_v.at[:, to]),
                r.local(r.heads_in.at[seq, :, lanes], r.heads_v.at[:, to]),
                r.local(
                    r.proj.at[seq, :, columns],
                    r.proj_v.at[:, pl.ds((2 * pair + seq) * 3 * LANES, 3 * LANES)],
                ),
            ]
        first.append(copies)
    out_loaded = r.local(r.out_grad_in, attn.shards.at[:, pl.ds(pieces[pairs].start, 2 * shard_rows)])
    r.meet()
    loading()
    inputs_in = load_rows(r, r.attn, r.inputs)
    weights = load_head_weight(r, layer)
    loads = [r.local(r.below, r.below_v), r.local(r.grad_middle_in, r.grad_v)]
    places = [[place_of(shard, owner, groups) for shard in range(groups)] for owner in (1 - core, core)]
    swaps, shared = {}, []

    def send_partial():
        for seq in range(seqs):
            here = slice(seq * rows, (seq + 1) * rows)
            value = dot_nt(r.grad_proj[part(seq, 1 - core)], r.w_qkv_v[...])
            r.heads_v[here] = value.astype(bf16)
            shared.append(r.send(r.heads_v.at[pl.ds(seq * rows, rows)], r.partial_got.at[seq]))

    def merge_pair(pair):
        swaps[pair].wait()
        for place in range(groups):
            piece = jnp.concatenate(
                [r.qkv_keep[pair % 2, place], r.qkv_got[pair, place, :shard_rows].astype(f32)], 0
            )
            attn.shards[place, pieces[pair]] = piece.astype(bf16)
        attn.start_a(pieces[pair])

    for pair in range(pairs):
        wait_all(first[pair])
        if pair == 0:
            before_first()
        one = attend_back_pair(r, layer, pair)
        lax.fori_loop(0, seqs, lambda seq, none: one(seq), None)
        if pair == pairs - 1:
            attention_done()
            wait_all(weights)
            if partial_first:
                send_partial()
        if pair == 0:
            wait_all([out_loaded, *inputs_in])
        else:
            merge_pair(pair - 1)
        columns = slice(pair * 3 * LANES, (pair + 1) * 3 * LANES)
        for at, owner in enumerate((1 - core, core)):
            value = dot_tn(r.inputs[:, span(owner, half)], r.grad_proj[:, columns])
            for shard in range(groups):
                piece = value[shard * shard_rows : (shard + 1) * shard_rows]
                if at == 0:
                    piece = jnp.concatenate([piece, jnp.zeros((32 - shard_rows, half), f32)], 0)
                    r.qkv_send[pair, places[0][shard]] = piece.astype(bf16)
                else:
                    r.qkv_keep[pair % 2, places[1][shard]] = piece
            if at == 0:
                swaps[pair] = r.send(r.qkv_send.at[pair], r.qkv_got.at[pair])
        after_pair(pair)
    if not partial_first:
        send_partial()
    merge_pair(pairs - 1)
    before_norm()
    wait_all(loads)
    gain_sum = offset_sum = 0.0
    for seq in range(seqs):
        r.total[...] = dot_nt(r.grad_proj[part(seq, core)], r.w_qkv_v[...])
        shared[seq].wait_recv()
        for block in blocks_of(rows, NORM_ROWS):
            here = r.total[block] + r.partial_got[seq, block].astype(f32)
            normed, scaling = normal(r.below_v[seq, block].astype(f32))
            gain_sum += jnp.sum(here * normed, 0, keepdims=True)
            offset_sum += jnp.sum(here, 0, keepdims=True)
            r.grad_v[seq, block] += norm_back(here, normed, scaling, norms[0:1])
    wait_sent(shared)
    r.norm_rows[3:4], r.norm_rows[4:5] = gain_sum, offset_sum
    r.taps_wide[...] = jnp.zeros_like(r.taps_wide)
    for pair in range(pairs):
        for kind in range(3):
            at = slice((3 * pair + kind) * LANES, (3 * pair + kind + 1) * LANES)
            to = pl.multiple_of(kind * width + core * half + pair * LANES, LANES)
            r.taps_wide[0:3, pl.ds(to, LANES)] = sum(r.grad_taps[seq, 0:3, at] for seq in range(seqs))


def project_back_shapes(seqs, rows, width, below, groups):
    f32, bf16 = jnp.float32, jnp.bfloat16
    cap, wide, half = 2 * rows, 3 * width // 2, width // 2
    pairs = half // LANES
    shard_rows = half // groups
    own = dict(
        grad_proj=pltpu.VMEM((seqs * cap, wide), bf16),
        grad_taps=pltpu.VMEM((seqs, 8, wide), f32),
        query_t_acc=pltpu.VMEM((LANES, cap), f32),
        shift_acc=pltpu.VMEM((3, cap + 8, LANES), f32),
        inputs=pltpu.VMEM((seqs * cap, width), bf16),
        w_qkv_v=pltpu.VMEM((width, wide), bf16),
        below_v=pltpu.VMEM((seqs, rows, width), below.dtype),
        qkv_send=pltpu.VMEM((pairs, groups, 32, half), bf16),
        qkv_keep=pltpu.VMEM((2, groups, shard_rows, half), f32),
    )
    shared = dict(
        partial_got=pltpu.VMEM((seqs, rows, width), bf16),
        qkv_got=pltpu.VMEM((pairs, groups, 32, half), bf16),
        total=pltpu.VMEM((rows, width), f32),
        grad_v=pltpu.VMEM((seqs, rows, width), f32),
        norm_rows=pltpu.VMEM((8, width), f32),
        taps_wide=pltpu.VMEM((8, 3 * width), f32),
    )
    operands = dict(
        mixed_v=pltpu.VMEM((pairs * cap, seqs * 3 * LANES), bf16),
        proj_v=pltpu.VMEM((cap, pairs * seqs * 3 * LANES), bf16),
        grad_heads_v=pltpu.VMEM((cap, seqs * half), bf16),
        heads_v=pltpu.VMEM((cap, seqs * half), bf16),
    )
    return own, shared, operands


def ff_quarters(rows):
    return [slice(rows * at // 4, rows * (at + 1) // 4) for at in range(4)]


def back_link(
    layer, lengths, saved, grad_heads, out_grad, grad_middle, ff_sum, lower, weights_qkv, weights, norms,
    groups, collective_id,
):
    below = saved["below"]
    seqs, rows, width = below.shape
    ff = weights["w_up"].shape[2]
    half = width // 2
    pairs = half // LANES
    shard_rows = half // groups
    bf16, f32 = jnp.bfloat16, jnp.float32
    outputs, scratch = back_shapes(seqs, rows, width, ff, groups)
    pieces = attn_rows(shard_rows, pairs)[: pairs + 1]
    all_ff = slice(0, ff_sum.shape[1])
    quarters = ff_quarters(all_ff.stop)
    own, shared, _ = project_back_shapes(seqs, rows, width, below, groups)
    shapes = feed_shapes(seqs, rows, width, ff)
    later = {name: scratch.pop(name) for name in ("pre", "ff_send")}
    del scratch["heads_all"]
    later.update({name: shapes.pop(name) for name in ("w_up_v", "middle_v")})
    del shapes["w_out_v"]
    scratch.update(shapes)

    def body(r):
        chain = Chain(r, r.ff_parts, (r.ff_got_a, r.ff_got_b, r.ff_got_z), r.ff_sum_in)
        attn_chain = Chain(r, r.attn_sum_v, (r.attn_got_a, r.attn_got_b, r.attn_got_z))
        summed, small = [], []

        def loading():
            attn_chain.start_a(pieces[pairs], r.out_grad_in)
            for quarter in quarters:
                chain.start_a(quarter)
            summed.append(r.local(lambda: r.ff_sum_in.at[pl.ds(8, 8)], r.ff_parts))

        def after_pair(pair):
            if pair == 0:
                summed[0].wait()
            chain.start_b(quarters[pair])
            if pair >= 1:
                chain.start_c(quarters[pair - 1])
            if pair >= 2:
                chain.start_d(quarters[pair - 2])

        def before_norm():
            chain.start_b(quarters[3])
            chain.start_c(quarters[2])
            chain.start_d(quarters[1])

        r.mixed_v, r.proj_v, r.grad_heads_v, r.heads_v = r.w_down_v, r.positive_v, r.ff_in_v, r.low
        loads = []

        def attention_done():
            loads.append(r.local(lambda: r.w_down.at[layer - 1], r.w_down_v))
            loads.append(r.local(r.positive, r.positive_v))
            loads.append(r.local(r.ff_in, r.ff_in_v))

        def first(*scope):
            vars(r).update(zip(own, scope))
            project_back(
                r, layer, seqs, rows, r.norms[layer, 0], attn_chain, after_pair, loading, attention_done,
                before_norm, partial_first=True,
            )
            small.append(r.local(r.norm_rows, r.norm_one))
            small.append(r.local(r.taps_wide, r.taps_done))

        pl.run_scoped(first, *own.values())

        def second(*scope):
            vars(r).update(zip(later, scope))
            r.ff_sum_v = r.ff_send
            r.down_done_v = r.total.at[pl.ds(0, done["down_done"].shape[0])]
            r.out_done_v = r.total.at[pl.ds(done["down_done"].shape[0], shard_rows)]
            r.heads_all = r.w_down_v.at[pl.ds(0, seqs * 2 * rows), pl.ds(0, half)]
            loads.append(r.local(r.w_up.at[layer - 1], r.w_up_v))
            loads.append(r.local(r.middle, r.middle_v))
            alls = []
            chain.start_c(quarters[3])
            chain.start_d(quarters[2])
            order = (pieces[pairs], *pieces[:pairs])
            early = []

            def needed(count):
                wait_all(loads[:count])
                del loads[:count]

            def after_first():
                chain.start_d(quarters[3])
                for piece in order:
                    attn_chain.start_b(piece)

            def before_products():
                r.w_out_v = r.w_up_v.at[:, pl.ds(0, width)]
                alls.append(r.local(r.w_out.at[layer - 1], r.w_out_v))
                alls.extend(load_rows(r, r.heads, r.heads_all))
                for piece in order:
                    attn_chain.start_c(piece)

            def after_ups():
                first = pl.ds(0, r.ups_got.shape[1])
                early.append(r.send(r.ff_sum_v.at[pl.ds(0, 8), first], r.ups_got, (0,)))
                for piece in order:
                    attn_chain.start_d(piece)

            sent, ends = feed_back(
                r, layer - 1, seqs, rows, r.norms[layer - 1, 1],
                (needed, after_first, before_products, after_ups),
            )
            wait_all(alls)
            ends += heads_back(r, sent, seqs, rows)
            set_out(r, attn_chain.end_d(pieces[pairs]), r.out_done_v)
            for pair in range(pairs):
                set_qkv(r, attn_chain.end_d(pieces[pair]), pair, r.qkv_done_v)
            ends += [r.local(r.out_done_v, r.out_done), r.local(r.qkv_done_v, r.qkv_done)]
            value = jnp.concatenate([chain.end_d(quarter) for quarter in quarters], 0)
            set_ff(r, value, r.up_done_v, r.down_done_v)
            ends += [r.local(r.up_done_v, r.up_done), r.local(r.down_done_v, r.down_done)]
            wait_all(ends + early + small)

        pl.run_scoped(second, *later.values())
        chain.close()
        attn_chain.close()

    attn_all = pieces[-1].stop
    done = done_shapes(width, ff, groups)
    outputs.update(
        norm_one=jax.ShapeDtypeStruct((8, width), f32),
        taps_done=jax.ShapeDtypeStruct((8, 3 * width), f32),
        ups_got=jax.ShapeDtypeStruct((8, all_ff.stop // 4, half), bf16),
        **done,
    )
    ff_got_a, ff_got_b, ff_got_z = chain_shapes(all_ff.stop, half)
    attn_got_a, attn_got_b, attn_got_z = chain_shapes(attn_all, half)
    for name in ("up_done", "qkv_done"):
        scratch[name + "_v"] = pltpu.VMEM(done[name].shape, f32)
    scratch.update(
        shared,
        ff_parts=pltpu.VMEM((8, all_ff.stop, half), bf16),
        ff_got_a=ff_got_a,
        ff_got_b=ff_got_b,
        ff_got_z=ff_got_z,
        attn_sum_v=pltpu.VMEM((groups, attn_all, half), bf16),
        attn_got_a=attn_got_a,
        attn_got_b=attn_got_b,
        attn_got_z=attn_got_z,
        partners=((), (0,), (1,), (2,), (3,)),
    )
    return stage(
        "back_link", body,
        dict(
            **{name: array for name, array in saved.items() if name != "logs"}, grad_heads_in=grad_heads, grad_middle_in=grad_middle, out_grad_in=out_grad.reshape(groups, -1, half),
            ff_sum_in=ff_sum, w_qkv=weights_qkv, **lower, **weights,
        ),
        dict(**norms, logs=saved["logs"]),
        outputs, scratch, (90, 52), groups, collective_id,
        2 * seqs * rows * width * (6 * width + 4 * ff + 2 * width), 60_000_000, lengths,
    )


def leave(
    lengths, saved, grad_heads, out_grad, grad_middle, ff_sum, ups_got, norm_two, small_above, weights_qkv, norms,
    ff, groups, collective_id,
):
    below = saved["below"]
    seqs, rows, width = below.shape
    half = width // 2
    pairs = half // LANES
    shard_rows = half // groups
    bf16, f32 = jnp.bfloat16, jnp.float32
    ff_rows = ff_sum.shape[1]
    quarters = ff_quarters(ff_rows)
    pieces = attn_rows(shard_rows, pairs)
    out_piece, small_piece = pieces[pairs], pieces[pairs + 1]
    done = done_shapes(width, ff, groups)

    def body(r):
        chain = Chain(r, r.ff_parts, (r.ff_got_a, r.ff_got_b, r.ff_got_z), r.ff_sum_in)
        attn_chain = Chain(r, r.attn_sum_v, (r.attn_got_a, r.attn_got_b, r.attn_got_z))
        summed = []

        def loading():
            attn_chain.start_a(out_piece, r.out_grad_in)
            for quarter in quarters[1:]:
                chain.start_a(quarter)
            summed.append(r.local(lambda: r.ff_sum_in.at[pl.ds(8, 8)], r.ff_parts))
            summed.append(r.local(r.ups_got, lambda: r.ff_got_a.at[:, pl.ds(0, quarters[0].stop)]))

        def after_pair(pair):
            chain.start_b(quarters[pair + 1])
            chain.start_c(quarters[pair])
            if pair >= 1:
                chain.start_d(quarters[pair - 1])
            if pair == 1:
                attn_chain.start_b(out_piece)
            if pair == pairs - 1:
                attn_chain.start_c(out_piece)

        def before_first():
            wait_all(summed)
            chain.start_b(quarters[0])

        def before_norm():
            attn_chain.start_b(pieces[0])
            chain.start_c(quarters[3])
            chain.start_d(quarters[2])

        outs = []
        project_back(
            r, 0, seqs, rows, r.norms[0, 0], attn_chain, after_pair, loading, before_norm=before_norm,
            before_first=before_first,
        )
        r.taps_rows[0:8] = r.taps_wide[...]
        r.taps_rows[8:16] = r.taps_above[...]
        r.norms_rows[...] = jnp.zeros_like(r.norms_rows)
        for at, (one, two) in enumerate(((r.norm_rows, r.norm_two), (r.norm_one_above, r.norm_two_above))):
            r.norms_rows[8 * at + 3 : 8 * at + 5] = one[3:5]
            r.norms_rows[8 * at + 5 : 8 * at + 7] = two[0:2]
        r.small_all[...] = jnp.zeros_like(r.small_all)
        for shard in range(2 * groups):
            taps_at, norms_at = 3 * shard_rows * shard, shard_rows * shard
            r.small_all[shard, :, 0 : 3 * shard_rows] = r.taps_rows[:, taps_at : taps_at + 3 * shard_rows]
            r.small_all[shard, :, LANES : LANES + shard_rows] = r.norms_rows[
                :, norms_at : norms_at + shard_rows
            ]
        for shard in range(groups):
            for owner, target in ((1 - r.core, r.small_send), (r.core, r.small_keep)):
                target[place_of(shard, owner, groups)] = r.small_all[owner * groups + shard].astype(bf16)
        swap = r.send(r.small_send, r.small_got)
        r.result_v[...] = r.grad_v[...].astype(bf16)
        outs.append(r.local(r.result_v, r.result))
        attn_chain.start_b(pieces[1])
        chain.start_d(quarters[3])
        attn_chain.start_d(out_piece)
        attn_chain.start_c(pieces[0])
        swap.wait()
        r.attn_sum_v[:, small_piece] = (
            r.small_keep[...].astype(f32) + r.small_got[...].astype(f32)
        ).astype(bf16)
        attn_chain.start_a(small_piece)
        for pair in range(2, pairs):
            attn_chain.start_b(pieces[pair])
        attn_chain.start_c(pieces[1])
        attn_chain.start_b(small_piece)
        attn_chain.start_d(pieces[0])
        for pair in range(2, pairs):
            attn_chain.start_c(pieces[pair])
        attn_chain.start_d(pieces[1])
        attn_chain.start_c(small_piece)
        set_out(r, attn_chain.end_d(out_piece), r.out_done_v)
        outs.append(r.local(r.out_done_v, r.out_done))
        for pair in range(2, pairs):
            attn_chain.start_d(pieces[pair])
        attn_chain.start_d(small_piece)
        set_ff(
            r, jnp.concatenate([chain.end_d(rows_of_ff) for rows_of_ff in quarters], 0),
            r.up_done_v, r.down_done_v,
        )
        outs += [r.local(r.up_done_v, r.up_done), r.local(r.down_done_v, r.down_done)]
        for pair in range(pairs):
            set_qkv(r, attn_chain.end_d(pieces[pair]), pair, r.qkv_done_v)
        outs.append(r.local(r.qkv_done_v, r.qkv_done))
        r.small_done_v[...] = attn_chain.end_d(small_piece)
        outs.append(r.local(r.small_done_v, r.small_done))
        wait_all(outs)
        chain.close()
        attn_chain.close()

    attn_all = small_piece.stop
    done["small_done"] = jax.ShapeDtypeStruct((16, half), f32)
    outputs = dict(result=jax.ShapeDtypeStruct(below.shape, bf16), **done)
    ff_got_a, ff_got_b, ff_got_z = chain_shapes(ff_rows, half)
    attn_got_a, attn_got_b, attn_got_z = chain_shapes(attn_all, half)
    piece = pltpu.VMEM((groups, 16, half), bf16)
    own, shared, operands = project_back_shapes(seqs, rows, width, below, groups)
    scratch = dict(
        **own,
        **shared,
        **operands,
        result_v=pltpu.VMEM((seqs, rows, width), bf16),
        taps_rows=pltpu.VMEM((16, 3 * width), f32),
        norms_rows=pltpu.VMEM((16, width), f32),
        small_all=pltpu.VMEM((2 * groups, 16, half), f32),
        small_send=piece, small_keep=piece, small_got=piece,
        ff_parts=pltpu.VMEM((8, ff_rows, half), bf16),
        ff_got_a=ff_got_a, ff_got_b=ff_got_b, ff_got_z=ff_got_z,
        **{name + "_v": pltpu.VMEM(shape.shape, f32) for name, shape in done.items()},
        attn_sum_v=pltpu.VMEM((groups, attn_all, half), bf16),
        attn_got_a=attn_got_a, attn_got_b=attn_got_b, attn_got_z=attn_got_z,
        partners=((), (0,), (1,), (2,), (3,)),
    )
    return stage(
        "leave", body,
        dict(
            **{name: array for name, array in saved.items() if name != "logs"}, grad_heads_in=grad_heads, grad_middle_in=grad_middle, out_grad_in=out_grad.reshape(groups, -1, half),
            ff_sum_in=ff_sum, ups_got=ups_got, w_qkv=weights_qkv,
        ),
        dict(
            **norms, logs=saved["logs"], norm_two=norm_two, **small_above,
        ),
        outputs, scratch, (70, 60), groups, collective_id,
        8 * seqs * rows * width * 3 * half, 40_000_000, lengths,
    )


def gather(whole, pairs, small, shard_rows):
    f32 = jnp.float32
    flat = list(whole) + [array for pair in pairs for array in pair]

    def kernel(*refs):
        ins, small_ref, refs = refs[: len(flat)], refs[len(flat)], refs[len(flat) + 1 :]
        outs, rooms = refs[: len(whole) + len(pairs) + 3], refs[len(whole) + len(pairs) + 3 : -2]
        targets = list(outs[: len(whole)])
        for out in outs[len(whole) : -3]:
            targets += [out.at[layer] for layer in range(LAYERS)]
        copies = []
        for at, room in enumerate(rooms):
            copies.append(pltpu.make_async_copy(ins[at], room, refs[-2].at[at]))
            copies[-1].start()
        taps_ref, gains_ref, biases_ref = outs[-3:]
        for layer in range(LAYERS):
            for lag in range(3):
                row = 8 * layer + lag
                taps_ref[lag, layer : layer + 1] = small_ref[row : row + 1, : 3 * shard_rows]
            for which in range(2):
                for out, row in ((gains_ref, 8 * layer + 3), (biases_ref, 8 * layer + 4)):
                    row += 2 * which
                    out[layer, which : which + 1] = small_ref[row : row + 1, LANES : LANES + shard_rows]
        for at, room in enumerate(rooms):
            copies[at].wait()
            copies[at] = pltpu.make_async_copy(room, targets[at], refs[-1].at[at])
            copies[at].start()
        for copy in copies:
            copy.wait()

    anywhere = pl.BlockSpec(memory_space=pl.ANY)
    vmem = pl.BlockSpec(memory_space=pltpu.VMEM)
    shapes = [jax.ShapeDtypeStruct(array.shape, array.dtype) for array in whole]
    shapes += [jax.ShapeDtypeStruct((LAYERS, *pair[0].shape), f32) for pair in pairs]
    shapes += [
        jax.ShapeDtypeStruct(shape, f32)
        for shape in ((3, LAYERS, 3 * shard_rows), (LAYERS, 2, shard_rows), (LAYERS, 2, shard_rows))
    ]
    return pl.pallas_call(
        kernel,
        in_specs=[anywhere] * len(flat) + [vmem],
        out_specs=[anywhere] * (len(shapes) - 3) + [vmem] * 3,
        out_shape=shapes,
        scratch_shapes=[pltpu.VMEM(array.shape, array.dtype) for array in flat]
        + [pltpu.SemaphoreType.DMA((len(flat),))] * 2,
        compiler_params=pltpu.CompilerParams(vmem_limit_bytes=VMEM_LIMIT),
        name="gather",
    )(*flat, small)


def local_pair(
    activations,
    cotangent,
    lengths,
    weights_qkv,
    conv_taps,
    weights_out,
    weights_up,
    weights_down,
    norm_gains,
    norm_biases,
):
    seqs, rows, width = activations.shape
    ff = weights_up.shape[2]
    groups = lax.axis_size("batch")
    norms = dict(
        all_taps=conv_taps.transpose(2, 0, 1),
        gains=norm_gains.transpose(0, 2, 1),
        biases=norm_biases.transpose(0, 2, 1),
    )
    weights = dict(w_out=weights_out, w_up=weights_up, w_down=weights_down)

    def saved(mixed, proj, attn, heads, logs, below):
        return dict(mixed=mixed, proj=proj, attn=attn, heads_in=heads, logs=logs, below=below)

    mixed0, proj0, attn0, mixed1, proj1, attn1, heads0, logs0, middle0, ff_in0, positive0, stream1 = feed_forward(
        lengths, activations, dict(**weights, w_qkv=weights_qkv), norms, groups, 1
    )
    ff_sum1, grad_middle1, norm_two1, grad_heads1, out_grad1, heads1, logs1, block_out = turn(
        1, lengths, mixed1, stream1, cotangent, weights, norms, groups, 2
    )
    lower = dict(positive=positive0, middle=middle0, ff_in=ff_in0, heads=heads0)
    ff_sum0, grad_middle0, norm_two0, grad_heads0, out_grad0, norm_one1, taps1, ups_got, qkv1, out1, up1, down1 = (
        back_link(
            1, lengths, saved(mixed1, proj1, attn1, heads1, logs1, stream1), grad_heads1, out_grad1,
            grad_middle1, ff_sum1, lower, weights_qkv, weights, norms, groups, 3,
        )
    )
    above = dict(norm_one_above=norm_one1, norm_two_above=norm_two1, taps_above=taps1)
    grad_input, qkv0, out0, up0, down0, small = leave(
        lengths, saved(mixed0, proj0, attn0, heads0, logs0, activations), grad_heads0, out_grad0, grad_middle0,
        ff_sum0, ups_got, norm_two0, above, weights_qkv, norms, ff, groups, 4,
    )
    block_out, grad_input, qkv, out, up, down, grad_taps, grad_gains, grad_biases = gather(
        (block_out, grad_input), ((qkv0, qkv1), (out0, out1), (up0, up1), (down0, down1)), small, up0.shape[0]
    )
    return (
        block_out,
        grad_input,
        qkv,
        grad_taps.transpose(1, 2, 0),
        out,
        up,
        down,
        grad_gains.transpose(0, 2, 1),
        grad_biases.transpose(0, 2, 1),
    )


def solution(mesh):
    chosen = local_pair if (mesh.shape["seq"], mesh.shape["batch"]) == (2, 16) else local
    placed = (
        P("batch", "seq", None),
        P("batch", "seq", None),
        P("batch"),
        P(),
        P(),
        P(),
        P(),
        P(),
        P(),
        P(),
    )
    return jax.shard_map(
        chosen,
        mesh=mesh,
        in_specs=placed,
        out_specs=(
            P("batch", "seq", None),
            P("batch", "seq", None),
            P(None, ("seq", "batch"), None),
            P(None, ("seq", "batch"), None),
            P(None, ("seq", "batch"), None),
            P(None, ("seq", "batch"), None),
            P(None, ("seq", "batch"), None),
            P(None, ("seq", "batch"), None),
            P(None, ("seq", "batch"), None),
        ),
        check_vma=False,
    )
```

```python
import functools
import types

import jax
import jax.numpy as jnp
from jax import lax
from jax.experimental import pallas as pl
from jax.experimental.pallas import tpu as pltpu
from jax.sharding import PartitionSpec as P

HEAD_DIM = 64
LAYERS = 2


def shifted(x, axis, by):
    size = lax.axis_size(axis)
    pairs = [(i, i + by) for i in range(size) if 0 <= i + by < size]
    return lax.ppermute(x, axis, pairs)


def normalize(stream):
    average = jnp.mean(stream, -1, keepdims=True)
    centered = stream - average
    scaling = lax.rsqrt(jnp.mean(centered * centered, -1, keepdims=True) + 1e-05)
    return (centered * scaling, scaling)


def norm_back(grad_norm, normed, scaling, gain):
    scaled = grad_norm * gain
    return scaling * (
        scaled
        - jnp.mean(scaled, -1, keepdims=True)
        - normed * jnp.mean(scaled * normed, -1, keepdims=True)
    )


def split_heads(block):
    return block.reshape(block.shape[0], -1, HEAD_DIM)


def masked_scores(query_seq, key_seq, length, positions):
    scores = jnp.einsum(
        "qhd,khd->hqk",
        split_heads(query_seq),
        split_heads(key_seq),
        preferred_element_type=jnp.float32,
    ) * HEAD_DIM ** (-0.5)
    key_place = jnp.arange(key_seq.shape[0], dtype=jnp.int32)
    allowed = (key_place[None, :] < length) & (
        (key_place[None, :] <= positions[:, None]) | (positions[:, None] >= length)
    )
    return jnp.where(allowed[None], scores, -1e30)


def attention_forward(queries, keys_all, values_all, lengths, positions):

    def one_sequence(items):
        query_seq, key_seq, value_seq, length = items
        scores = masked_scores(query_seq, key_seq, length, positions)
        highest = jnp.max(scores, -1, keepdims=True)
        expo = jnp.exp(scores - highest)
        totals = jnp.sum(expo, -1, keepdims=True)
        probs = (expo / totals).astype(jnp.bfloat16)
        mixed = jnp.einsum(
            "hqk,khd->qhd", probs, split_heads(value_seq), preferred_element_type=jnp.float32
        )
        log_total = (highest + jnp.log(totals))[..., 0]
        return (mixed.reshape(query_seq.shape).astype(jnp.bfloat16), log_total)

    return lax.map(one_sequence, (queries, keys_all, values_all, lengths))


def attention_backward(
    queries, keys_all, values_all, lengths, positions, log_totals, grad_attended
):

    def one_sequence(items):
        query_seq, key_seq, value_seq, length, log_total, grad_seq = items
        scores = masked_scores(query_seq, key_seq, length, positions)
        probs = jnp.exp(scores - log_total[..., None])
        grad_heads = split_heads(grad_seq)
        grad_probs = jnp.einsum(
            "qhd,khd->hqk", grad_heads, split_heads(value_seq), preferred_element_type=jnp.float32
        )
        inner = jnp.sum(probs * grad_probs, -1, keepdims=True)
        grad_scores = (probs * (grad_probs - inner)).astype(jnp.bfloat16)
        grad_query = jnp.einsum(
            "hqk,khd->qhd", grad_scores, split_heads(key_seq), preferred_element_type=jnp.float32
        ) * HEAD_DIM ** (-0.5)
        grad_key = jnp.einsum(
            "hqk,qhd->khd", grad_scores, split_heads(query_seq), preferred_element_type=jnp.float32
        ) * HEAD_DIM ** (-0.5)
        grad_value = jnp.einsum(
            "hqk,qhd->khd",
            probs.astype(jnp.bfloat16),
            grad_heads,
            preferred_element_type=jnp.float32,
        )
        return (
            grad_query.reshape(query_seq.shape),
            grad_key.reshape(key_seq.shape),
            grad_value.reshape(key_seq.shape),
        )

    return lax.map(
        one_sequence, (queries, keys_all, values_all, lengths, log_totals, grad_attended)
    )


def layer_forward(stream, lengths, positions, w_qkv, taps, w_out, w_up, w_down, gains, offsets):
    seqs_here, rows, width = stream.shape
    tokens = seqs_here * rows
    normed_one, scale_one = normalize(stream)
    attn_in = (normed_one * gains[:, 0] + offsets[:, 0]).astype(jnp.bfloat16)
    projected = jnp.dot(
        attn_in.reshape(tokens, width), w_qkv, preferred_element_type=jnp.float32
    ).reshape(seqs_here, rows, 3 * width)
    before = shifted(projected[:, rows - 2 :, :].astype(jnp.bfloat16), "seq", 1).astype(jnp.float32)
    extended = jnp.concatenate([before, projected], 1)
    conv_out = (
        taps[:, 0] * extended[:, 2:]
        + taps[:, 1] * extended[:, 1 : rows + 1]
        + taps[:, 2] * extended[:, :rows]
    )
    mixed_qkv = conv_out.astype(jnp.bfloat16)
    queries = mixed_qkv[..., :width]
    keys_here = mixed_qkv[..., width : 2 * width]
    values_here = mixed_qkv[..., 2 * width :]
    keys_all, values_all = (
        lax.all_gather(keys_here, "seq", axis=1, tiled=True),
        lax.all_gather(values_here, "seq", axis=1, tiled=True),
    )
    attended, log_totals = attention_forward(queries, keys_all, values_all, lengths, positions)
    branch = jnp.dot(attended.reshape(tokens, width), w_out, preferred_element_type=jnp.float32)
    middle = stream + branch.reshape(stream.shape)
    normed_two, scale_two = normalize(middle)
    ff_in = (normed_two * gains[:, 1] + offsets[:, 1]).astype(jnp.bfloat16).reshape(tokens, width)
    hidden_pre = jnp.dot(ff_in, w_up, preferred_element_type=jnp.float32)
    hidden = (jax.nn.relu(hidden_pre) ** 2).astype(jnp.bfloat16)
    result = middle + jnp.dot(hidden, w_down, preferred_element_type=jnp.float32).reshape(
        stream.shape
    )
    kept_keys = (keys_all, values_all)
    saved = (
        normed_one,
        scale_one,
        attn_in,
        extended,
        queries,
        kept_keys,
        attended,
        log_totals,
        normed_two,
        scale_two,
        ff_in,
        hidden_pre,
        hidden,
    )
    return (result, saved)


def layer_backward(grad_stream, lengths, positions, saved, w_qkv, taps, w_out, w_up, w_down, gains):
    (
        normed_one,
        scale_one,
        attn_in,
        extended,
        queries,
        kept_keys,
        attended,
        log_totals,
        normed_two,
        scale_two,
        ff_in,
        hidden_pre,
        hidden,
    ) = saved
    seqs_here, rows, width = grad_stream.shape
    tokens = seqs_here * rows
    grad_down_in = grad_stream.reshape(tokens, width).astype(jnp.bfloat16)
    grad_down = jnp.einsum("tf,td->fd", hidden, grad_down_in, preferred_element_type=jnp.float32)
    grad_hidden = jnp.dot(grad_down_in, w_down.T, preferred_element_type=jnp.float32)
    grad_pre = (grad_hidden * 2.0 * jax.nn.relu(hidden_pre)).astype(jnp.bfloat16)
    grad_up = jnp.einsum("td,tf->df", ff_in, grad_pre, preferred_element_type=jnp.float32)
    grad_ffin = jnp.dot(grad_pre, w_up.T, preferred_element_type=jnp.float32).reshape(
        grad_stream.shape
    )
    gain_two = jnp.sum(grad_ffin * normed_two, (0, 1))
    offset_two = jnp.sum(grad_ffin, (0, 1))
    grad_middle = grad_stream + norm_back(grad_ffin, normed_two, scale_two, gains[:, 1])
    grad_branch = grad_middle.reshape(tokens, width).astype(jnp.bfloat16)
    grad_out = jnp.einsum(
        "td,te->de",
        attended.reshape(tokens, width),
        grad_branch,
        preferred_element_type=jnp.float32,
    )
    grad_attended = jnp.dot(grad_branch, w_out.T, preferred_element_type=jnp.float32)
    grad_attended = grad_attended.astype(jnp.bfloat16).reshape(grad_stream.shape)
    keys_all, values_all = kept_keys
    grad_query, grad_key_all, grad_value_all = attention_backward(
        queries, keys_all, values_all, lengths, positions, log_totals, grad_attended
    )
    grad_key, grad_value = (
        lax.psum_scatter(
            grad_key_all.astype(jnp.bfloat16), "seq", scatter_dimension=1, tiled=True
        ).astype(jnp.float32),
        lax.psum_scatter(
            grad_value_all.astype(jnp.bfloat16), "seq", scatter_dimension=1, tiled=True
        ).astype(jnp.float32),
    )
    grad_conv = jnp.concatenate([grad_query, grad_key, grad_value], -1)
    after = shifted(grad_conv[:, :2, :].astype(jnp.bfloat16), "seq", -1).astype(jnp.float32)
    grad_ext = jnp.concatenate([grad_conv, after], 1)
    grad_proj = (
        taps[:, 0] * grad_ext[:, :rows]
        + taps[:, 1] * grad_ext[:, 1 : rows + 1]
        + taps[:, 2] * grad_ext[:, 2:]
    )
    grad_taps = jnp.stack(
        [
            jnp.sum(grad_conv * extended[:, 2:], (0, 1)),
            jnp.sum(grad_conv * extended[:, 1 : rows + 1], (0, 1)),
            jnp.sum(grad_conv * extended[:, :rows], (0, 1)),
        ],
        -1,
    )
    grad_proj_low = grad_proj.reshape(tokens, 3 * width).astype(jnp.bfloat16)
    grad_qkv = jnp.einsum(
        "td,tf->df",
        attn_in.reshape(tokens, width),
        grad_proj_low,
        preferred_element_type=jnp.float32,
    )
    grad_attn_in = jnp.dot(grad_proj_low, w_qkv.T, preferred_element_type=jnp.float32).reshape(
        grad_stream.shape
    )
    gain_one = jnp.sum(grad_attn_in * normed_one, (0, 1))
    offset_one = jnp.sum(grad_attn_in, (0, 1))
    grad_input = grad_middle + norm_back(grad_attn_in, normed_one, scale_one, gains[:, 0])
    grad_gains = jnp.stack([gain_one, gain_two], -1)
    grad_biases = jnp.stack([offset_one, offset_two], -1)
    return (
        grad_input,
        (grad_qkv, grad_taps, grad_out, grad_up, grad_down, grad_gains, grad_biases),
    )


def reduce_grads(grad_qkv, grad_taps, grad_out, grad_up, grad_down, grad_gains, grad_biases):
    part_qkv, part_taps, part_out, part_up, part_down, part_gains, part_biases = (
        lax.psum_scatter(
            grad_qkv.astype(jnp.bfloat16), "seq", scatter_dimension=0, tiled=True
        ).astype(jnp.float32),
        lax.psum_scatter(
            grad_taps.astype(jnp.bfloat16), "seq", scatter_dimension=0, tiled=True
        ).astype(jnp.float32),
        lax.psum_scatter(
            grad_out.astype(jnp.bfloat16), "seq", scatter_dimension=0, tiled=True
        ).astype(jnp.float32),
        lax.psum_scatter(
            grad_up.astype(jnp.bfloat16), "seq", scatter_dimension=0, tiled=True
        ).astype(jnp.float32),
        lax.psum_scatter(
            grad_down.astype(jnp.bfloat16), "seq", scatter_dimension=0, tiled=True
        ).astype(jnp.float32),
        lax.psum_scatter(
            grad_gains.astype(jnp.bfloat16), "seq", scatter_dimension=0, tiled=True
        ).astype(jnp.float32),
        lax.psum_scatter(
            grad_biases.astype(jnp.bfloat16), "seq", scatter_dimension=0, tiled=True
        ).astype(jnp.float32),
    )
    return (
        lax.psum_scatter(
            part_qkv.astype(jnp.bfloat16), "batch", scatter_dimension=0, tiled=True
        ).astype(jnp.float32),
        lax.psum_scatter(
            part_taps.astype(jnp.bfloat16), "batch", scatter_dimension=0, tiled=True
        ).astype(jnp.float32),
        lax.psum_scatter(
            part_out.astype(jnp.bfloat16), "batch", scatter_dimension=0, tiled=True
        ).astype(jnp.float32),
        lax.psum_scatter(
            part_up.astype(jnp.bfloat16), "batch", scatter_dimension=0, tiled=True
        ).astype(jnp.float32),
        lax.psum_scatter(
            part_down.astype(jnp.bfloat16), "batch", scatter_dimension=0, tiled=True
        ).astype(jnp.float32),
        lax.psum_scatter(
            part_gains.astype(jnp.bfloat16), "batch", scatter_dimension=0, tiled=True
        ).astype(jnp.float32),
        lax.psum_scatter(
            part_biases.astype(jnp.bfloat16), "batch", scatter_dimension=0, tiled=True
        ).astype(jnp.float32),
    )


def local(
    activations,
    cotangent,
    lengths,
    weights_qkv,
    conv_taps,
    weights_out,
    weights_up,
    weights_down,
    norm_gains,
    norm_biases,
):
    seqs_here, rows, width = activations.shape
    positions = lax.axis_index("seq") * rows + jnp.arange(rows, dtype=jnp.int32)
    stream = activations.astype(jnp.float32)
    saved_all = []
    for layer_num in range(LAYERS):
        stream, saved = layer_forward(
            stream,
            lengths,
            positions,
            weights_qkv[layer_num],
            conv_taps[layer_num],
            weights_out[layer_num],
            weights_up[layer_num],
            weights_down[layer_num],
            norm_gains[layer_num],
            norm_biases[layer_num],
        )
        saved_all.append(saved)
    block_out = stream.astype(jnp.bfloat16)
    grad_stream = cotangent.astype(jnp.float32)
    collected = []
    for layer_num in reversed(range(LAYERS)):
        grad_stream, layer_grads = layer_backward(
            grad_stream,
            lengths,
            positions,
            saved_all[layer_num],
            weights_qkv[layer_num],
            conv_taps[layer_num],
            weights_out[layer_num],
            weights_up[layer_num],
            weights_down[layer_num],
            norm_gains[layer_num],
        )
        grad_qkv, grad_taps, grad_out, grad_up, grad_down, grad_gains, grad_biases = layer_grads
        collected.append(
            reduce_grads(grad_qkv, grad_taps, grad_out, grad_up, grad_down, grad_gains, grad_biases)
        )
    collected = collected[::-1]
    stacked = [jnp.stack([member[index] for member in collected], 0) for index in range(7)]
    return (
        block_out,
        grad_stream.astype(jnp.bfloat16),
        stacked[0],
        stacked[1],
        stacked[2],
        stacked[3],
        stacked[4],
        stacked[5],
        stacked[6],
    )


TILE = 256
LANES = 128
VMEM_LIMIT = 60 * 2**20


def dot_nt(left, right):
    return lax.dot_general(
        left, right, (((1,), (1,)), ((), ())), preferred_element_type=jnp.float32
    )


def dot_nn(left, right):
    return lax.dot_general(
        left, right, (((1,), (0,)), ((), ())), preferred_element_type=jnp.float32
    )


def dot_tn(left, right):
    return lax.dot_general(
        left, right, (((0,), (0,)), ((), ())), preferred_element_type=jnp.float32
    )


def head_lanes(head):
    lane = lax.broadcasted_iota(jnp.int32, (1, LANES), 1)
    return (lane >= head * HEAD_DIM) & (lane < (head + 1) * HEAD_DIM)


def causal_tile():
    keys = lax.broadcasted_iota(jnp.int32, (TILE, TILE), 0)
    queries = lax.broadcasted_iota(jnp.int32, (TILE, TILE), 1)
    return keys <= queries


def attend_heads(whole, conv_ref, out_ref, log_ref):
    cap = conv_ref.shape[0]
    hidden = jnp.where(whole, 0.0, -1e30)
    queries = conv_ref[:, :LANES]
    keys = conv_ref[:, LANES : 2 * LANES] * jnp.bfloat16(HEAD_DIM**-0.5)
    keys = [jnp.where(head_lanes(head), keys, jnp.bfloat16(0)) for head in range(2)]
    values_t = conv_ref[:, 2 * LANES :].T
    ones = jnp.ones((16, cap), jnp.bfloat16)
    values = [
        jnp.concatenate([values_t[head * HEAD_DIM : (head + 1) * HEAD_DIM], ones], 0) for head in range(2)
    ]

    def scores_of(block, head):
        rows = slice(block * TILE, (block + 1) * TILE)
        parts = []
        for start in range(0, (block + 1) * TILE, TILE):
            part = dot_nt(keys[head][start : start + TILE], queries[rows])
            if start == block * TILE:
                part = jnp.where(causal_tile(), part, -1e30)
            if start >= cap // 2:
                part = part + hidden
            parts.append(part)
        return parts

    def weights_of(parts):
        highest = functools.reduce(jnp.maximum, [jnp.max(part, 0, keepdims=True) for part in parts])
        return highest, [jnp.exp(part - highest).astype(jnp.bfloat16) for part in parts]

    def finish(block, head, highest, expo):
        got = sum(
            dot_nn(values[head][:, at * TILE : (at + 1) * TILE], part) for at, part in enumerate(expo)
        )
        total = got[HEAD_DIM : HEAD_DIM + 1]
        log_ref[head : head + 1, block * TILE : (block + 1) * TILE] = highest + jnp.log(total)
        return got[:HEAD_DIM] / total

    items = [(block, head) for block in range(cap // TILE) for head in range(2)]
    ahead = scores_of(*items[0])
    waiting = None
    mixed = []

    def close(item):
        mixed.append(finish(*item))
        if len(mixed) == 2:
            rows = slice(item[0] * TILE, (item[0] + 1) * TILE)
            out_ref[rows, :] = jnp.concatenate(mixed, 0).T.astype(jnp.bfloat16)
            mixed.clear()

    for at, item in enumerate(items):
        parts = ahead
        if at + 1 < len(items):
            ahead = scores_of(*items[at + 1])
        if waiting is not None:
            close(waiting)
        waiting = (*item, *weights_of(parts))
    close(waiting)


def attend_back_heads(
    whole, conv_ref, proj_ref, grad_ref, out_ref, log_ref, taps_ref, back_ref, grad_taps_ref, query_t_acc, shift_acc
):
    cap = conv_ref.shape[0]
    factor = jnp.bfloat16(HEAD_DIM**-0.5)
    queries = conv_ref[:, :LANES] * factor
    grads = grad_ref[...]
    keys = [
        jnp.where(head_lanes(head), conv_ref[:, LANES : 2 * LANES], jnp.bfloat16(0)) for head in range(2)
    ]
    values = [
        jnp.where(head_lanes(head), conv_ref[:, 2 * LANES :], jnp.bfloat16(0)) for head in range(2)
    ]
    keys_t = (conv_ref[:, LANES : 2 * LANES] * factor).T
    queries_t = queries.T
    grads_t = grads.T
    product_t = (grads.astype(jnp.float32) * out_ref[...].astype(jnp.float32)).T
    inner = [
        jnp.sum(product_t[head * HEAD_DIM : (head + 1) * HEAD_DIM], 0, keepdims=True)
        for head in range(2)
    ]
    logs = [log_ref[head : head + 1, :] for head in range(2)]
    blocks = cap // TILE

    def products(item):
        head, key, query = item
        rows, cols = slice(key * TILE, (key + 1) * TILE), slice(query * TILE, (query + 1) * TILE)
        return dot_nt(keys[head][rows], queries[cols]), dot_nt(values[head][rows], grads[cols])

    def weights_of(item, raw):
        head, key, query = item
        cols = slice(query * TILE, (query + 1) * TILE)
        log = logs[head][:, cols]
        if key * TILE >= cap // 2:
            log = jnp.where(whole, log, 1e30)
        probs = jnp.exp(raw[0] - log)
        if key == query:
            probs = jnp.where(causal_tile(), probs, 0.0)
        scores = probs * (raw[1] - inner[head][:, cols])
        return probs.astype(jnp.bfloat16), scores.astype(jnp.bfloat16)

    query_t_acc[...] = jnp.zeros_like(query_t_acc)
    grad_value = {}
    grad_key = {}
    grad_query = {}

    def add(store, at, term):
        store[at] = term if at not in store else store[at] + term

    def finish(item, probs, scores):
        head, key, query = item
        lanes = slice(head * HEAD_DIM, (head + 1) * HEAD_DIM)
        rows, cols = slice(key * TILE, (key + 1) * TILE), slice(query * TILE, (query + 1) * TILE)
        add(grad_value, (head, key), dot_nt(grads_t[lanes, cols], probs))
        add(grad_key, (head, key), dot_nt(queries_t[lanes, cols], scores))
        query_t_acc[lanes, cols] += dot_nn(keys_t[lanes, rows], scores)

    items = [(head, key, query) for key in range(blocks) for head in range(2) for query in range(key, blocks)]
    ahead = products(items[0])
    waiting = None
    for at, item in enumerate(items):
        raw = ahead
        if at + 1 < len(items):
            ahead = products(items[at + 1])
        if waiting is not None:
            finish(*waiting)
        waiting = (item, *weights_of(item, raw))
    finish(*waiting)
    for key in range(blocks):
        rows = slice(key * TILE, (key + 1) * TILE)
        shift_acc[1, rows, :] = jnp.concatenate([grad_key[0, key], grad_key[1, key]], 0).T
        shift_acc[2, rows, :] = jnp.concatenate([grad_value[0, key], grad_value[1, key]], 0).T
    shift_acc[0, :cap, :] = query_t_acc[...].T
    shift_acc[:, pl.ds(cap, 8), :] = jnp.zeros((3, 8, LANES), jnp.float32)
    for kind in range(3):
        lanes = slice(kind * LANES, (kind + 1) * LANES)
        proj = proj_ref[:, lanes].astype(jnp.float32)
        total = 0.0
        for lag in range(3):
            moved = shift_acc[kind, lag : lag + cap, :]
            total = total + taps_ref[lag : lag + 1, lanes] * moved
            grad_taps_ref[lag : lag + 1, lanes] = jnp.sum(moved * proj, 0, keepdims=True)
        back_ref[:, lanes] = total.astype(jnp.bfloat16)


def normal(x):
    average = jnp.mean(x, -1, keepdims=True)
    centered = x - average
    scaling = lax.rsqrt(jnp.mean(centered * centered, -1, keepdims=True) + 1e-05)
    return centered * scaling, scaling


def blocks_of(rows, size=512):
    return [slice(at, at + size) for at in range(0, rows, size)]


def greet(partners):
    barrier = pltpu.get_barrier_semaphore()
    for device in partners:
        pl.semaphore_signal(barrier, inc=1, device_id=device, device_id_type=pl.DeviceIdType.MESH)


def remote(source, target, sends, receives, device):
    return pltpu.make_async_remote_copy(
        src_ref=source,
        dst_ref=target,
        send_sem=sends,
        recv_sem=receives,
        device_id=device,
        device_id_type=pl.DeviceIdType.MESH,
    )


def full_spec(shape):
    return pl.BlockSpec(shape, lambda *_: (0,) * len(shape))


def stage(
    name, body, inputs, small, outputs, scratch, copies, groups, collective_id, flops, moved, lengths=None
):
    partners = scratch.pop("partners")
    scalars = {} if lengths is None else dict(lengths=lengths)
    width = small["gains"].shape[2]
    scratch["norms"] = pltpu.VMEM((LAYERS, 2, 2, width), jnp.float32)
    scratch["taps"] = pltpu.VMEM((LAYERS, 3, 3 * width // 2), jnp.float32)
    names = [*scalars, *inputs, *small, *outputs, *scratch]

    def kernel(*refs):
        r = types.SimpleNamespace(**dict(zip(names, refs)))
        local_sems, send_sems, get_sems = refs[len(names) :]
        counts = [0, 0]

        def local(source, target):
            at = counts[0]
            counts[0] += 1
            return Move(lambda: pltpu.make_async_copy(ref(source), ref(target), local_sems.at[at]))

        def send(source, target, flips=()):
            at = counts[1]
            counts[1] += 1

            def make():
                return remote(
                    ref(source), ref(target), send_sems.at[at], get_sems.at[at], r.devices[flips]
                )

            return Move(make)

        r.local, r.send, r.groups = local, send, groups
        r.core = lax.axis_index("seq")
        group = lax.axis_index("batch")
        r.bits = [group // 2**bit % 2 for bit in range(4)]
        moves = [(1 - 2 * value) * 2**bit for bit, value in enumerate(r.bits)]
        first = (1 - r.core) * moves[0] + r.core * moves[1]
        steps = [first, moves[0] + moves[1] - first, moves[2], moves[3]]
        r.devices = {(at,): dict(seq=r.core, batch=group + step) for at, step in enumerate(steps)}
        r.devices[()] = dict(seq=1 - r.core, batch=group)
        greet([r.devices[flips] for flips in partners])
        r.meet = lambda: pl.semaphore_wait(pltpu.get_barrier_semaphore(), len(partners))
        for layer in range(LAYERS):
            for which in range(2):
                r.norms[layer, which, 0:1] = r.gains[layer, which : which + 1]
                r.norms[layer, which, 1:2] = r.biases[layer, which : which + 1]
            for block in range(3 * width // 2 // LANES):
                pair, kind = block // 3, block % 3
                at = pl.multiple_of(kind * width + r.core * (width // 2) + pair * LANES, LANES)
                for lag in range(3):
                    row = r.all_taps[lag, layer : layer + 1, pl.ds(at, LANES)]
                    r.taps[layer, lag : lag + 1, block * LANES : (block + 1) * LANES] = row
        body(r)
        assert counts[0] <= copies[0] and counts[1] <= copies[1], counts

    anywhere = pl.BlockSpec(memory_space=pl.ANY)
    return pl.pallas_call(
        kernel,
        in_specs=[pl.BlockSpec(memory_space=pltpu.SMEM)] * len(scalars)
        + [anywhere] * len(inputs)
        + [pl.BlockSpec(memory_space=pltpu.VMEM)] * len(small),
        out_specs=[anywhere] * len(outputs),
        out_shape=list(outputs.values()),
        scratch_shapes=list(scratch.values())
        + [pltpu.SemaphoreType.DMA((count,)) for count in (copies[0], copies[1], copies[1])],
        compiler_params=pltpu.CompilerParams(
            vmem_limit_bytes=VMEM_LIMIT + 3 * 2**20, collective_id=collective_id, has_side_effects=True
        ),
        cost_estimate=pl.CostEstimate(
            flops=int(flops), bytes_accessed=int(moved), transcendentals=0
        ),
        name=name,
    )(*scalars.values(), *inputs.values(), *small.values())


NORM_ROWS = 64


def rows_of(r, seq, block=None):
    rows = r.result.shape[1] if hasattr(r, "result") else r.grad_middle.shape[1]
    block = block or slice(0, rows)
    return slice(seq * rows + block.start, seq * rows + block.stop)


def ref(given):
    return given() if callable(given) else given


class Move:
    def __init__(self, make):
        self.make = make
        make().start()

    def wait(self):
        self.make().wait()

    def wait_recv(self):
        self.make().wait_recv()

    def wait_send(self):
        self.make().wait_send()


def ahead(makers):
    later = None
    for make in makers:
        now, later = later, make()
        if now is not None:
            yield now
    yield later


def span(index, size):
    return pl.ds(pl.multiple_of(index * size, size), size)


def wait_all(copies):
    for copy in copies:
        copy.wait()


def wait_sent(copies):
    for copy in copies:
        copy.wait_send()


def load_head_weight(r, layer):
    width, wide = r.w_qkv_v.shape
    copies = []
    for pair in range(wide // (3 * LANES)):
        for kind in range(3):
            at = pl.multiple_of(kind * width + r.core * (width // 2) + pair * LANES, LANES)
            copies.append(
                r.local(
                    r.w_qkv.at[layer, :, pl.ds(at, LANES)],
                    r.w_qkv_v.at[:, pl.ds((3 * pair + kind) * LANES, LANES)],
                )
            )
    return copies


def scaled(normed, norms):
    return (normed * norms[0:1] + norms[1:2]).astype(jnp.bfloat16)


def norm_rows(r, stream, seq, norms):
    rows = stream.shape[1]
    for block in blocks_of(rows, NORM_ROWS):
        normed, _ = normal(stream[seq, block].astype(jnp.float32))
        at = pl.multiple_of(r.core * rows + block.start, NORM_ROWS)
        r.attn_v[seq, pl.ds(at, NORM_ROWS)] = scaled(normed, norms)


def project(r, layer, seq, targets):
    cap = r.attn_v.shape[1]
    taps = r.taps[layer]
    r.longer[0:8] = jnp.zeros((8, r.longer.shape[1]), jnp.float32)
    blocks = blocks_of(cap, TILE)
    products = ahead(
        [functools.partial(lambda block: dot_nn(r.attn_v[seq, block], r.w_qkv_v[...]), b) for b in blocks]
    )
    for block, here in zip(blocks, products):
        at = 8 + block.start
        r.longer[at : at + TILE, :] = here
        r.proj_v[seq, block] = here.astype(jnp.bfloat16)
        r.mixed_v[seq, block] = (
            taps[0:1] * here
            + taps[1:2] * r.longer[at - 1 : at - 1 + TILE, :]
            + taps[2:3] * r.longer[at - 2 : at - 2 + TILE, :]
        ).astype(jnp.bfloat16)
    sources = (r.mixed_v, r.proj_v, r.attn_v)
    return [r.local(source.at[seq], target.at[seq]) for source, target in zip(sources, targets)]


def project_shapes(seqs, rows, width):
    bf16, f32 = jnp.bfloat16, jnp.float32
    wide = 3 * width // 2
    outputs = {}
    for layer in range(LAYERS):
        for name, columns in (("mixed", wide), ("proj", wide), ("attn", width)):
            outputs[name + str(layer)] = jax.ShapeDtypeStruct((seqs, 2 * rows, columns), bf16)
    scratch = dict(
        w_qkv_v=pltpu.VMEM((width, wide), bf16),
        attn_v=pltpu.VMEM((seqs, 2 * rows, width), bf16),
        longer=pltpu.VMEM((2 * rows + 8, wide), f32),
        proj_v=pltpu.VMEM((seqs, 2 * rows, wide), bf16),
        mixed_v=pltpu.VMEM((seqs, 2 * rows, wide), bf16),
    )
    return outputs, scratch


def load_rows(r, source, target):
    seqs, rows, _ = source.shape
    return [
        r.local(source.at[seq], target.at[pl.ds(seq * rows, rows)]) for seq in range(seqs)
    ]


def share_rows(r, buffer, seq, rows):
    here = span(r.core, rows)
    return r.send(buffer.at[seq, here], buffer.at[seq, here])


def attention(r, seqs, rows, before_send=None):
    half = r.heads_all.shape[1]
    cap = 2 * rows
    mine, theirs = span(r.core, rows), span(1 - r.core, rows)
    loads, sends, outs = [], [], []
    pairs = half // LANES
    if not before_send:
        for pair in range(pairs):
            columns = pl.ds(pair * 3 * LANES, 3 * LANES)
            loads.append(r.local(r.mixed_in.at[:, :, columns], r.mixed_v.at[:, :, columns]))
        r.meet()
    yield
    for pair in range(pairs):
        columns = slice(pair * 3 * LANES, (pair + 1) * 3 * LANES)
        lanes = slice(pair * LANES, (pair + 1) * LANES)
        if loads:
            loads[pair].wait()

        def one(seq, none):
            attend_heads(
                r.lengths[seq] == cap,
                r.mixed_v.at[seq, :, columns],
                r.heads_all.at[pl.ds(pl.multiple_of(seq * cap, cap), cap), lanes],
                r.logs_v.at[seq, pair],
            )

        lax.fori_loop(0, seqs, one, None)
        if pair == 0 and before_send:
            before_send()
        for seq in range(seqs):
            to = pl.ds(pl.multiple_of(r.core * half + pair * LANES, LANES), LANES)
            here = pl.ds(seq * rows, rows)
            own, other = (span(2 * seq + owner, rows) for owner in (r.core, 1 - r.core))
            sends.append(r.send(r.heads_all.at[other, pl.ds(pair * LANES, LANES)], r.heads_v.at[here, to]))
            r.heads_v[here, to] = r.heads_all[own, lanes]
    for seq in range(seqs):
        outs.append(r.local(r.heads_all.at[pl.ds(seq * cap, cap)], r.heads.at[seq]))
    outs.append(r.local(r.logs_v, r.logs))
    for copy in sends:
        copy.wait()
    yield outs


def attention_shapes(seqs, rows, width):
    half = width // 2
    pairs = half // LANES
    bf16, f32 = jnp.bfloat16, jnp.float32
    outputs = dict(
        heads=jax.ShapeDtypeStruct((seqs, 2 * rows, half), bf16),
        logs=jax.ShapeDtypeStruct((seqs, pairs, 2, 2 * rows), f32),
    )
    scratch = dict(
        mixed_v=pltpu.VMEM((seqs, 2 * rows, 3 * half), bf16),
        heads_all=pltpu.VMEM((seqs * 2 * rows, half), bf16),
        logs_v=pltpu.VMEM((seqs, pairs, 2, 2 * rows), f32),
        heads_v=pltpu.VMEM((seqs * rows, width), bf16),
    )
    return outputs, scratch


def out_project(r, layer, seq, norms):
    r.middle_v[seq] += dot_nn(r.heads_v[rows_of(r, seq)], r.w_out_v[...])
    for block in blocks_of(r.middle_v.shape[1], NORM_ROWS):
        normed, _ = normal(r.middle_v[seq, block])
        r.ff_in_v[rows_of(r, seq, block)] = scaled(normed, norms)


def feed(r, seq, hidden, result):
    ff = r.w_up_v.shape[1]
    here = rows_of(r, seq)
    chunks = blocks_of(ff, 768)
    products = ahead(
        [functools.partial(lambda lanes: dot_nn(r.ff_in_v[here], r.w_up_v[:, lanes]), c) for c in chunks]
    )
    for lanes, value in zip(chunks, products):
        positive = jnp.maximum(value, 0.0)
        r.positive_v[here, lanes] = positive.astype(jnp.bfloat16)
        hidden[:, lanes] = (positive * positive).astype(jnp.bfloat16)
    for lanes in blocks_of(r.middle_v.shape[2], TILE):
        value = r.middle_v[seq, :, lanes] + dot_nn(hidden[...], r.w_down_v[:, lanes])
        result[seq, :, lanes] = value.astype(result.dtype)


def load_feed_weights(r, layer):
    return [
        r.local(r.w_out.at[layer], r.w_out_v),
        r.local(r.w_up.at[layer], r.w_up_v),
        r.local(r.w_down.at[layer], r.w_down_v),
    ]


def feed_shapes(seqs, rows, width, ff):
    bf16, f32 = jnp.bfloat16, jnp.float32
    return dict(
        w_out_v=pltpu.VMEM((width, width), bf16),
        w_up_v=pltpu.VMEM((width, ff), bf16),
        w_down_v=pltpu.VMEM((ff, width), bf16),
        middle_v=pltpu.VMEM((seqs, rows, width), f32),
        ff_in_v=pltpu.VMEM((seqs * rows, width), bf16),
        positive_v=pltpu.VMEM((seqs * rows, ff), bf16),
    )


def feed_forward(lengths, stream, weights, norms, groups, collective_id):
    layer = 0
    seqs, rows, width = stream.shape
    ff = weights["w_up"].shape[2]
    tokens = (seqs, rows, width)
    bf16, f32 = jnp.bfloat16, jnp.float32
    outputs, scratch = project_shapes(seqs, rows, width)

    def body(r):
        streams = [r.local(r.stream.at[seq], r.stream_v.at[seq]) for seq in range(seqs)]
        heads_weight = load_head_weight(r, 0)
        r.meet()
        shared, early = [], []
        for seq in range(seqs):
            streams[seq].wait()
            norm_rows(r, r.stream_v, seq, r.norms[0, 0])
            shared.append(share_rows(r, r.attn_v, seq, rows))
        feeds = load_feed_weights(r, layer)
        wait_all(heads_weight)
        for seq in range(seqs):
            shared[seq].wait()
            early += project(r, 0, seq, (r.mixed0, r.proj0, r.attn0))
        feeds += load_head_weight(r, 1)
        heads = attention(r, seqs, rows, lambda: wait_all(early))
        next(heads)
        outs = next(heads)
        wait_all(feeds)
        shared = []
        for seq in range(seqs):
            r.middle_v[seq] = r.stream_v[seq].astype(f32)
            out_project(r, layer, seq, r.norms[layer, 1])
            outs.append(r.local(r.middle_v.at[seq], r.middle.at[seq]))
            here = pl.ds(seq * rows, rows)
            outs.append(r.local(r.ff_in_v.at[here], r.ff_in.at[here]))
            feed(r, seq, r.hidden_v, r.result_v)
            outs.append(r.local(r.positive_v.at[here], r.positive.at[here]))
            outs.append(r.local(r.result_v.at[seq], r.result.at[seq]))
            norm_rows(r, r.result_v, seq, r.norms[layer + 1, 0])
            shared.append(share_rows(r, r.attn_v, seq, rows))
        for seq in range(seqs):
            shared[seq].wait_recv()
            outs += project(r, layer + 1, seq, (r.mixed1, r.proj1, r.attn1))
        wait_sent(shared)
        wait_all(outs)

    more, room = attention_shapes(seqs, rows, width)
    outputs.update(
        more,
        middle=jax.ShapeDtypeStruct(tokens, f32),
        ff_in=jax.ShapeDtypeStruct((seqs * rows, width), bf16),
        positive=jax.ShapeDtypeStruct((seqs * rows, ff), bf16),
        result=jax.ShapeDtypeStruct(tokens, f32),
    )
    scratch.update(room)
    scratch.update(feed_shapes(seqs, rows, width, ff))
    scratch.update(
        stream_v=pltpu.VMEM(tokens, stream.dtype),
        hidden_v=pltpu.VMEM((rows, ff), bf16),
        result_v=pltpu.VMEM(tokens, f32),
        partners=((),),
    )
    return stage(
        "feed_forward", body, dict(stream=stream, **weights), norms,
        outputs, scratch, (60, 12), groups, collective_id,
        2 * seqs * rows * width * (9 * width + 2 * ff), 60_000_000, lengths,
    )


def place_of(r, shard, owner):
    same = [r.bits[bit] if shard // 2**bit % 2 else 1 - r.bits[bit] for bit in range(2)]
    line = shard // 4
    return 4 * ((2 - owner) * same[0] + (1 + owner) * same[1]) + 2 * (line % 2) + line // 2


def feed_back(r, layer, seqs, rows, norms, hooks=None):
    groups, core = r.groups, r.core
    width, ff = r.w_up_v.shape
    half = width // 2
    shard_rows = half // groups
    f32, bf16 = jnp.float32, jnp.bfloat16
    chunk = 768
    hooks = hooks or (lambda *_: None,) * 4
    needed, after_first, before_products, after_ups = hooks
    gain_sum = offset_sum = 0.0
    shared, outs = [], []
    for seq in range(seqs):
        if seq == 1:
            after_first()
        here = rows_of(r, seq)
        r.low[here] = r.grad_v[seq].astype(bf16)
        if seq == 0:
            needed(2)
        chunks = blocks_of(ff, chunk)
        backs = ahead(
            [functools.partial(lambda lanes: dot_nt(r.low[here], r.w_down_v[lanes]), c) for c in chunks]
        )
        for lanes, back in zip(chunks, backs):
            r.pre[here, lanes] = (back * (2.0 * r.positive_v[here, lanes].astype(f32))).astype(bf16)
        if seq == 0:
            needed(3)
        for lanes in blocks_of(width, TILE):
            r.total[:, lanes] = dot_nt(r.pre[here], r.w_up_v[lanes])
        for block in blocks_of(rows, NORM_ROWS):
            grad_in = r.total[block]
            normed, scaling = normal(r.middle_v[seq, block])
            gain_sum += jnp.sum(grad_in * normed, 0, keepdims=True)
            offset_sum += jnp.sum(grad_in, 0, keepdims=True)
            value = r.grad_v[seq, block].astype(f32) + norm_back(grad_in, normed, scaling, norms[0:1])
            r.middle_v[seq, block] = value
            at = pl.multiple_of((2 * seq + core) * rows + block.start, NORM_ROWS)
            r.branch[pl.ds(at, NORM_ROWS)] = value.astype(bf16)
        at = span(2 * seq + core, rows)
        shared.append(r.send(r.branch.at[at], r.branch.at[at]))
        outs.append(r.local(r.middle_v.at[seq], r.grad_middle.at[seq]))
    r.norm_grad_v[0:1] = gain_sum
    r.norm_grad_v[1:2] = offset_sum
    outs.append(r.local(r.norm_grad_v, r.norm_grad))
    before_products()

    up_rows, down_rows = 2 * shard_rows, ff // 2 // groups
    down_start = up_rows * (ff // chunk)

    def up_product(owner, lanes):
        return dot_tn(r.ff_in_v[:, span(owner, half)], r.pre[:, lanes])

    def down_product(owner, lanes):
        at = pl.multiple_of(owner * (ff // 2) + lanes.start, chunk)
        positive = r.positive_v[:, pl.ds(at, chunk)].astype(f32)
        return dot_tn((positive * positive).astype(bf16), r.low[...])

    def products(owner):
        ups, downs = blocks_of(ff, chunk), blocks_of(ff // 2, chunk)
        makers = [functools.partial(up_product, owner, lanes) for lanes in ups]
        makers += [functools.partial(down_product, owner, lanes) for lanes in downs]
        for at, value in enumerate(ahead(makers)):
            size = shard_rows if at < len(ups) else down_rows
            first = 0 if at < len(ups) else (at - len(ups)) * (chunk // down_rows)
            row = at * up_rows if at < len(ups) else down_start
            yield [
                (first + count, row, halves(value[count * size : (count + 1) * size]))
                for count in range(value.shape[0] // size)
            ]

    places = [[place_of(r, shard, owner) for shard in range(groups)] for owner in (1 - core, core)]
    sends = []
    for at, pieces in enumerate(products(1 - core)):
        for shard, row, piece in pieces:
            r.ff_send[places[0][shard], row : row + piece.shape[0]] = piece.astype(bf16)
        if at == ff // chunk - 1:
            where = (slice(None), pl.ds(0, down_start))
            sends.append(r.send(r.ff_send.at[where], r.ff_got.at[where]))
    where = (slice(None), pl.ds(down_start, 2 * down_rows))
    sends.append(r.send(r.ff_send.at[where], r.ff_got.at[where]))
    for at, pieces in enumerate(products(core)):
        if at == 0:
            sends[0].wait()
        if at == ff // chunk:
            sends[1].wait()
        for shard, row, piece in pieces:
            place = places[1][shard]
            rows_of_piece = slice(row, row + piece.shape[0])
            r.ff_sum_v[place, rows_of_piece] = (
                piece + r.ff_got[place, rows_of_piece].astype(f32)
            ).astype(bf16)
        if at == ff // chunk // 2 - 1:
            after_ups()
        if at == ff // chunk - 1:
            where = (slice(None), pl.ds(0, down_start))
            outs.append(r.local(r.ff_sum_v.at[where], r.ff_sum.at[where]))
    where = (slice(None), pl.ds(down_start, 2 * down_rows))
    outs.append(r.local(r.ff_sum_v.at[where], r.ff_sum.at[where]))
    return shared, outs


def halves(value):
    half = value.shape[1] // 2
    return jnp.concatenate([value[:, :half], value[:, half:]], 0)


def heads_back(r, shared, seqs, rows):
    groups, core = r.groups, r.core
    half = r.grad_heads.shape[2]
    shard_rows = half // groups
    out_grad = r.low.at[pl.ds(0, 2 * half), pl.ds(0, half)]
    outs = []
    for copy in shared:
        copy.wait_recv()
    places = [place_of(r, shard, core) for shard in range(groups)]
    total = dot_tn(r.heads_all[...], r.branch[...])
    for shard, place in enumerate(places):
        piece = halves(total[shard * shard_rows : (shard + 1) * shard_rows])
        out_grad[span(place, 2 * shard_rows)] = piece.astype(jnp.bfloat16)
    for seq in range(seqs):
        here = slice(seq * 2 * rows, (seq + 1) * 2 * rows)
        grad = dot_nt(r.branch[here], r.w_out_v[span(core, half)])
        r.heads_all[here] = grad.astype(jnp.bfloat16)
        where = pl.ds(here.start, 2 * rows)
        outs.append(r.local(r.heads_all.at[where], r.grad_heads.at[seq]))
    outs.append(r.local(out_grad, r.out_grad))
    wait_sent(shared)
    return outs


def back_shapes(seqs, rows, width, ff, groups):
    bf16, f32 = jnp.bfloat16, jnp.float32
    half = width // 2
    shard_rows = half // groups
    tokens = (seqs, rows, width)
    outputs = dict(
        ff_sum=jax.ShapeDtypeStruct((groups, 4 * ff // groups // 2, half), bf16),
        grad_middle=jax.ShapeDtypeStruct(tokens, f32),
        norm_grad=jax.ShapeDtypeStruct((8, width), f32),
        grad_heads=jax.ShapeDtypeStruct((seqs, 2 * rows, half), bf16),
        out_grad=jax.ShapeDtypeStruct((groups * 2 * shard_rows, half), bf16),
    )
    scratch = dict(
        low=pltpu.VMEM((seqs * rows, width), bf16),
        pre=pltpu.VMEM((seqs * rows, ff), bf16),
        branch=pltpu.VMEM((seqs * 2 * rows, width), bf16),
        norm_grad_v=pltpu.VMEM((8, width), f32),
        ff_send=pltpu.VMEM((groups, 4 * ff // groups // 2, half), bf16),
        ff_got=pltpu.VMEM((groups, 4 * ff // groups // 2, half), bf16),
        heads_all=pltpu.VMEM((seqs * 2 * rows, half), bf16),
    )
    return outputs, scratch


def turn(layer, lengths, mixed, stream, cotangent, weights, norms, groups, collective_id):
    seqs, rows, width = stream.shape
    ff = weights["w_up"].shape[2]
    tokens = (seqs, rows, width)
    bf16, f32 = jnp.bfloat16, jnp.float32
    outputs, scratch = back_shapes(seqs, rows, width, ff, groups)

    def body(r):
        r.low, r.ff_sum_v = r.heads_v, r.ff_send
        heads = attention(r, seqs, rows)
        next(heads)
        loads = [r.local(r.stream, r.middle_v), *load_feed_weights(r, layer), r.local(r.grad, r.grad_v)]
        outs = next(heads)
        wait_all(loads)
        for seq in range(seqs):
            out_project(r, layer, seq, r.norms[layer, 1])
            feed(r, seq, r.pre.at[rows_of(r, seq)], r.result_v)
            outs.append(r.local(r.result_v.at[seq], r.result.at[seq]))
        wait_all(outs[:seqs])
        shared, more = feed_back(r, layer, seqs, rows, r.norms[layer, 1])
        wait_all(outs[seqs:] + more + heads_back(r, shared, seqs, rows))

    more, room = attention_shapes(seqs, rows, width)
    del scratch["low"]
    outputs.update(more, result=jax.ShapeDtypeStruct(tokens, bf16))
    scratch.update(room)
    scratch.update(feed_shapes(seqs, rows, width, ff))
    scratch.update(
        total=pltpu.VMEM((rows, width), f32),
        result_v=pltpu.VMEM(tokens, bf16),
        grad_v=pltpu.VMEM(tokens, cotangent.dtype),
        partners=((),),
    )
    return stage(
        "turn", body, dict(mixed_in=mixed, stream=stream, grad=cotangent, **weights), norms,
        outputs, scratch, (40, 16), groups, collective_id,
        2 * seqs * rows * width * (3 * width + 6 * ff + 2 * width), 60_000_000, lengths,
    )


class Chain:
    def __init__(self, r, shards, got, source=None):
        self.r, self.shards, self.first = r, shards, 8 if source is not None else 0
        self.source = shards if source is None else source
        self.got_a, self.got_b, self.got_z = got
        self.sends = {}

    def part(self, ref, start, count, rows):
        return ref.at[pl.ds(start, count), pl.ds(rows.start, rows.stop - rows.start)]

    def add(self, start, got, rows):
        f32 = jnp.float32
        for at in range(got.shape[0]):
            to = start - self.first + at
            self.shards[to, rows] = (
                self.shards[to, rows].astype(f32) + got[at, rows].astype(f32)
            ).astype(jnp.bfloat16)

    def start_a(self, rows, alone=None):
        source = self.part(self.source, 0, 8, rows) if alone is None else alone.at[pl.ds(0, 8)]
        self.sends["a", rows.start] = self.r.send(source, self.part(self.got_a, 0, 8, rows), (0,))

    def start_b(self, rows):
        if ("a", rows.start) in self.sends:
            self.sends["a", rows.start].wait_recv()
        self.add(8, self.got_a, rows)
        self.sends["b", rows.start] = self.r.send(
            self.part(self.shards, 8 - self.first, 4, rows), self.part(self.got_b, 0, 4, rows), (1,)
        )

    def end_b(self, rows):
        self.sends["b", rows.start].wait_recv()
        self.add(12, self.got_b, rows)

    def start_c(self, rows):
        self.end_b(rows)
        self.sends["c", rows.start] = self.r.send(
            lambda: self.part(self.shards, 12 - self.first + 2 * (1 - self.r.bits[2]), 2, rows),
            self.part(self.got_z, 0, 2, rows),
            (2,),
        )

    def start_d(self, rows):
        self.sends["c", rows.start].wait_recv()
        low, high = self.r.bits[2:]
        to = 12 - self.first + 2 * low
        for at in range(2):
            self.shards[to + at, rows] = (
                self.shards[to + at, rows].astype(jnp.float32) + self.got_z[at, rows].astype(jnp.float32)
            ).astype(jnp.bfloat16)
        self.sends["d", rows.start] = self.r.send(
            lambda: self.part(
                self.shards, 12 - self.first + 2 * self.r.bits[2] + 1 - self.r.bits[3], 1, rows
            ),
            self.part(self.got_z, 2, 1, rows),
            (3,),
        )

    def end_d(self, rows):
        low, high = self.r.bits[2:]
        mine = 12 - self.first + 2 * low + high
        self.sends["d", rows.start].wait_recv()
        return self.shards[mine, rows].astype(jnp.float32) + self.got_z[2, rows].astype(jnp.float32)

    def close(self):
        wait_sent(self.sends.values())


def done_shapes(width, ff, groups):
    rows = width // 2 // groups
    return {
        name: jax.ShapeDtypeStruct(shape, jnp.float32)
        for name, shape in (
            ("qkv_done", (rows, 3 * width)),
            ("out_done", (rows, width)),
            ("up_done", (rows, ff)),
            ("down_done", (ff // 2 // groups, width)),
        )
    }


def attn_rows(shard_rows, pairs):
    size = 2 * shard_rows
    starts = [size * at for at in range(pairs + 2)]
    return [slice(start, start + size) for start in starts[:-1]] + [slice(starts[-1], starts[-1] + 16)]


def set_ff(r, total, up, down):
    shard_rows, ff = up.shape
    half = total.shape[1]
    for at in range(ff // half):
        up[:, at * half : (at + 1) * half] = total[at * shard_rows : (at + 1) * shard_rows]
    start = (ff // half) * shard_rows
    down_rows = down.shape[0]
    for at in range(2):
        first = start + at * down_rows
        down[:, at * half : (at + 1) * half] = total[first : first + down_rows]


def set_qkv(r, total, pair, qkv):
    shard_rows, columns = qkv.shape
    width = columns // 3
    for at, owner in enumerate((r.core, 1 - r.core)):
        for kind in range(3):
            to = pl.multiple_of(kind * width + owner * (width // 2) + pair * LANES, LANES)
            qkv[:, pl.ds(to, LANES)] = total[
                at * shard_rows : (at + 1) * shard_rows, kind * LANES : (kind + 1) * LANES
            ]


def set_out(r, total, out):
    shard_rows, width = out.shape
    out[:, : width // 2] = total[:shard_rows]
    out[:, width // 2 :] = total[shard_rows : 2 * shard_rows]


def chain_shapes(rows, columns):
    bf16 = jnp.bfloat16
    return [pltpu.VMEM((count, rows, columns), bf16) for count in (8, 4, 3)]


def attend_back_pair(r, layer, pair):
    columns = slice(pair * 3 * LANES, (pair + 1) * 3 * LANES)
    half = r.grad_heads_v.shape[1] // 2

    def one(seq):
        cap = r.proj_v.shape[0]
        at = pl.ds(pl.multiple_of(seq * 3 * LANES, LANES), 3 * LANES)
        to = pl.ds(pl.multiple_of(seq * half + pair * LANES, LANES), LANES)
        attend_back_heads(
            r.lengths[seq] == cap,
            r.mixed_v.at[pl.ds(pair * cap, cap), at],
            r.proj_v.at[:, pl.ds(pl.multiple_of((2 * pair + seq) * 3 * LANES, LANES), 3 * LANES)],
            r.grad_heads_v.at[:, to],
            r.heads_v.at[:, to],
            r.logs.at[seq, pair],
            r.taps.at[layer, :, columns],
            r.grad_proj.at[pl.ds(pl.multiple_of(seq * cap, cap), cap), columns],
            r.grad_taps.at[seq, :, columns],
            r.query_t_acc,
            r.shift_acc,
        )

    return one


def project_back(
    r, layer, seqs, rows, norms, attn, after_pair, loading, attention_done=lambda: None,
    before_norm=lambda: None, before_first=lambda: None, partial_first=False,
):
    groups, core = r.groups, r.core
    width, wide = r.w_qkv_v.shape
    half = width // 2
    pairs = half // LANES
    shard_rows = half // groups
    pieces = attn_rows(shard_rows, pairs)
    f32, bf16 = jnp.float32, jnp.bfloat16

    def part(seq, owner):
        return span(2 * seq + owner, rows)

    cap = 2 * rows
    first = []
    for pair in range(pairs):
        columns = pl.ds(pair * 3 * LANES, 3 * LANES)
        lanes = pl.ds(pair * LANES, LANES)
        copies = []
        for seq in range(seqs):
            to = pl.ds(seq * half + pair * LANES, LANES)
            copies += [
                r.local(
                    r.mixed.at[seq, :, columns],
                    r.mixed_v.at[pl.ds(pair * cap, cap), pl.ds(seq * 3 * LANES, 3 * LANES)],
                ),
                r.local(r.grad_heads_in.at[seq, :, lanes], r.grad_heads_v.at[:, to]),
                r.local(r.heads_in.at[seq, :, lanes], r.heads_v.at[:, to]),
                r.local(
                    r.proj.at[seq, :, columns],
                    r.proj_v.at[:, pl.ds((2 * pair + seq) * 3 * LANES, 3 * LANES)],
                ),
            ]
        first.append(copies)
    out_loaded = r.local(r.out_grad_in, attn.shards.at[:, pl.ds(pieces[pairs].start, 2 * shard_rows)])
    r.meet()
    loading()
    inputs_in = load_rows(r, r.attn, r.inputs)
    weights = load_head_weight(r, layer)
    loads = [r.local(r.below, r.below_v), r.local(r.grad_middle_in, r.grad_v)]
    places = [[place_of(r, shard, owner) for shard in range(groups)] for owner in (1 - core, core)]
    swaps, shared = {}, []

    def send_partial():
        for seq in range(seqs):
            here = slice(seq * rows, (seq + 1) * rows)
            value = dot_nt(r.grad_proj[part(seq, 1 - core)], r.w_qkv_v[...])
            r.heads_v[here] = value.astype(bf16)
            shared.append(r.send(r.heads_v.at[pl.ds(seq * rows, rows)], r.partial_got.at[seq]))

    def merge_pair(pair):
        swaps[pair].wait()
        for place in range(groups):
            piece = jnp.concatenate(
                [r.qkv_keep[pair % 2, place], r.qkv_got[pair, place, :shard_rows].astype(f32)], 0
            )
            attn.shards[place, pieces[pair]] = piece.astype(bf16)
        attn.start_a(pieces[pair])

    for pair in range(pairs):
        wait_all(first[pair])
        if pair == 0:
            before_first()
        one = attend_back_pair(r, layer, pair)
        lax.fori_loop(0, seqs, lambda seq, none: one(seq), None)
        if pair == pairs - 1:
            attention_done()
            wait_all(weights)
            if partial_first:
                send_partial()
        if pair == 0:
            wait_all([out_loaded, *inputs_in])
        else:
            merge_pair(pair - 1)
        columns = slice(pair * 3 * LANES, (pair + 1) * 3 * LANES)
        for at, owner in enumerate((1 - core, core)):
            value = dot_tn(r.inputs[:, span(owner, half)], r.grad_proj[:, columns])
            for shard in range(groups):
                piece = value[shard * shard_rows : (shard + 1) * shard_rows]
                if at == 0:
                    piece = jnp.concatenate([piece, jnp.zeros((32 - shard_rows, half), f32)], 0)
                    r.qkv_send[pair, places[0][shard]] = piece.astype(bf16)
                else:
                    r.qkv_keep[pair % 2, places[1][shard]] = piece
            if at == 0:
                swaps[pair] = r.send(r.qkv_send.at[pair], r.qkv_got.at[pair])
        after_pair(pair)
    if not partial_first:
        send_partial()
    merge_pair(pairs - 1)
    before_norm()
    wait_all(loads)
    gain_sum = offset_sum = 0.0
    for seq in range(seqs):
        r.total[...] = dot_nt(r.grad_proj[part(seq, core)], r.w_qkv_v[...])
        shared[seq].wait_recv()
        for block in blocks_of(rows, NORM_ROWS):
            here = r.total[block] + r.partial_got[seq, block].astype(f32)
            normed, scaling = normal(r.below_v[seq, block].astype(f32))
            gain_sum += jnp.sum(here * normed, 0, keepdims=True)
            offset_sum += jnp.sum(here, 0, keepdims=True)
            r.grad_v[seq, block] += norm_back(here, normed, scaling, norms[0:1])
    wait_sent(shared)
    r.norm_rows[3:4], r.norm_rows[4:5] = gain_sum, offset_sum
    r.taps_wide[...] = jnp.zeros_like(r.taps_wide)
    for pair in range(pairs):
        for kind in range(3):
            at = slice((3 * pair + kind) * LANES, (3 * pair + kind + 1) * LANES)
            to = pl.multiple_of(kind * width + core * half + pair * LANES, LANES)
            r.taps_wide[0:3, pl.ds(to, LANES)] = sum(r.grad_taps[seq, 0:3, at] for seq in range(seqs))


def project_back_shapes(seqs, rows, width, below, groups):
    f32, bf16 = jnp.float32, jnp.bfloat16
    cap, wide, half = 2 * rows, 3 * width // 2, width // 2
    pairs = half // LANES
    shard_rows = half // groups
    own = dict(
        grad_proj=pltpu.VMEM((seqs * cap, wide), bf16),
        grad_taps=pltpu.VMEM((seqs, 8, wide), f32),
        query_t_acc=pltpu.VMEM((LANES, cap), f32),
        shift_acc=pltpu.VMEM((3, cap + 8, LANES), f32),
        inputs=pltpu.VMEM((seqs * cap, width), bf16),
        w_qkv_v=pltpu.VMEM((width, wide), bf16),
        below_v=pltpu.VMEM((seqs, rows, width), below.dtype),
        qkv_send=pltpu.VMEM((pairs, groups, 32, half), bf16),
        qkv_keep=pltpu.VMEM((2, groups, shard_rows, half), f32),
    )
    shared = dict(
        partial_got=pltpu.VMEM((seqs, rows, width), bf16),
        qkv_got=pltpu.VMEM((pairs, groups, 32, half), bf16),
        total=pltpu.VMEM((rows, width), f32),
        grad_v=pltpu.VMEM((seqs, rows, width), f32),
        norm_rows=pltpu.VMEM((8, width), f32),
        taps_wide=pltpu.VMEM((8, 3 * width), f32),
    )
    operands = dict(
        mixed_v=pltpu.VMEM((pairs * cap, seqs * 3 * LANES), bf16),
        proj_v=pltpu.VMEM((cap, pairs * seqs * 3 * LANES), bf16),
        grad_heads_v=pltpu.VMEM((cap, seqs * half), bf16),
        heads_v=pltpu.VMEM((cap, seqs * half), bf16),
    )
    return own, shared, operands


def ff_quarters(rows):
    return [slice(rows * at // 4, rows * (at + 1) // 4) for at in range(4)]


def back_link(
    layer, lengths, saved, grad_heads, out_grad, grad_middle, ff_sum, lower, weights_qkv, weights, norms,
    groups, collective_id,
):
    below = saved["below"]
    seqs, rows, width = below.shape
    ff = weights["w_up"].shape[2]
    half = width // 2
    pairs = half // LANES
    shard_rows = half // groups
    bf16, f32 = jnp.bfloat16, jnp.float32
    outputs, scratch = back_shapes(seqs, rows, width, ff, groups)
    pieces = attn_rows(shard_rows, pairs)[: pairs + 1]
    all_ff = slice(0, ff_sum.shape[1])
    quarters = ff_quarters(all_ff.stop)
    own, shared, _ = project_back_shapes(seqs, rows, width, below, groups)
    shapes = feed_shapes(seqs, rows, width, ff)
    later = {name: scratch.pop(name) for name in ("pre", "ff_send")}
    del scratch["heads_all"]
    later.update({name: shapes.pop(name) for name in ("w_up_v", "middle_v")})
    del shapes["w_out_v"]
    scratch.update(shapes)

    def body(r):
        chain = Chain(r, r.ff_parts, (r.ff_got_a, r.ff_got_b, r.ff_got_z), r.ff_sum_in)
        attn_chain = Chain(r, r.attn_sum_v, (r.attn_got_a, r.attn_got_b, r.attn_got_z))
        summed, small = [], []

        def loading():
            for quarter in quarters:
                chain.start_a(quarter)
            attn_chain.start_a(pieces[pairs], r.out_grad_in)
            summed.append(r.local(lambda: r.ff_sum_in.at[pl.ds(8, 8)], r.ff_parts))

        def after_pair(pair):
            if pair == 0:
                summed[0].wait()
            chain.start_b(quarters[pair])
            if pair >= 1:
                chain.start_c(quarters[pair - 1])
            if pair >= 2:
                chain.start_d(quarters[pair - 2])

        def before_norm():
            chain.start_b(quarters[3])
            chain.start_d(quarters[1])

        r.mixed_v, r.proj_v, r.grad_heads_v, r.heads_v = r.w_down_v, r.positive_v, r.ff_in_v, r.low
        loads = []

        def attention_done():
            loads.append(r.local(lambda: r.w_down.at[layer - 1], r.w_down_v))
            loads.append(r.local(r.positive, r.positive_v))
            loads.append(r.local(r.ff_in, r.ff_in_v))

        def first(*scope):
            vars(r).update(zip(own, scope))
            project_back(
                r, layer, seqs, rows, r.norms[layer, 0], attn_chain, after_pair, loading, attention_done,
                before_norm, partial_first=True,
            )
            small.append(r.local(r.norm_rows, r.norm_one))
            small.append(r.local(r.taps_wide, r.taps_done))

        pl.run_scoped(first, *own.values())

        def second(*scope):
            vars(r).update(zip(later, scope))
            r.ff_sum_v = r.ff_send
            r.down_done_v = r.total.at[pl.ds(0, done["down_done"].shape[0])]
            r.out_done_v = r.total.at[pl.ds(done["down_done"].shape[0], shard_rows)]
            r.heads_all = r.w_down_v.at[pl.ds(0, seqs * 2 * rows), pl.ds(0, half)]
            loads.append(r.local(r.w_up.at[layer - 1], r.w_up_v))
            loads.append(r.local(r.middle, r.middle_v))
            alls = []
            chain.start_c(quarters[2])
            chain.start_c(quarters[3])
            order = (pieces[pairs], *pieces[:pairs])
            early = []

            def needed(count):
                wait_all(loads[:count])
                del loads[:count]

            def after_first():
                chain.start_d(quarters[2])
                chain.start_d(quarters[3])
                for piece in order:
                    attn_chain.start_b(piece)

            def before_products():
                r.w_out_v = r.w_up_v.at[:, pl.ds(0, width)]
                alls.append(r.local(r.w_out.at[layer - 1], r.w_out_v))
                alls.extend(load_rows(r, r.heads, r.heads_all))
                for piece in order:
                    attn_chain.start_c(piece)

            def after_ups():
                first = pl.ds(0, r.ups_got.shape[1])
                early.append(r.send(r.ff_sum_v.at[pl.ds(0, 8), first], r.ups_got, (0,)))
                for piece in order:
                    attn_chain.start_d(piece)

            sent, ends = feed_back(
                r, layer - 1, seqs, rows, r.norms[layer - 1, 1],
                (needed, after_first, before_products, after_ups),
            )
            wait_all(alls)
            ends += heads_back(r, sent, seqs, rows)
            set_out(r, attn_chain.end_d(pieces[pairs]), r.out_done_v)
            for pair in range(pairs):
                set_qkv(r, attn_chain.end_d(pieces[pair]), pair, r.qkv_done_v)
            ends += [r.local(r.out_done_v, r.out_done), r.local(r.qkv_done_v, r.qkv_done)]
            value = jnp.concatenate([chain.end_d(quarter) for quarter in quarters], 0)
            set_ff(r, value, r.up_done_v, r.down_done_v)
            ends += [r.local(r.up_done_v, r.up_done), r.local(r.down_done_v, r.down_done)]
            wait_all(ends + early + small)

        pl.run_scoped(second, *later.values())
        chain.close()
        attn_chain.close()

    attn_all = pieces[-1].stop
    done = done_shapes(width, ff, groups)
    outputs.update(
        norm_one=jax.ShapeDtypeStruct((8, width), f32),
        taps_done=jax.ShapeDtypeStruct((8, 3 * width), f32),
        ups_got=jax.ShapeDtypeStruct((8, all_ff.stop // 4, half), bf16),
        **done,
    )
    ff_got_a, ff_got_b, ff_got_z = chain_shapes(all_ff.stop, half)
    attn_got_a, attn_got_b, attn_got_z = chain_shapes(attn_all, half)
    for name in ("up_done", "qkv_done"):
        scratch[name + "_v"] = pltpu.VMEM(done[name].shape, f32)
    scratch.update(
        shared,
        ff_parts=pltpu.VMEM((8, all_ff.stop, half), bf16),
        ff_got_a=ff_got_a,
        ff_got_b=ff_got_b,
        ff_got_z=ff_got_z,
        attn_sum_v=pltpu.VMEM((groups, attn_all, half), bf16),
        attn_got_a=attn_got_a,
        attn_got_b=attn_got_b,
        attn_got_z=attn_got_z,
        partners=((), (0,), (1,), (2,), (3,)),
    )
    return stage(
        "back_link", body,
        dict(
            **{name: array for name, array in saved.items() if name != "logs"}, grad_heads_in=grad_heads, grad_middle_in=grad_middle, out_grad_in=out_grad.reshape(groups, -1, half),
            ff_sum_in=ff_sum, w_qkv=weights_qkv, **lower, **weights,
        ),
        dict(**norms, logs=saved["logs"]),
        outputs, scratch, (90, 52), groups, collective_id,
        2 * seqs * rows * width * (6 * width + 4 * ff + 2 * width), 60_000_000, lengths,
    )


def leave(
    lengths, saved, grad_heads, out_grad, grad_middle, ff_sum, ups_got, norm_two, small_above, weights_qkv, norms,
    ff, groups, collective_id,
):
    below = saved["below"]
    seqs, rows, width = below.shape
    half = width // 2
    pairs = half // LANES
    shard_rows = half // groups
    bf16, f32 = jnp.bfloat16, jnp.float32
    ff_rows = ff_sum.shape[1]
    quarters = ff_quarters(ff_rows)
    pieces = attn_rows(shard_rows, pairs)
    out_piece, small_piece = pieces[pairs], pieces[pairs + 1]
    done = done_shapes(width, ff, groups)

    def body(r):
        chain = Chain(r, r.ff_parts, (r.ff_got_a, r.ff_got_b, r.ff_got_z), r.ff_sum_in)
        attn_chain = Chain(r, r.attn_sum_v, (r.attn_got_a, r.attn_got_b, r.attn_got_z))
        summed = []

        def loading():
            for quarter in quarters[1:]:
                chain.start_a(quarter)
            attn_chain.start_a(out_piece, r.out_grad_in)
            summed.append(r.local(lambda: r.ff_sum_in.at[pl.ds(8, 8)], r.ff_parts))
            summed.append(r.local(r.ups_got, lambda: r.ff_got_a.at[:, pl.ds(0, quarters[0].stop)]))

        def after_pair(pair):
            chain.start_b(quarters[pair + 1])
            chain.start_c(quarters[pair])
            if pair >= 1:
                chain.start_d(quarters[pair - 1])
            if pair == pairs - 1:
                attn_chain.start_b(out_piece)

        def before_first():
            wait_all(summed)
            chain.start_b(quarters[0])

        def before_norm():
            attn_chain.start_b(pieces[0])

        outs = []
        project_back(
            r, 0, seqs, rows, r.norms[0, 0], attn_chain, after_pair, loading, before_norm=before_norm,
            before_first=before_first,
        )
        r.taps_rows[0:8] = r.taps_wide[...]
        r.taps_rows[8:16] = r.taps_above[...]
        r.norms_rows[...] = jnp.zeros_like(r.norms_rows)
        for at, (one, two) in enumerate(((r.norm_rows, r.norm_two), (r.norm_one_above, r.norm_two_above))):
            r.norms_rows[8 * at + 3 : 8 * at + 5] = one[3:5]
            r.norms_rows[8 * at + 5 : 8 * at + 7] = two[0:2]
        r.small_all[...] = jnp.zeros_like(r.small_all)
        for shard in range(2 * groups):
            taps_at, norms_at = 3 * shard_rows * shard, shard_rows * shard
            r.small_all[shard, :, 0 : 3 * shard_rows] = r.taps_rows[:, taps_at : taps_at + 3 * shard_rows]
            r.small_all[shard, :, LANES : LANES + shard_rows] = r.norms_rows[
                :, norms_at : norms_at + shard_rows
            ]
        for shard in range(groups):
            for owner, target in ((1 - r.core, r.small_send), (r.core, r.small_keep)):
                target[place_of(r, shard, owner)] = r.small_all[owner * groups + shard].astype(bf16)
        swap = r.send(r.small_send, r.small_got)
        r.result_v[...] = r.grad_v[...].astype(bf16)
        outs.append(r.local(r.result_v, r.result))
        chain.start_d(quarters[2])
        attn_chain.start_b(pieces[1])
        chain.start_c(quarters[3])
        attn_chain.start_c(out_piece)
        attn_chain.start_c(pieces[0])
        swap.wait()
        r.attn_sum_v[:, small_piece] = (
            r.small_keep[...].astype(f32) + r.small_got[...].astype(f32)
        ).astype(bf16)
        attn_chain.start_a(small_piece)
        for pair in range(2, pairs):
            attn_chain.start_b(pieces[pair])
        chain.start_d(quarters[3])
        attn_chain.start_d(out_piece)
        attn_chain.start_c(pieces[1])
        attn_chain.start_b(small_piece)
        attn_chain.start_d(pieces[0])
        for pair in range(2, pairs):
            attn_chain.start_c(pieces[pair])
        attn_chain.start_d(pieces[1])
        attn_chain.start_c(small_piece)
        set_out(r, attn_chain.end_d(out_piece), r.out_done_v)
        outs.append(r.local(r.out_done_v, r.out_done))
        for pair in range(2, pairs):
            attn_chain.start_d(pieces[pair])
        attn_chain.start_d(small_piece)
        set_ff(
            r, jnp.concatenate([chain.end_d(rows_of_ff) for rows_of_ff in quarters], 0),
            r.up_done_v, r.down_done_v,
        )
        outs += [r.local(r.up_done_v, r.up_done), r.local(r.down_done_v, r.down_done)]
        for pair in range(pairs):
            set_qkv(r, attn_chain.end_d(pieces[pair]), pair, r.qkv_done_v)
        outs.append(r.local(r.qkv_done_v, r.qkv_done))
        r.small_done_v[...] = attn_chain.end_d(small_piece)
        outs.append(r.local(r.small_done_v, r.small_done))
        wait_all(outs)
        chain.close()
        attn_chain.close()

    attn_all = small_piece.stop
    done["small_done"] = jax.ShapeDtypeStruct((16, half), f32)
    outputs = dict(result=jax.ShapeDtypeStruct(below.shape, bf16), **done)
    ff_got_a, ff_got_b, ff_got_z = chain_shapes(ff_rows, half)
    attn_got_a, attn_got_b, attn_got_z = chain_shapes(attn_all, half)
    piece = pltpu.VMEM((groups, 16, half), bf16)
    own, shared, operands = project_back_shapes(seqs, rows, width, below, groups)
    scratch = dict(
        **own,
        **shared,
        **operands,
        result_v=pltpu.VMEM((seqs, rows, width), bf16),
        taps_rows=pltpu.VMEM((16, 3 * width), f32),
        norms_rows=pltpu.VMEM((16, width), f32),
        small_all=pltpu.VMEM((2 * groups, 16, half), f32),
        small_send=piece, small_keep=piece, small_got=piece,
        ff_parts=pltpu.VMEM((8, ff_rows, half), bf16),
        ff_got_a=ff_got_a, ff_got_b=ff_got_b, ff_got_z=ff_got_z,
        **{name + "_v": pltpu.VMEM(shape.shape, f32) for name, shape in done.items()},
        attn_sum_v=pltpu.VMEM((groups, attn_all, half), bf16),
        attn_got_a=attn_got_a, attn_got_b=attn_got_b, attn_got_z=attn_got_z,
        partners=((), (0,), (1,), (2,), (3,)),
    )
    return stage(
        "leave", body,
        dict(
            **{name: array for name, array in saved.items() if name != "logs"}, grad_heads_in=grad_heads, grad_middle_in=grad_middle, out_grad_in=out_grad.reshape(groups, -1, half),
            ff_sum_in=ff_sum, ups_got=ups_got, w_qkv=weights_qkv,
        ),
        dict(
            **norms, logs=saved["logs"], norm_two=norm_two, **small_above,
        ),
        outputs, scratch, (70, 60), groups, collective_id,
        8 * seqs * rows * width * 3 * half, 40_000_000, lengths,
    )


def gather(whole, pairs, small, shard_rows):
    f32 = jnp.float32
    flat = list(whole) + [array for pair in pairs for array in pair]

    def kernel(*refs):
        ins, small_ref, refs = refs[: len(flat)], refs[len(flat)], refs[len(flat) + 1 :]
        outs, rooms = refs[: len(whole) + len(pairs) + 3], refs[len(whole) + len(pairs) + 3 : -2]
        targets = list(outs[: len(whole)])
        for out in outs[len(whole) : -3]:
            targets += [out.at[layer] for layer in range(LAYERS)]
        copies = []
        for at, room in enumerate(rooms):
            copies.append(pltpu.make_async_copy(ins[at], room, refs[-2].at[at]))
            copies[-1].start()
        taps_ref, gains_ref, biases_ref = outs[-3:]
        for layer in range(LAYERS):
            for lag in range(3):
                row = 8 * layer + lag
                taps_ref[lag, layer : layer + 1] = small_ref[row : row + 1, : 3 * shard_rows]
            for which in range(2):
                for out, row in ((gains_ref, 8 * layer + 3), (biases_ref, 8 * layer + 4)):
                    row += 2 * which
                    out[layer, which : which + 1] = small_ref[row : row + 1, LANES : LANES + shard_rows]
        for at, room in enumerate(rooms):
            copies[at].wait()
            copies[at] = pltpu.make_async_copy(room, targets[at], refs[-1].at[at])
            copies[at].start()
        for copy in copies:
            copy.wait()

    anywhere = pl.BlockSpec(memory_space=pl.ANY)
    vmem = pl.BlockSpec(memory_space=pltpu.VMEM)
    shapes = [jax.ShapeDtypeStruct(array.shape, array.dtype) for array in whole]
    shapes += [jax.ShapeDtypeStruct((LAYERS, *pair[0].shape), f32) for pair in pairs]
    shapes += [
        jax.ShapeDtypeStruct(shape, f32)
        for shape in ((3, LAYERS, 3 * shard_rows), (LAYERS, 2, shard_rows), (LAYERS, 2, shard_rows))
    ]
    return pl.pallas_call(
        kernel,
        in_specs=[anywhere] * len(flat) + [vmem],
        out_specs=[anywhere] * (len(shapes) - 3) + [vmem] * 3,
        out_shape=shapes,
        scratch_shapes=[pltpu.VMEM(array.shape, array.dtype) for array in flat]
        + [pltpu.SemaphoreType.DMA((len(flat),))] * 2,
        compiler_params=pltpu.CompilerParams(vmem_limit_bytes=VMEM_LIMIT),
        name="gather",
    )(*flat, small)


def local_pair(
    activations,
    cotangent,
    lengths,
    weights_qkv,
    conv_taps,
    weights_out,
    weights_up,
    weights_down,
    norm_gains,
    norm_biases,
):
    seqs, rows, width = activations.shape
    ff = weights_up.shape[2]
    groups = lax.axis_size("batch")
    norms = dict(
        all_taps=conv_taps.transpose(2, 0, 1),
        gains=norm_gains.transpose(0, 2, 1),
        biases=norm_biases.transpose(0, 2, 1),
    )
    weights = dict(w_out=weights_out, w_up=weights_up, w_down=weights_down)

    def saved(mixed, proj, attn, heads, logs, below):
        return dict(mixed=mixed, proj=proj, attn=attn, heads_in=heads, logs=logs, below=below)

    mixed0, proj0, attn0, mixed1, proj1, attn1, heads0, logs0, middle0, ff_in0, positive0, stream1 = feed_forward(
        lengths, activations, dict(**weights, w_qkv=weights_qkv), norms, groups, 1
    )
    ff_sum1, grad_middle1, norm_two1, grad_heads1, out_grad1, heads1, logs1, block_out = turn(
        1, lengths, mixed1, stream1, cotangent, weights, norms, groups, 2
    )
    lower = dict(positive=positive0, middle=middle0, ff_in=ff_in0, heads=heads0)
    ff_sum0, grad_middle0, norm_two0, grad_heads0, out_grad0, norm_one1, taps1, ups_got, qkv1, out1, up1, down1 = (
        back_link(
            1, lengths, saved(mixed1, proj1, attn1, heads1, logs1, stream1), grad_heads1, out_grad1,
            grad_middle1, ff_sum1, lower, weights_qkv, weights, norms, groups, 3,
        )
    )
    above = dict(norm_one_above=norm_one1, norm_two_above=norm_two1, taps_above=taps1)
    grad_input, qkv0, out0, up0, down0, small = leave(
        lengths, saved(mixed0, proj0, attn0, heads0, logs0, activations), grad_heads0, out_grad0, grad_middle0,
        ff_sum0, ups_got, norm_two0, above, weights_qkv, norms, ff, groups, 4,
    )
    block_out, grad_input, qkv, out, up, down, grad_taps, grad_gains, grad_biases = gather(
        (block_out, grad_input), ((qkv0, qkv1), (out0, out1), (up0, up1), (down0, down1)), small, up0.shape[0]
    )
    return (
        block_out,
        grad_input,
        qkv,
        grad_taps.transpose(1, 2, 0),
        out,
        up,
        down,
        grad_gains.transpose(0, 2, 1),
        grad_biases.transpose(0, 2, 1),
    )


def solution(mesh):
    chosen = local_pair if (mesh.shape["seq"], mesh.shape["batch"]) == (2, 16) else local
    placed = (
        P("batch", "seq", None),
        P("batch", "seq", None),
        P("batch"),
        P(),
        P(),
        P(),
        P(),
        P(),
        P(),
        P(),
    )
    return jax.shard_map(
        chosen,
        mesh=mesh,
        in_specs=placed,
        out_specs=(
            P("batch", "seq", None),
            P("batch", "seq", None),
            P(None, ("seq", "batch"), None),
            P(None, ("seq", "batch"), None),
            P(None, ("seq", "batch"), None),
            P(None, ("seq", "batch"), None),
            P(None, ("seq", "batch"), None),
            P(None, ("seq", "batch"), None),
            P(None, ("seq", "batch"), None),
        ),
        check_vma=False,
    )
```

```python
import functools
import types

import jax
import jax.numpy as jnp
from jax import lax
from jax.experimental import pallas as pl
from jax.experimental.pallas import tpu as pltpu
from jax.sharding import PartitionSpec as P

HEAD_DIM = 64
LAYERS = 2


def shifted(x, axis, by):
    size = lax.axis_size(axis)
    pairs = [(i, i + by) for i in range(size) if 0 <= i + by < size]
    return lax.ppermute(x, axis, pairs)


def normalize(stream):
    average = jnp.mean(stream, -1, keepdims=True)
    centered = stream - average
    scaling = lax.rsqrt(jnp.mean(centered * centered, -1, keepdims=True) + 1e-05)
    return (centered * scaling, scaling)


def norm_back(grad_norm, normed, scaling, gain):
    scaled = grad_norm * gain
    return scaling * (
        scaled
        - jnp.mean(scaled, -1, keepdims=True)
        - normed * jnp.mean(scaled * normed, -1, keepdims=True)
    )


def split_heads(block):
    return block.reshape(block.shape[0], -1, HEAD_DIM)


def masked_scores(query_seq, key_seq, length, positions):
    scores = jnp.einsum(
        "qhd,khd->hqk",
        split_heads(query_seq),
        split_heads(key_seq),
        preferred_element_type=jnp.float32,
    ) * HEAD_DIM ** (-0.5)
    key_place = jnp.arange(key_seq.shape[0], dtype=jnp.int32)
    allowed = (key_place[None, :] < length) & (
        (key_place[None, :] <= positions[:, None]) | (positions[:, None] >= length)
    )
    return jnp.where(allowed[None], scores, -1e30)


def attention_forward(queries, keys_all, values_all, lengths, positions):

    def one_sequence(items):
        query_seq, key_seq, value_seq, length = items
        scores = masked_scores(query_seq, key_seq, length, positions)
        highest = jnp.max(scores, -1, keepdims=True)
        expo = jnp.exp(scores - highest)
        totals = jnp.sum(expo, -1, keepdims=True)
        probs = (expo / totals).astype(jnp.bfloat16)
        mixed = jnp.einsum(
            "hqk,khd->qhd", probs, split_heads(value_seq), preferred_element_type=jnp.float32
        )
        log_total = (highest + jnp.log(totals))[..., 0]
        return (mixed.reshape(query_seq.shape).astype(jnp.bfloat16), log_total)

    return lax.map(one_sequence, (queries, keys_all, values_all, lengths))


def attention_backward(
    queries, keys_all, values_all, lengths, positions, log_totals, grad_attended
):

    def one_sequence(items):
        query_seq, key_seq, value_seq, length, log_total, grad_seq = items
        scores = masked_scores(query_seq, key_seq, length, positions)
        probs = jnp.exp(scores - log_total[..., None])
        grad_heads = split_heads(grad_seq)
        grad_probs = jnp.einsum(
            "qhd,khd->hqk", grad_heads, split_heads(value_seq), preferred_element_type=jnp.float32
        )
        inner = jnp.sum(probs * grad_probs, -1, keepdims=True)
        grad_scores = (probs * (grad_probs - inner)).astype(jnp.bfloat16)
        grad_query = jnp.einsum(
            "hqk,khd->qhd", grad_scores, split_heads(key_seq), preferred_element_type=jnp.float32
        ) * HEAD_DIM ** (-0.5)
        grad_key = jnp.einsum(
            "hqk,qhd->khd", grad_scores, split_heads(query_seq), preferred_element_type=jnp.float32
        ) * HEAD_DIM ** (-0.5)
        grad_value = jnp.einsum(
            "hqk,qhd->khd",
            probs.astype(jnp.bfloat16),
            grad_heads,
            preferred_element_type=jnp.float32,
        )
        return (
            grad_query.reshape(query_seq.shape),
            grad_key.reshape(key_seq.shape),
            grad_value.reshape(key_seq.shape),
        )

    return lax.map(
        one_sequence, (queries, keys_all, values_all, lengths, log_totals, grad_attended)
    )


def layer_forward(stream, lengths, positions, w_qkv, taps, w_out, w_up, w_down, gains, offsets):
    seqs_here, rows, width = stream.shape
    tokens = seqs_here * rows
    normed_one, scale_one = normalize(stream)
    attn_in = (normed_one * gains[:, 0] + offsets[:, 0]).astype(jnp.bfloat16)
    projected = jnp.dot(
        attn_in.reshape(tokens, width), w_qkv, preferred_element_type=jnp.float32
    ).reshape(seqs_here, rows, 3 * width)
    before = shifted(projected[:, rows - 2 :, :].astype(jnp.bfloat16), "seq", 1).astype(jnp.float32)
    extended = jnp.concatenate([before, projected], 1)
    conv_out = (
        taps[:, 0] * extended[:, 2:]
        + taps[:, 1] * extended[:, 1 : rows + 1]
        + taps[:, 2] * extended[:, :rows]
    )
    mixed_qkv = conv_out.astype(jnp.bfloat16)
    queries = mixed_qkv[..., :width]
    keys_here = mixed_qkv[..., width : 2 * width]
    values_here = mixed_qkv[..., 2 * width :]
    keys_all, values_all = (
        lax.all_gather(keys_here, "seq", axis=1, tiled=True),
        lax.all_gather(values_here, "seq", axis=1, tiled=True),
    )
    attended, log_totals = attention_forward(queries, keys_all, values_all, lengths, positions)
    branch = jnp.dot(attended.reshape(tokens, width), w_out, preferred_element_type=jnp.float32)
    middle = stream + branch.reshape(stream.shape)
    normed_two, scale_two = normalize(middle)
    ff_in = (normed_two * gains[:, 1] + offsets[:, 1]).astype(jnp.bfloat16).reshape(tokens, width)
    hidden_pre = jnp.dot(ff_in, w_up, preferred_element_type=jnp.float32)
    hidden = (jax.nn.relu(hidden_pre) ** 2).astype(jnp.bfloat16)
    result = middle + jnp.dot(hidden, w_down, preferred_element_type=jnp.float32).reshape(
        stream.shape
    )
    kept_keys = (keys_all, values_all)
    saved = (
        normed_one,
        scale_one,
        attn_in,
        extended,
        queries,
        kept_keys,
        attended,
        log_totals,
        normed_two,
        scale_two,
        ff_in,
        hidden_pre,
        hidden,
    )
    return (result, saved)


def layer_backward(grad_stream, lengths, positions, saved, w_qkv, taps, w_out, w_up, w_down, gains):
    (
        normed_one,
        scale_one,
        attn_in,
        extended,
        queries,
        kept_keys,
        attended,
        log_totals,
        normed_two,
        scale_two,
        ff_in,
        hidden_pre,
        hidden,
    ) = saved
    seqs_here, rows, width = grad_stream.shape
    tokens = seqs_here * rows
    grad_down_in = grad_stream.reshape(tokens, width).astype(jnp.bfloat16)
    grad_down = jnp.einsum("tf,td->fd", hidden, grad_down_in, preferred_element_type=jnp.float32)
    grad_hidden = jnp.dot(grad_down_in, w_down.T, preferred_element_type=jnp.float32)
    grad_pre = (grad_hidden * 2.0 * jax.nn.relu(hidden_pre)).astype(jnp.bfloat16)
    grad_up = jnp.einsum("td,tf->df", ff_in, grad_pre, preferred_element_type=jnp.float32)
    grad_ffin = jnp.dot(grad_pre, w_up.T, preferred_element_type=jnp.float32).reshape(
        grad_stream.shape
    )
    gain_two = jnp.sum(grad_ffin * normed_two, (0, 1))
    offset_two = jnp.sum(grad_ffin, (0, 1))
    grad_middle = grad_stream + norm_back(grad_ffin, normed_two, scale_two, gains[:, 1])
    grad_branch = grad_middle.reshape(tokens, width).astype(jnp.bfloat16)
    grad_out = jnp.einsum(
        "td,te->de",
        attended.reshape(tokens, width),
        grad_branch,
        preferred_element_type=jnp.float32,
    )
    grad_attended = jnp.dot(grad_branch, w_out.T, preferred_element_type=jnp.float32)
    grad_attended = grad_attended.astype(jnp.bfloat16).reshape(grad_stream.shape)
    keys_all, values_all = kept_keys
    grad_query, grad_key_all, grad_value_all = attention_backward(
        queries, keys_all, values_all, lengths, positions, log_totals, grad_attended
    )
    grad_key, grad_value = (
        lax.psum_scatter(
            grad_key_all.astype(jnp.bfloat16), "seq", scatter_dimension=1, tiled=True
        ).astype(jnp.float32),
        lax.psum_scatter(
            grad_value_all.astype(jnp.bfloat16), "seq", scatter_dimension=1, tiled=True
        ).astype(jnp.float32),
    )
    grad_conv = jnp.concatenate([grad_query, grad_key, grad_value], -1)
    after = shifted(grad_conv[:, :2, :].astype(jnp.bfloat16), "seq", -1).astype(jnp.float32)
    grad_ext = jnp.concatenate([grad_conv, after], 1)
    grad_proj = (
        taps[:, 0] * grad_ext[:, :rows]
        + taps[:, 1] * grad_ext[:, 1 : rows + 1]
        + taps[:, 2] * grad_ext[:, 2:]
    )
    grad_taps = jnp.stack(
        [
            jnp.sum(grad_conv * extended[:, 2:], (0, 1)),
            jnp.sum(grad_conv * extended[:, 1 : rows + 1], (0, 1)),
            jnp.sum(grad_conv * extended[:, :rows], (0, 1)),
        ],
        -1,
    )
    grad_proj_low = grad_proj.reshape(tokens, 3 * width).astype(jnp.bfloat16)
    grad_qkv = jnp.einsum(
        "td,tf->df",
        attn_in.reshape(tokens, width),
        grad_proj_low,
        preferred_element_type=jnp.float32,
    )
    grad_attn_in = jnp.dot(grad_proj_low, w_qkv.T, preferred_element_type=jnp.float32).reshape(
        grad_stream.shape
    )
    gain_one = jnp.sum(grad_attn_in * normed_one, (0, 1))
    offset_one = jnp.sum(grad_attn_in, (0, 1))
    grad_input = grad_middle + norm_back(grad_attn_in, normed_one, scale_one, gains[:, 0])
    grad_gains = jnp.stack([gain_one, gain_two], -1)
    grad_biases = jnp.stack([offset_one, offset_two], -1)
    return (
        grad_input,
        (grad_qkv, grad_taps, grad_out, grad_up, grad_down, grad_gains, grad_biases),
    )


def reduce_grads(grad_qkv, grad_taps, grad_out, grad_up, grad_down, grad_gains, grad_biases):
    part_qkv, part_taps, part_out, part_up, part_down, part_gains, part_biases = (
        lax.psum_scatter(
            grad_qkv.astype(jnp.bfloat16), "seq", scatter_dimension=0, tiled=True
        ).astype(jnp.float32),
        lax.psum_scatter(
            grad_taps.astype(jnp.bfloat16), "seq", scatter_dimension=0, tiled=True
        ).astype(jnp.float32),
        lax.psum_scatter(
            grad_out.astype(jnp.bfloat16), "seq", scatter_dimension=0, tiled=True
        ).astype(jnp.float32),
        lax.psum_scatter(
            grad_up.astype(jnp.bfloat16), "seq", scatter_dimension=0, tiled=True
        ).astype(jnp.float32),
        lax.psum_scatter(
            grad_down.astype(jnp.bfloat16), "seq", scatter_dimension=0, tiled=True
        ).astype(jnp.float32),
        lax.psum_scatter(
            grad_gains.astype(jnp.bfloat16), "seq", scatter_dimension=0, tiled=True
        ).astype(jnp.float32),
        lax.psum_scatter(
            grad_biases.astype(jnp.bfloat16), "seq", scatter_dimension=0, tiled=True
        ).astype(jnp.float32),
    )
    return (
        lax.psum_scatter(
            part_qkv.astype(jnp.bfloat16), "batch", scatter_dimension=0, tiled=True
        ).astype(jnp.float32),
        lax.psum_scatter(
            part_taps.astype(jnp.bfloat16), "batch", scatter_dimension=0, tiled=True
        ).astype(jnp.float32),
        lax.psum_scatter(
            part_out.astype(jnp.bfloat16), "batch", scatter_dimension=0, tiled=True
        ).astype(jnp.float32),
        lax.psum_scatter(
            part_up.astype(jnp.bfloat16), "batch", scatter_dimension=0, tiled=True
        ).astype(jnp.float32),
        lax.psum_scatter(
            part_down.astype(jnp.bfloat16), "batch", scatter_dimension=0, tiled=True
        ).astype(jnp.float32),
        lax.psum_scatter(
            part_gains.astype(jnp.bfloat16), "batch", scatter_dimension=0, tiled=True
        ).astype(jnp.float32),
        lax.psum_scatter(
            part_biases.astype(jnp.bfloat16), "batch", scatter_dimension=0, tiled=True
        ).astype(jnp.float32),
    )


def local(
    activations,
    cotangent,
    lengths,
    weights_qkv,
    conv_taps,
    weights_out,
    weights_up,
    weights_down,
    norm_gains,
    norm_biases,
):
    seqs_here, rows, width = activations.shape
    positions = lax.axis_index("seq") * rows + jnp.arange(rows, dtype=jnp.int32)
    stream = activations.astype(jnp.float32)
    saved_all = []
    for layer_num in range(LAYERS):
        stream, saved = layer_forward(
            stream,
            lengths,
            positions,
            weights_qkv[layer_num],
            conv_taps[layer_num],
            weights_out[layer_num],
            weights_up[layer_num],
            weights_down[layer_num],
            norm_gains[layer_num],
            norm_biases[layer_num],
        )
        saved_all.append(saved)
    block_out = stream.astype(jnp.bfloat16)
    grad_stream = cotangent.astype(jnp.float32)
    collected = []
    for layer_num in reversed(range(LAYERS)):
        grad_stream, layer_grads = layer_backward(
            grad_stream,
            lengths,
            positions,
            saved_all[layer_num],
            weights_qkv[layer_num],
            conv_taps[layer_num],
            weights_out[layer_num],
            weights_up[layer_num],
            weights_down[layer_num],
            norm_gains[layer_num],
        )
        grad_qkv, grad_taps, grad_out, grad_up, grad_down, grad_gains, grad_biases = layer_grads
        collected.append(
            reduce_grads(grad_qkv, grad_taps, grad_out, grad_up, grad_down, grad_gains, grad_biases)
        )
    collected = collected[::-1]
    stacked = [jnp.stack([member[index] for member in collected], 0) for index in range(7)]
    return (
        block_out,
        grad_stream.astype(jnp.bfloat16),
        stacked[0],
        stacked[1],
        stacked[2],
        stacked[3],
        stacked[4],
        stacked[5],
        stacked[6],
    )


TILE = 256
LANES = 128
VMEM_LIMIT = 60 * 2**20


def dot_nt(left, right):
    return lax.dot_general(
        left, right, (((1,), (1,)), ((), ())), preferred_element_type=jnp.float32
    )


def dot_nn(left, right):
    return lax.dot_general(
        left, right, (((1,), (0,)), ((), ())), preferred_element_type=jnp.float32
    )


def dot_tn(left, right):
    return lax.dot_general(
        left, right, (((0,), (0,)), ((), ())), preferred_element_type=jnp.float32
    )


def head_lanes(head):
    lane = lax.broadcasted_iota(jnp.int32, (1, LANES), 1)
    return (lane >= head * HEAD_DIM) & (lane < (head + 1) * HEAD_DIM)


def causal_tile():
    keys = lax.broadcasted_iota(jnp.int32, (TILE, TILE), 0)
    queries = lax.broadcasted_iota(jnp.int32, (TILE, TILE), 1)
    return keys <= queries


def attend_heads(whole, conv_ref, out_ref, log_ref):
    cap = conv_ref.shape[0]
    hidden = jnp.where(whole, 0.0, -1e30)
    queries = conv_ref[:, :LANES]
    keys = conv_ref[:, LANES : 2 * LANES] * jnp.bfloat16(HEAD_DIM**-0.5)
    keys = [jnp.where(head_lanes(head), keys, jnp.bfloat16(0)) for head in range(2)]
    values_t = conv_ref[:, 2 * LANES :].T
    ones = jnp.ones((16, cap), jnp.bfloat16)
    values = [
        jnp.concatenate([values_t[head * HEAD_DIM : (head + 1) * HEAD_DIM], ones], 0) for head in range(2)
    ]

    def scores_of(block, head):
        rows = slice(block * TILE, (block + 1) * TILE)
        parts = []
        for start in range(0, (block + 1) * TILE, TILE):
            part = dot_nt(keys[head][start : start + TILE], queries[rows])
            if start == block * TILE:
                part = jnp.where(causal_tile(), part, -1e30)
            if start >= cap // 2:
                part = part + hidden
            parts.append(part)
        return parts

    def weights_of(parts):
        highest = functools.reduce(jnp.maximum, [jnp.max(part, 0, keepdims=True) for part in parts])
        return highest, [jnp.exp(part - highest).astype(jnp.bfloat16) for part in parts]

    def finish(block, head, highest, expo):
        got = sum(
            dot_nn(values[head][:, at * TILE : (at + 1) * TILE], part) for at, part in enumerate(expo)
        )
        total = got[HEAD_DIM : HEAD_DIM + 1]
        log_ref[head : head + 1, block * TILE : (block + 1) * TILE] = highest + jnp.log(total)
        return got[:HEAD_DIM] / total

    items = [(block, head) for block in range(cap // TILE) for head in range(2)]
    ahead = scores_of(*items[0])
    waiting = None
    mixed = []

    def close(item):
        mixed.append(finish(*item))
        if len(mixed) == 2:
            rows = slice(item[0] * TILE, (item[0] + 1) * TILE)
            out_ref[rows, :] = jnp.concatenate(mixed, 0).T.astype(jnp.bfloat16)
            mixed.clear()

    for at, item in enumerate(items):
        parts = ahead
        if at + 1 < len(items):
            ahead = scores_of(*items[at + 1])
        if waiting is not None:
            close(waiting)
        waiting = (*item, *weights_of(parts))
    close(waiting)


def attend_back_heads(
    whole, conv_ref, proj_ref, grad_ref, out_ref, log_ref, taps_ref, back_ref, grad_taps_ref, query_t_acc, shift_acc
):
    cap = conv_ref.shape[0]
    factor = jnp.bfloat16(HEAD_DIM**-0.5)
    queries = conv_ref[:, :LANES] * factor
    grads = grad_ref[...]
    keys = [
        jnp.where(head_lanes(head), conv_ref[:, LANES : 2 * LANES], jnp.bfloat16(0)) for head in range(2)
    ]
    values = [
        jnp.where(head_lanes(head), conv_ref[:, 2 * LANES :], jnp.bfloat16(0)) for head in range(2)
    ]
    keys_t = (conv_ref[:, LANES : 2 * LANES] * factor).T
    queries_t = queries.T
    grads_t = grads.T
    product_t = (grads.astype(jnp.float32) * out_ref[...].astype(jnp.float32)).T
    inner = [
        jnp.sum(product_t[head * HEAD_DIM : (head + 1) * HEAD_DIM], 0, keepdims=True)
        for head in range(2)
    ]
    logs = [log_ref[head : head + 1, :] for head in range(2)]
    blocks = cap // TILE

    def products(item):
        head, key, query = item
        rows, cols = slice(key * TILE, (key + 1) * TILE), slice(query * TILE, (query + 1) * TILE)
        return dot_nt(keys[head][rows], queries[cols]), dot_nt(values[head][rows], grads[cols])

    def weights_of(item, raw):
        head, key, query = item
        cols = slice(query * TILE, (query + 1) * TILE)
        log = logs[head][:, cols]
        if key * TILE >= cap // 2:
            log = jnp.where(whole, log, 1e30)
        probs = jnp.exp(raw[0] - log)
        if key == query:
            probs = jnp.where(causal_tile(), probs, 0.0)
        scores = probs * (raw[1] - inner[head][:, cols])
        return probs.astype(jnp.bfloat16), scores.astype(jnp.bfloat16)

    query_t_acc[...] = jnp.zeros_like(query_t_acc)
    grad_value = {}
    grad_key = {}
    grad_query = {}

    def add(store, at, term):
        store[at] = term if at not in store else store[at] + term

    def finish(item, probs, scores):
        head, key, query = item
        lanes = slice(head * HEAD_DIM, (head + 1) * HEAD_DIM)
        rows, cols = slice(key * TILE, (key + 1) * TILE), slice(query * TILE, (query + 1) * TILE)
        add(grad_value, (head, key), dot_nt(grads_t[lanes, cols], probs))
        add(grad_key, (head, key), dot_nt(queries_t[lanes, cols], scores))
        query_t_acc[lanes, cols] += dot_nn(keys_t[lanes, rows], scores)

    items = [(head, key, query) for key in range(blocks) for head in range(2) for query in range(key, blocks)]
    ahead = products(items[0])
    waiting = None
    for at, item in enumerate(items):
        raw = ahead
        if at + 1 < len(items):
            ahead = products(items[at + 1])
        if waiting is not None:
            finish(*waiting)
        waiting = (item, *weights_of(item, raw))
    finish(*waiting)
    for key in range(blocks):
        rows = slice(key * TILE, (key + 1) * TILE)
        shift_acc[1, rows, :] = jnp.concatenate([grad_key[0, key], grad_key[1, key]], 0).T
        shift_acc[2, rows, :] = jnp.concatenate([grad_value[0, key], grad_value[1, key]], 0).T
    shift_acc[0, :cap, :] = query_t_acc[...].T
    shift_acc[:, pl.ds(cap, 8), :] = jnp.zeros((3, 8, LANES), jnp.float32)
    for kind in range(3):
        lanes = slice(kind * LANES, (kind + 1) * LANES)
        proj = proj_ref[:, lanes].astype(jnp.float32)
        total = 0.0
        for lag in range(3):
            moved = shift_acc[kind, lag : lag + cap, :]
            total = total + taps_ref[lag : lag + 1, lanes] * moved
            grad_taps_ref[lag : lag + 1, lanes] = jnp.sum(moved * proj, 0, keepdims=True)
        back_ref[:, lanes] = total.astype(jnp.bfloat16)


def normal(x):
    average = jnp.mean(x, -1, keepdims=True)
    centered = x - average
    scaling = lax.rsqrt(jnp.mean(centered * centered, -1, keepdims=True) + 1e-05)
    return centered * scaling, scaling


def blocks_of(rows, size=512):
    return [slice(at, at + size) for at in range(0, rows, size)]


def greet(partners):
    barrier = pltpu.get_barrier_semaphore()
    for device in partners:
        pl.semaphore_signal(barrier, inc=1, device_id=device, device_id_type=pl.DeviceIdType.MESH)


def remote(source, target, sends, receives, device):
    return pltpu.make_async_remote_copy(
        src_ref=source,
        dst_ref=target,
        send_sem=sends,
        recv_sem=receives,
        device_id=device,
        device_id_type=pl.DeviceIdType.MESH,
    )


def full_spec(shape):
    return pl.BlockSpec(shape, lambda *_: (0,) * len(shape))


def stage(
    name, body, inputs, small, outputs, scratch, copies, groups, collective_id, flops, moved, lengths=None
):
    partners = scratch.pop("partners")
    scalars = {} if lengths is None else dict(lengths=lengths)
    width = small["gains"].shape[2]
    scratch["norms"] = pltpu.VMEM((LAYERS, 2, 2, width), jnp.float32)
    scratch["taps"] = pltpu.VMEM((LAYERS, 3, 3 * width // 2), jnp.float32)
    names = [*scalars, *inputs, *small, *outputs, *scratch]

    def kernel(*refs):
        r = types.SimpleNamespace(**dict(zip(names, refs)))
        local_sems, send_sems, get_sems = refs[len(names) :]
        counts = [0, 0]

        def local(source, target):
            at = counts[0]
            counts[0] += 1
            return Move(lambda: pltpu.make_async_copy(ref(source), ref(target), local_sems.at[at]))

        def send(source, target, flips=()):
            at = counts[1]
            counts[1] += 1

            def make():
                return remote(
                    ref(source), ref(target), send_sems.at[at], get_sems.at[at], r.devices[flips]
                )

            return Move(make)

        r.local, r.send, r.groups = local, send, groups
        r.core = lax.axis_index("seq")
        group = lax.axis_index("batch")
        r.bits = [group // 2**bit % 2 for bit in range(4)]
        moves = [(1 - 2 * value) * 2**bit for bit, value in enumerate(r.bits)]
        first = (1 - r.core) * moves[0] + r.core * moves[1]
        steps = [first, moves[0] + moves[1] - first, moves[2], moves[3]]
        r.devices = {(at,): dict(seq=r.core, batch=group + step) for at, step in enumerate(steps)}
        r.devices[()] = dict(seq=1 - r.core, batch=group)
        greet([r.devices[flips] for flips in partners])
        r.meet = lambda: pl.semaphore_wait(pltpu.get_barrier_semaphore(), len(partners))
        for layer in range(LAYERS):
            for which in range(2):
                r.norms[layer, which, 0:1] = r.gains[layer, which : which + 1]
                r.norms[layer, which, 1:2] = r.biases[layer, which : which + 1]
            for block in range(3 * width // 2 // LANES):
                pair, kind = block // 3, block % 3
                at = pl.multiple_of(kind * width + r.core * (width // 2) + pair * LANES, LANES)
                for lag in range(3):
                    row = r.all_taps[lag, layer : layer + 1, pl.ds(at, LANES)]
                    r.taps[layer, lag : lag + 1, block * LANES : (block + 1) * LANES] = row
        body(r)
        assert counts[0] <= copies[0] and counts[1] <= copies[1], counts

    anywhere = pl.BlockSpec(memory_space=pl.ANY)
    return pl.pallas_call(
        kernel,
        in_specs=[pl.BlockSpec(memory_space=pltpu.SMEM)] * len(scalars)
        + [anywhere] * len(inputs)
        + [pl.BlockSpec(memory_space=pltpu.VMEM)] * len(small),
        out_specs=[anywhere] * len(outputs),
        out_shape=list(outputs.values()),
        scratch_shapes=list(scratch.values())
        + [pltpu.SemaphoreType.DMA((count,)) for count in (copies[0], copies[1], copies[1])],
        compiler_params=pltpu.CompilerParams(
            vmem_limit_bytes=VMEM_LIMIT + 3 * 2**20, collective_id=collective_id, has_side_effects=True
        ),
        cost_estimate=pl.CostEstimate(
            flops=int(flops), bytes_accessed=int(moved), transcendentals=0
        ),
        name=name,
    )(*scalars.values(), *inputs.values(), *small.values())


NORM_ROWS = 64


def rows_of(r, seq, block=None):
    rows = r.result.shape[1] if hasattr(r, "result") else r.grad_middle.shape[1]
    block = block or slice(0, rows)
    return slice(seq * rows + block.start, seq * rows + block.stop)


def ref(given):
    return given() if callable(given) else given


class Move:
    def __init__(self, make):
        self.make = make
        make().start()

    def wait(self):
        self.make().wait()

    def wait_recv(self):
        self.make().wait_recv()

    def wait_send(self):
        self.make().wait_send()


def ahead(makers):
    later = None
    for make in makers:
        now, later = later, make()
        if now is not None:
            yield now
    yield later


def span(index, size):
    return pl.ds(pl.multiple_of(index * size, size), size)


def wait_all(copies):
    for copy in copies:
        copy.wait()


def wait_sent(copies):
    for copy in copies:
        copy.wait_send()


def load_head_weight(r, layer):
    width, wide = r.w_qkv_v.shape
    copies = []
    for pair in range(wide // (3 * LANES)):
        for kind in range(3):
            at = pl.multiple_of(kind * width + r.core * (width // 2) + pair * LANES, LANES)
            copies.append(
                r.local(
                    r.w_qkv.at[layer, :, pl.ds(at, LANES)],
                    r.w_qkv_v.at[:, pl.ds((3 * pair + kind) * LANES, LANES)],
                )
            )
    return copies


def scaled(normed, norms):
    return (normed * norms[0:1] + norms[1:2]).astype(jnp.bfloat16)


def norm_rows(r, stream, seq, norms):
    rows = stream.shape[1]
    for block in blocks_of(rows, NORM_ROWS):
        normed, _ = normal(stream[seq, block].astype(jnp.float32))
        at = pl.multiple_of(r.core * rows + block.start, NORM_ROWS)
        r.attn_v[seq, pl.ds(at, NORM_ROWS)] = scaled(normed, norms)


def project(r, layer, seq, targets):
    cap = r.attn_v.shape[1]
    taps = r.taps[layer]
    r.longer[0:8] = jnp.zeros((8, r.longer.shape[1]), jnp.float32)
    blocks = blocks_of(cap, TILE)
    products = ahead(
        [functools.partial(lambda block: dot_nn(r.attn_v[seq, block], r.w_qkv_v[...]), b) for b in blocks]
    )
    for block, here in zip(blocks, products):
        at = 8 + block.start
        r.longer[at : at + TILE, :] = here
        r.proj_v[seq, block] = here.astype(jnp.bfloat16)
        r.mixed_v[seq, block] = (
            taps[0:1] * here
            + taps[1:2] * r.longer[at - 1 : at - 1 + TILE, :]
            + taps[2:3] * r.longer[at - 2 : at - 2 + TILE, :]
        ).astype(jnp.bfloat16)
    sources = (r.mixed_v, r.proj_v, r.attn_v)
    return [r.local(source.at[seq], target.at[seq]) for source, target in zip(sources, targets)]


def project_shapes(seqs, rows, width):
    bf16, f32 = jnp.bfloat16, jnp.float32
    wide = 3 * width // 2
    outputs = {}
    for layer in range(LAYERS):
        for name, columns in (("mixed", wide), ("proj", wide), ("attn", width)):
            outputs[name + str(layer)] = jax.ShapeDtypeStruct((seqs, 2 * rows, columns), bf16)
    scratch = dict(
        w_qkv_v=pltpu.VMEM((width, wide), bf16),
        attn_v=pltpu.VMEM((seqs, 2 * rows, width), bf16),
        longer=pltpu.VMEM((2 * rows + 8, wide), f32),
        proj_v=pltpu.VMEM((seqs, 2 * rows, wide), bf16),
        mixed_v=pltpu.VMEM((seqs, 2 * rows, wide), bf16),
    )
    return outputs, scratch


def load_rows(r, source, target):
    seqs, rows, _ = source.shape
    return [
        r.local(source.at[seq], target.at[pl.ds(seq * rows, rows)]) for seq in range(seqs)
    ]


def share_rows(r, buffer, seq, rows):
    here = span(r.core, rows)
    return r.send(buffer.at[seq, here], buffer.at[seq, here])


def attention(r, seqs, rows, before_send=None):
    half = r.heads_all.shape[1]
    cap = 2 * rows
    mine, theirs = span(r.core, rows), span(1 - r.core, rows)
    loads, sends, outs = [], [], []
    pairs = half // LANES
    if not before_send:
        for pair in range(pairs):
            columns = pl.ds(pair * 3 * LANES, 3 * LANES)
            loads.append(r.local(r.mixed_in.at[:, :, columns], r.mixed_v.at[:, :, columns]))
        r.meet()
    yield
    for pair in range(pairs):
        columns = slice(pair * 3 * LANES, (pair + 1) * 3 * LANES)
        lanes = slice(pair * LANES, (pair + 1) * LANES)
        if loads:
            loads[pair].wait()

        def one(seq, none):
            attend_heads(
                r.lengths[seq] == cap,
                r.mixed_v.at[seq, :, columns],
                r.heads_all.at[pl.ds(pl.multiple_of(seq * cap, cap), cap), lanes],
                r.logs_v.at[seq, pair],
            )

        lax.fori_loop(0, seqs, one, None)
        if pair == 0 and before_send:
            before_send()
        for seq in range(seqs):
            to = pl.ds(pl.multiple_of(r.core * half + pair * LANES, LANES), LANES)
            here = pl.ds(seq * rows, rows)
            own, other = (span(2 * seq + owner, rows) for owner in (r.core, 1 - r.core))
            sends.append(r.send(r.heads_all.at[other, pl.ds(pair * LANES, LANES)], r.heads_v.at[here, to]))
            r.heads_v[here, to] = r.heads_all[own, lanes]
    for seq in range(seqs):
        outs.append(r.local(r.heads_all.at[pl.ds(seq * cap, cap)], r.heads.at[seq]))
    outs.append(r.local(r.logs_v, r.logs))
    for copy in sends:
        copy.wait()
    yield outs


def attention_shapes(seqs, rows, width):
    half = width // 2
    pairs = half // LANES
    bf16, f32 = jnp.bfloat16, jnp.float32
    outputs = dict(
        heads=jax.ShapeDtypeStruct((seqs, 2 * rows, half), bf16),
        logs=jax.ShapeDtypeStruct((seqs, pairs, 2, 2 * rows), f32),
    )
    scratch = dict(
        mixed_v=pltpu.VMEM((seqs, 2 * rows, 3 * half), bf16),
        heads_all=pltpu.VMEM((seqs * 2 * rows, half), bf16),
        logs_v=pltpu.VMEM((seqs, pairs, 2, 2 * rows), f32),
        heads_v=pltpu.VMEM((seqs * rows, width), bf16),
    )
    return outputs, scratch


def out_project(r, layer, seq, norms):
    r.middle_v[seq] += dot_nn(r.heads_v[rows_of(r, seq)], r.w_out_v[...])
    for block in blocks_of(r.middle_v.shape[1], NORM_ROWS):
        normed, _ = normal(r.middle_v[seq, block])
        r.ff_in_v[rows_of(r, seq, block)] = scaled(normed, norms)


def feed(r, seq, hidden, result):
    ff = r.w_up_v.shape[1]
    here = rows_of(r, seq)
    chunks = blocks_of(ff, 768)
    products = ahead(
        [functools.partial(lambda lanes: dot_nn(r.ff_in_v[here], r.w_up_v[:, lanes]), c) for c in chunks]
    )
    for lanes, value in zip(chunks, products):
        positive = jnp.maximum(value, 0.0)
        r.positive_v[here, lanes] = positive.astype(jnp.bfloat16)
        hidden[:, lanes] = (positive * positive).astype(jnp.bfloat16)
    for lanes in blocks_of(r.middle_v.shape[2], TILE):
        value = r.middle_v[seq, :, lanes] + dot_nn(hidden[...], r.w_down_v[:, lanes])
        result[seq, :, lanes] = value.astype(result.dtype)


def load_feed_weights(r, layer):
    return [
        r.local(r.w_out.at[layer], r.w_out_v),
        r.local(r.w_up.at[layer], r.w_up_v),
        r.local(r.w_down.at[layer], r.w_down_v),
    ]


def feed_shapes(seqs, rows, width, ff):
    bf16, f32 = jnp.bfloat16, jnp.float32
    return dict(
        w_out_v=pltpu.VMEM((width, width), bf16),
        w_up_v=pltpu.VMEM((width, ff), bf16),
        w_down_v=pltpu.VMEM((ff, width), bf16),
        middle_v=pltpu.VMEM((seqs, rows, width), f32),
        ff_in_v=pltpu.VMEM((seqs * rows, width), bf16),
        positive_v=pltpu.VMEM((seqs * rows, ff), bf16),
    )


def feed_forward(lengths, stream, weights, norms, groups, collective_id):
    layer = 0
    seqs, rows, width = stream.shape
    ff = weights["w_up"].shape[2]
    tokens = (seqs, rows, width)
    bf16, f32 = jnp.bfloat16, jnp.float32
    outputs, scratch = project_shapes(seqs, rows, width)

    def body(r):
        streams = [r.local(r.stream.at[seq], r.stream_v.at[seq]) for seq in range(seqs)]
        heads_weight = load_head_weight(r, 0)
        r.meet()
        shared, early = [], []
        for seq in range(seqs):
            streams[seq].wait()
            norm_rows(r, r.stream_v, seq, r.norms[0, 0])
            shared.append(share_rows(r, r.attn_v, seq, rows))
        feeds = load_feed_weights(r, layer)
        wait_all(heads_weight)
        for seq in range(seqs):
            shared[seq].wait()
            early += project(r, 0, seq, (r.mixed0, r.proj0, r.attn0))
        feeds += load_head_weight(r, 1)
        heads = attention(r, seqs, rows, lambda: wait_all(early))
        next(heads)
        outs = next(heads)
        wait_all(feeds)
        shared = []
        for seq in range(seqs):
            r.middle_v[seq] = r.stream_v[seq].astype(f32)
            out_project(r, layer, seq, r.norms[layer, 1])
            outs.append(r.local(r.middle_v.at[seq], r.middle.at[seq]))
            here = pl.ds(seq * rows, rows)
            outs.append(r.local(r.ff_in_v.at[here], r.ff_in.at[here]))
            feed(r, seq, r.hidden_v, r.result_v)
            outs.append(r.local(r.positive_v.at[here], r.positive.at[here]))
            outs.append(r.local(r.result_v.at[seq], r.result.at[seq]))
            norm_rows(r, r.result_v, seq, r.norms[layer + 1, 0])
            shared.append(share_rows(r, r.attn_v, seq, rows))
        for seq in range(seqs):
            shared[seq].wait_recv()
            outs += project(r, layer + 1, seq, (r.mixed1, r.proj1, r.attn1))
        wait_sent(shared)
        wait_all(outs)

    more, room = attention_shapes(seqs, rows, width)
    outputs.update(
        more,
        middle=jax.ShapeDtypeStruct(tokens, f32),
        ff_in=jax.ShapeDtypeStruct((seqs * rows, width), bf16),
        positive=jax.ShapeDtypeStruct((seqs * rows, ff), bf16),
        result=jax.ShapeDtypeStruct(tokens, f32),
    )
    scratch.update(room)
    scratch.update(feed_shapes(seqs, rows, width, ff))
    scratch.update(
        stream_v=pltpu.VMEM(tokens, stream.dtype),
        hidden_v=pltpu.VMEM((rows, ff), bf16),
        result_v=pltpu.VMEM(tokens, f32),
        partners=((),),
    )
    return stage(
        "feed_forward", body, dict(stream=stream, **weights), norms,
        outputs, scratch, (60, 12), groups, collective_id,
        2 * seqs * rows * width * (9 * width + 2 * ff), 60_000_000, lengths,
    )


def place_of(r, shard, owner):
    same = [r.bits[bit] if shard // 2**bit % 2 else 1 - r.bits[bit] for bit in range(2)]
    line = shard // 4
    return 4 * ((2 - owner) * same[0] + (1 + owner) * same[1]) + 2 * (line % 2) + line // 2


def feed_back(r, layer, seqs, rows, norms, hooks=None):
    groups, core = r.groups, r.core
    width, ff = r.w_up_v.shape
    half = width // 2
    shard_rows = half // groups
    f32, bf16 = jnp.float32, jnp.bfloat16
    chunk = 768
    hooks = hooks or (lambda *_: None,) * 4
    needed, after_first, before_products, after_ups = hooks
    gain_sum = offset_sum = 0.0
    shared, outs = [], []
    for seq in range(seqs):
        if seq == 1:
            after_first()
        here = rows_of(r, seq)
        r.low[here] = r.grad_v[seq].astype(bf16)
        if seq == 0:
            needed(2)
        chunks = blocks_of(ff, chunk)
        backs = ahead(
            [functools.partial(lambda lanes: dot_nt(r.low[here], r.w_down_v[lanes]), c) for c in chunks]
        )
        for lanes, back in zip(chunks, backs):
            r.pre[here, lanes] = (back * (2.0 * r.positive_v[here, lanes].astype(f32))).astype(bf16)
        if seq == 0:
            needed(3)
        for lanes in blocks_of(width, TILE):
            r.total[:, lanes] = dot_nt(r.pre[here], r.w_up_v[lanes])
        for block in blocks_of(rows, NORM_ROWS):
            grad_in = r.total[block]
            normed, scaling = normal(r.middle_v[seq, block])
            gain_sum += jnp.sum(grad_in * normed, 0, keepdims=True)
            offset_sum += jnp.sum(grad_in, 0, keepdims=True)
            value = r.grad_v[seq, block].astype(f32) + norm_back(grad_in, normed, scaling, norms[0:1])
            r.middle_v[seq, block] = value
            at = pl.multiple_of((2 * seq + core) * rows + block.start, NORM_ROWS)
            r.branch[pl.ds(at, NORM_ROWS)] = value.astype(bf16)
        at = span(2 * seq + core, rows)
        shared.append(r.send(r.branch.at[at], r.branch.at[at]))
        outs.append(r.local(r.middle_v.at[seq], r.grad_middle.at[seq]))
    r.norm_grad_v[0:1] = gain_sum
    r.norm_grad_v[1:2] = offset_sum
    outs.append(r.local(r.norm_grad_v, r.norm_grad))
    before_products()

    up_rows, down_rows = 2 * shard_rows, ff // 2 // groups
    down_start = up_rows * (ff // chunk)

    def up_product(owner, lanes):
        return dot_tn(r.ff_in_v[:, span(owner, half)], r.pre[:, lanes])

    def down_product(owner, lanes):
        at = pl.multiple_of(owner * (ff // 2) + lanes.start, chunk)
        positive = r.positive_v[:, pl.ds(at, chunk)].astype(f32)
        return dot_tn((positive * positive).astype(bf16), r.low[...])

    def products(owner):
        ups, downs = blocks_of(ff, chunk), blocks_of(ff // 2, chunk)
        makers = [functools.partial(up_product, owner, lanes) for lanes in ups]
        makers += [functools.partial(down_product, owner, lanes) for lanes in downs]
        for at, value in enumerate(ahead(makers)):
            size = shard_rows if at < len(ups) else down_rows
            first = 0 if at < len(ups) else (at - len(ups)) * (chunk // down_rows)
            row = at * up_rows if at < len(ups) else down_start
            yield [
                (first + count, row, halves(value[count * size : (count + 1) * size]))
                for count in range(value.shape[0] // size)
            ]

    places = [[place_of(r, shard, owner) for shard in range(groups)] for owner in (1 - core, core)]
    sends = []
    for at, pieces in enumerate(products(1 - core)):
        for shard, row, piece in pieces:
            r.ff_send[places[0][shard], row : row + piece.shape[0]] = piece.astype(bf16)
        if at == ff // chunk - 1:
            where = (slice(None), pl.ds(0, down_start))
            sends.append(r.send(r.ff_send.at[where], r.ff_got.at[where]))
    where = (slice(None), pl.ds(down_start, 2 * down_rows))
    sends.append(r.send(r.ff_send.at[where], r.ff_got.at[where]))
    for at, pieces in enumerate(products(core)):
        if at == 0:
            sends[0].wait()
        if at == ff // chunk:
            sends[1].wait()
        for shard, row, piece in pieces:
            place = places[1][shard]
            rows_of_piece = slice(row, row + piece.shape[0])
            r.ff_sum_v[place, rows_of_piece] = (
                piece + r.ff_got[place, rows_of_piece].astype(f32)
            ).astype(bf16)
        if at == ff // chunk // 2 - 1:
            after_ups()
        if at == ff // chunk - 1:
            where = (slice(None), pl.ds(0, down_start))
            outs.append(r.local(r.ff_sum_v.at[where], r.ff_sum.at[where]))
    where = (slice(None), pl.ds(down_start, 2 * down_rows))
    outs.append(r.local(r.ff_sum_v.at[where], r.ff_sum.at[where]))
    return shared, outs


def halves(value):
    half = value.shape[1] // 2
    return jnp.concatenate([value[:, :half], value[:, half:]], 0)


def heads_back(r, shared, seqs, rows):
    groups, core = r.groups, r.core
    half = r.grad_heads.shape[2]
    shard_rows = half // groups
    out_grad = r.low.at[pl.ds(0, 2 * half), pl.ds(0, half)]
    outs = []
    for copy in shared:
        copy.wait_recv()
    places = [place_of(r, shard, core) for shard in range(groups)]
    total = dot_tn(r.heads_all[...], r.branch[...])
    for shard, place in enumerate(places):
        piece = halves(total[shard * shard_rows : (shard + 1) * shard_rows])
        out_grad[span(place, 2 * shard_rows)] = piece.astype(jnp.bfloat16)
    for seq in range(seqs):
        here = slice(seq * 2 * rows, (seq + 1) * 2 * rows)
        grad = dot_nt(r.branch[here], r.w_out_v[span(core, half)])
        r.heads_all[here] = grad.astype(jnp.bfloat16)
        where = pl.ds(here.start, 2 * rows)
        outs.append(r.local(r.heads_all.at[where], r.grad_heads.at[seq]))
    outs.append(r.local(out_grad, r.out_grad))
    wait_sent(shared)
    return outs


def back_shapes(seqs, rows, width, ff, groups):
    bf16, f32 = jnp.bfloat16, jnp.float32
    half = width // 2
    shard_rows = half // groups
    tokens = (seqs, rows, width)
    outputs = dict(
        ff_sum=jax.ShapeDtypeStruct((groups, 4 * ff // groups // 2, half), bf16),
        grad_middle=jax.ShapeDtypeStruct(tokens, f32),
        norm_grad=jax.ShapeDtypeStruct((8, width), f32),
        grad_heads=jax.ShapeDtypeStruct((seqs, 2 * rows, half), bf16),
        out_grad=jax.ShapeDtypeStruct((groups * 2 * shard_rows, half), bf16),
    )
    scratch = dict(
        low=pltpu.VMEM((seqs * rows, width), bf16),
        pre=pltpu.VMEM((seqs * rows, ff), bf16),
        branch=pltpu.VMEM((seqs * 2 * rows, width), bf16),
        norm_grad_v=pltpu.VMEM((8, width), f32),
        ff_send=pltpu.VMEM((groups, 4 * ff // groups // 2, half), bf16),
        ff_got=pltpu.VMEM((groups, 4 * ff // groups // 2, half), bf16),
        heads_all=pltpu.VMEM((seqs * 2 * rows, half), bf16),
    )
    return outputs, scratch


def turn(layer, lengths, mixed, stream, cotangent, weights, norms, groups, collective_id):
    seqs, rows, width = stream.shape
    ff = weights["w_up"].shape[2]
    tokens = (seqs, rows, width)
    bf16, f32 = jnp.bfloat16, jnp.float32
    outputs, scratch = back_shapes(seqs, rows, width, ff, groups)

    def body(r):
        r.low, r.ff_sum_v = r.heads_v, r.ff_send
        heads = attention(r, seqs, rows)
        next(heads)
        loads = [r.local(r.stream, r.middle_v), *load_feed_weights(r, layer), r.local(r.grad, r.grad_v)]
        outs = next(heads)
        wait_all(loads)
        for seq in range(seqs):
            out_project(r, layer, seq, r.norms[layer, 1])
            feed(r, seq, r.pre.at[rows_of(r, seq)], r.result_v)
            outs.append(r.local(r.result_v.at[seq], r.result.at[seq]))
        wait_all(outs[:seqs])
        shared, more = feed_back(r, layer, seqs, rows, r.norms[layer, 1])
        wait_all(outs[seqs:] + more + heads_back(r, shared, seqs, rows))

    more, room = attention_shapes(seqs, rows, width)
    del scratch["low"]
    outputs.update(more, result=jax.ShapeDtypeStruct(tokens, bf16))
    scratch.update(room)
    scratch.update(feed_shapes(seqs, rows, width, ff))
    scratch.update(
        total=pltpu.VMEM((rows, width), f32),
        result_v=pltpu.VMEM(tokens, bf16),
        grad_v=pltpu.VMEM(tokens, cotangent.dtype),
        partners=((),),
    )
    return stage(
        "turn", body, dict(mixed_in=mixed, stream=stream, grad=cotangent, **weights), norms,
        outputs, scratch, (40, 16), groups, collective_id,
        2 * seqs * rows * width * (3 * width + 6 * ff + 2 * width), 60_000_000, lengths,
    )


class Chain:
    def __init__(self, r, shards, got, source=None):
        self.r, self.shards, self.first = r, shards, 8 if source is not None else 0
        self.source = shards if source is None else source
        self.got_a, self.got_b, self.got_z = got
        self.sends = {}

    def part(self, ref, start, count, rows):
        return ref.at[pl.ds(start, count), pl.ds(rows.start, rows.stop - rows.start)]

    def add(self, start, got, rows):
        f32 = jnp.float32
        for at in range(got.shape[0]):
            to = start - self.first + at
            self.shards[to, rows] = (
                self.shards[to, rows].astype(f32) + got[at, rows].astype(f32)
            ).astype(jnp.bfloat16)

    def start_a(self, rows, alone=None):
        source = self.part(self.source, 0, 8, rows) if alone is None else alone.at[pl.ds(0, 8)]
        self.sends["a", rows.start] = self.r.send(source, self.part(self.got_a, 0, 8, rows), (0,))

    def start_b(self, rows):
        if ("a", rows.start) in self.sends:
            self.sends["a", rows.start].wait_recv()
        self.add(8, self.got_a, rows)
        self.sends["b", rows.start] = self.r.send(
            self.part(self.shards, 8 - self.first, 4, rows), self.part(self.got_b, 0, 4, rows), (1,)
        )

    def end_b(self, rows):
        self.sends["b", rows.start].wait_recv()
        self.add(12, self.got_b, rows)

    def start_c(self, rows):
        self.end_b(rows)
        self.sends["c", rows.start] = self.r.send(
            lambda: self.part(self.shards, 12 - self.first + 2 * (1 - self.r.bits[2]), 2, rows),
            self.part(self.got_z, 0, 2, rows),
            (2,),
        )

    def start_d(self, rows):
        self.sends["c", rows.start].wait_recv()
        low, high = self.r.bits[2:]
        to = 12 - self.first + 2 * low
        for at in range(2):
            self.shards[to + at, rows] = (
                self.shards[to + at, rows].astype(jnp.float32) + self.got_z[at, rows].astype(jnp.float32)
            ).astype(jnp.bfloat16)
        self.sends["d", rows.start] = self.r.send(
            lambda: self.part(
                self.shards, 12 - self.first + 2 * self.r.bits[2] + 1 - self.r.bits[3], 1, rows
            ),
            self.part(self.got_z, 2, 1, rows),
            (3,),
        )

    def end_d(self, rows):
        low, high = self.r.bits[2:]
        mine = 12 - self.first + 2 * low + high
        self.sends["d", rows.start].wait_recv()
        return self.shards[mine, rows].astype(jnp.float32) + self.got_z[2, rows].astype(jnp.float32)

    def close(self):
        wait_sent(self.sends.values())


def done_shapes(width, ff, groups):
    rows = width // 2 // groups
    return {
        name: jax.ShapeDtypeStruct(shape, jnp.float32)
        for name, shape in (
            ("qkv_done", (rows, 3 * width)),
            ("out_done", (rows, width)),
            ("up_done", (rows, ff)),
            ("down_done", (ff // 2 // groups, width)),
        )
    }


def attn_rows(shard_rows, pairs):
    size = 2 * shard_rows
    starts = [size * at for at in range(pairs + 2)]
    return [slice(start, start + size) for start in starts[:-1]] + [slice(starts[-1], starts[-1] + 16)]


def set_ff(r, total, up, down):
    shard_rows, ff = up.shape
    half = total.shape[1]
    for at in range(ff // half):
        up[:, at * half : (at + 1) * half] = total[at * shard_rows : (at + 1) * shard_rows]
    start = (ff // half) * shard_rows
    down_rows = down.shape[0]
    for at in range(2):
        first = start + at * down_rows
        down[:, at * half : (at + 1) * half] = total[first : first + down_rows]


def set_qkv(r, total, pair, qkv):
    shard_rows, columns = qkv.shape
    width = columns // 3
    for at, owner in enumerate((r.core, 1 - r.core)):
        for kind in range(3):
            to = pl.multiple_of(kind * width + owner * (width // 2) + pair * LANES, LANES)
            qkv[:, pl.ds(to, LANES)] = total[
                at * shard_rows : (at + 1) * shard_rows, kind * LANES : (kind + 1) * LANES
            ]


def set_out(r, total, out):
    shard_rows, width = out.shape
    out[:, : width // 2] = total[:shard_rows]
    out[:, width // 2 :] = total[shard_rows : 2 * shard_rows]


def chain_shapes(rows, columns):
    bf16 = jnp.bfloat16
    return [pltpu.VMEM((count, rows, columns), bf16) for count in (8, 4, 3)]


def attend_back_pair(r, layer, pair):
    columns = slice(pair * 3 * LANES, (pair + 1) * 3 * LANES)
    half = r.grad_heads_v.shape[1] // 2

    def one(seq):
        cap = r.proj_v.shape[0]
        at = pl.ds(pl.multiple_of(seq * 3 * LANES, LANES), 3 * LANES)
        to = pl.ds(pl.multiple_of(seq * half + pair * LANES, LANES), LANES)
        attend_back_heads(
            r.lengths[seq] == cap,
            r.mixed_v.at[pl.ds(pair * cap, cap), at],
            r.proj_v.at[:, pl.ds(pl.multiple_of((2 * pair + seq) * 3 * LANES, LANES), 3 * LANES)],
            r.grad_heads_v.at[:, to],
            r.heads_v.at[:, to],
            r.logs.at[seq, pair],
            r.taps.at[layer, :, columns],
            r.grad_proj.at[pl.ds(pl.multiple_of(seq * cap, cap), cap), columns],
            r.grad_taps.at[seq, :, columns],
            r.query_t_acc,
            r.shift_acc,
        )

    return one


def project_back(
    r, layer, seqs, rows, norms, attn, after_pair, loading, attention_done=lambda: None,
    before_norm=lambda: None, before_first=lambda: None, partial_first=False,
):
    groups, core = r.groups, r.core
    width, wide = r.w_qkv_v.shape
    half = width // 2
    pairs = half // LANES
    shard_rows = half // groups
    pieces = attn_rows(shard_rows, pairs)
    f32, bf16 = jnp.float32, jnp.bfloat16

    def part(seq, owner):
        return span(2 * seq + owner, rows)

    cap = 2 * rows
    first = []
    for pair in range(pairs):
        columns = pl.ds(pair * 3 * LANES, 3 * LANES)
        lanes = pl.ds(pair * LANES, LANES)
        copies = []
        for seq in range(seqs):
            to = pl.ds(seq * half + pair * LANES, LANES)
            copies += [
                r.local(
                    r.mixed.at[seq, :, columns],
                    r.mixed_v.at[pl.ds(pair * cap, cap), pl.ds(seq * 3 * LANES, 3 * LANES)],
                ),
                r.local(r.grad_heads_in.at[seq, :, lanes], r.grad_heads_v.at[:, to]),
                r.local(r.heads_in.at[seq, :, lanes], r.heads_v.at[:, to]),
                r.local(
                    r.proj.at[seq, :, columns],
                    r.proj_v.at[:, pl.ds((2 * pair + seq) * 3 * LANES, 3 * LANES)],
                ),
            ]
        first.append(copies)
    out_loaded = r.local(r.out_grad_in, attn.shards.at[:, pl.ds(pieces[pairs].start, 2 * shard_rows)])
    r.meet()
    loading()
    inputs_in = load_rows(r, r.attn, r.inputs)
    weights = load_head_weight(r, layer)
    loads = [r.local(r.below, r.below_v), r.local(r.grad_middle_in, r.grad_v)]
    places = [[place_of(r, shard, owner) for shard in range(groups)] for owner in (1 - core, core)]
    swaps, shared = {}, []

    def send_partial():
        for seq in range(seqs):
            here = slice(seq * rows, (seq + 1) * rows)
            value = dot_nt(r.grad_proj[part(seq, 1 - core)], r.w_qkv_v[...])
            r.heads_v[here] = value.astype(bf16)
            shared.append(r.send(r.heads_v.at[pl.ds(seq * rows, rows)], r.partial_got.at[seq]))

    def merge_pair(pair):
        swaps[pair].wait()
        for place in range(groups):
            piece = jnp.concatenate(
                [r.qkv_keep[pair % 2, place], r.qkv_got[pair, place, :shard_rows].astype(f32)], 0
            )
            attn.shards[place, pieces[pair]] = piece.astype(bf16)
        attn.start_a(pieces[pair])

    for pair in range(pairs):
        wait_all(first[pair])
        if pair == 0:
            before_first()
        one = attend_back_pair(r, layer, pair)
        lax.fori_loop(0, seqs, lambda seq, none: one(seq), None)
        if pair == pairs - 1:
            attention_done()
            wait_all(weights)
            if partial_first:
                send_partial()
        if pair == 0:
            wait_all([out_loaded, *inputs_in])
        else:
            merge_pair(pair - 1)
        columns = slice(pair * 3 * LANES, (pair + 1) * 3 * LANES)
        for at, owner in enumerate((1 - core, core)):
            value = dot_tn(r.inputs[:, span(owner, half)], r.grad_proj[:, columns])
            for shard in range(groups):
                piece = value[shard * shard_rows : (shard + 1) * shard_rows]
                if at == 0:
                    piece = jnp.concatenate([piece, jnp.zeros((32 - shard_rows, half), f32)], 0)
                    r.qkv_send[pair, places[0][shard]] = piece.astype(bf16)
                else:
                    r.qkv_keep[pair % 2, places[1][shard]] = piece
            if at == 0:
                swaps[pair] = r.send(r.qkv_send.at[pair], r.qkv_got.at[pair])
        after_pair(pair)
    if not partial_first:
        send_partial()
    merge_pair(pairs - 1)
    before_norm()
    wait_all(loads)
    gain_sum = offset_sum = 0.0
    for seq in range(seqs):
        r.total[...] = dot_nt(r.grad_proj[part(seq, core)], r.w_qkv_v[...])
        shared[seq].wait_recv()
        for block in blocks_of(rows, NORM_ROWS):
            here = r.total[block] + r.partial_got[seq, block].astype(f32)
            normed, scaling = normal(r.below_v[seq, block].astype(f32))
            gain_sum += jnp.sum(here * normed, 0, keepdims=True)
            offset_sum += jnp.sum(here, 0, keepdims=True)
            r.grad_v[seq, block] += norm_back(here, normed, scaling, norms[0:1])
    wait_sent(shared)
    r.norm_rows[3:4], r.norm_rows[4:5] = gain_sum, offset_sum
    r.taps_wide[...] = jnp.zeros_like(r.taps_wide)
    for pair in range(pairs):
        for kind in range(3):
            at = slice((3 * pair + kind) * LANES, (3 * pair + kind + 1) * LANES)
            to = pl.multiple_of(kind * width + core * half + pair * LANES, LANES)
            r.taps_wide[0:3, pl.ds(to, LANES)] = sum(r.grad_taps[seq, 0:3, at] for seq in range(seqs))


def project_back_shapes(seqs, rows, width, below, groups):
    f32, bf16 = jnp.float32, jnp.bfloat16
    cap, wide, half = 2 * rows, 3 * width // 2, width // 2
    pairs = half // LANES
    shard_rows = half // groups
    own = dict(
        grad_proj=pltpu.VMEM((seqs * cap, wide), bf16),
        grad_taps=pltpu.VMEM((seqs, 8, wide), f32),
        query_t_acc=pltpu.VMEM((LANES, cap), f32),
        shift_acc=pltpu.VMEM((3, cap + 8, LANES), f32),
        inputs=pltpu.VMEM((seqs * cap, width), bf16),
        w_qkv_v=pltpu.VMEM((width, wide), bf16),
        below_v=pltpu.VMEM((seqs, rows, width), below.dtype),
        qkv_send=pltpu.VMEM((pairs, groups, 32, half), bf16),
        qkv_keep=pltpu.VMEM((2, groups, shard_rows, half), f32),
    )
    shared = dict(
        partial_got=pltpu.VMEM((seqs, rows, width), bf16),
        qkv_got=pltpu.VMEM((pairs, groups, 32, half), bf16),
        total=pltpu.VMEM((rows, width), f32),
        grad_v=pltpu.VMEM((seqs, rows, width), f32),
        norm_rows=pltpu.VMEM((8, width), f32),
        taps_wide=pltpu.VMEM((8, 3 * width), f32),
    )
    operands = dict(
        mixed_v=pltpu.VMEM((pairs * cap, seqs * 3 * LANES), bf16),
        proj_v=pltpu.VMEM((cap, pairs * seqs * 3 * LANES), bf16),
        grad_heads_v=pltpu.VMEM((cap, seqs * half), bf16),
        heads_v=pltpu.VMEM((cap, seqs * half), bf16),
    )
    return own, shared, operands


def ff_quarters(rows):
    return [slice(rows * at // 4, rows * (at + 1) // 4) for at in range(4)]


def back_link(
    layer, lengths, saved, grad_heads, out_grad, grad_middle, ff_sum, lower, weights_qkv, weights, norms,
    groups, collective_id,
):
    below = saved["below"]
    seqs, rows, width = below.shape
    ff = weights["w_up"].shape[2]
    half = width // 2
    pairs = half // LANES
    shard_rows = half // groups
    bf16, f32 = jnp.bfloat16, jnp.float32
    outputs, scratch = back_shapes(seqs, rows, width, ff, groups)
    pieces = attn_rows(shard_rows, pairs)[: pairs + 1]
    all_ff = slice(0, ff_sum.shape[1])
    quarters = ff_quarters(all_ff.stop)
    own, shared, _ = project_back_shapes(seqs, rows, width, below, groups)
    shapes = feed_shapes(seqs, rows, width, ff)
    later = {name: scratch.pop(name) for name in ("pre", "ff_send")}
    del scratch["heads_all"]
    later.update({name: shapes.pop(name) for name in ("w_up_v", "middle_v")})
    del shapes["w_out_v"]
    scratch.update(shapes)

    def body(r):
        chain = Chain(r, r.ff_parts, (r.ff_got_a, r.ff_got_b, r.ff_got_z), r.ff_sum_in)
        attn_chain = Chain(r, r.attn_sum_v, (r.attn_got_a, r.attn_got_b, r.attn_got_z))
        summed, small = [], []

        def loading():
            for quarter in quarters:
                chain.start_a(quarter)
            attn_chain.start_a(pieces[pairs], r.out_grad_in)
            summed.append(r.local(lambda: r.ff_sum_in.at[pl.ds(8, 8)], r.ff_parts))

        def after_pair(pair):
            if pair == 0:
                summed[0].wait()
            chain.start_b(quarters[pair])
            if pair >= 1:
                chain.start_c(quarters[pair - 1])
            if pair >= 2:
                chain.start_d(quarters[pair - 2])

        def before_norm():
            chain.start_b(quarters[3])
            chain.start_d(quarters[1])

        r.mixed_v, r.proj_v, r.grad_heads_v, r.heads_v = r.w_down_v, r.positive_v, r.ff_in_v, r.low
        loads = []

        def attention_done():
            loads.append(r.local(lambda: r.w_down.at[layer - 1], r.w_down_v))
            loads.append(r.local(r.positive, r.positive_v))
            loads.append(r.local(r.ff_in, r.ff_in_v))

        def first(*scope):
            vars(r).update(zip(own, scope))
            project_back(
                r, layer, seqs, rows, r.norms[layer, 0], attn_chain, after_pair, loading, attention_done,
                before_norm, partial_first=True,
            )
            small.append(r.local(r.norm_rows, r.norm_one))
            small.append(r.local(r.taps_wide, r.taps_done))

        pl.run_scoped(first, *own.values())

        def second(*scope):
            vars(r).update(zip(later, scope))
            r.ff_sum_v = r.ff_send
            r.down_done_v = r.total.at[pl.ds(0, done["down_done"].shape[0])]
            r.out_done_v = r.total.at[pl.ds(done["down_done"].shape[0], shard_rows)]
            r.heads_all = r.w_down_v.at[pl.ds(0, seqs * 2 * rows), pl.ds(0, half)]
            loads.append(r.local(r.w_up.at[layer - 1], r.w_up_v))
            loads.append(r.local(r.middle, r.middle_v))
            alls = []
            chain.start_c(quarters[2])
            chain.start_c(quarters[3])
            order = (pieces[pairs], *pieces[:pairs])
            early = []

            def needed(count):
                wait_all(loads[:count])
                del loads[:count]

            def after_first():
                chain.start_d(quarters[2])
                for piece in order:
                    attn_chain.start_b(piece)

            def before_products():
                r.w_out_v = r.w_up_v.at[:, pl.ds(0, width)]
                alls.append(r.local(r.w_out.at[layer - 1], r.w_out_v))
                alls.extend(load_rows(r, r.heads, r.heads_all))
                chain.start_d(quarters[3])
                for piece in order:
                    attn_chain.start_c(piece)

            def after_ups():
                first = pl.ds(0, r.ups_got.shape[1])
                early.append(r.send(r.ff_sum_v.at[pl.ds(0, 8), first], r.ups_got, (0,)))
                for piece in order:
                    attn_chain.start_d(piece)

            sent, ends = feed_back(
                r, layer - 1, seqs, rows, r.norms[layer - 1, 1],
                (needed, after_first, before_products, after_ups),
            )
            wait_all(alls)
            ends += heads_back(r, sent, seqs, rows)
            set_out(r, attn_chain.end_d(pieces[pairs]), r.out_done_v)
            for pair in range(pairs):
                set_qkv(r, attn_chain.end_d(pieces[pair]), pair, r.qkv_done_v)
            ends += [r.local(r.out_done_v, r.out_done), r.local(r.qkv_done_v, r.qkv_done)]
            value = jnp.concatenate([chain.end_d(quarter) for quarter in quarters], 0)
            set_ff(r, value, r.up_done_v, r.down_done_v)
            ends += [r.local(r.up_done_v, r.up_done), r.local(r.down_done_v, r.down_done)]
            wait_all(ends + early + small)

        pl.run_scoped(second, *later.values())
        chain.close()
        attn_chain.close()

    attn_all = pieces[-1].stop
    done = done_shapes(width, ff, groups)
    outputs.update(
        norm_one=jax.ShapeDtypeStruct((8, width), f32),
        taps_done=jax.ShapeDtypeStruct((8, 3 * width), f32),
        ups_got=jax.ShapeDtypeStruct((8, all_ff.stop // 4, half), bf16),
        **done,
    )
    ff_got_a, ff_got_b, ff_got_z = chain_shapes(all_ff.stop, half)
    attn_got_a, attn_got_b, attn_got_z = chain_shapes(attn_all, half)
    for name in ("up_done", "qkv_done"):
        scratch[name + "_v"] = pltpu.VMEM(done[name].shape, f32)
    scratch.update(
        shared,
        ff_parts=pltpu.VMEM((8, all_ff.stop, half), bf16),
        ff_got_a=ff_got_a,
        ff_got_b=ff_got_b,
        ff_got_z=ff_got_z,
        attn_sum_v=pltpu.VMEM((groups, attn_all, half), bf16),
        attn_got_a=attn_got_a,
        attn_got_b=attn_got_b,
        attn_got_z=attn_got_z,
        partners=((), (0,), (1,), (2,), (3,)),
    )
    return stage(
        "back_link", body,
        dict(
            **{name: array for name, array in saved.items() if name != "logs"}, grad_heads_in=grad_heads, grad_middle_in=grad_middle, out_grad_in=out_grad.reshape(groups, -1, half),
            ff_sum_in=ff_sum, w_qkv=weights_qkv, **lower, **weights,
        ),
        dict(**norms, logs=saved["logs"]),
        outputs, scratch, (90, 52), groups, collective_id,
        2 * seqs * rows * width * (6 * width + 4 * ff + 2 * width), 60_000_000, lengths,
    )


def leave(
    lengths, saved, grad_heads, out_grad, grad_middle, ff_sum, ups_got, norm_two, small_above, weights_qkv, norms,
    ff, groups, collective_id,
):
    below = saved["below"]
    seqs, rows, width = below.shape
    half = width // 2
    pairs = half // LANES
    shard_rows = half // groups
    bf16, f32 = jnp.bfloat16, jnp.float32
    ff_rows = ff_sum.shape[1]
    quarters = ff_quarters(ff_rows)
    pieces = attn_rows(shard_rows, pairs)
    out_piece, small_piece = pieces[pairs], pieces[pairs + 1]
    done = done_shapes(width, ff, groups)

    def body(r):
        chain = Chain(r, r.ff_parts, (r.ff_got_a, r.ff_got_b, r.ff_got_z), r.ff_sum_in)
        attn_chain = Chain(r, r.attn_sum_v, (r.attn_got_a, r.attn_got_b, r.attn_got_z))
        summed = []

        def loading():
            for quarter in quarters[1:]:
                chain.start_a(quarter)
            attn_chain.start_a(out_piece, r.out_grad_in)
            summed.append(r.local(lambda: r.ff_sum_in.at[pl.ds(8, 8)], r.ff_parts))
            summed.append(r.local(r.ups_got, lambda: r.ff_got_a.at[:, pl.ds(0, quarters[0].stop)]))

        def after_pair(pair):
            chain.start_b(quarters[pair + 1])
            chain.start_c(quarters[pair])
            if pair >= 1:
                chain.start_d(quarters[pair - 1])
            if pair == pairs - 1:
                attn_chain.start_b(out_piece)

        def before_first():
            wait_all(summed)
            chain.start_b(quarters[0])

        def before_norm():
            attn_chain.start_b(pieces[0])

        outs = []
        project_back(
            r, 0, seqs, rows, r.norms[0, 0], attn_chain, after_pair, loading, before_norm=before_norm,
            before_first=before_first,
        )
        r.taps_rows[0:8] = r.taps_wide[...]
        r.taps_rows[8:16] = r.taps_above[...]
        r.norms_rows[...] = jnp.zeros_like(r.norms_rows)
        for at, (one, two) in enumerate(((r.norm_rows, r.norm_two), (r.norm_one_above, r.norm_two_above))):
            r.norms_rows[8 * at + 3 : 8 * at + 5] = one[3:5]
            r.norms_rows[8 * at + 5 : 8 * at + 7] = two[0:2]
        r.small_all[...] = jnp.zeros_like(r.small_all)
        for shard in range(2 * groups):
            taps_at, norms_at = 3 * shard_rows * shard, shard_rows * shard
            r.small_all[shard, :, 0 : 3 * shard_rows] = r.taps_rows[:, taps_at : taps_at + 3 * shard_rows]
            r.small_all[shard, :, LANES : LANES + shard_rows] = r.norms_rows[
                :, norms_at : norms_at + shard_rows
            ]
        for shard in range(groups):
            for owner, target in ((1 - r.core, r.small_send), (r.core, r.small_keep)):
                target[place_of(r, shard, owner)] = r.small_all[owner * groups + shard].astype(bf16)
        swap = r.send(r.small_send, r.small_got)
        r.result_v[...] = r.grad_v[...].astype(bf16)
        outs.append(r.local(r.result_v, r.result))
        chain.start_d(quarters[2])
        attn_chain.start_b(pieces[1])
        chain.start_c(quarters[3])
        attn_chain.start_c(out_piece)
        attn_chain.start_c(pieces[0])
        swap.wait()
        r.attn_sum_v[:, small_piece] = (
            r.small_keep[...].astype(f32) + r.small_got[...].astype(f32)
        ).astype(bf16)
        attn_chain.start_a(small_piece)
        for pair in range(2, pairs):
            attn_chain.start_b(pieces[pair])
        chain.start_d(quarters[3])
        attn_chain.start_d(out_piece)
        attn_chain.start_c(pieces[1])
        attn_chain.start_b(small_piece)
        attn_chain.start_d(pieces[0])
        for pair in range(2, pairs):
            attn_chain.start_c(pieces[pair])
        attn_chain.start_d(pieces[1])
        attn_chain.start_c(small_piece)
        set_out(r, attn_chain.end_d(out_piece), r.out_done_v)
        outs.append(r.local(r.out_done_v, r.out_done))
        for pair in range(2, pairs):
            attn_chain.start_d(pieces[pair])
        attn_chain.start_d(small_piece)
        set_ff(
            r, jnp.concatenate([chain.end_d(rows_of_ff) for rows_of_ff in quarters], 0),
            r.up_done_v, r.down_done_v,
        )
        outs += [r.local(r.up_done_v, r.up_done), r.local(r.down_done_v, r.down_done)]
        for pair in range(pairs):
            set_qkv(r, attn_chain.end_d(pieces[pair]), pair, r.qkv_done_v)
        outs.append(r.local(r.qkv_done_v, r.qkv_done))
        r.small_done_v[...] = attn_chain.end_d(small_piece)
        outs.append(r.local(r.small_done_v, r.small_done))
        wait_all(outs)
        chain.close()
        attn_chain.close()

    attn_all = small_piece.stop
    done["small_done"] = jax.ShapeDtypeStruct((16, half), f32)
    outputs = dict(result=jax.ShapeDtypeStruct(below.shape, bf16), **done)
    ff_got_a, ff_got_b, ff_got_z = chain_shapes(ff_rows, half)
    attn_got_a, attn_got_b, attn_got_z = chain_shapes(attn_all, half)
    piece = pltpu.VMEM((groups, 16, half), bf16)
    own, shared, operands = project_back_shapes(seqs, rows, width, below, groups)
    scratch = dict(
        **own,
        **shared,
        **operands,
        result_v=pltpu.VMEM((seqs, rows, width), bf16),
        taps_rows=pltpu.VMEM((16, 3 * width), f32),
        norms_rows=pltpu.VMEM((16, width), f32),
        small_all=pltpu.VMEM((2 * groups, 16, half), f32),
        small_send=piece, small_keep=piece, small_got=piece,
        ff_parts=pltpu.VMEM((8, ff_rows, half), bf16),
        ff_got_a=ff_got_a, ff_got_b=ff_got_b, ff_got_z=ff_got_z,
        **{name + "_v": pltpu.VMEM(shape.shape, f32) for name, shape in done.items()},
        attn_sum_v=pltpu.VMEM((groups, attn_all, half), bf16),
        attn_got_a=attn_got_a, attn_got_b=attn_got_b, attn_got_z=attn_got_z,
        partners=((), (0,), (1,), (2,), (3,)),
    )
    return stage(
        "leave", body,
        dict(
            **{name: array for name, array in saved.items() if name != "logs"}, grad_heads_in=grad_heads, grad_middle_in=grad_middle, out_grad_in=out_grad.reshape(groups, -1, half),
            ff_sum_in=ff_sum, ups_got=ups_got, w_qkv=weights_qkv,
        ),
        dict(
            **norms, logs=saved["logs"], norm_two=norm_two, **small_above,
        ),
        outputs, scratch, (70, 60), groups, collective_id,
        8 * seqs * rows * width * 3 * half, 40_000_000, lengths,
    )


def gather(whole, pairs, small, shard_rows):
    f32 = jnp.float32
    flat = list(whole) + [array for pair in pairs for array in pair]

    def kernel(*refs):
        ins, small_ref, refs = refs[: len(flat)], refs[len(flat)], refs[len(flat) + 1 :]
        outs, rooms = refs[: len(whole) + len(pairs) + 3], refs[len(whole) + len(pairs) + 3 : -2]
        targets = list(outs[: len(whole)])
        for out in outs[len(whole) : -3]:
            targets += [out.at[layer] for layer in range(LAYERS)]
        copies = []
        for at, room in enumerate(rooms):
            copies.append(pltpu.make_async_copy(ins[at], room, refs[-2].at[at]))
            copies[-1].start()
        taps_ref, gains_ref, biases_ref = outs[-3:]
        for layer in range(LAYERS):
            for lag in range(3):
                row = 8 * layer + lag
                taps_ref[lag, layer : layer + 1] = small_ref[row : row + 1, : 3 * shard_rows]
            for which in range(2):
                for out, row in ((gains_ref, 8 * layer + 3), (biases_ref, 8 * layer + 4)):
                    row += 2 * which
                    out[layer, which : which + 1] = small_ref[row : row + 1, LANES : LANES + shard_rows]
        for at, room in enumerate(rooms):
            copies[at].wait()
            copies[at] = pltpu.make_async_copy(room, targets[at], refs[-1].at[at])
            copies[at].start()
        for copy in copies:
            copy.wait()

    anywhere = pl.BlockSpec(memory_space=pl.ANY)
    vmem = pl.BlockSpec(memory_space=pltpu.VMEM)
    shapes = [jax.ShapeDtypeStruct(array.shape, array.dtype) for array in whole]
    shapes += [jax.ShapeDtypeStruct((LAYERS, *pair[0].shape), f32) for pair in pairs]
    shapes += [
        jax.ShapeDtypeStruct(shape, f32)
        for shape in ((3, LAYERS, 3 * shard_rows), (LAYERS, 2, shard_rows), (LAYERS, 2, shard_rows))
    ]
    return pl.pallas_call(
        kernel,
        in_specs=[anywhere] * len(flat) + [vmem],
        out_specs=[anywhere] * (len(shapes) - 3) + [vmem] * 3,
        out_shape=shapes,
        scratch_shapes=[pltpu.VMEM(array.shape, array.dtype) for array in flat]
        + [pltpu.SemaphoreType.DMA((len(flat),))] * 2,
        compiler_params=pltpu.CompilerParams(vmem_limit_bytes=VMEM_LIMIT),
        name="gather",
    )(*flat, small)


def local_pair(
    activations,
    cotangent,
    lengths,
    weights_qkv,
    conv_taps,
    weights_out,
    weights_up,
    weights_down,
    norm_gains,
    norm_biases,
):
    seqs, rows, width = activations.shape
    ff = weights_up.shape[2]
    groups = lax.axis_size("batch")
    norms = dict(
        all_taps=conv_taps.transpose(2, 0, 1),
        gains=norm_gains.transpose(0, 2, 1),
        biases=norm_biases.transpose(0, 2, 1),
    )
    weights = dict(w_out=weights_out, w_up=weights_up, w_down=weights_down)

    def saved(mixed, proj, attn, heads, logs, below):
        return dict(mixed=mixed, proj=proj, attn=attn, heads_in=heads, logs=logs, below=below)

    mixed0, proj0, attn0, mixed1, proj1, attn1, heads0, logs0, middle0, ff_in0, positive0, stream1 = feed_forward(
        lengths, activations, dict(**weights, w_qkv=weights_qkv), norms, groups, 1
    )
    ff_sum1, grad_middle1, norm_two1, grad_heads1, out_grad1, heads1, logs1, block_out = turn(
        1, lengths, mixed1, stream1, cotangent, weights, norms, groups, 2
    )
    lower = dict(positive=positive0, middle=middle0, ff_in=ff_in0, heads=heads0)
    ff_sum0, grad_middle0, norm_two0, grad_heads0, out_grad0, norm_one1, taps1, ups_got, qkv1, out1, up1, down1 = (
        back_link(
            1, lengths, saved(mixed1, proj1, attn1, heads1, logs1, stream1), grad_heads1, out_grad1,
            grad_middle1, ff_sum1, lower, weights_qkv, weights, norms, groups, 3,
        )
    )
    above = dict(norm_one_above=norm_one1, norm_two_above=norm_two1, taps_above=taps1)
    grad_input, qkv0, out0, up0, down0, small = leave(
        lengths, saved(mixed0, proj0, attn0, heads0, logs0, activations), grad_heads0, out_grad0, grad_middle0,
        ff_sum0, ups_got, norm_two0, above, weights_qkv, norms, ff, groups, 4,
    )
    block_out, grad_input, qkv, out, up, down, grad_taps, grad_gains, grad_biases = gather(
        (block_out, grad_input), ((qkv0, qkv1), (out0, out1), (up0, up1), (down0, down1)), small, up0.shape[0]
    )
    return (
        block_out,
        grad_input,
        qkv,
        grad_taps.transpose(1, 2, 0),
        out,
        up,
        down,
        grad_gains.transpose(0, 2, 1),
        grad_biases.transpose(0, 2, 1),
    )


def solution(mesh):
    chosen = local_pair if (mesh.shape["seq"], mesh.shape["batch"]) == (2, 16) else local
    placed = (
        P("batch", "seq", None),
        P("batch", "seq", None),
        P("batch"),
        P(),
        P(),
        P(),
        P(),
        P(),
        P(),
        P(),
    )
    return jax.shard_map(
        chosen,
        mesh=mesh,
        in_specs=placed,
        out_specs=(
            P("batch", "seq", None),
            P("batch", "seq", None),
            P(None, ("seq", "batch"), None),
            P(None, ("seq", "batch"), None),
            P(None, ("seq", "batch"), None),
            P(None, ("seq", "batch"), None),
            P(None, ("seq", "batch"), None),
            P(None, ("seq", "batch"), None),
            P(None, ("seq", "batch"), None),
        ),
        check_vma=False,
    )
```
